512 devices in a mesh: sample: 16 (over y, core), atom: 32 (over x, z).
Axes of the slice: x: 4, y: 8, z: 8, core: 2. Of those that a mesh axis runs over, the one named last changes fastest.
Arguments:
- positions: float32 [3, 131072], P(None, ('sample', 'atom')), parts along dimension 1, may hold values from -6 to 6
- fresh_noise: float32 [3, 131072], P(None, ('sample', 'atom')), parts along dimension 1, may hold values from -6 to 6
- timestep: int32 [1], replicated, may hold values from 0 to 199
- atom_single: bfloat16 [8192, 128], P('atom'), may hold values from -6 to 6
- pos_weight: float32 [3, 128], replicated, may hold values from -3.5 to 3.5
- ln_gain: float32 [2, 2, 128], replicated, may hold values from 0.1 to 1.9
- w_query: bfloat16 [2, 128, 128], replicated
- w_key: bfloat16 [2, 128, 128], replicated
- w_value: bfloat16 [2, 128, 128], replicated, may hold values from -0.5 to 0.5
- w_out: bfloat16 [2, 128, 128], replicated, may hold values from -0.5 to 0.5
- w_gate_up: bfloat16 [2, 128, 512], replicated, may hold values from -0.5 to 0.5
- w_down: bfloat16 [2, 256, 128], replicated, may hold values from -0.375 to 0.375
- w_head: float32 [3, 128], replicated, may hold values from -0.5 to 0.5
- key_window: int32 [64, 8], P('atom'), may hold values from 0 to 63, as said below
- block_pairs: int32 [2, 2048], P(None, 'atom'), may hold values from 0 to 63, as said below
- pair_count: int32 [32], P('atom'), may hold values from 0 to 64, as said below
- bond_atoms: int32 [2, 64, 128], P(None, 'atom'), may hold values from 0 to 127
Outputs:
- next_positions: float32 [3, 131072], P(None, ('sample', 'atom')), parts along dimension 1
The draws below stay inside these ranges and needn't reach their ends.
There are 16 independent parts, one for each index of `sample`. The reference program is written for one: setup_inputs(seed, part) draws one part's arguments, and reference() takes and returns one part's arrays. A program takes and returns all parts, laid end to end along the dimension named above; an argument that names none is the same for every part. Nothing has to cross between parts.
Inputs may be any that keep to these rules, and one draw needn't show every extreme that they name: `key_window`: every entry lies within 2 blocks of its row's block; in every row both distances 2 below and above are used where the grid has them, and the row's own block is in it. `block_pairs`: the two blocks of a column differ. Among the live columns of one owner, at most 6 of the entries of both rows together name blocks of one device (blocks d * 2 to (d + 1) * 2 - 1), and the owner with 64 live columns has exactly 6 on some device. `pair_count`: the entries sum to exactly 512.
All inputs are finite; a program needn't handle non-finite values.
Results may differ from the reference program's by a relative error of at most 0.0015.
Values may be sent and summed in bfloat16 or wider, within the bound.
No kernel may reach another device: no remote copies, remote signals or barrier semaphores. Data moves between devices by JAX's collectives and lax.ppermute only.
A program may use at most 64 MiB of HBM per device.

```python
import jax
import jax.numpy as jnp
from jax import lax

C = 128
HEADS = 4
FF = 256
ABLK = 128
WIN = 8
LAYERS = 2
NBOND = 128
BLK_DEV = 2
PAIR_MEAN = 16
PAIR_DEV = 64
PAIR_CAP = 6
NBLK = 64
ATOMS = 8192
PAIRS = 2048
N_ATOM = 32


def draw_w_query(key, part):
    key = jax.random.fold_in(key, 3)
    own = jax.random.normal(key, (LAYERS, C, C), jnp.float32)
    mixed = own * (1.4 * C ** (-0.5))
    return mixed.astype(jnp.bfloat16)


def draw_w_key(key, part):
    key = jax.random.fold_in(key, 5)
    own = jax.random.normal(key, (LAYERS, C, C), jnp.float32)
    mixed = own * (1.4 * C ** (-0.5))
    return mixed.astype(jnp.bfloat16)


def draw_key_window(key, part):
    key = jax.random.fold_in(key, 7)
    blocks = jnp.arange(NBLK, dtype=jnp.int32)[:, None]
    offsets = jax.random.randint(key, (NBLK, WIN), -BLK_DEV, BLK_DEV + 1, dtype=jnp.int32)
    offsets = offsets.at[:, 0].set(0).at[:, 1].set(-BLK_DEV).at[:, 2].set(BLK_DEV)
    return jnp.clip(blocks + offsets, 0, NBLK - 1).astype(jnp.int32)


def owner_columns(key, owner):
    key = jax.random.fold_in(key, owner)
    pool_key, order_key, local_key, pick_key = jax.random.split(key, 4)
    pool_size = N_ATOM * PAIR_CAP
    pool = jax.random.permutation(pool_key, pool_size)
    devices = (pool // PAIR_CAP).astype(jnp.int32)
    forced = jax.random.randint(pick_key, (), 0, N_ATOM, dtype=jnp.int32)
    rank_keys = jnp.where(devices == forced, 0, 1 + jnp.arange(pool_size, dtype=jnp.int32))
    order = jnp.argsort(rank_keys, stable=True)
    taken = devices[order][:2 * PAIR_DEV]
    taken = jax.random.permutation(order_key, taken).reshape(2, PAIR_DEV)
    local = jax.random.randint(local_key, (2, PAIR_DEV), 0, BLK_DEV, dtype=jnp.int32)
    first = taken[0] * BLK_DEV + local[0]
    second_local = jnp.where((taken[0] == taken[1]) & (local[0] == local[1]), (local[1] + 1) % BLK_DEV, local[1])
    second = taken[1] * BLK_DEV + second_local
    return jnp.stack([first, second]).astype(jnp.int32)


def draw_block_pairs(key, part):
    key = jax.random.fold_in(key, 9)
    owners = jnp.arange(N_ATOM, dtype=jnp.int32)
    columns = jax.vmap(lambda owner: owner_columns(key, owner))(owners)
    return jnp.moveaxis(columns, 1, 0).reshape(2, PAIRS).astype(jnp.int32)


def draw_pair_count(key, part):
    key = jax.random.fold_in(key, 11)
    shift_key, order_key = jax.random.split(key)
    others = N_ATOM - 1
    remainder = (N_ATOM - 4) * PAIR_MEAN
    base = remainder // others
    extra = remainder - base * others
    counts = base + (jnp.arange(others, dtype=jnp.int32) < extra).astype(jnp.int32)
    halves = others // 2
    spread = base // 2
    shifts = jax.random.randint(shift_key, (halves,), -spread, spread + 1, dtype=jnp.int32)
    counts = counts.at[0:2 * halves:2].add(shifts)
    counts = counts.at[1:2 * halves:2].add(-shifts)
    full = jnp.concatenate([jnp.full((1,), PAIR_DEV, jnp.int32), counts])
    order = jax.random.permutation(order_key, N_ATOM)
    return full[order].astype(jnp.int32)


def set_ends(drawn, own_key, smallest, largest):
    longest = drawn.shape.index(max(drawn.shape))
    spots = []
    for shift in (0, 1):
        where = [jax.random.randint(jax.random.fold_in(own_key, axis), (), 0, length) for axis, length in enumerate(drawn.shape)]
        where[longest] = (where[longest] + shift) % drawn.shape[longest]
        spots.append(tuple(where))
    return drawn.at[spots[0]].set(smallest).at[spots[1]].set(largest)


def block_levels(rng, shape, pieces, low, largest):
    def one(position, parts):
        draws = jax.random.uniform(jax.random.fold_in(jax.random.fold_in(rng, 6), position), (parts,), jnp.float32, low / len(pieces), largest / len(pieces))
        return jnp.repeat(jnp.exp(draws), shape[position] // parts).reshape((-1,) + (1,) * (len(shape) - position - 1))

    factor_of = one(*pieces[0])
    for cut in pieces[1:]:
        factor_of = factor_of * one(*cut)
    return factor_of


def centred(key, dims, scale, bound, shards=(), kind=jnp.bfloat16):
    values = scale * jax.random.normal(key, dims, jnp.float32)
    if shards:
        values = values * block_levels(key, dims, shards, -0.22, 0.18)
    return jnp.clip(values, -bound, bound).astype(kind)


def setup_inputs(seed: int = 0, part: int = 0) -> dict:
    streams_of = jax.random.split(jax.random.key(seed), 18)
    part_keys = jax.random.split(jax.random.fold_in(streams_of[17], part), 18)
    return {
        "positions": centred(part_keys[0], (3, ATOMS), 1.0, 6.0, ((1, 32),), jnp.float32),
        "fresh_noise": centred(part_keys[1], (3, ATOMS), 1.0, 6.0, ((1, 32),), jnp.float32),
        "timestep": jax.random.randint(streams_of[2], (1,), 0, 200).astype(jnp.int32),
        "atom_single": centred(streams_of[3], (ATOMS, C), 1.0, 6.0, ((0, 32),)),
        "pos_weight": centred(streams_of[4], (3, C), 3 ** -0.5, 3.5, (), jnp.float32),
        "ln_gain": jnp.clip(1.0 + 0.18 * jax.random.normal(streams_of[5], (LAYERS, 2, C), jnp.float32), 0.1, 1.9),
        "w_query": draw_w_query(jax.random.fold_in(streams_of[17], 71), part),
        "w_key": draw_w_key(jax.random.fold_in(streams_of[17], 71), part),
        "w_value": centred(streams_of[8], (LAYERS, C, C), C ** -0.5, 0.5),
        "w_out": centred(streams_of[9], (LAYERS, C, C), C ** -0.5, 0.5),
        "w_gate_up": centred(streams_of[10], (LAYERS, C, 2 * FF), C ** -0.5, 0.5),
        "w_down": centred(streams_of[11], (LAYERS, FF, C), FF ** -0.5, 0.375),
        "w_head": centred(streams_of[12], (3, C), C ** -0.5, 0.5, (), jnp.float32),
        "key_window": draw_key_window(jax.random.fold_in(streams_of[17], 71), part),
        "block_pairs": draw_block_pairs(jax.random.fold_in(streams_of[17], 71), part),
        "pair_count": draw_pair_count(jax.random.fold_in(streams_of[17], 71), part),
        "bond_atoms": set_ends(jax.random.randint(streams_of[16], (2, NBLK, NBOND), 0, ABLK), jax.random.fold_in(streams_of[16], 1), 0, ABLK - 1).astype(jnp.int32),
    }


clash_strength = 1.0
clash_width_sq = 0.25
bond_stiffness = 0.05
bond_rest = 1.0
steer_scale = 0.3
norm_eps = 1e-05

def layer_norm(values_in):
    center = values_in - lax.optimization_barrier(jnp.mean(values_in, axis=-1, keepdims=True))
    spread = lax.optimization_barrier(jnp.mean(center * center, axis=-1, keepdims=True))
    return center / jnp.sqrt(spread + norm_eps)

def tile_forces(first_block, second_block):
    offsets = first_block[:, :, None] - second_block[:, None, :]
    dist_sq = lax.optimization_barrier(jnp.sum(offsets * offsets, axis=0))
    weights_tile = 2.0 * clash_strength / clash_width_sq * jnp.exp(-dist_sq / clash_width_sq)
    pushed = weights_tile[None] * offsets
    return jnp.stack([lax.optimization_barrier(jnp.sum(pushed, axis=2)), -lax.optimization_barrier(jnp.sum(pushed, axis=1))])

def pair_canvas(blocks_all, chosen, live_mask):

    def one_pair(column):
        return tile_forces(blocks_all[:, column[0]], blocks_all[:, column[1]])
    tiles = lax.map(one_pair, chosen.T) * live_mask[:, None, None, None]
    canvas = jnp.zeros(blocks_all.shape, jnp.float32)
    canvas = canvas.at[:, chosen[0]].add(jnp.moveaxis(tiles[:, 0], 0, 1))
    canvas = canvas.at[:, chosen[1]].add(jnp.moveaxis(tiles[:, 1], 0, 1))
    return canvas

def bond_forces(blocks, bond_atoms):
    first_atoms = jnp.take_along_axis(blocks, bond_atoms[0][None], axis=2)
    second_atoms = jnp.take_along_axis(blocks, bond_atoms[1][None], axis=2)
    offsets = first_atoms - second_atoms
    stretch = lax.optimization_barrier(jnp.sum(offsets * offsets, axis=0)) - bond_rest
    pulls = -4.0 * bond_stiffness * stretch[None] * offsets
    atom_ids = jnp.arange(blocks.shape[2], dtype=jnp.int32)
    incidence = (bond_atoms[0][..., None] == atom_ids).astype(jnp.float32) - (bond_atoms[1][..., None] == atom_ids).astype(jnp.float32)
    return jnp.einsum('cbm,bma->cba', pulls, incidence, precision=lax.Precision.HIGHEST)

def attend_all(queries, key_rows, value_rows, key_window):
    head_size = C // HEADS
    query_blocks = queries.reshape(NBLK, ABLK, C)
    key_blocks = key_rows.reshape(NBLK, ABLK, C)
    value_blocks = value_rows.reshape(NBLK, ABLK, C)

    def one_block(inputs):
        query_block, window = inputs
        keys_here = key_blocks[window].reshape(WIN * ABLK, HEADS, head_size).astype(jnp.float32)
        values_here = value_blocks[window].reshape(WIN * ABLK, HEADS, head_size).astype(jnp.float32)
        query_heads = query_block.reshape(ABLK, HEADS, head_size).astype(jnp.float32)
        scores = jnp.einsum('qhd,khd->hqk', query_heads, keys_here) * head_size ** (-0.5)
        weights = jax.nn.softmax(scores, axis=-1).astype(jnp.bfloat16)
        weights = lax.optimization_barrier(weights).astype(jnp.float32)
        mixed = jnp.einsum('hqk,khd->qhd', weights, values_here)
        return mixed.reshape(ABLK, C).astype(jnp.bfloat16)
    return lax.map(one_block, (query_blocks, key_window)).reshape(ATOMS, C)

def reference(positions, fresh_noise, timestep, atom_single, pos_weight, ln_gain, w_query, w_key, w_value, w_out, w_gate_up, w_down, w_head, key_window, block_pairs, pair_count, bond_atoms):
    noise_level = 0.2 + 0.02 * timestep[0].astype(jnp.float32)
    next_level = 0.85 * noise_level
    spread_sq = noise_level * noise_level + 1.0
    c_input = 1.0 / jnp.sqrt(spread_sq)
    c_skip = 1.0 / spread_sq
    c_output = noise_level * c_input
    stream = atom_single.astype(jnp.float32) + jnp.dot((positions * c_input).T, pos_weight, precision=lax.Precision.HIGHEST, preferred_element_type=jnp.float32)
    for layer_index in range(LAYERS):
        normed = (layer_norm(stream) * ln_gain[layer_index, 0]).astype(jnp.bfloat16)
        queries = jnp.dot(normed, w_query[layer_index], preferred_element_type=jnp.float32).astype(jnp.bfloat16)
        key_rows = jnp.dot(normed, w_key[layer_index], preferred_element_type=jnp.float32).astype(jnp.bfloat16)
        value_rows = jnp.dot(normed, w_value[layer_index], preferred_element_type=jnp.float32).astype(jnp.bfloat16)
        attended = attend_all(queries, key_rows, value_rows, key_window)
        stream = stream + jnp.dot(attended, w_out[layer_index], preferred_element_type=jnp.float32)
        normed_two = (layer_norm(stream) * ln_gain[layer_index, 1]).astype(jnp.bfloat16)
        gate_up = jnp.dot(normed_two, w_gate_up[layer_index], preferred_element_type=jnp.float32)
        hidden = (jax.nn.silu(gate_up[:, :FF]) * gate_up[:, FF:]).astype(jnp.bfloat16)
        stream = stream + jnp.dot(hidden, w_down[layer_index], preferred_element_type=jnp.float32)
    final_normed = layer_norm(stream)
    update = jnp.dot(w_head, final_normed.T, precision=lax.Precision.HIGHEST, preferred_element_type=jnp.float32)
    denoised = c_skip * positions + c_output * update
    blocks_all = positions.reshape(3, NBLK, ABLK)
    slot_ids = jnp.arange(PAIRS, dtype=jnp.int32) % PAIR_DEV
    owner_ids = jnp.arange(PAIRS, dtype=jnp.int32) // PAIR_DEV
    live_mask = (slot_ids < pair_count[owner_ids]).astype(jnp.float32)
    clash_force = pair_canvas(blocks_all, block_pairs, live_mask)
    total_force = (clash_force + bond_forces(blocks_all, bond_atoms)).reshape(3, ATOMS)
    steered = denoised + steer_scale * total_force
    return steered + next_level * (0.8 * (positions - denoised) / noise_level + 0.6 * fresh_noise)
```

```python
import functools
import math

import jax
import jax.numpy as jnp
from jax import lax
from jax.experimental import pallas as pl
from jax.experimental.pallas import tpu as pltpu
from jax.sharding import PartitionSpec as P

HEADS = 4
LANES = 128
NORM_EPS = 1e-05
STEER = 0.3
ABSENT = -1e30
LOG2E = 1.4426950408889634
KAPPA = 2.0 * math.sqrt(LOG2E)

f32 = jnp.float32
bf16 = jnp.bfloat16


def pack_kernel(first_ref, count_ref, positions_ref, pairs_ref, window_ref, out_ref, tile):
    for row in range(6):
        part = slice((row % 2) * LANES, (row % 2 + 1) * LANES)
        tile[row : row + 1, :] = positions_ref[row // 2 : row // 2 + 1, part]
    pairs = pairs_ref[...]
    lane = lax.broadcasted_iota(jnp.int32, (1, pairs.shape[1]), 1)
    codes = jnp.where(lane < count_ref[0], pairs[0:1] * 64 + pairs[1:2], -1).astype(f32)
    tile[6:7, :] = jnp.concatenate([codes, codes], axis=1)
    window = window_ref[...]
    own = first_ref[0] * 2 + lax.broadcasted_iota(jnp.int32, window.shape, 0)
    lane = lax.broadcasted_iota(jnp.int32, (1, LANES), 1)
    counts = jnp.zeros((1, LANES), f32)
    for offset in range(5):
        hit = jnp.sum((window == own + (offset - 2)).astype(f32), axis=1, keepdims=True)
        counts = jnp.where(lane == offset, hit[0:1], counts)
        counts = jnp.where(lane == 8 + offset, hit[1:2], counts)
    tile[7:8, :] = jnp.where(counts > 0.0, jnp.log2(jnp.maximum(counts, 1.0)), ABSENT)
    out_ref[...] = jnp.broadcast_to(tile[...][None], out_ref.shape)


def split3(values):
    high = values.astype(bf16)
    rest = values - high.astype(f32)
    mid = rest.astype(bf16)
    low = (rest - mid.astype(f32)).astype(bf16)
    return jnp.concatenate([high, mid, low], axis=0)


def join3(values):
    rows = values.shape[0] // 3
    return values[:rows] + values[rows : 2 * rows] + values[2 * rows :]


def norm_columns(values):
    center = values - jnp.mean(values, axis=0, keepdims=True)
    spread = jnp.mean(center * center, axis=0, keepdims=True)
    return center * lax.rsqrt(spread + NORM_EPS)


def dot_t(left, right):
    return lax.dot_general(left, right, (((0,), (0,)), ((), ())), preferred_element_type=f32)


def dot_nt(left, right):
    return lax.dot_general(left, right, (((1,), (1,)), ((), ())), preferred_element_type=f32)


def dot(left, right):
    return jnp.dot(left, right, preferred_element_type=f32)


def step_kernel(
    first_ref,
    time_ref,
    tiles_ref,
    left2_ref,
    left1_ref,
    own_ref,
    right1_ref,
    right2_ref,
    positions_ref,
    noise_ref,
    pos_weight_ref,
    gain_ref,
    w_query_ref,
    w_key_ref,
    w_value_ref,
    w_out_ref,
    w_gate_up_ref,
    w_down_ref,
    w_head_ref,
    bonds_ref,
    out_ref,
    stream,
    queries,
    keys,
    values,
    spread_own,
    push,
    list_v,
    bias_v,
    list_s,
    bias_s,
    sems,
):
    me = first_ref[0]
    last = tiles_ref.shape[0] - 1

    codes = tiles_ref[:, 6, :].astype(jnp.int32)
    half = lax.broadcasted_iota(jnp.int32, codes.shape, 1) // 64
    mine = me * 2 + half
    first = jnp.where(codes < 0, -1, codes // 64)
    second = jnp.where(codes < 0, -1, codes % 64)
    partner = jnp.where(first == mine, second, jnp.where(second == mine, first, -1)).astype(f32)
    block_id = lax.broadcasted_iota(jnp.int32, (64, LANES), 0).astype(f32)
    hits = jnp.zeros((64, LANES), f32)
    for row in range(codes.shape[0]):
        hits = hits + jnp.where(partner[row : row + 1] == block_id, 1.0, 0.0)
    row_half = lax.broadcasted_iota(jnp.int32, (LANES, LANES), 0) // 64
    col_half = lax.broadcasted_iota(jnp.int32, (LANES, LANES), 1) // 64
    count = dot(hits.astype(bf16), (row_half == col_half).astype(bf16))
    present = count > 0.5
    lower = lax.broadcasted_iota(jnp.int32, (64, 64), 1) < lax.broadcasted_iota(jnp.int32, (64, 64), 0)
    rank = dot(lower.astype(bf16), present.astype(bf16))
    slot = (lax.broadcasted_iota(jnp.int32, (64, LANES), 1) % 64).astype(f32)
    chosen = present & (rank == slot)
    listed = jnp.sum(jnp.where(chosen, block_id, 0.0), axis=0, keepdims=True)
    times = jnp.sum(jnp.where(chosen, count, 0.0), axis=0, keepdims=True)
    total = jnp.sum(present.astype(f32), axis=0, keepdims=True)
    list_v[0:1, :] = listed.astype(jnp.int32)
    list_v[1:2, :] = total.astype(jnp.int32)
    bias_v[0:1, :] = jnp.where(times > 0.5, jnp.log2(jnp.maximum(times, 1.0)), ABSENT)
    list_copy = pltpu.make_async_copy(list_v, list_s, sems.at[0])
    bias_copy = pltpu.make_async_copy(bias_v, bias_s, sems.at[1])
    list_copy.start()
    bias_copy.start()

    level = 0.2 + 0.02 * jnp.full((1, 2 * LANES), time_ref[0], jnp.int32).astype(f32)
    spread_sq = level * level + 1.0
    c_input = 1.0 / jnp.sqrt(spread_sq)

    weight_columns = jnp.concatenate([pos_weight_ref[...], jnp.zeros((5, LANES), f32)], axis=0).T
    for place, ref in enumerate((left2_ref, left1_ref, own_ref, right1_ref, right2_ref)):
        device = jnp.clip(me + (place - 2), 0, last)
        total_t = ref[...].astype(f32).T
        for comp in range(3):
            row = jnp.concatenate(
                [tiles_ref[device, 2 * comp : 2 * comp + 1, :], tiles_ref[device, 2 * comp + 1 : 2 * comp + 2, :]],
                axis=1,
            )
            total_t = total_t + weight_columns[:, comp : comp + 1] * (row * c_input)
        stream[place] = total_t

    gain_columns = jnp.concatenate(
        [gain_ref[0], gain_ref[1], jnp.zeros((4, LANES), f32)], axis=0
    ).T
    query_scale = LOG2E * (LANES // HEADS) ** -0.5
    head_size = LANES // HEADS
    ones_rows = jnp.ones((16, 2 * LANES), bf16)

    for layer in range(2):
        gain_a = gain_columns[:, 2 * layer : 2 * layer + 1]
        gain_b = gain_columns[:, 2 * layer + 1 : 2 * layer + 2]
        low, high = layer, 5 - layer

        def project(place, carry, layer=layer, gain_a=gain_a):
            normed = (norm_columns(stream[place]) * gain_a).astype(bf16)
            keys[place] = dot_t(normed, w_key_ref[layer]).astype(bf16)
            value_t = dot_t(w_value_ref[layer], normed).astype(bf16)
            for head in range(HEADS):
                values[place, head * 48 : head * 48 + 32, :] = value_t[head * 32 : head * 32 + 32]
                values[place, head * 48 + 32 : head * 48 + 48, :] = ones_rows
            queries[place] = (dot_t(w_query_ref[layer], normed) * query_scale).astype(bf16)
            return carry

        lax.fori_loop(low, high, project, 0)

        def mix(place, carry, layer=layer, gain_b=gain_b):
            device = jnp.clip(me + (place - 2), 0, last)
            window = tiles_ref[device, 7:8, :]
            query_t = queries[place]
            pieces = []
            for head in range(HEADS):
                parts = []
                if head:
                    parts.append(jnp.zeros((head * head_size, 2 * LANES), bf16))
                parts.append(query_t[head * head_size : (head + 1) * head_size])
                if head < HEADS - 1:
                    parts.append(jnp.zeros(((HEADS - 1 - head) * head_size, 2 * LANES), bf16))
                masked = jnp.concatenate(parts, axis=0)
                scores = [dot(keys[place - 1 + j], masked) for j in range(3)]
                weights = []
                for block in range(2):
                    lanes = slice(block * LANES, (block + 1) * LANES)
                    tiles = []
                    for offset in range(5):
                        chunk = block + offset
                        tile = scores[chunk // 2][(chunk % 2) * LANES : (chunk % 2 + 1) * LANES, lanes]
                        tiles.append(tile + window[:, block * 8 + offset : block * 8 + offset + 1])
                    top = functools.reduce(jnp.maximum, tiles)
                    top = jnp.max(top, axis=0, keepdims=True)
                    blank = [jnp.zeros((LANES, LANES), bf16)]
                    tiles = [jnp.exp2(tile - top).astype(bf16) for tile in tiles]
                    weights.append(blank + tiles if block else tiles + blank)
                mixed = None
                for j in range(3):
                    weight = jnp.concatenate(
                        [
                            jnp.concatenate([weights[0][2 * j], weights[1][2 * j]], axis=1),
                            jnp.concatenate([weights[0][2 * j + 1], weights[1][2 * j + 1]], axis=1),
                        ],
                        axis=0,
                    )
                    part = dot(values[place - 1 + j, head * 48 : (head + 1) * 48, :], weight)
                    mixed = part if mixed is None else mixed + part
                pieces.append(mixed[:head_size] * (1.0 / mixed[head_size : head_size + 1]))
            attended = jnp.concatenate(pieces, axis=0).astype(bf16)
            now = stream[place] + dot_t(w_out_ref[layer], attended)
            normed = (norm_columns(now) * gain_b).astype(bf16)
            gate_up = dot_t(w_gate_up_ref[layer], normed)
            width = gate_up.shape[0] // 2
            gate, up = gate_up[:width], gate_up[width:]
            hidden = (gate / (1.0 + jnp.exp2(gate * -LOG2E)) * up).astype(bf16)
            stream[place] = now + dot_t(w_down_ref[layer], hidden)
            return carry

        lax.fori_loop(low + 1, high - 1, mix, 0)

    final = norm_columns(stream[2])
    head_rows = jnp.concatenate([w_head_ref[...], jnp.zeros((5, LANES), f32)], axis=0)
    update = jnp.dot(head_rows, final, precision=lax.Precision.HIGHEST, preferred_element_type=f32)

    positions = jnp.concatenate([positions_ref[...], jnp.zeros((5, 2 * LANES), f32)], axis=0)
    fresh = jnp.concatenate([noise_ref[...], jnp.zeros((5, 2 * LANES), f32)], axis=0)

    forces = []
    atom_id = lax.broadcasted_iota(jnp.int32, (LANES, LANES), 0)
    for block in range(2):
        incidence = (
            (atom_id == bonds_ref[0, block : block + 1, :]).astype(f32)
            - (atom_id == bonds_ref[1, block : block + 1, :]).astype(f32)
        ).astype(bf16)
        offset = join3(dot(split3(positions[:, block * LANES : (block + 1) * LANES]), incidence))
        stretch = jnp.sum(offset * offset, axis=0, keepdims=True) - 1.0
        pull = (-0.2 * stretch) * offset
        forces.append(join3(dot_nt(split3(pull), incidence)))

    list_copy.wait()
    bias_copy.wait()
    for block in range(2):
        for comp in range(3):
            row = positions_ref[comp : comp + 1, block * LANES : (block + 1) * LANES] * KAPPA
            spread_own[comp] = jnp.broadcast_to(row, (LANES, LANES)).T
            push[comp] = jnp.zeros((LANES, LANES), f32)

        def one_pair(index, carry, block=block):
            partners = []
            for sub in range(2):
                entry = block * 64 + 2 * index + sub
                partner = list_s[0, entry]
                device = partner // 2
                within = partner % 2
                rows = [
                    tiles_ref[device, pl.ds(2 * comp + within, 1), :] * KAPPA for comp in range(3)
                ]
                partners.append((rows, bias_s[0, entry]))
            for group in range(0, LANES, 8):
                own = [spread_own[comp, group : group + 8, :] for comp in range(3)]
                sums = [push[comp, group : group + 8, :] for comp in range(3)]
                for rows, bias in partners:
                    offset = [own[comp] - rows[comp] for comp in range(3)]
                    power = bias - offset[0] * offset[0]
                    power = power - offset[1] * offset[1]
                    power = power - offset[2] * offset[2]
                    weight = jnp.exp2(power)
                    sums = [sums[comp] + weight * offset[comp] for comp in range(3)]
                for comp in range(3):
                    push[comp, group : group + 8, :] = sums[comp]
            return carry

        lax.fori_loop(0, (list_s[1, block * 64] + 1) // 2, one_pair, 0)
        rows = [jnp.sum(push[comp].T, axis=0, keepdims=True) for comp in range(3)]
        clash = jnp.concatenate(rows + [jnp.zeros((5, LANES), f32)], axis=0)
        forces[block] = forces[block] + clash * (8.0 / KAPPA)
    force = jnp.concatenate(forces, axis=1)

    denoised = positions * (1.0 / spread_sq) + (level * c_input) * update
    following = 0.85 * level
    result = denoised + STEER * force + following * (0.8 * (positions - denoised) / level + 0.6 * fresh)
    out_ref[...] = result[:3]


def body(
    positions,
    fresh_noise,
    timestep,
    atom_single,
    pos_weight,
    ln_gain,
    w_query,
    w_key,
    w_value,
    w_out,
    w_gate_up,
    w_down,
    w_head,
    key_window,
    block_pairs,
    pair_count,
    bond_atoms,
):
    devices = lax.axis_size("atom")
    first = lax.axis_index("atom").astype(jnp.int32).reshape(1)
    smem = pl.BlockSpec(memory_space=pltpu.SMEM)
    vmem = pl.BlockSpec(memory_space=pltpu.VMEM)

    def shifted(array, shift):
        pairs = [(i, (i + shift) % devices) for i in range(devices)]
        return lax.ppermute(array, "atom", pairs)

    left1 = shifted(atom_single, 1)
    right1 = shifted(atom_single, -1)
    left2 = shifted(atom_single, 2)
    right2 = shifted(atom_single, -2)

    packed = pl.pallas_call(
        pack_kernel,
        out_shape=jax.ShapeDtypeStruct((devices, 8, LANES), f32),
        in_specs=[smem, smem, vmem, vmem, vmem],
        out_specs=vmem,
        scratch_shapes=[pltpu.VMEM((8, LANES), f32)],
    )(first, pair_count, positions, block_pairs, key_window)
    tiles = lax.all_to_all(packed, "atom", 0, 0)

    wide = (5, LANES, 2 * LANES)
    return pl.pallas_call(
        step_kernel,
        out_shape=jax.ShapeDtypeStruct(positions.shape, f32),
        in_specs=[smem, smem] + [vmem] * 18,
        out_specs=vmem,
        scratch_shapes=[
            pltpu.VMEM(wide, f32),
            pltpu.VMEM(wide, bf16),
            pltpu.VMEM((5, 2 * LANES, LANES), bf16),
            pltpu.VMEM((5, HEADS * 48, 2 * LANES), bf16),
            pltpu.VMEM((3, LANES, LANES), f32),
            pltpu.VMEM((3, LANES, LANES), f32),
            pltpu.VMEM((8, LANES), jnp.int32),
            pltpu.VMEM((8, LANES), f32),
            pltpu.SMEM((8, LANES), jnp.int32),
            pltpu.SMEM((8, LANES), f32),
            pltpu.SemaphoreType.DMA((2,)),
        ],
        compiler_params=pltpu.CompilerParams(vmem_limit_bytes=32 * 1024 * 1024),
    )(
        first,
        timestep,
        tiles,
        left2,
        left1,
        atom_single,
        right1,
        right2,
        positions,
        fresh_noise,
        pos_weight,
        ln_gain,
        w_query,
        w_key,
        w_value,
        w_out,
        w_gate_up,
        w_down,
        w_head,
        bond_atoms,
    )


def solution(mesh):
    in_specs = (
        P(None, ("sample", "atom")),
        P(None, ("sample", "atom")),
        P(),
        P("atom", None),
        P(),
        P(),
        P(),
        P(),
        P(),
        P(),
        P(),
        P(),
        P(),
        P("atom", None),
        P(None, "atom"),
        P("atom"),
        P(None, "atom", None),
    )
    out_specs = P(None, ("sample", "atom"))
    return jax.shard_map(body, mesh=mesh, in_specs=in_specs, out_specs=out_specs, check_vma=False)
```

```python
import functools
import math

import jax
import jax.numpy as jnp
from jax import lax
from jax.experimental import pallas as pl
from jax.experimental.pallas import tpu as pltpu
from jax.sharding import PartitionSpec as P

HEADS = 4
LANES = 128
NORM_EPS = 1e-05
STEER = 0.3
ABSENT = -1e30
LOG2E = 1.4426950408889634
KAPPA = 2.0 * math.sqrt(LOG2E)

f32 = jnp.float32
bf16 = jnp.bfloat16


def pack_kernel(first_ref, count_ref, positions_ref, pairs_ref, window_ref, out_ref, tile):
    for row in range(6):
        part = slice((row % 2) * LANES, (row % 2 + 1) * LANES)
        tile[row : row + 1, :] = positions_ref[row // 2 : row // 2 + 1, part]
    pairs = pairs_ref[...]
    lane = lax.broadcasted_iota(jnp.int32, (1, pairs.shape[1]), 1)
    codes = jnp.where(lane < count_ref[0], pairs[0:1] * 64 + pairs[1:2], -1).astype(f32)
    tile[6:7, :] = jnp.concatenate([codes, codes], axis=1)
    window = window_ref[...]
    own = first_ref[0] * 2 + lax.broadcasted_iota(jnp.int32, window.shape, 0)
    lane = lax.broadcasted_iota(jnp.int32, (1, LANES), 1)
    counts = jnp.zeros((1, LANES), f32)
    for offset in range(5):
        hit = jnp.sum((window == own + (offset - 2)).astype(f32), axis=1, keepdims=True)
        counts = jnp.where(lane == offset, hit[0:1], counts)
        counts = jnp.where(lane == 8 + offset, hit[1:2], counts)
    tile[7:8, :] = jnp.where(counts > 0.0, jnp.log2(jnp.maximum(counts, 1.0)), ABSENT)
    out_ref[...] = jnp.broadcast_to(tile[...][None], out_ref.shape)


def split3(values):
    high = values.astype(bf16)
    rest = values - high.astype(f32)
    mid = rest.astype(bf16)
    low = (rest - mid.astype(f32)).astype(bf16)
    return jnp.concatenate([high, mid, low], axis=0)


def join3(values):
    rows = values.shape[0] // 3
    return values[:rows] + values[rows : 2 * rows] + values[2 * rows :]


def norm_columns(values):
    center = values - jnp.mean(values, axis=0, keepdims=True)
    spread = jnp.mean(center * center, axis=0, keepdims=True)
    return center * lax.rsqrt(spread + NORM_EPS)


def dot_t(left, right):
    return lax.dot_general(left, right, (((0,), (0,)), ((), ())), preferred_element_type=f32)


def dot_nt(left, right):
    return lax.dot_general(left, right, (((1,), (1,)), ((), ())), preferred_element_type=f32)


def dot(left, right):
    return jnp.dot(left, right, preferred_element_type=f32)


def force_kernel(first_ref, tiles_ref, positions_ref, bonds_ref, out_ref, spread_own, push, list_v, bias_v, list_s, bias_s, sems):
    me = first_ref[0]

    codes = tiles_ref[:, 6, :].astype(jnp.int32)
    half = lax.broadcasted_iota(jnp.int32, codes.shape, 1) // 64
    mine = me * 2 + half
    first = jnp.where(codes < 0, -1, codes // 64)
    second = jnp.where(codes < 0, -1, codes % 64)
    partner = jnp.where(first == mine, second, jnp.where(second == mine, first, -1)).astype(f32)
    block_id = lax.broadcasted_iota(jnp.int32, (64, LANES), 0).astype(f32)
    hits = jnp.zeros((64, LANES), f32)
    for row in range(codes.shape[0]):
        hits = hits + jnp.where(partner[row : row + 1] == block_id, 1.0, 0.0)
    row_half = lax.broadcasted_iota(jnp.int32, (LANES, LANES), 0) // 64
    col_half = lax.broadcasted_iota(jnp.int32, (LANES, LANES), 1) // 64
    count = dot(hits.astype(bf16), (row_half == col_half).astype(bf16))
    present = count > 0.5
    lower = lax.broadcasted_iota(jnp.int32, (64, 64), 1) < lax.broadcasted_iota(jnp.int32, (64, 64), 0)
    rank = dot(lower.astype(bf16), present.astype(bf16))
    slot = (lax.broadcasted_iota(jnp.int32, (64, LANES), 1) % 64).astype(f32)
    chosen = present & (rank == slot)
    listed = jnp.sum(jnp.where(chosen, block_id, 0.0), axis=0, keepdims=True)
    times = jnp.sum(jnp.where(chosen, count, 0.0), axis=0, keepdims=True)
    total = jnp.sum(present.astype(f32), axis=0, keepdims=True)
    list_v[0:1, :] = listed.astype(jnp.int32)
    list_v[1:2, :] = total.astype(jnp.int32)
    bias_v[0:1, :] = jnp.where(times > 0.5, jnp.log2(jnp.maximum(times, 1.0)), ABSENT)
    list_copy = pltpu.make_async_copy(list_v, list_s, sems.at[0])
    bias_copy = pltpu.make_async_copy(bias_v, bias_s, sems.at[1])
    list_copy.start()
    bias_copy.start()

    positions = jnp.concatenate([positions_ref[...], jnp.zeros((5, 2 * LANES), f32)], axis=0)

    forces = []
    atom_id = lax.broadcasted_iota(jnp.int32, (LANES, LANES), 0)
    for block in range(2):
        incidence = (
            (atom_id == bonds_ref[0, block : block + 1, :]).astype(f32)
            - (atom_id == bonds_ref[1, block : block + 1, :]).astype(f32)
        ).astype(bf16)
        offset = join3(dot(split3(positions[:, block * LANES : (block + 1) * LANES]), incidence))
        stretch = jnp.sum(offset * offset, axis=0, keepdims=True) - 1.0
        pull = (-0.2 * stretch) * offset
        forces.append(join3(dot_nt(split3(pull), incidence)))

    list_copy.wait()
    bias_copy.wait()
    for block in range(2):
        for comp in range(3):
            row = positions_ref[comp : comp + 1, block * LANES : (block + 1) * LANES] * KAPPA
            spread_own[comp] = jnp.broadcast_to(row, (LANES, LANES)).T
            push[comp] = jnp.zeros((LANES, LANES), f32)

        def one_pair(index, carry, block=block):
            partners = []
            for sub in range(2):
                entry = block * 64 + 2 * index + sub
                partner = list_s[0, entry]
                device = partner // 2
                within = partner % 2
                rows = [
                    tiles_ref[device, pl.ds(2 * comp + within, 1), :] * KAPPA for comp in range(3)
                ]
                partners.append((rows, bias_s[0, entry]))
            for group in range(0, LANES, 8):
                own = [spread_own[comp, group : group + 8, :] for comp in range(3)]
                sums = [push[comp, group : group + 8, :] for comp in range(3)]
                for rows, bias in partners:
                    offset = [own[comp] - rows[comp] for comp in range(3)]
                    power = bias - offset[0] * offset[0]
                    power = power - offset[1] * offset[1]
                    power = power - offset[2] * offset[2]
                    weight = jnp.exp2(power)
                    sums = [sums[comp] + weight * offset[comp] for comp in range(3)]
                for comp in range(3):
                    push[comp, group : group + 8, :] = sums[comp]
            return carry

        lax.fori_loop(0, (list_s[1, block * 64] + 1) // 2, one_pair, 0)
        rows = [jnp.sum(push[comp].T, axis=0, keepdims=True) for comp in range(3)]
        clash = jnp.concatenate(rows + [jnp.zeros((5, LANES), f32)], axis=0)
        forces[block] = forces[block] + clash * (8.0 / KAPPA)
    out_ref[...] = jnp.concatenate(forces, axis=1)


def step_kernel(
    first_ref,
    time_ref,
    tiles_ref,
    others_ref,
    own_ref,
    positions_ref,
    noise_ref,
    force_ref,
    pos_weight_ref,
    gain_ref,
    w_head_ref,
    w_query_hbm,
    w_key_hbm,
    w_value_hbm,
    w_out_hbm,
    w_gate_up_hbm,
    w_down_hbm,
    out_ref,
    stream,
    queries,
    keys,
    values,
    w_query_ref,
    w_key_ref,
    w_value_ref,
    w_out_ref,
    w_gate_up_ref,
    w_down_ref,
    sems,
):
    me = first_ref[0]
    last = tiles_ref.shape[0] - 1
    copies = [
        pltpu.make_async_copy(source, target, sems.at[index])
        for index, (source, target) in enumerate(
            (
                (w_key_hbm, w_key_ref),
                (w_value_hbm, w_value_ref),
                (w_query_hbm, w_query_ref),
                (w_out_hbm, w_out_ref),
                (w_gate_up_hbm, w_gate_up_ref),
                (w_down_hbm, w_down_ref),
            )
        )
    ]
    for copy in copies:
        copy.start()

    level = 0.2 + 0.02 * jnp.full((1, 2 * LANES), time_ref[0], jnp.int32).astype(f32)
    spread_sq = level * level + 1.0
    c_input = 1.0 / jnp.sqrt(spread_sq)

    weight_columns = jnp.concatenate([pos_weight_ref[...], jnp.zeros((5, LANES), f32)], axis=0).T
    for place, other in enumerate((0, 1, None, 2, 3)):
        device = jnp.clip(me + (place - 2), 0, last)
        block = own_ref[...] if other is None else others_ref[other]
        total_t = block.astype(f32).T
        for comp in range(3):
            row = jnp.concatenate(
                [tiles_ref[device, 2 * comp : 2 * comp + 1, :], tiles_ref[device, 2 * comp + 1 : 2 * comp + 2, :]],
                axis=1,
            )
            total_t = total_t + weight_columns[:, comp : comp + 1] * (row * c_input)
        stream[place] = total_t

    gain_columns = jnp.concatenate(
        [gain_ref[0], gain_ref[1], jnp.zeros((4, LANES), f32)], axis=0
    ).T
    query_scale = LOG2E * (LANES // HEADS) ** -0.5
    head_size = LANES // HEADS
    ones_rows = jnp.ones((16, 2 * LANES), bf16)

    for copy in copies:
        copy.wait()

    for layer in range(2):
        gain_a = gain_columns[:, 2 * layer : 2 * layer + 1]
        gain_b = gain_columns[:, 2 * layer + 1 : 2 * layer + 2]
        low, high = layer, 5 - layer

        def project(place, carry, layer=layer, gain_a=gain_a):
            normed = (norm_columns(stream[place]) * gain_a).astype(bf16)
            keys[pl.ds(pl.multiple_of(place * 2 * LANES, 2 * LANES), 2 * LANES), :] = dot_t(
                normed, w_key_ref[layer]
            ).astype(bf16)
            value_t = dot_t(w_value_ref[layer], normed).astype(bf16)
            for head in range(HEADS):
                values[place, head * 48 : head * 48 + 32, :] = value_t[head * 32 : head * 32 + 32]
                values[place, head * 48 + 32 : head * 48 + 48, :] = ones_rows
            queries[place] = (dot_t(w_query_ref[layer], normed) * query_scale).astype(bf16)
            return carry

        lax.fori_loop(low, high, project, 0)

        def mix(place, carry, layer=layer, gain_b=gain_b):
            device = jnp.clip(me + (place - 2), 0, last)
            window = tiles_ref[device, 7:8, :]
            query_t = queries[place]
            near = keys[pl.ds(pl.multiple_of((place - 1) * 2 * LANES, 2 * LANES), 6 * LANES), :]
            pieces = []
            for head in range(HEADS):
                parts = []
                if head:
                    parts.append(jnp.zeros((head * head_size, 2 * LANES), bf16))
                parts.append(query_t[head * head_size : (head + 1) * head_size])
                if head < HEADS - 1:
                    parts.append(jnp.zeros(((HEADS - 1 - head) * head_size, 2 * LANES), bf16))
                masked = jnp.concatenate(parts, axis=0)
                scores = dot(near, masked)
                weights = []
                for block in range(2):
                    lanes = slice(block * LANES, (block + 1) * LANES)
                    tiles = []
                    for offset in range(5):
                        chunk = block + offset
                        tile = scores[chunk * LANES : (chunk + 1) * LANES, lanes]
                        tiles.append(tile + window[:, block * 8 + offset : block * 8 + offset + 1])
                    top = functools.reduce(jnp.maximum, tiles)
                    top = jnp.max(top, axis=0, keepdims=True)
                    blank = [jnp.zeros((LANES, LANES), bf16)]
                    tiles = [jnp.exp2(tile - top).astype(bf16) for tile in tiles]
                    weights.append(blank + tiles if block else tiles + blank)
                mixed = None
                for j in range(3):
                    weight = jnp.concatenate(
                        [
                            jnp.concatenate([weights[0][2 * j], weights[1][2 * j]], axis=1),
                            jnp.concatenate([weights[0][2 * j + 1], weights[1][2 * j + 1]], axis=1),
                        ],
                        axis=0,
                    )
                    part = dot(values[place - 1 + j, head * 48 : (head + 1) * 48, :], weight)
                    mixed = part if mixed is None else mixed + part
                pieces.append(mixed[:head_size] * (1.0 / mixed[head_size : head_size + 1]))
            attended = jnp.concatenate(pieces, axis=0).astype(bf16)
            now = stream[place] + dot_t(w_out_ref[layer], attended)
            normed = (norm_columns(now) * gain_b).astype(bf16)
            gate_up = dot_t(w_gate_up_ref[layer], normed)
            width = gate_up.shape[0] // 2
            gate, up = gate_up[:width], gate_up[width:]
            hidden = (gate / (1.0 + jnp.exp2(gate * -LOG2E)) * up).astype(bf16)
            stream[place] = now + dot_t(w_down_ref[layer], hidden)
            return carry

        lax.fori_loop(low + 1, high - 1, mix, 0)

    final = norm_columns(stream[2])
    head_rows = jnp.concatenate([w_head_ref[...], jnp.zeros((5, LANES), f32)], axis=0)
    update = jnp.dot(head_rows, final, precision=lax.Precision.HIGHEST, preferred_element_type=f32)

    positions = jnp.concatenate([positions_ref[...], jnp.zeros((5, 2 * LANES), f32)], axis=0)
    fresh = jnp.concatenate([noise_ref[...], jnp.zeros((5, 2 * LANES), f32)], axis=0)

    denoised = positions * (1.0 / spread_sq) + (level * c_input) * update
    following = 0.85 * level
    result = denoised + STEER * force_ref[...] + following * (0.8 * (positions - denoised) / level + 0.6 * fresh)
    out_ref[...] = result[:3]


def body(
    positions,
    fresh_noise,
    timestep,
    atom_single,
    pos_weight,
    ln_gain,
    w_query,
    w_key,
    w_value,
    w_out,
    w_gate_up,
    w_down,
    w_head,
    key_window,
    block_pairs,
    pair_count,
    bond_atoms,
):
    devices = lax.axis_size("atom")
    first = lax.axis_index("atom").astype(jnp.int32).reshape(1)
    smem = pl.BlockSpec(memory_space=pltpu.SMEM)
    vmem = pl.BlockSpec(memory_space=pltpu.VMEM)

    samples = lax.axis_size("sample")
    shifts = (-2, -1, 1, 2)
    pairs = [
        (sample * devices + (device + shifts[sample % 4]) % devices, sample * devices + device)
        for sample in range(samples)
        for device in range(devices)
    ]
    fetched = lax.ppermute(atom_single, ("sample", "atom"), pairs)
    others = lax.all_to_all(
        jnp.broadcast_to(fetched[None], (4,) + fetched.shape),
        "sample",
        0,
        0,
        axis_index_groups=[[4 * i + j for j in range(4)] for i in range(samples // 4)],
    )

    packed = pl.pallas_call(
        pack_kernel,
        out_shape=jax.ShapeDtypeStruct((devices, 8, LANES), f32),
        in_specs=[smem, smem, vmem, vmem, vmem],
        out_specs=vmem,
        scratch_shapes=[pltpu.VMEM((8, LANES), f32)],
    )(first, pair_count, positions, block_pairs, key_window)
    tiles = lax.all_to_all(packed, "atom", 0, 0)

    any_space = pl.BlockSpec(memory_space=pl.ANY)
    force = pl.pallas_call(
        force_kernel,
        out_shape=jax.ShapeDtypeStruct((8, 2 * LANES), f32),
        in_specs=[smem, vmem, vmem, vmem],
        out_specs=vmem,
        scratch_shapes=[
            pltpu.VMEM((3, LANES, LANES), f32),
            pltpu.VMEM((3, LANES, LANES), f32),
            pltpu.VMEM((8, LANES), jnp.int32),
            pltpu.VMEM((8, LANES), f32),
            pltpu.SMEM((8, LANES), jnp.int32),
            pltpu.SMEM((8, LANES), f32),
            pltpu.SemaphoreType.DMA((2,)),
        ],
        cost_estimate=pl.CostEstimate(flops=40_000_000, bytes_accessed=200_000, transcendentals=1_000_000),
    )(first, tiles, positions, bond_atoms)

    wide = (5, LANES, 2 * LANES)
    weights = (w_query, w_key, w_value, w_out, w_gate_up, w_down)
    return pl.pallas_call(
        step_kernel,
        out_shape=jax.ShapeDtypeStruct(positions.shape, f32),
        in_specs=[smem, smem] + [vmem] * 9 + [any_space] * 6,
        out_specs=vmem,
        scratch_shapes=[
            pltpu.VMEM(wide, f32),
            pltpu.VMEM(wide, bf16),
            pltpu.VMEM((10 * LANES, LANES), bf16),
            pltpu.VMEM((5, HEADS * 48, 2 * LANES), bf16),
        ]
        + [pltpu.VMEM(weight.shape, bf16) for weight in weights]
        + [pltpu.SemaphoreType.DMA((6,))],
        cost_estimate=pl.CostEstimate(flops=2_000_000_000, bytes_accessed=1_200_000, transcendentals=3_000_000),
        compiler_params=pltpu.CompilerParams(vmem_limit_bytes=48 * 1024 * 1024),
    )(
        first,
        timestep,
        tiles,
        others,
        atom_single,
        positions,
        fresh_noise,
        force,
        pos_weight,
        ln_gain,
        w_head,
        *weights,
    )


def solution(mesh):
    in_specs = (
        P(None, ("sample", "atom")),
        P(None, ("sample", "atom")),
        P(),
        P("atom", None),
        P(),
        P(),
        P(),
        P(),
        P(),
        P(),
        P(),
        P(),
        P(),
        P("atom", None),
        P(None, "atom"),
        P("atom"),
        P(None, "atom", None),
    )
    out_specs = P(None, ("sample", "atom"))
    return jax.shard_map(body, mesh=mesh, in_specs=in_specs, out_specs=out_specs, check_vma=False)
```

```python
import functools
import math

import jax
import jax.numpy as jnp
from jax import lax
from jax.experimental import pallas as pl
from jax.experimental.pallas import tpu as pltpu
from jax.sharding import PartitionSpec as P

HEADS = 4
LANES = 128
VMEM_GRANT = 60 * 1024 * 1024
NORM_EPS = 1e-05
STEER = 0.3
ABSENT = -1e30
LOG2E = 1.4426950408889634
KAPPA = 2.0 * math.sqrt(LOG2E)

f32 = jnp.float32
bf16 = jnp.bfloat16


def pack_kernel(*refs):
    first_ref, sources, (out_ref, counts_ref) = refs[0], refs[1:5], refs[6:8]
    tile, targets, sems = refs[8], refs[9:13], refs[13]
    count_ref, positions_ref, pairs_ref, window_ref = targets
    for copy in start_copies(sources, targets, sems):
        copy.wait()
    for row in range(6):
        part = slice((row % 2) * LANES, (row % 2 + 1) * LANES)
        tile[row : row + 1, :] = positions_ref[row // 2 : row // 2 + 1, part]
    pairs = pairs_ref[...]
    lane = lax.broadcasted_iota(jnp.int32, (1, pairs.shape[1]), 1)
    codes = jnp.where(lane < count_ref[0], pairs[0:1] * 64 + pairs[1:2], -1).astype(f32)
    tile[6:7, :] = jnp.concatenate([codes, codes], axis=1)
    window = window_ref[...]
    own = first_ref[0] * 2 + lax.broadcasted_iota(jnp.int32, window.shape, 0)
    lane = lax.broadcasted_iota(jnp.int32, (1, LANES), 1)
    counts = jnp.zeros((1, LANES), f32)
    for offset in range(5):
        hit = jnp.sum((window == own + (offset - 2)).astype(f32), axis=1, keepdims=True)
        counts = jnp.where(lane == offset, hit[0:1], counts)
        counts = jnp.where(lane == 8 + offset, hit[1:2], counts)
    tile[7:8, :] = jnp.zeros((1, LANES), f32)
    counts_ref[...] = jnp.where(counts > 0.0, jnp.log2(jnp.maximum(counts, 1.0)), ABSENT)
    out_ref[...] = jnp.broadcast_to(tile[...][None], out_ref.shape)


def split3(values):
    high = values.astype(bf16)
    rest = values - high.astype(f32)
    mid = rest.astype(bf16)
    low = (rest - mid.astype(f32)).astype(bf16)
    return jnp.concatenate([high, mid, low], axis=0)


def join3(values):
    rows = values.shape[0] // 3
    return values[:rows] + values[rows : 2 * rows] + values[2 * rows :]


def norm_columns(values):
    center = values - jnp.mean(values, axis=0, keepdims=True)
    spread = jnp.mean(center * center, axis=0, keepdims=True)
    return center * lax.rsqrt(spread + NORM_EPS)


def dot_t(left, right):
    return lax.dot_general(left, right, (((0,), (0,)), ((), ())), preferred_element_type=f32)


def dot_nt(left, right):
    return lax.dot_general(left, right, (((1,), (1,)), ((), ())), preferred_element_type=f32)


def dot(left, right):
    return jnp.dot(left, right, preferred_element_type=f32)


def force_kernel(first_ref, tiles_ref, positions_ref, bonds_ref, out_ref, spread_own, push, list_v, bias_v, list_s, bias_s, sems):
    me = first_ref[0]

    codes = tiles_ref[:, 6, :].astype(jnp.int32)
    half = lax.broadcasted_iota(jnp.int32, codes.shape, 1) // 64
    mine = me * 2 + half
    first = jnp.where(codes < 0, -1, codes // 64)
    second = jnp.where(codes < 0, -1, codes % 64)
    partner = jnp.where(first == mine, second, jnp.where(second == mine, first, -1)).astype(f32)
    block_id = lax.broadcasted_iota(jnp.int32, (64, LANES), 0).astype(f32)
    hits = jnp.zeros((64, LANES), f32)
    for row in range(codes.shape[0]):
        hits = hits + jnp.where(partner[row : row + 1] == block_id, 1.0, 0.0)
    row_half = lax.broadcasted_iota(jnp.int32, (LANES, LANES), 0) // 64
    col_half = lax.broadcasted_iota(jnp.int32, (LANES, LANES), 1) // 64
    count = dot(hits.astype(bf16), (row_half == col_half).astype(bf16))
    present = count > 0.5
    lower = lax.broadcasted_iota(jnp.int32, (64, 64), 1) < lax.broadcasted_iota(jnp.int32, (64, 64), 0)
    rank = dot(lower.astype(bf16), present.astype(bf16))
    slot = (lax.broadcasted_iota(jnp.int32, (64, LANES), 1) % 64).astype(f32)
    chosen = present & (rank == slot)
    listed = jnp.sum(jnp.where(chosen, block_id, 0.0), axis=0, keepdims=True)
    times = jnp.sum(jnp.where(chosen, count, 0.0), axis=0, keepdims=True)
    total = jnp.sum(present.astype(f32), axis=0, keepdims=True)
    list_v[0:1, :] = listed.astype(jnp.int32)
    list_v[1:2, :] = total.astype(jnp.int32)
    bias_v[0:1, :] = jnp.where(times > 0.5, jnp.log2(jnp.maximum(times, 1.0)), ABSENT)
    list_copy = pltpu.make_async_copy(list_v, list_s, sems.at[0])
    bias_copy = pltpu.make_async_copy(bias_v, bias_s, sems.at[1])
    list_copy.start()
    bias_copy.start()

    positions = jnp.concatenate([positions_ref[...], jnp.zeros((5, 2 * LANES), f32)], axis=0)

    forces = []
    atom_id = lax.broadcasted_iota(jnp.int32, (LANES, LANES), 0)
    for block in range(2):
        incidence = (
            (atom_id == bonds_ref[0, block : block + 1, :]).astype(f32)
            - (atom_id == bonds_ref[1, block : block + 1, :]).astype(f32)
        ).astype(bf16)
        offset = join3(dot(split3(positions[:, block * LANES : (block + 1) * LANES]), incidence))
        stretch = jnp.sum(offset * offset, axis=0, keepdims=True) - 1.0
        pull = (-0.2 * stretch) * offset
        forces.append(join3(dot_nt(split3(pull), incidence)))

    list_copy.wait()
    bias_copy.wait()
    for block in range(2):
        for comp in range(3):
            row = positions_ref[comp : comp + 1, block * LANES : (block + 1) * LANES] * KAPPA
            spread_own[comp] = jnp.broadcast_to(row, (LANES, LANES)).T
            push[comp] = jnp.zeros((LANES, LANES), f32)

        def one_pair(index, carry, block=block):
            partners = []
            for sub in range(2):
                entry = block * 64 + 2 * index + sub
                partner = list_s[0, entry]
                device = partner // 2
                within = partner % 2
                rows = [
                    tiles_ref[device, pl.ds(2 * comp + within, 1), :] * KAPPA for comp in range(3)
                ]
                partners.append((rows, bias_s[0, entry]))
            for group in range(0, LANES, 8):
                own = [spread_own[comp, group : group + 8, :] for comp in range(3)]
                sums = [push[comp, group : group + 8, :] for comp in range(3)]
                for rows, bias in partners:
                    offset = [own[comp] - rows[comp] for comp in range(3)]
                    power = bias - offset[0] * offset[0]
                    power = power - offset[1] * offset[1]
                    power = power - offset[2] * offset[2]
                    weight = jnp.exp2(power)
                    sums = [sums[comp] + weight * offset[comp] for comp in range(3)]
                for comp in range(3):
                    push[comp, group : group + 8, :] = sums[comp]
            return carry

        lax.fori_loop(0, (list_s[1, block * 64] + 1) // 2, one_pair, 0)
        rows = [jnp.sum(push[comp].T, axis=0, keepdims=True) for comp in range(3)]
        clash = jnp.concatenate(rows + [jnp.zeros((5, LANES), f32)], axis=0)
        forces[block] = forces[block] + clash * (8.0 / KAPPA)
    out_ref[...] = jnp.concatenate(forces, axis=1)


def noise_rows(time_ref):
    level = 0.2 + 0.02 * jnp.full((1, 2 * LANES), time_ref[0], jnp.int32).astype(f32)
    spread_sq = level * level + 1.0
    return level, spread_sq, 1.0 / jnp.sqrt(spread_sq)


def start_copies(sources, targets, sems):
    copies = [
        pltpu.make_async_copy(source, target, sems.at[index])
        for index, (source, target) in enumerate(zip(sources, targets))
    ]
    for copy in copies:
        copy.start()
    return copies


def prepare_kernel(*refs):
    sources, (stream_ref, normed_ref), targets, sems = refs[:5], refs[5:7], refs[7:12], refs[12]
    time_ref, positions_ref, single_ref, pos_weight_ref, gain_ref = targets
    for copy in start_copies(sources, targets, sems):
        copy.wait()
    c_input = noise_rows(time_ref)[2]
    columns = jnp.concatenate(
        [pos_weight_ref[...], gain_ref[0, 0:1], jnp.zeros((4, LANES), f32)], axis=0
    ).T
    stream = single_ref[...].astype(f32).T
    for comp in range(3):
        stream = stream + columns[:, comp : comp + 1] * (positions_ref[comp : comp + 1, :] * c_input)
    stream_ref[...] = stream
    normed_ref[...] = (norm_columns(stream) * columns[:, 3:4]).T.astype(bf16)


def layer_values(
    layer, left_ref, own_ref, right_ref, stream_ref, counts_ref, gain_ref, weights, copies
):
    w_key_ref, w_value_ref, w_query_ref, w_out_ref, w_gate_up_ref, w_down_ref = weights
    head_size = LANES // HEADS
    query_scale = LOG2E * head_size ** -0.5
    near = jnp.concatenate([left_ref[...], own_ref[...], right_ref[...]], axis=0)
    window = counts_ref[...]
    copies[0].wait()
    keys = dot(near, w_key_ref[...]).astype(bf16)
    copies[1].wait()
    values = dot_nt(w_value_ref[...].T, near).astype(bf16)
    copies[2].wait()
    query_t = (dot_nt(w_query_ref[...].T, own_ref[...]) * query_scale).astype(bf16)
    ones_rows = jnp.ones((16, 6 * LANES), bf16)
    pieces = []
    for head in range(HEADS):
        parts = []
        if head:
            parts.append(jnp.zeros((head * head_size, 2 * LANES), bf16))
        parts.append(query_t[head * head_size : (head + 1) * head_size])
        if head < HEADS - 1:
            parts.append(jnp.zeros(((HEADS - 1 - head) * head_size, 2 * LANES), bf16))
        scores = dot(keys, jnp.concatenate(parts, axis=0))
        weights_t = []
        for block in range(2):
            lanes = slice(block * LANES, (block + 1) * LANES)
            tiles = []
            for offset in range(5):
                chunk = block + offset
                tile = scores[chunk * LANES : (chunk + 1) * LANES, lanes]
                tiles.append(tile + window[:, block * 8 + offset : block * 8 + offset + 1])
            top = functools.reduce(jnp.maximum, tiles)
            top = jnp.max(top, axis=0, keepdims=True)
            blank = [jnp.zeros((LANES, LANES), bf16)]
            tiles = [jnp.exp2(tile - top).astype(bf16) for tile in tiles]
            weights_t.append(jnp.concatenate(blank + tiles if block else tiles + blank, axis=0))
        value_rows = jnp.concatenate(
            [values[head * head_size : (head + 1) * head_size], ones_rows], axis=0
        )
        mixed = dot(value_rows, jnp.concatenate(weights_t, axis=1))
        pieces.append(mixed[:head_size] * (1.0 / mixed[head_size : head_size + 1]))
    attended = jnp.concatenate(pieces, axis=0).astype(bf16)
    copies[3].wait()
    stream = stream_ref[...] + dot(w_out_ref[...].T, attended)
    gains = jnp.concatenate([gain_ref[0], gain_ref[1], jnp.zeros((4, LANES), f32)], axis=0).T
    normed = (norm_columns(stream) * gains[:, 2 * layer + 1 : 2 * layer + 2]).astype(bf16)
    copies[4].wait()
    gate_up = dot(w_gate_up_ref[...].T, normed)
    width = gate_up.shape[0] // 2
    gate, up = gate_up[:width], gate_up[width:]
    hidden = (gate / (1.0 + jnp.exp2(gate * -LOG2E)) * up).astype(bf16)
    copies[5].wait()
    stream = stream + dot(w_down_ref[...].T, hidden)
    return stream, gains


def first_layer_kernel(left_ref, own_ref, right_ref, stream_ref, counts_ref, gain_ref, *refs):
    sources, (out_ref, normed_ref), targets, sems = refs[:6], refs[6:8], refs[8:14], refs[14]
    copies = start_copies([source.at[0] for source in sources], targets, sems)
    stream, gains = layer_values(
        0, left_ref, own_ref, right_ref, stream_ref, counts_ref, gain_ref, targets, copies
    )
    out_ref[...] = stream
    normed_ref[...] = (norm_columns(stream) * gains[:, 2:3]).T.astype(bf16)


def last_layer_kernel(
    time_ref,
    left_ref,
    own_ref,
    right_ref,
    stream_ref,
    counts_ref,
    gain_ref,
    positions_ref,
    noise_ref,
    force_ref,
    w_head_ref,
    *refs,
):
    sources, out_ref, targets, sems = refs[:6], refs[6], refs[7:13], refs[13]
    copies = start_copies([source.at[1] for source in sources], targets, sems)
    stream, _ = layer_values(
        1, left_ref, own_ref, right_ref, stream_ref, counts_ref, gain_ref, targets, copies
    )
    final = norm_columns(stream)
    head_rows = jnp.concatenate([w_head_ref[...], jnp.zeros((5, LANES), f32)], axis=0)
    update = jnp.dot(head_rows, final, precision=lax.Precision.HIGHEST, preferred_element_type=f32)
    level, spread_sq, c_input = noise_rows(time_ref)
    positions = jnp.concatenate([positions_ref[...], jnp.zeros((5, 2 * LANES), f32)], axis=0)
    fresh = jnp.concatenate([noise_ref[...], jnp.zeros((5, 2 * LANES), f32)], axis=0)
    denoised = positions * (1.0 / spread_sq) + (level * c_input) * update
    following = 0.85 * level
    result = denoised + STEER * force_ref[...] + following * (0.8 * (positions - denoised) / level + 0.6 * fresh)
    out_ref[...] = result[:3]


def body(
    positions,
    fresh_noise,
    timestep,
    atom_single,
    pos_weight,
    ln_gain,
    w_query,
    w_key,
    w_value,
    w_out,
    w_gate_up,
    w_down,
    w_head,
    key_window,
    block_pairs,
    pair_count,
    bond_atoms,
):
    devices = lax.axis_size("atom")
    first = lax.axis_index("atom").astype(jnp.int32).reshape(1)
    smem = pl.BlockSpec(memory_space=pltpu.SMEM)
    vmem = pl.BlockSpec(memory_space=pltpu.VMEM)
    hbm = pl.BlockSpec(memory_space=pltpu.HBM)
    rows = atom_single.shape[0]

    def from_neighbours(array):
        up = [(i, (i + 1) % devices) for i in range(devices)]
        down = [(j, i) for i, j in up]
        return lax.ppermute(array, "atom", up), lax.ppermute(array, "atom", down)

    stream, normed = pl.pallas_call(
        prepare_kernel,
        out_shape=(
            jax.ShapeDtypeStruct((LANES, rows), f32),
            jax.ShapeDtypeStruct((rows, LANES), bf16),
        ),
        in_specs=[hbm] * 5,
        out_specs=(vmem, vmem),
        scratch_shapes=[
            pltpu.SMEM(timestep.shape, jnp.int32),
            pltpu.VMEM(positions.shape, f32),
            pltpu.VMEM(atom_single.shape, bf16),
            pltpu.VMEM(pos_weight.shape, f32),
            pltpu.VMEM(ln_gain.shape, f32),
            pltpu.SemaphoreType.DMA((5,)),
        ],
        compiler_params=pltpu.CompilerParams(vmem_limit_bytes=VMEM_GRANT),
    )(timestep, positions, atom_single, pos_weight, ln_gain)
    left, right = from_neighbours(normed)

    packed, counts = pl.pallas_call(
        pack_kernel,
        out_shape=(
            jax.ShapeDtypeStruct((devices, 8, LANES), f32),
            jax.ShapeDtypeStruct((1, LANES), f32),
        ),
        in_specs=[smem] + [hbm] * 4 + [pl.BlockSpec(memory_space=pl.ANY)],
        out_specs=(vmem, vmem),
        scratch_shapes=[
            pltpu.VMEM((8, LANES), f32),
            pltpu.SMEM(pair_count.shape, jnp.int32),
            pltpu.VMEM(positions.shape, f32),
            pltpu.VMEM(block_pairs.shape, jnp.int32),
            pltpu.VMEM(key_window.shape, jnp.int32),
            pltpu.SemaphoreType.DMA((4,)),
        ],
        compiler_params=pltpu.CompilerParams(vmem_limit_bytes=VMEM_GRANT),
    )(first, pair_count, positions, block_pairs, key_window, normed)
    tiles = lax.all_to_all(packed, "atom", 0, 0)

    weights = (w_key, w_value, w_query, w_out, w_gate_up, w_down)
    weight_scratch = [pltpu.VMEM(weight.shape[1:], bf16) for weight in weights]
    layer_cost = pl.CostEstimate(flops=600_000_000, bytes_accessed=800_000, transcendentals=800_000)
    stream, normed = pl.pallas_call(
        first_layer_kernel,
        out_shape=(
            jax.ShapeDtypeStruct((LANES, rows), f32),
            jax.ShapeDtypeStruct((rows, LANES), bf16),
        ),
        in_specs=[vmem] * 6 + [hbm] * 6,
        out_specs=(vmem, vmem),
        scratch_shapes=weight_scratch + [pltpu.SemaphoreType.DMA((6,))],
        cost_estimate=layer_cost,
        compiler_params=pltpu.CompilerParams(vmem_limit_bytes=32 * 1024 * 1024),
    )(left, normed, right, stream, counts, ln_gain, *weights)
    left, right = from_neighbours(normed)

    force = pl.pallas_call(
        force_kernel,
        out_shape=jax.ShapeDtypeStruct((8, rows), f32),
        in_specs=[smem, vmem, vmem, vmem],
        out_specs=vmem,
        scratch_shapes=[
            pltpu.VMEM((3, LANES, LANES), f32),
            pltpu.VMEM((3, LANES, LANES), f32),
            pltpu.VMEM((8, LANES), jnp.int32),
            pltpu.VMEM((8, LANES), f32),
            pltpu.SMEM((8, LANES), jnp.int32),
            pltpu.SMEM((8, LANES), f32),
            pltpu.SemaphoreType.DMA((2,)),
        ],
        cost_estimate=pl.CostEstimate(flops=40_000_000, bytes_accessed=200_000, transcendentals=1_000_000),
    )(first, tiles, positions, bond_atoms)

    return pl.pallas_call(
        last_layer_kernel,
        out_shape=jax.ShapeDtypeStruct(positions.shape, f32),
        in_specs=[smem] + [vmem] * 10 + [hbm] * 6,
        out_specs=vmem,
        scratch_shapes=weight_scratch + [pltpu.SemaphoreType.DMA((6,))],
        cost_estimate=layer_cost,
        compiler_params=pltpu.CompilerParams(vmem_limit_bytes=32 * 1024 * 1024),
    )(timestep, left, normed, right, stream, counts, ln_gain, positions, fresh_noise, force, w_head, *weights)


def solution(mesh):
    in_specs = (
        P(None, ("sample", "atom")),
        P(None, ("sample", "atom")),
        P(),
        P("atom", None),
        P(),
        P(),
        P(),
        P(),
        P(),
        P(),
        P(),
        P(),
        P(),
        P("atom", None),
        P(None, "atom"),
        P("atom"),
        P(None, "atom", None),
    )
    out_specs = P(None, ("sample", "atom"))
    return jax.shard_map(body, mesh=mesh, in_specs=in_specs, out_specs=out_specs, check_vma=False)
```

```python
import functools
import math

import jax
import jax.numpy as jnp
from jax import lax
from jax.experimental import pallas as pl
from jax.experimental.pallas import tpu as pltpu
from jax.sharding import PartitionSpec as P

HEADS = 4
LANES = 128
VMEM_GRANT = 60 * 1024 * 1024
NORM_EPS = 1e-05
STEER = 0.3
ABSENT = -1e30
LOG2E = 1.4426950408889634
KAPPA = 2.0 * math.sqrt(LOG2E)

f32 = jnp.float32
bf16 = jnp.bfloat16


def pack_kernel(*refs):
    first_ref, sources, (out_ref, counts_ref) = refs[0], refs[1:5], refs[6:8]
    tile, targets, sems = refs[8], refs[9:13], refs[13]
    count_ref, positions_ref, pairs_ref, window_ref = targets
    for copy in start_copies(sources, targets, sems):
        copy.wait()
    for row in range(6):
        part = slice((row % 2) * LANES, (row % 2 + 1) * LANES)
        tile[row : row + 1, :] = positions_ref[row // 2 : row // 2 + 1, part]
    pairs = pairs_ref[...]
    lane = lax.broadcasted_iota(jnp.int32, (1, pairs.shape[1]), 1)
    codes = jnp.where(lane < count_ref[0], pairs[0:1] * 64 + pairs[1:2], -1).astype(f32)
    tile[6:7, :] = jnp.concatenate([codes, codes], axis=1)
    window = window_ref[...]
    own = first_ref[0] * 2 + lax.broadcasted_iota(jnp.int32, window.shape, 0)
    lane = lax.broadcasted_iota(jnp.int32, (1, LANES), 1)
    counts = jnp.zeros((1, LANES), f32)
    for offset in range(5):
        hit = jnp.sum((window == own + (offset - 2)).astype(f32), axis=1, keepdims=True)
        counts = jnp.where(lane == offset, hit[0:1], counts)
        counts = jnp.where(lane == 8 + offset, hit[1:2], counts)
    tile[7:8, :] = jnp.zeros((1, LANES), f32)
    counts_ref[...] = jnp.where(counts > 0.0, jnp.log2(jnp.maximum(counts, 1.0)), ABSENT)
    out_ref[...] = jnp.broadcast_to(tile[...][None], out_ref.shape)


def split3(values):
    high = values.astype(bf16)
    rest = values - high.astype(f32)
    mid = rest.astype(bf16)
    low = (rest - mid.astype(f32)).astype(bf16)
    return jnp.concatenate([high, mid, low], axis=0)


def join3(values):
    rows = values.shape[0] // 3
    return values[:rows] + values[rows : 2 * rows] + values[2 * rows :]


def norm_columns(values):
    center = values - jnp.mean(values, axis=0, keepdims=True)
    spread = jnp.mean(center * center, axis=0, keepdims=True)
    return center * lax.rsqrt(spread + NORM_EPS)


def dot_t(left, right):
    return lax.dot_general(left, right, (((0,), (0,)), ((), ())), preferred_element_type=f32)


def dot_nt(left, right):
    return lax.dot_general(left, right, (((1,), (1,)), ((), ())), preferred_element_type=f32)


def dot(left, right):
    return jnp.dot(left, right, preferred_element_type=f32)


def force_kernel(first_ref, tiles_ref, positions_ref, bonds_ref, out_ref, spread_own, push, list_v, bias_v, list_s, bias_s, sems):
    me = first_ref[0]

    codes = tiles_ref[:, 6, :].astype(jnp.int32)
    half = lax.broadcasted_iota(jnp.int32, codes.shape, 1) // 64
    mine = me * 2 + half
    first = jnp.where(codes < 0, -1, codes // 64)
    second = jnp.where(codes < 0, -1, codes % 64)
    partner = jnp.where(first == mine, second, jnp.where(second == mine, first, -1)).astype(f32)
    block_id = lax.broadcasted_iota(jnp.int32, (64, LANES), 0).astype(f32)
    hits = jnp.zeros((64, LANES), f32)
    for row in range(codes.shape[0]):
        hits = hits + jnp.where(partner[row : row + 1] == block_id, 1.0, 0.0)
    row_half = lax.broadcasted_iota(jnp.int32, (LANES, LANES), 0) // 64
    col_half = lax.broadcasted_iota(jnp.int32, (LANES, LANES), 1) // 64
    count = dot(hits.astype(bf16), (row_half == col_half).astype(bf16))
    present = count > 0.5
    lower = lax.broadcasted_iota(jnp.int32, (64, 64), 1) < lax.broadcasted_iota(jnp.int32, (64, 64), 0)
    rank = dot(lower.astype(bf16), present.astype(bf16))
    slot = (lax.broadcasted_iota(jnp.int32, (64, LANES), 1) % 64).astype(f32)
    chosen = present & (rank == slot)
    listed = jnp.sum(jnp.where(chosen, block_id, 0.0), axis=0, keepdims=True)
    times = jnp.sum(jnp.where(chosen, count, 0.0), axis=0, keepdims=True)
    total = jnp.sum(present.astype(f32), axis=0, keepdims=True)
    list_v[0:1, :] = listed.astype(jnp.int32)
    list_v[1:2, :] = total.astype(jnp.int32)
    bias_v[0:1, :] = jnp.where(times > 0.5, jnp.log2(jnp.maximum(times, 1.0)), ABSENT)
    list_copy = pltpu.make_async_copy(list_v, list_s, sems.at[0])
    bias_copy = pltpu.make_async_copy(bias_v, bias_s, sems.at[1])
    list_copy.start()
    bias_copy.start()

    positions = jnp.concatenate([positions_ref[...], jnp.zeros((5, 2 * LANES), f32)], axis=0)

    forces = []
    atom_id = lax.broadcasted_iota(jnp.int32, (LANES, LANES), 0)
    for block in range(2):
        incidence = (
            (atom_id == bonds_ref[0, block : block + 1, :]).astype(f32)
            - (atom_id == bonds_ref[1, block : block + 1, :]).astype(f32)
        ).astype(bf16)
        offset = join3(dot(split3(positions[:, block * LANES : (block + 1) * LANES]), incidence))
        stretch = jnp.sum(offset * offset, axis=0, keepdims=True) - 1.0
        pull = (-0.2 * stretch) * offset
        forces.append(join3(dot_nt(split3(pull), incidence)))

    list_copy.wait()
    bias_copy.wait()
    for block in range(2):
        for comp in range(3):
            row = positions_ref[comp : comp + 1, block * LANES : (block + 1) * LANES] * KAPPA
            spread_own[comp] = jnp.broadcast_to(row, (LANES, LANES)).T
            push[comp] = jnp.zeros((LANES, LANES), f32)

        def one_pair(index, carry, block=block):
            partners = []
            for sub in range(2):
                entry = block * 64 + 2 * index + sub
                partner = list_s[0, entry]
                device = partner // 2
                within = partner % 2
                rows = [
                    tiles_ref[device, pl.ds(2 * comp + within, 1), :] * KAPPA for comp in range(3)
                ]
                partners.append((rows, bias_s[0, entry]))
            for group in range(0, LANES, 8):
                own = [spread_own[comp, group : group + 8, :] for comp in range(3)]
                sums = [push[comp, group : group + 8, :] for comp in range(3)]
                for rows, bias in partners:
                    offset = [own[comp] - rows[comp] for comp in range(3)]
                    power = bias - offset[0] * offset[0]
                    power = power - offset[1] * offset[1]
                    power = power - offset[2] * offset[2]
                    weight = jnp.exp2(power)
                    sums = [sums[comp] + weight * offset[comp] for comp in range(3)]
                for comp in range(3):
                    push[comp, group : group + 8, :] = sums[comp]
            return carry

        lax.fori_loop(0, (list_s[1, block * 64] + 1) // 2, one_pair, 0)
        rows = [jnp.sum(push[comp].T, axis=0, keepdims=True) for comp in range(3)]
        clash = jnp.concatenate(rows + [jnp.zeros((5, LANES), f32)], axis=0)
        forces[block] = forces[block] + clash * (8.0 / KAPPA)
    out_ref[...] = jnp.concatenate(forces, axis=1)


def start_copies(sources, targets, sems):
    copies = [
        pltpu.make_async_copy(source, target, sems.at[index])
        for index, (source, target) in enumerate(zip(sources, targets))
    ]
    for copy in copies:
        copy.start()
    return copies


def prepare_kernel(*refs):
    sources, (stream_ref, normed_ref, rows_ref), targets, sems = refs[:5], refs[5:8], refs[8:13], refs[13]
    time_ref, positions_ref, single_ref, pos_weight_ref, gain_ref = targets
    for copy in start_copies(sources, targets, sems):
        copy.wait()
    level = 0.2 + 0.02 * jnp.full((1, 2 * LANES), time_ref[0], jnp.int32).astype(f32)
    spread_sq = level * level + 1.0
    c_input = 1.0 / jnp.sqrt(spread_sq)
    rows_ref[...] = jnp.concatenate([level, spread_sq, c_input, jnp.zeros((5, 2 * LANES), f32)], axis=0)
    columns = jnp.concatenate(
        [pos_weight_ref[...], gain_ref[0, 0:1], jnp.zeros((4, LANES), f32)], axis=0
    ).T
    stream = single_ref[...].astype(f32).T
    for comp in range(3):
        stream = stream + columns[:, comp : comp + 1] * (positions_ref[comp : comp + 1, :] * c_input)
    stream_ref[...] = stream
    normed_ref[...] = (norm_columns(stream) * columns[:, 3:4]).T.astype(bf16)


def layer_values(
    layer, left_ref, own_ref, right_ref, stream_ref, counts_ref, gain_ref, weights, copies
):
    w_key_ref, w_value_ref, w_query_ref, w_out_ref, w_gate_up_ref, w_down_ref = weights
    head_size = LANES // HEADS
    query_scale = LOG2E * head_size ** -0.5
    near = jnp.concatenate([left_ref[...], own_ref[...], right_ref[...]], axis=0)
    window = counts_ref[...]
    copies[0].wait()
    keys = dot(near, w_key_ref[...]).astype(bf16)
    copies[1].wait()
    values = dot_nt(w_value_ref[...].T, near).astype(bf16)
    copies[2].wait()
    query_t = (dot_nt(w_query_ref[...].T, own_ref[...]) * query_scale).astype(bf16)
    ones_rows = jnp.ones((16, 6 * LANES), bf16)
    pieces = []
    for head in range(HEADS):
        parts = []
        if head:
            parts.append(jnp.zeros((head * head_size, 2 * LANES), bf16))
        parts.append(query_t[head * head_size : (head + 1) * head_size])
        if head < HEADS - 1:
            parts.append(jnp.zeros(((HEADS - 1 - head) * head_size, 2 * LANES), bf16))
        scores = dot(keys, jnp.concatenate(parts, axis=0))
        weights_t = []
        for block in range(2):
            lanes = slice(block * LANES, (block + 1) * LANES)
            tiles = []
            for offset in range(5):
                chunk = block + offset
                tile = scores[chunk * LANES : (chunk + 1) * LANES, lanes]
                tiles.append(tile + window[:, block * 8 + offset : block * 8 + offset + 1])
            top = functools.reduce(jnp.maximum, tiles)
            top = jnp.max(top, axis=0, keepdims=True)
            blank = [jnp.zeros((LANES, LANES), bf16)]
            tiles = [jnp.exp2(tile - top).astype(bf16) for tile in tiles]
            weights_t.append(jnp.concatenate(blank + tiles if block else tiles + blank, axis=0))
        value_rows = jnp.concatenate(
            [values[head * head_size : (head + 1) * head_size], ones_rows], axis=0
        )
        mixed = dot(value_rows, jnp.concatenate(weights_t, axis=1))
        pieces.append(mixed[:head_size] * (1.0 / mixed[head_size : head_size + 1]))
    attended = jnp.concatenate(pieces, axis=0).astype(bf16)
    copies[3].wait()
    stream = stream_ref[...] + dot(w_out_ref[...].T, attended)
    gains = jnp.concatenate([gain_ref[0], gain_ref[1], jnp.zeros((4, LANES), f32)], axis=0).T
    normed = (norm_columns(stream) * gains[:, 2 * layer + 1 : 2 * layer + 2]).astype(bf16)
    copies[4].wait()
    gate_up = dot(w_gate_up_ref[...].T, normed)
    width = gate_up.shape[0] // 2
    gate, up = gate_up[:width], gate_up[width:]
    hidden = (gate / (1.0 + jnp.exp2(gate * -LOG2E)) * up).astype(bf16)
    copies[5].wait()
    stream = stream + dot(w_down_ref[...].T, hidden)
    return stream, gains


def first_layer_kernel(left_ref, own_ref, right_ref, stream_ref, counts_ref, gain_ref, *refs):
    sources, (out_ref, normed_ref), targets, sems = refs[:6], refs[6:8], refs[8:14], refs[14]
    copies = start_copies([source.at[0] for source in sources], targets, sems)
    stream, gains = layer_values(
        0, left_ref, own_ref, right_ref, stream_ref, counts_ref, gain_ref, targets, copies
    )
    out_ref[...] = stream
    normed_ref[...] = (norm_columns(stream) * gains[:, 2:3]).T.astype(bf16)


def last_layer_kernel(
    rows_ref,
    left_ref,
    own_ref,
    right_ref,
    stream_ref,
    counts_ref,
    gain_ref,
    positions_ref,
    noise_ref,
    force_ref,
    w_head_ref,
    *refs,
):
    sources, out_ref, targets, sems = refs[:6], refs[6], refs[7:13], refs[13]
    copies = start_copies([source.at[1] for source in sources], targets, sems)
    stream, _ = layer_values(
        1, left_ref, own_ref, right_ref, stream_ref, counts_ref, gain_ref, targets, copies
    )
    final = norm_columns(stream)
    head_rows = jnp.concatenate([w_head_ref[...], jnp.zeros((5, LANES), f32)], axis=0)
    update = jnp.dot(head_rows, final, precision=lax.Precision.HIGHEST, preferred_element_type=f32)
    level, spread_sq, c_input = rows_ref[0:1], rows_ref[1:2], rows_ref[2:3]
    positions = jnp.concatenate([positions_ref[...], jnp.zeros((5, 2 * LANES), f32)], axis=0)
    fresh = jnp.concatenate([noise_ref[...], jnp.zeros((5, 2 * LANES), f32)], axis=0)
    denoised = positions * (1.0 / spread_sq) + (level * c_input) * update
    following = 0.85 * level
    result = denoised + STEER * force_ref[...] + following * (0.8 * (positions - denoised) / level + 0.6 * fresh)
    out_ref[...] = result[:3]


def body(
    positions,
    fresh_noise,
    timestep,
    atom_single,
    pos_weight,
    ln_gain,
    w_query,
    w_key,
    w_value,
    w_out,
    w_gate_up,
    w_down,
    w_head,
    key_window,
    block_pairs,
    pair_count,
    bond_atoms,
):
    devices = lax.axis_size("x") * lax.axis_size("z")
    first = lax.axis_index(("x", "z")).astype(jnp.int32).reshape(1)
    smem = pl.BlockSpec(memory_space=pltpu.SMEM)
    vmem = pl.BlockSpec(memory_space=pltpu.VMEM)
    hbm = pl.BlockSpec(memory_space=pltpu.HBM)
    rows = atom_single.shape[0]

    def from_neighbours(array):
        up = [(i, (i + 1) % devices) for i in range(devices)]
        down = [(j, i) for i, j in up]
        return lax.ppermute(array, ("x", "z"), up), lax.ppermute(array, ("x", "z"), down)

    stream, normed, schedule = pl.pallas_call(
        prepare_kernel,
        out_shape=(
            jax.ShapeDtypeStruct((LANES, rows), f32),
            jax.ShapeDtypeStruct((rows, LANES), bf16),
            jax.ShapeDtypeStruct((8, rows), f32),
        ),
        in_specs=[hbm] * 5,
        out_specs=(vmem, vmem, vmem),
        scratch_shapes=[
            pltpu.SMEM(timestep.shape, jnp.int32),
            pltpu.VMEM(positions.shape, f32),
            pltpu.VMEM(atom_single.shape, bf16),
            pltpu.VMEM(pos_weight.shape, f32),
            pltpu.VMEM(ln_gain.shape, f32),
            pltpu.SemaphoreType.DMA((5,)),
        ],
        compiler_params=pltpu.CompilerParams(vmem_limit_bytes=VMEM_GRANT),
    )(timestep, positions, atom_single, pos_weight, ln_gain)
    left, right = from_neighbours(normed)

    packed, counts = pl.pallas_call(
        pack_kernel,
        out_shape=(
            jax.ShapeDtypeStruct((lax.axis_size("z"), 8, LANES), f32),
            jax.ShapeDtypeStruct((1, LANES), f32),
        ),
        in_specs=[smem] + [hbm] * 4 + [vmem],
        out_specs=(vmem, vmem),
        scratch_shapes=[
            pltpu.VMEM((8, LANES), f32),
            pltpu.SMEM(pair_count.shape, jnp.int32),
            pltpu.VMEM(positions.shape, f32),
            pltpu.VMEM(block_pairs.shape, jnp.int32),
            pltpu.VMEM(key_window.shape, jnp.int32),
            pltpu.SemaphoreType.DMA((4,)),
        ],
        cost_estimate=pl.CostEstimate(flops=40_000_000, bytes_accessed=10_000_000, transcendentals=1_000_000),
    )(first, pair_count, positions, block_pairs, key_window, schedule)
    line = lax.all_to_all(packed, "z", 0, 0)
    plane = jnp.broadcast_to(line[None], (lax.axis_size("x"),) + line.shape)
    tiles = lax.all_to_all(plane, "x", 0, 0).reshape(devices, 8, LANES)

    weights = (w_key, w_value, w_query, w_out, w_gate_up, w_down)
    weight_scratch = [pltpu.VMEM(weight.shape[1:], bf16) for weight in weights]
    layer_cost = pl.CostEstimate(flops=2_000_000_000, bytes_accessed=12_000_000, transcendentals=2_000_000)
    stream, normed = pl.pallas_call(
        first_layer_kernel,
        out_shape=(
            jax.ShapeDtypeStruct((LANES, rows), f32),
            jax.ShapeDtypeStruct((rows, LANES), bf16),
        ),
        in_specs=[vmem] * 6 + [hbm] * 6,
        out_specs=(vmem, vmem),
        scratch_shapes=weight_scratch + [pltpu.SemaphoreType.DMA((6,))],
        cost_estimate=layer_cost,
        compiler_params=pltpu.CompilerParams(vmem_limit_bytes=32 * 1024 * 1024),
    )(left, normed, right, stream, counts, ln_gain, *weights)
    left, right = from_neighbours(normed)

    force = pl.pallas_call(
        force_kernel,
        out_shape=jax.ShapeDtypeStruct((8, rows), f32),
        in_specs=[smem, vmem, vmem, vmem],
        out_specs=vmem,
        scratch_shapes=[
            pltpu.VMEM((3, LANES, LANES), f32),
            pltpu.VMEM((3, LANES, LANES), f32),
            pltpu.VMEM((8, LANES), jnp.int32),
            pltpu.VMEM((8, LANES), f32),
            pltpu.SMEM((8, LANES), jnp.int32),
            pltpu.SMEM((8, LANES), f32),
            pltpu.SemaphoreType.DMA((2,)),
        ],
        cost_estimate=pl.CostEstimate(flops=80_000_000, bytes_accessed=16_000_000, transcendentals=2_000_000),
    )(first, tiles, positions, bond_atoms)

    return pl.pallas_call(
        last_layer_kernel,
        out_shape=jax.ShapeDtypeStruct(positions.shape, f32),
        in_specs=[vmem] * 11 + [hbm] * 6,
        out_specs=vmem,
        scratch_shapes=weight_scratch + [pltpu.SemaphoreType.DMA((6,))],
        cost_estimate=layer_cost,
        compiler_params=pltpu.CompilerParams(vmem_limit_bytes=32 * 1024 * 1024),
    )(schedule, left, normed, right, stream, counts, ln_gain, positions, fresh_noise, force, w_head, *weights)


def solution(mesh):
    in_specs = (
        P(None, ("sample", "x", "z")),
        P(None, ("sample", "x", "z")),
        P(),
        P(("x", "z"), None),
        P(),
        P(),
        P(),
        P(),
        P(),
        P(),
        P(),
        P(),
        P(),
        P(("x", "z"), None),
        P(None, ("x", "z")),
        P(("x", "z")),
        P(None, ("x", "z"), None),
    )
    out_specs = P(None, ("sample", "x", "z"))
    mesh = jax.sharding.Mesh(mesh.devices.reshape(-1, 4, 8), ("sample", "x", "z"))
    return jax.shard_map(body, mesh=mesh, in_specs=in_specs, out_specs=out_specs, check_vma=False)
```

```python
import functools
import math

import jax
import jax.numpy as jnp
from jax import lax
from jax.experimental import pallas as pl
from jax.experimental.pallas import tpu as pltpu
from jax.sharding import PartitionSpec as P

HEADS = 4
LANES = 128
ROWS = 256
NORM_EPS = 1e-05
STEER = 0.3
ABSENT = -(2.0**120)
LOG2E = 1.4426950408889634
KAPPA = 2.0 * math.sqrt(LOG2E)

f32 = jnp.float32
bf16 = jnp.bfloat16


def pack_kernel(first_ref, count_ref, positions_ref, pairs_ref, window_ref, out_ref, tile):
    for row in range(6):
        part = slice((row % 2) * LANES, (row % 2 + 1) * LANES)
        tile[row : row + 1, :] = positions_ref[row // 2 : row // 2 + 1, part]
    pairs = pairs_ref[...]
    lane = lax.broadcasted_iota(jnp.int32, (1, pairs.shape[1]), 1)
    codes = jnp.where(lane < count_ref[0], pairs[0:1] * 64 + pairs[1:2], -1).astype(f32)
    tile[6:7, :] = jnp.concatenate([codes, codes], axis=1)
    window = window_ref[...]
    own = first_ref[0] * 2 + lax.broadcasted_iota(jnp.int32, window.shape, 0)
    lane = lax.broadcasted_iota(jnp.int32, (1, LANES), 1)
    counts = jnp.zeros((1, LANES), f32)
    for offset in range(5):
        hit = jnp.sum((window == own + (offset - 2)).astype(f32), axis=1, keepdims=True)
        counts = jnp.where(lane == offset, hit[0:1], counts)
        counts = jnp.where(lane == 8 + offset, hit[1:2], counts)
    tile[7:8, :] = jnp.where(counts > 0.0, jnp.log2(jnp.maximum(counts, 1.0)), ABSENT)
    out_ref[...] = jnp.broadcast_to(tile[...][None], out_ref.shape)


def split3(values):
    high = values.astype(bf16)
    rest = values - high.astype(f32)
    mid = rest.astype(bf16)
    low = (rest - mid.astype(f32)).astype(bf16)
    return jnp.concatenate([high, mid, low], axis=0)


def join3(values):
    rows = values.shape[0] // 3
    return values[:rows] + values[rows : 2 * rows] + values[2 * rows :]


def norm_columns(values):
    center = values - jnp.mean(values, axis=0, keepdims=True)
    spread = jnp.mean(center * center, axis=0, keepdims=True)
    return center * lax.rsqrt(spread + NORM_EPS)


def dot_t(left, right):
    return lax.dot_general(left, right, (((0,), (0,)), ((), ())), preferred_element_type=f32)


def dot_nt(left, right):
    return lax.dot_general(left, right, (((1,), (1,)), ((), ())), preferred_element_type=f32)


def dot(left, right):
    return jnp.dot(left, right, preferred_element_type=f32)


def force_kernel(first_ref, tiles_ref, positions_ref, bonds_ref, out_ref, spread_own, push, list_v, bias_v, list_s, bias_s, sems):
    me = first_ref[0]

    codes = tiles_ref[:, 6, :].astype(jnp.int32)
    half = lax.broadcasted_iota(jnp.int32, codes.shape, 1) // 64
    mine = me * 2 + half
    first = jnp.where(codes < 0, -1, codes // 64)
    second = jnp.where(codes < 0, -1, codes % 64)
    partner = jnp.where(first == mine, second, jnp.where(second == mine, first, -1)).astype(f32)
    block_id = lax.broadcasted_iota(jnp.int32, (64, LANES), 0).astype(f32)
    hits = jnp.zeros((64, LANES), f32)
    for row in range(codes.shape[0]):
        hits = hits + jnp.where(partner[row : row + 1] == block_id, 1.0, 0.0)
    row_half = lax.broadcasted_iota(jnp.int32, (LANES, LANES), 0) // 64
    col_half = lax.broadcasted_iota(jnp.int32, (LANES, LANES), 1) // 64
    count = dot(hits.astype(bf16), (row_half == col_half).astype(bf16))
    present = count > 0.5
    lower = lax.broadcasted_iota(jnp.int32, (64, 64), 1) < lax.broadcasted_iota(jnp.int32, (64, 64), 0)
    rank = dot(lower.astype(bf16), present.astype(bf16))
    slot = (lax.broadcasted_iota(jnp.int32, (64, LANES), 1) % 64).astype(f32)
    chosen = present & (rank == slot)
    listed = jnp.sum(jnp.where(chosen, block_id, 0.0), axis=0, keepdims=True)
    times = jnp.sum(jnp.where(chosen, count, 0.0), axis=0, keepdims=True)
    total = jnp.sum(present.astype(f32), axis=0, keepdims=True)
    list_v[0:1, :] = listed.astype(jnp.int32)
    list_v[1:2, :] = total.astype(jnp.int32)
    bias_v[0:1, :] = jnp.where(times > 0.5, jnp.log2(jnp.maximum(times, 1.0)), ABSENT)
    list_copy = pltpu.make_async_copy(list_v, list_s, sems.at[0])
    bias_copy = pltpu.make_async_copy(bias_v, bias_s, sems.at[1])
    list_copy.start()
    bias_copy.start()

    positions = jnp.concatenate([positions_ref[...], jnp.zeros((5, 2 * LANES), f32)], axis=0)

    forces = []
    atom_id = lax.broadcasted_iota(jnp.int32, (LANES, LANES), 0)
    for block in range(2):
        incidence = (
            (atom_id == bonds_ref[0, block : block + 1, :]).astype(f32)
            - (atom_id == bonds_ref[1, block : block + 1, :]).astype(f32)
        ).astype(bf16)
        offset = join3(dot(split3(positions[:, block * LANES : (block + 1) * LANES]), incidence))
        stretch = jnp.sum(offset * offset, axis=0, keepdims=True) - 1.0
        pull = (-0.2 * stretch) * offset
        forces.append(join3(dot_nt(split3(pull), incidence)))

    list_copy.wait()
    bias_copy.wait()
    for block in range(2):
        for comp in range(3):
            row = positions_ref[comp : comp + 1, block * LANES : (block + 1) * LANES] * KAPPA
            spread_own[comp] = jnp.broadcast_to(row, (LANES, LANES)).T
            push[comp] = jnp.zeros((LANES, LANES), f32)

        def one_pair(index, carry, block=block):
            partners = []
            for sub in range(2):
                entry = block * 64 + 2 * index + sub
                partner = list_s[0, entry]
                device = partner // 2
                within = partner % 2
                rows = [
                    tiles_ref[device, pl.ds(2 * comp + within, 1), :] * KAPPA for comp in range(3)
                ]
                partners.append((rows, bias_s[0, entry]))
            for group in range(0, LANES, 8):
                own = [spread_own[comp, group : group + 8, :] for comp in range(3)]
                sums = [push[comp, group : group + 8, :] for comp in range(3)]
                for rows, bias in partners:
                    offset = [own[comp] - rows[comp] for comp in range(3)]
                    power = bias - offset[0] * offset[0]
                    power = power - offset[1] * offset[1]
                    power = power - offset[2] * offset[2]
                    weight = jnp.exp2(power)
                    sums = [sums[comp] + weight * offset[comp] for comp in range(3)]
                for comp in range(3):
                    push[comp, group : group + 8, :] = sums[comp]
            return carry

        lax.fori_loop(0, (list_s[1, block * 64] + 1) // 2, one_pair, 0)
        rows = [jnp.sum(push[comp].T, axis=0, keepdims=True) for comp in range(3)]
        clash = jnp.concatenate(rows + [jnp.zeros((5, LANES), f32)], axis=0)
        forces[block] = forces[block] + clash * (8.0 / KAPPA)
    out_ref[...] = jnp.concatenate(forces, axis=1)


def step_kernel(
    first_ref,
    time_ref,
    tiles_ref,
    others_ref,
    own_ref,
    positions_ref,
    noise_ref,
    force_ref,
    pos_weight_ref,
    gain_ref,
    w_head_ref,
    w_query_ref,
    w_key_ref,
    w_value_ref,
    w_out_ref,
    w_gate_up_ref,
    w_down_ref,
    out_ref,
    stream,
    near,
    queries,
    keys,
    values,
    bias,
    attended,
    low_high,
):
    me = first_ref[0]
    last = tiles_ref.shape[0] - 1
    head_size = LANES // HEADS
    query_scale = LOG2E * head_size ** -0.5

    level = 0.2 + 0.02 * jnp.full((1, ROWS), time_ref[0], jnp.int32).astype(f32)
    spread_sq = level * level + 1.0
    c_input = 1.0 / jnp.sqrt(spread_sq)

    columns = jnp.concatenate(
        [pos_weight_ref[...], gain_ref[0], gain_ref[1], jnp.zeros((1, LANES), f32)], axis=0
    ).T

    row_block = lax.broadcasted_iota(jnp.int32, (5 * ROWS, LANES), 0) // LANES
    lane = lax.broadcasted_iota(jnp.int32, (5 * ROWS, LANES), 1)
    keys[:, LANES:] = jnp.where((lane % 16 == row_block) & (lane < 32), 1.0, 0.0).astype(bf16)
    for place in range(1, 4):
        window = tiles_ref[jnp.clip(me + (place - 2), 0, last), 7:8, :]
        rows = []
        for chunk in range(16):
            sides = []
            for block in range(2):
                offset = chunk - 2 * (place - 1) - block
                if 0 <= offset < 5:
                    lane_id = block * 8 + offset
                    sides.append(jnp.broadcast_to(window[:, lane_id : lane_id + 1], (1, LANES)))
                else:
                    sides.append(jnp.full((1, LANES), ABSENT, f32))
            rows.append(jnp.concatenate(sides, axis=1))
        rows = jnp.concatenate(rows, axis=0)
        high = rows.astype(bf16)
        low = (rows - high.astype(f32)).astype(bf16)
        bias[place - 1] = jnp.concatenate([high, low, jnp.zeros((LANES - 32, ROWS), bf16)], axis=0)

    for place, other in enumerate((0, 1, None, 2, 3)):
        device = jnp.clip(me + (place - 2), 0, last)
        block = own_ref[...] if other is None else others_ref[other]
        total_t = block.astype(f32).T
        for comp in range(3):
            row = jnp.concatenate(
                [tiles_ref[device, 2 * comp : 2 * comp + 1, :], tiles_ref[device, 2 * comp + 1 : 2 * comp + 2, :]],
                axis=1,
            )
            total_t = total_t + columns[:, comp : comp + 1] * (row * c_input)
        stream[:, place * ROWS : (place + 1) * ROWS] = total_t

    def window_of(place):
        return pl.ds(pl.multiple_of((place - 1) * ROWS, ROWS), 3 * ROWS)

    def attend(place, exact):
        window = window_of(place)
        here = pl.ds(pl.multiple_of(place * ROWS, ROWS), ROWS)
        key_rows = keys[window, :]
        query_t = queries[:, here]
        counts = bias[place - 1]
        pieces = []
        sums = []
        for head in range(HEADS):
            parts = []
            if head:
                parts.append(jnp.zeros((head * head_size, ROWS), bf16))
            parts.append(query_t[head * head_size : (head + 1) * head_size])
            if head < HEADS - 1:
                parts.append(jnp.zeros(((HEADS - 1 - head) * head_size, ROWS), bf16))
            scores = dot(key_rows, jnp.concatenate(parts + [counts], axis=0))
            if exact:
                scores = scores - jnp.max(scores, axis=0, keepdims=True)
            blank = jnp.zeros((LANES, LANES), bf16)
            weights = jnp.concatenate(
                [
                    jnp.concatenate([jnp.exp2(scores[: 5 * LANES, :LANES]).astype(bf16), blank], axis=0),
                    jnp.concatenate([blank, jnp.exp2(scores[LANES:, LANES:]).astype(bf16)], axis=0),
                ],
                axis=1,
            )
            mixed = dot(values[head * 48 : (head + 1) * 48, window], weights)
            total = mixed[head_size : head_size + 1]
            sums.append(total)
            pieces.append(mixed[:head_size] * (1.0 / total))
        attended[:, here] = jnp.concatenate(pieces, axis=0).astype(bf16)
        return jnp.concatenate(sums, axis=0)

    for layer in range(2):
        first, stop = layer, 5 - layer
        for place in range(first, stop):
            here = slice(place * ROWS, (place + 1) * ROWS)
            normed = norm_columns(stream[:, here]) * columns[:, 3 + 2 * layer : 4 + 2 * layer]
            near[here, :] = normed.T.astype(bf16)
        span = slice(first * ROWS, stop * ROWS)
        inner = slice((first + 1) * ROWS, (stop - 1) * ROWS)
        keys[span, :LANES] = dot(near[span, :], w_key_ref[layer]).astype(bf16)
        queries[:, inner] = (dot_nt(w_query_ref[layer].T, near[inner, :]) * query_scale).astype(bf16)
        value_t = dot_nt(w_value_ref[layer].T, near[span, :]).astype(bf16)
        for head in range(HEADS):
            values[head * 48 : head * 48 + 32, span] = value_t[head * 32 : head * 32 + 32]
            values[head * 48 + 32 : head * 48 + 48, span] = jnp.ones((16, (stop - first) * ROWS), bf16)

        low_high[0:4, :] = jnp.full((4, ROWS), 1.0, f32)
        low_high[4:8, :] = jnp.full((4, ROWS), 1.0, f32)

        def quick(place, carry):
            sums = attend(place, False)
            low_high[0:4, :] = jnp.minimum(low_high[0:4, :], sums)
            low_high[4:8, :] = jnp.maximum(low_high[4:8, :], sums)
            return carry

        lax.fori_loop(first + 1, stop - 1, quick, 0)
        lowest = jnp.min(low_high[0:4, :])
        highest = jnp.max(low_high[4:8, :])
        safe = (lowest > 2.0**-80) & (highest < 2.0**100)

        @pl.when(jnp.logical_not(safe))
        def _():
            def exactly(place, carry):
                attend(place, True)
                return carry

            lax.fori_loop(first + 1, stop - 1, exactly, 0)

        now = stream[:, inner] + dot(w_out_ref[layer].T, attended[:, inner])
        normed = (norm_columns(now) * columns[:, 4 + 2 * layer : 5 + 2 * layer]).astype(bf16)
        gate_up = dot(w_gate_up_ref[layer].T, normed)
        width = gate_up.shape[0] // 2
        gate, up = gate_up[:width], gate_up[width:]
        hidden = (gate / (1.0 + jnp.exp2(gate * -LOG2E)) * up).astype(bf16)
        stream[:, inner] = now + dot(w_down_ref[layer].T, hidden)

    final = norm_columns(stream[:, 2 * ROWS : 3 * ROWS])
    head_rows = jnp.concatenate([w_head_ref[...], jnp.zeros((5, LANES), f32)], axis=0)
    update = jnp.dot(head_rows, final, precision=lax.Precision.HIGHEST, preferred_element_type=f32)

    positions = jnp.concatenate([positions_ref[...], jnp.zeros((5, ROWS), f32)], axis=0)
    fresh = jnp.concatenate([noise_ref[...], jnp.zeros((5, ROWS), f32)], axis=0)
    denoised = positions * (1.0 / spread_sq) + (level * c_input) * update
    following = 0.85 * level
    result = denoised + STEER * force_ref[...] + following * (0.8 * (positions - denoised) / level + 0.6 * fresh)
    out_ref[...] = result[:3]


def body(
    positions,
    fresh_noise,
    timestep,
    atom_single,
    pos_weight,
    ln_gain,
    w_query,
    w_key,
    w_value,
    w_out,
    w_gate_up,
    w_down,
    w_head,
    key_window,
    block_pairs,
    pair_count,
    bond_atoms,
):
    devices = lax.axis_size("atom")
    first = lax.axis_index("atom").astype(jnp.int32).reshape(1)
    smem = pl.BlockSpec(memory_space=pltpu.SMEM)
    vmem = pl.BlockSpec(memory_space=pltpu.VMEM)

    samples = lax.axis_size("sample")
    shifts = (-2, -1, 1, 2)
    pairs = [
        (sample * devices + (device + shifts[sample % 4]) % devices, sample * devices + device)
        for sample in range(samples)
        for device in range(devices)
    ]
    fetched = lax.ppermute(atom_single, ("sample", "atom"), pairs)
    others = lax.all_to_all(
        jnp.broadcast_to(fetched[None], (4,) + fetched.shape),
        "sample",
        0,
        0,
        axis_index_groups=[[4 * i + j for j in range(4)] for i in range(samples // 4)],
    )

    packed = pl.pallas_call(
        pack_kernel,
        out_shape=jax.ShapeDtypeStruct((devices, 8, LANES), f32),
        in_specs=[smem, smem, vmem, vmem, vmem],
        out_specs=vmem,
        scratch_shapes=[pltpu.VMEM((8, LANES), f32)],
        cost_estimate=pl.CostEstimate(flops=40_000_000, bytes_accessed=10_000_000, transcendentals=1_000_000),
    )(first, pair_count, positions, block_pairs, key_window)
    tiles = lax.all_to_all(packed, "atom", 0, 0)

    force = pl.pallas_call(
        force_kernel,
        out_shape=jax.ShapeDtypeStruct((8, 2 * LANES), f32),
        in_specs=[smem, vmem, vmem, vmem],
        out_specs=vmem,
        scratch_shapes=[
            pltpu.VMEM((3, LANES, LANES), f32),
            pltpu.VMEM((3, LANES, LANES), f32),
            pltpu.VMEM((8, LANES), jnp.int32),
            pltpu.VMEM((8, LANES), f32),
            pltpu.SMEM((8, LANES), jnp.int32),
            pltpu.SMEM((8, LANES), f32),
            pltpu.SemaphoreType.DMA((2,)),
        ],
        cost_estimate=pl.CostEstimate(flops=80_000_000, bytes_accessed=16_000_000, transcendentals=2_000_000),
    )(first, tiles, positions, bond_atoms)

    rows = atom_single.shape[0]
    weights = (w_query, w_key, w_value, w_out, w_gate_up, w_down)
    return pl.pallas_call(
        step_kernel,
        out_shape=jax.ShapeDtypeStruct(positions.shape, f32),
        in_specs=[smem, smem] + [vmem] * 15,
        out_specs=vmem,
        scratch_shapes=[
            pltpu.VMEM((LANES, 5 * rows), f32),
            pltpu.VMEM((5 * rows, LANES), bf16),
            pltpu.VMEM((LANES, 5 * rows), bf16),
            pltpu.VMEM((5 * rows, 2 * LANES), bf16),
            pltpu.VMEM((HEADS * 48, 5 * rows), bf16),
            pltpu.VMEM((3, LANES, rows), bf16),
            pltpu.VMEM((LANES, 5 * rows), bf16),
            pltpu.VMEM((8, rows), f32),
        ],
        cost_estimate=pl.CostEstimate(flops=2_000_000_000, bytes_accessed=1_200_000, transcendentals=3_000_000),
        compiler_params=pltpu.CompilerParams(vmem_limit_bytes=48 * 1024 * 1024),
    )(
        first,
        timestep,
        tiles,
        others,
        atom_single,
        positions,
        fresh_noise,
        force,
        pos_weight,
        ln_gain,
        w_head,
        *weights,
    )


def solution(mesh):
    in_specs = (
        P(None, ("sample", "atom")),
        P(None, ("sample", "atom")),
        P(),
        P("atom", None),
        P(),
        P(),
        P(),
        P(),
        P(),
        P(),
        P(),
        P(),
        P(),
        P("atom", None),
        P(None, "atom"),
        P("atom"),
        P(None, "atom", None),
    )
    out_specs = P(None, ("sample", "atom"))
    return jax.shard_map(body, mesh=mesh, in_specs=in_specs, out_specs=out_specs, check_vma=False)
```

```python
import functools
import math

import jax
import jax.numpy as jnp
from jax import lax
from jax.experimental import pallas as pl
from jax.experimental.pallas import tpu as pltpu
from jax.sharding import PartitionSpec as P

HEADS = 4
LANES = 128
ROWS = 256
NORM_EPS = 1e-05
STEER = 0.3
ABSENT = -(2.0**120)
LOG2E = 1.4426950408889634
KAPPA = 2.0 * math.sqrt(LOG2E)

f32 = jnp.float32
bf16 = jnp.bfloat16


def pack_kernel(first_ref, count_ref, positions_ref, pairs_ref, window_ref, fetched_ref, out_ref, copies_ref, tile):
    for row in range(6):
        part = slice((row % 2) * LANES, (row % 2 + 1) * LANES)
        tile[row : row + 1, :] = positions_ref[row // 2 : row // 2 + 1, part]
    pairs = pairs_ref[...]
    lane = lax.broadcasted_iota(jnp.int32, (1, pairs.shape[1]), 1)
    codes = jnp.where(lane < count_ref[...], pairs[0:1] * 64 + pairs[1:2], -1).astype(f32)
    tile[6:7, :] = jnp.concatenate([codes, codes], axis=1)
    window = window_ref[...]
    own = first_ref[0] * 2 + lax.broadcasted_iota(jnp.int32, window.shape, 0)
    lane = lax.broadcasted_iota(jnp.int32, (1, LANES), 1)
    counts = jnp.zeros((1, LANES), f32)
    for offset in range(5):
        hit = jnp.sum((window == own + (offset - 2)).astype(f32), axis=1, keepdims=True)
        counts = jnp.where(lane == offset, hit[0:1], counts)
        counts = jnp.where(lane == 8 + offset, hit[1:2], counts)
    tile[7:8, :] = jnp.where(counts > 0.0, jnp.log2(jnp.maximum(counts, 1.0)), ABSENT)
    out_ref[...] = jnp.broadcast_to(tile[...][None], out_ref.shape)
    for copy in range(4):
        copies_ref[copy] = fetched_ref[...]


def split3(values):
    high = values.astype(bf16)
    rest = values - high.astype(f32)
    mid = rest.astype(bf16)
    low = (rest - mid.astype(f32)).astype(bf16)
    return jnp.concatenate([high, mid, low], axis=0)


def join3(values):
    rows = values.shape[0] // 3
    return values[:rows] + values[rows : 2 * rows] + values[2 * rows :]


def norm_columns(values):
    center = values - jnp.mean(values, axis=0, keepdims=True)
    spread = jnp.mean(center * center, axis=0, keepdims=True)
    return center * lax.rsqrt(spread + NORM_EPS)


def dot_t(left, right):
    return lax.dot_general(left, right, (((0,), (0,)), ((), ())), preferred_element_type=f32)


def dot_nt(left, right):
    return lax.dot_general(left, right, (((1,), (1,)), ((), ())), preferred_element_type=f32)


def dot(left, right):
    return jnp.dot(left, right, preferred_element_type=f32)


def force_kernel(first_ref, tiles_ref, positions_ref, bonds_ref, out_ref, spread_own, push, list_v, bias_v, list_s, bias_s, sems):
    me = first_ref[0]

    codes = tiles_ref[:, 6, :].astype(jnp.int32)
    half = lax.broadcasted_iota(jnp.int32, codes.shape, 1) // 64
    mine = me * 2 + half
    first = jnp.where(codes < 0, -1, codes // 64)
    second = jnp.where(codes < 0, -1, codes % 64)
    partner = jnp.where(first == mine, second, jnp.where(second == mine, first, -1)).astype(f32)
    block_id = lax.broadcasted_iota(jnp.int32, (64, LANES), 0).astype(f32)
    hits = jnp.zeros((64, LANES), f32)
    for row in range(codes.shape[0]):
        hits = hits + jnp.where(partner[row : row + 1] == block_id, 1.0, 0.0)
    row_half = lax.broadcasted_iota(jnp.int32, (LANES, LANES), 0) // 64
    col_half = lax.broadcasted_iota(jnp.int32, (LANES, LANES), 1) // 64
    count = dot(hits.astype(bf16), (row_half == col_half).astype(bf16))
    present = count > 0.5
    lower = lax.broadcasted_iota(jnp.int32, (64, 64), 1) < lax.broadcasted_iota(jnp.int32, (64, 64), 0)
    rank = dot(lower.astype(bf16), present.astype(bf16))
    slot = (lax.broadcasted_iota(jnp.int32, (64, LANES), 1) % 64).astype(f32)
    chosen = present & (rank == slot)
    listed = jnp.sum(jnp.where(chosen, block_id, 0.0), axis=0, keepdims=True)
    times = jnp.sum(jnp.where(chosen, count, 0.0), axis=0, keepdims=True)
    total = jnp.sum(present.astype(f32), axis=0, keepdims=True)
    list_v[0:1, :] = listed.astype(jnp.int32)
    list_v[1:2, :] = total.astype(jnp.int32)
    bias_v[0:1, :] = jnp.where(times > 0.5, jnp.log2(jnp.maximum(times, 1.0)), ABSENT)
    list_copy = pltpu.make_async_copy(list_v, list_s, sems.at[0])
    bias_copy = pltpu.make_async_copy(bias_v, bias_s, sems.at[1])
    list_copy.start()
    bias_copy.start()

    positions = jnp.concatenate([positions_ref[...], jnp.zeros((5, 2 * LANES), f32)], axis=0)

    forces = []
    atom_id = lax.broadcasted_iota(jnp.int32, (LANES, LANES), 0)
    for block in range(2):
        incidence = (
            (atom_id == bonds_ref[0, block : block + 1, :]).astype(f32)
            - (atom_id == bonds_ref[1, block : block + 1, :]).astype(f32)
        ).astype(bf16)
        offset = join3(dot(split3(positions[:, block * LANES : (block + 1) * LANES]), incidence))
        stretch = jnp.sum(offset * offset, axis=0, keepdims=True) - 1.0
        pull = (-0.2 * stretch) * offset
        forces.append(join3(dot_nt(split3(pull), incidence)))

    list_copy.wait()
    bias_copy.wait()
    for block in range(2):
        for comp in range(3):
            row = positions_ref[comp : comp + 1, block * LANES : (block + 1) * LANES] * KAPPA
            spread_own[comp] = jnp.broadcast_to(row, (LANES, LANES)).T
            push[comp] = jnp.zeros((LANES, LANES), f32)

        def one_pair(index, carry, block=block):
            partners = []
            for sub in range(2):
                entry = block * 64 + 2 * index + sub
                partner = list_s[0, entry]
                device = partner // 2
                within = partner % 2
                rows = [
                    tiles_ref[device, pl.ds(2 * comp + within, 1), :] * KAPPA for comp in range(3)
                ]
                partners.append((rows, bias_s[0, entry]))
            for group in range(0, LANES, 8):
                own = [spread_own[comp, group : group + 8, :] for comp in range(3)]
                sums = [push[comp, group : group + 8, :] for comp in range(3)]
                for rows, bias in partners:
                    offset = [own[comp] - rows[comp] for comp in range(3)]
                    power = bias - offset[0] * offset[0]
                    power = power - offset[1] * offset[1]
                    power = power - offset[2] * offset[2]
                    weight = jnp.exp2(power)
                    sums = [sums[comp] + weight * offset[comp] for comp in range(3)]
                for comp in range(3):
                    push[comp, group : group + 8, :] = sums[comp]
            return carry

        lax.fori_loop(0, (list_s[1, block * 64] + 1) // 2, one_pair, 0)
        rows = [jnp.sum(push[comp].T, axis=0, keepdims=True) for comp in range(3)]
        clash = jnp.concatenate(rows + [jnp.zeros((5, LANES), f32)], axis=0)
        forces[block] = forces[block] + clash * (8.0 / KAPPA)
    out_ref[...] = jnp.concatenate(forces, axis=1)


def step_kernel(
    first_ref,
    time_ref,
    tiles_ref,
    others_ref,
    own_ref,
    positions_ref,
    noise_ref,
    force_ref,
    pos_weight_ref,
    gain_ref,
    w_head_ref,
    w_query_ref,
    w_key_ref,
    w_value_ref,
    w_out_ref,
    w_gate_up_ref,
    w_down_ref,
    out_ref,
    stream,
    near,
    queries,
    keys,
    values,
    bias,
    attended,
    low_high,
):
    me = first_ref[0]
    last = tiles_ref.shape[0] - 1
    head_size = LANES // HEADS
    query_scale = LOG2E * head_size ** -0.5

    level = 0.2 + 0.02 * jnp.broadcast_to(time_ref[...].astype(f32), (1, ROWS))
    spread_sq = level * level + 1.0
    c_input = 1.0 / jnp.sqrt(spread_sq)

    columns = jnp.concatenate(
        [pos_weight_ref[...], gain_ref[0], gain_ref[1], jnp.zeros((1, LANES), f32)], axis=0
    ).T

    row_block = lax.broadcasted_iota(jnp.int32, (5 * ROWS, LANES), 0) // LANES
    lane = lax.broadcasted_iota(jnp.int32, (5 * ROWS, LANES), 1)
    keys[:, LANES:] = jnp.where((lane % 16 == row_block) & (lane < 32), 1.0, 0.0).astype(bf16)
    for place in range(1, 4):
        window = tiles_ref[jnp.clip(me + (place - 2), 0, last), 7:8, :]
        rows = []
        for chunk in range(16):
            sides = []
            for block in range(2):
                offset = chunk - 2 * (place - 1) - block
                if 0 <= offset < 5:
                    lane_id = block * 8 + offset
                    sides.append(jnp.broadcast_to(window[:, lane_id : lane_id + 1], (1, LANES)))
                else:
                    sides.append(jnp.full((1, LANES), ABSENT, f32))
            rows.append(jnp.concatenate(sides, axis=1))
        rows = jnp.concatenate(rows, axis=0)
        high = rows.astype(bf16)
        low = (rows - high.astype(f32)).astype(bf16)
        bias[place - 1] = jnp.concatenate([high, low, jnp.zeros((LANES - 32, ROWS), bf16)], axis=0)

    for place, other in enumerate((0, 1, None, 2, 3)):
        device = jnp.clip(me + (place - 2), 0, last)
        block = own_ref[...] if other is None else others_ref[other]
        total_t = block.astype(f32).T
        for comp in range(3):
            row = jnp.concatenate(
                [tiles_ref[device, 2 * comp : 2 * comp + 1, :], tiles_ref[device, 2 * comp + 1 : 2 * comp + 2, :]],
                axis=1,
            )
            total_t = total_t + columns[:, comp : comp + 1] * (row * c_input)
        stream[:, place * ROWS : (place + 1) * ROWS] = total_t

    def window_of(place):
        return pl.ds(pl.multiple_of((place - 1) * ROWS, ROWS), 3 * ROWS)

    def attend(place, exact):
        window = window_of(place)
        here = pl.ds(pl.multiple_of(place * ROWS, ROWS), ROWS)
        key_rows = keys[window, :]
        query_t = queries[:, here]
        counts = bias[place - 1]
        pieces = []
        sums = []
        for head in range(HEADS):
            parts = []
            if head:
                parts.append(jnp.zeros((head * head_size, ROWS), bf16))
            parts.append(query_t[head * head_size : (head + 1) * head_size])
            if head < HEADS - 1:
                parts.append(jnp.zeros(((HEADS - 1 - head) * head_size, ROWS), bf16))
            scores = dot(key_rows, jnp.concatenate(parts + [counts], axis=0))
            if exact:
                scores = scores - jnp.max(scores, axis=0, keepdims=True)
            blank = jnp.zeros((LANES, LANES), bf16)
            weights = jnp.concatenate(
                [
                    jnp.concatenate([jnp.exp2(scores[: 5 * LANES, :LANES]).astype(bf16), blank], axis=0),
                    jnp.concatenate([blank, jnp.exp2(scores[LANES:, LANES:]).astype(bf16)], axis=0),
                ],
                axis=1,
            )
            mixed = dot(values[head * 48 : (head + 1) * 48, window], weights)
            total = mixed[head_size : head_size + 1]
            sums.append(total)
            pieces.append(mixed[:head_size] * (1.0 / total))
        attended[:, here] = jnp.concatenate(pieces, axis=0).astype(bf16)
        return jnp.concatenate(sums, axis=0)

    for layer in range(2):
        first, stop = layer, 5 - layer
        for place in range(first, stop):
            here = slice(place * ROWS, (place + 1) * ROWS)
            normed = norm_columns(stream[:, here]) * columns[:, 3 + 2 * layer : 4 + 2 * layer]
            near[here, :] = normed.T.astype(bf16)
        span = slice(first * ROWS, stop * ROWS)
        inner = slice((first + 1) * ROWS, (stop - 1) * ROWS)
        keys[span, :LANES] = dot(near[span, :], w_key_ref[layer]).astype(bf16)
        queries[:, inner] = (dot_nt(w_query_ref[layer].T, near[inner, :]) * query_scale).astype(bf16)
        value_t = dot_nt(w_value_ref[layer].T, near[span, :]).astype(bf16)
        for head in range(HEADS):
            values[head * 48 : head * 48 + 32, span] = value_t[head * 32 : head * 32 + 32]
            values[head * 48 + 32 : head * 48 + 48, span] = jnp.ones((16, (stop - first) * ROWS), bf16)

        low_high[0:4, :] = jnp.full((4, ROWS), 1.0, f32)
        low_high[4:8, :] = jnp.full((4, ROWS), 1.0, f32)

        def quick(place, carry):
            sums = attend(place, False)
            low_high[0:4, :] = jnp.minimum(low_high[0:4, :], sums)
            low_high[4:8, :] = jnp.maximum(low_high[4:8, :], sums)
            return carry

        lax.fori_loop(first + 1, stop - 1, quick, 0)
        lowest = jnp.min(low_high[0:4, :])
        highest = jnp.max(low_high[4:8, :])
        safe = (lowest > 2.0**-80) & (highest < 2.0**100)

        @pl.when(jnp.logical_not(safe))
        def _():
            def exactly(place, carry):
                attend(place, True)
                return carry

            lax.fori_loop(first + 1, stop - 1, exactly, 0)

        now = stream[:, inner] + dot(w_out_ref[layer].T, attended[:, inner])
        normed = (norm_columns(now) * columns[:, 4 + 2 * layer : 5 + 2 * layer]).astype(bf16)
        gate_up = dot(w_gate_up_ref[layer].T, normed)
        width = gate_up.shape[0] // 2
        gate, up = gate_up[:width], gate_up[width:]
        hidden = (gate / (1.0 + jnp.exp2(gate * -LOG2E)) * up).astype(bf16)
        stream[:, inner] = now + dot(w_down_ref[layer].T, hidden)

    final = norm_columns(stream[:, 2 * ROWS : 3 * ROWS])
    head_rows = jnp.concatenate([w_head_ref[...], jnp.zeros((5, LANES), f32)], axis=0)
    update = jnp.dot(head_rows, final, precision=lax.Precision.HIGHEST, preferred_element_type=f32)

    positions = jnp.concatenate([positions_ref[...], jnp.zeros((5, ROWS), f32)], axis=0)
    fresh = jnp.concatenate([noise_ref[...], jnp.zeros((5, ROWS), f32)], axis=0)
    denoised = positions * (1.0 / spread_sq) + (level * c_input) * update
    following = 0.85 * level
    result = denoised + STEER * force_ref[...] + following * (0.8 * (positions - denoised) / level + 0.6 * fresh)
    out_ref[...] = result[:3]


def body(
    positions,
    fresh_noise,
    timestep,
    atom_single,
    pos_weight,
    ln_gain,
    w_query,
    w_key,
    w_value,
    w_out,
    w_gate_up,
    w_down,
    w_head,
    key_window,
    block_pairs,
    pair_count,
    bond_atoms,
):
    devices = lax.axis_size("atom")
    first = lax.axis_index("atom").astype(jnp.int32).reshape(1)
    smem = pl.BlockSpec(memory_space=pltpu.SMEM)
    vmem = pl.BlockSpec(memory_space=pltpu.VMEM)

    samples = lax.axis_size("sample")
    shifts = (-2, -1, 1, 2)
    pairs = [
        (sample * devices + (device + shifts[sample % 4]) % devices, sample * devices + device)
        for sample in range(samples)
        for device in range(devices)
    ]
    fetched = lax.ppermute(atom_single, ("sample", "atom"), pairs)
    packed, copies = pl.pallas_call(
        pack_kernel,
        out_shape=(
            jax.ShapeDtypeStruct((devices, 8, LANES), f32),
            jax.ShapeDtypeStruct((4,) + fetched.shape, bf16),
        ),
        in_specs=[smem] + [vmem] * 5,
        out_specs=(vmem, vmem),
        scratch_shapes=[pltpu.VMEM((8, LANES), f32)],
        cost_estimate=pl.CostEstimate(flops=40_000_000, bytes_accessed=10_000_000, transcendentals=1_000_000),
    )(first, pair_count.reshape(1, 1), positions, block_pairs, key_window, fetched)
    tiles = lax.all_to_all(packed, "atom", 0, 0)
    others = lax.all_to_all(
        copies,
        "sample",
        0,
        0,
        axis_index_groups=[[4 * i + j for j in range(4)] for i in range(samples // 4)],
    )

    force = pl.pallas_call(
        force_kernel,
        out_shape=jax.ShapeDtypeStruct((8, 2 * LANES), f32),
        in_specs=[smem, vmem, vmem, vmem],
        out_specs=vmem,
        scratch_shapes=[
            pltpu.VMEM((3, LANES, LANES), f32),
            pltpu.VMEM((3, LANES, LANES), f32),
            pltpu.VMEM((8, LANES), jnp.int32),
            pltpu.VMEM((8, LANES), f32),
            pltpu.SMEM((8, LANES), jnp.int32),
            pltpu.SMEM((8, LANES), f32),
            pltpu.SemaphoreType.DMA((2,)),
        ],
        cost_estimate=pl.CostEstimate(flops=80_000_000, bytes_accessed=16_000_000, transcendentals=2_000_000),
    )(first, tiles, positions, bond_atoms)

    rows = atom_single.shape[0]
    weights = (w_query, w_key, w_value, w_out, w_gate_up, w_down)
    return pl.pallas_call(
        step_kernel,
        out_shape=jax.ShapeDtypeStruct(positions.shape, f32),
        in_specs=[smem] + [vmem] * 16,
        out_specs=vmem,
        scratch_shapes=[
            pltpu.VMEM((LANES, 5 * rows), f32),
            pltpu.VMEM((5 * rows, LANES), bf16),
            pltpu.VMEM((LANES, 5 * rows), bf16),
            pltpu.VMEM((5 * rows, 2 * LANES), bf16),
            pltpu.VMEM((HEADS * 48, 5 * rows), bf16),
            pltpu.VMEM((3, LANES, rows), bf16),
            pltpu.VMEM((LANES, 5 * rows), bf16),
            pltpu.VMEM((8, rows), f32),
        ],
        cost_estimate=pl.CostEstimate(flops=2_000_000_000, bytes_accessed=1_200_000, transcendentals=3_000_000),
        compiler_params=pltpu.CompilerParams(vmem_limit_bytes=48 * 1024 * 1024),
    )(
        first,
        timestep.reshape(1, 1),
        tiles,
        others,
        atom_single,
        positions,
        fresh_noise,
        force,
        pos_weight,
        ln_gain,
        w_head,
        *weights,
    )


def solution(mesh):
    in_specs = (
        P(None, ("sample", "atom")),
        P(None, ("sample", "atom")),
        P(),
        P("atom", None),
        P(),
        P(),
        P(),
        P(),
        P(),
        P(),
        P(),
        P(),
        P(),
        P("atom", None),
        P(None, "atom"),
        P("atom"),
        P(None, "atom", None),
    )
    out_specs = P(None, ("sample", "atom"))
    return jax.shard_map(body, mesh=mesh, in_specs=in_specs, out_specs=out_specs, check_vma=False)
```

```python
import functools
import math

import jax
import jax.numpy as jnp
from jax import lax
from jax.experimental import pallas as pl
from jax.experimental.pallas import tpu as pltpu
from jax.sharding import PartitionSpec as P

HEADS = 4
LANES = 128
ROWS = 256
NORM_EPS = 1e-05
STEER = 0.3
ABSENT = -(2.0**120)
LOG2E = 1.4426950408889634
KAPPA = 2.0 * math.sqrt(LOG2E)

f32 = jnp.float32
bf16 = jnp.bfloat16


def pack_kernel(first_ref, count_ref, positions_ref, pairs_ref, window_ref, out_ref, tile):
    for row in range(6):
        part = slice((row % 2) * LANES, (row % 2 + 1) * LANES)
        tile[row : row + 1, :] = positions_ref[row // 2 : row // 2 + 1, part]
    pairs = pairs_ref[...]
    lane = lax.broadcasted_iota(jnp.int32, (1, pairs.shape[1]), 1)
    codes = jnp.where(lane < count_ref[0], pairs[0:1] * 64 + pairs[1:2], -1).astype(f32)
    tile[6:7, :] = jnp.concatenate([codes, codes], axis=1)
    window = window_ref[...]
    own = first_ref[0] * 2 + lax.broadcasted_iota(jnp.int32, window.shape, 0)
    lane = lax.broadcasted_iota(jnp.int32, (1, LANES), 1)
    counts = jnp.zeros((1, LANES), f32)
    for offset in range(5):
        hit = jnp.sum((window == own + (offset - 2)).astype(f32), axis=1, keepdims=True)
        counts = jnp.where(lane == offset, hit[0:1], counts)
        counts = jnp.where(lane == 8 + offset, hit[1:2], counts)
    tile[7:8, :] = jnp.where(counts > 0.0, jnp.log2(jnp.maximum(counts, 1.0)), ABSENT)
    out_ref[...] = jnp.broadcast_to(tile[...][None], out_ref.shape)


def split3(values):
    high = values.astype(bf16)
    rest = values - high.astype(f32)
    mid = rest.astype(bf16)
    low = (rest - mid.astype(f32)).astype(bf16)
    return jnp.concatenate([high, mid, low], axis=0)


def join3(values):
    rows = values.shape[0] // 3
    return values[:rows] + values[rows : 2 * rows] + values[2 * rows :]


def norm_columns(values):
    center = values - jnp.mean(values, axis=0, keepdims=True)
    spread = jnp.mean(center * center, axis=0, keepdims=True)
    return center * lax.rsqrt(spread + NORM_EPS)


def dot_t(left, right):
    return lax.dot_general(left, right, (((0,), (0,)), ((), ())), preferred_element_type=f32)


def dot_nt(left, right):
    return lax.dot_general(left, right, (((1,), (1,)), ((), ())), preferred_element_type=f32)


def dot(left, right):
    return jnp.dot(left, right, preferred_element_type=f32)


def force_kernel(first_ref, tiles_ref, positions_ref, bonds_ref, out_ref, spread_own, push, list_v, bias_v, list_s, bias_s, sems):
    me = first_ref[0]

    codes = tiles_ref[:, 6, :].astype(jnp.int32)
    half = lax.broadcasted_iota(jnp.int32, codes.shape, 1) // 64
    mine = me * 2 + half
    first = jnp.where(codes < 0, -1, codes // 64)
    second = jnp.where(codes < 0, -1, codes % 64)
    partner = jnp.where(first == mine, second, jnp.where(second == mine, first, -1)).astype(f32)
    block_id = lax.broadcasted_iota(jnp.int32, (64, LANES), 0).astype(f32)
    hits = jnp.zeros((64, LANES), f32)
    for row in range(codes.shape[0]):
        hits = hits + jnp.where(partner[row : row + 1] == block_id, 1.0, 0.0)
    row_half = lax.broadcasted_iota(jnp.int32, (LANES, LANES), 0) // 64
    col_half = lax.broadcasted_iota(jnp.int32, (LANES, LANES), 1) // 64
    count = dot(hits.astype(bf16), (row_half == col_half).astype(bf16))
    present = count > 0.5
    lower = lax.broadcasted_iota(jnp.int32, (64, 64), 1) < lax.broadcasted_iota(jnp.int32, (64, 64), 0)
    rank = dot(lower.astype(bf16), present.astype(bf16))
    slot = (lax.broadcasted_iota(jnp.int32, (64, LANES), 1) % 64).astype(f32)
    chosen = present & (rank == slot)
    listed = jnp.sum(jnp.where(chosen, block_id, 0.0), axis=0, keepdims=True)
    times = jnp.sum(jnp.where(chosen, count, 0.0), axis=0, keepdims=True)
    total = jnp.sum(present.astype(f32), axis=0, keepdims=True)
    list_v[0:1, :] = listed.astype(jnp.int32)
    list_v[1:2, :] = total.astype(jnp.int32)
    bias_v[0:1, :] = jnp.where(times > 0.5, jnp.log2(jnp.maximum(times, 1.0)), ABSENT)
    list_copy = pltpu.make_async_copy(list_v, list_s, sems.at[0])
    bias_copy = pltpu.make_async_copy(bias_v, bias_s, sems.at[1])
    list_copy.start()
    bias_copy.start()

    positions = jnp.concatenate([positions_ref[...], jnp.zeros((5, 2 * LANES), f32)], axis=0)

    forces = []
    atom_id = lax.broadcasted_iota(jnp.int32, (LANES, LANES), 0)
    for block in range(2):
        incidence = (
            (atom_id == bonds_ref[0, block : block + 1, :]).astype(f32)
            - (atom_id == bonds_ref[1, block : block + 1, :]).astype(f32)
        ).astype(bf16)
        offset = join3(dot(split3(positions[:, block * LANES : (block + 1) * LANES]), incidence))
        stretch = jnp.sum(offset * offset, axis=0, keepdims=True) - 1.0
        pull = (-0.2 * stretch) * offset
        forces.append(join3(dot_nt(split3(pull), incidence)))

    list_copy.wait()
    bias_copy.wait()
    for block in range(2):
        for comp in range(3):
            row = positions_ref[comp : comp + 1, block * LANES : (block + 1) * LANES] * KAPPA
            spread_own[comp] = jnp.broadcast_to(row, (LANES, LANES)).T
            push[comp] = jnp.zeros((LANES, LANES), f32)

        def one_pair(index, carry, block=block):
            partners = []
            for sub in range(2):
                entry = block * 64 + 2 * index + sub
                partner = list_s[0, entry]
                device = partner // 2
                within = partner % 2
                rows = [
                    tiles_ref[device, pl.ds(2 * comp + within, 1), :] * KAPPA for comp in range(3)
                ]
                partners.append((rows, bias_s[0, entry]))
            for group in range(0, LANES, 8):
                own = [spread_own[comp, group : group + 8, :] for comp in range(3)]
                sums = [push[comp, group : group + 8, :] for comp in range(3)]
                for rows, bias in partners:
                    offset = [own[comp] - rows[comp] for comp in range(3)]
                    power = bias - offset[0] * offset[0]
                    power = power - offset[1] * offset[1]
                    power = power - offset[2] * offset[2]
                    weight = jnp.exp2(power)
                    sums = [sums[comp] + weight * offset[comp] for comp in range(3)]
                for comp in range(3):
                    push[comp, group : group + 8, :] = sums[comp]
            return carry

        lax.fori_loop(0, (list_s[1, block * 64] + 1) // 2, one_pair, 0)
        rows = [jnp.sum(push[comp].T, axis=0, keepdims=True) for comp in range(3)]
        clash = jnp.concatenate(rows + [jnp.zeros((5, LANES), f32)], axis=0)
        forces[block] = forces[block] + clash * (8.0 / KAPPA)
    out_ref[...] = jnp.concatenate(forces, axis=1)


def step_kernel(
    first_ref,
    time_ref,
    tiles_ref,
    others_ref,
    own_ref,
    positions_ref,
    noise_ref,
    force_ref,
    pos_weight_ref,
    gain_ref,
    w_head_ref,
    w_query_ref,
    w_key_ref,
    w_value_ref,
    w_out_ref,
    w_gate_up_ref,
    w_down_ref,
    out_ref,
    stream,
    near,
    queries,
    keys,
    values,
    bias,
    attended,
    low_high,
):
    me = first_ref[0]
    last = tiles_ref.shape[0] - 1
    head_size = LANES // HEADS
    query_scale = LOG2E * head_size ** -0.5

    level = 0.2 + 0.02 * jnp.full((1, ROWS), time_ref[0], jnp.int32).astype(f32)
    spread_sq = level * level + 1.0
    c_input = 1.0 / jnp.sqrt(spread_sq)

    columns = jnp.concatenate(
        [pos_weight_ref[...], gain_ref[0], gain_ref[1], jnp.zeros((1, LANES), f32)], axis=0
    ).T

    row_block = lax.broadcasted_iota(jnp.int32, (5 * ROWS, LANES), 0) // LANES
    lane = lax.broadcasted_iota(jnp.int32, (5 * ROWS, LANES), 1)
    keys[:, LANES:] = jnp.where((lane % 16 == row_block) & (lane < 32), 1.0, 0.0).astype(bf16)
    for place in range(1, 4):
        window = tiles_ref[jnp.clip(me + (place - 2), 0, last), 7:8, :]
        rows = []
        for chunk in range(16):
            sides = []
            for block in range(2):
                offset = chunk - 2 * (place - 1) - block
                if 0 <= offset < 5:
                    lane_id = block * 8 + offset
                    sides.append(jnp.broadcast_to(window[:, lane_id : lane_id + 1], (1, LANES)))
                else:
                    sides.append(jnp.full((1, LANES), ABSENT, f32))
            rows.append(jnp.concatenate(sides, axis=1))
        rows = jnp.concatenate(rows, axis=0)
        high = rows.astype(bf16)
        low = (rows - high.astype(f32)).astype(bf16)
        bias[place - 1] = jnp.concatenate([high, low, jnp.zeros((LANES - 32, ROWS), bf16)], axis=0)

    identity = (
        lax.broadcasted_iota(jnp.int32, (LANES, LANES), 0)
        == lax.broadcasted_iota(jnp.int32, (LANES, LANES), 1)
    ).astype(f32).astype(bf16)
    for place, other in enumerate((0, 1, None, 2, 3)):
        device = jnp.clip(me + (place - 2), 0, last)
        block = own_ref[...] if other is None else others_ref[other]
        total_t = dot_nt(identity, block)
        for comp in range(3):
            row = jnp.concatenate(
                [tiles_ref[device, 2 * comp : 2 * comp + 1, :], tiles_ref[device, 2 * comp + 1 : 2 * comp + 2, :]],
                axis=1,
            )
            total_t = total_t + columns[:, comp : comp + 1] * (row * c_input)
        stream[:, place * ROWS : (place + 1) * ROWS] = total_t

    def window_of(place):
        return pl.ds(pl.multiple_of((place - 1) * ROWS, ROWS), 3 * ROWS)

    def attend(place, exact):
        window = window_of(place)
        here = pl.ds(pl.multiple_of(place * ROWS, ROWS), ROWS)
        key_rows = keys[window, :]
        query_t = queries[:, here]
        counts = bias[place - 1]
        pieces = []
        sums = []

        def scores_of(head):
            parts = []
            if head:
                parts.append(jnp.zeros((head * head_size, ROWS), bf16))
            parts.append(query_t[head * head_size : (head + 1) * head_size])
            if head < HEADS - 1:
                parts.append(jnp.zeros(((HEADS - 1 - head) * head_size, ROWS), bf16))
            return dot(key_rows, jnp.concatenate(parts + [counts], axis=0))

        following = scores_of(0)
        for head in range(HEADS):
            scores = following
            if head < HEADS - 1:
                following = scores_of(head + 1)
            if exact:
                scores = scores - jnp.max(scores, axis=0, keepdims=True)
            blank = jnp.zeros((LANES, LANES), bf16)
            weights = jnp.concatenate(
                [
                    jnp.concatenate([jnp.exp2(scores[: 5 * LANES, :LANES]).astype(bf16), blank], axis=0),
                    jnp.concatenate([blank, jnp.exp2(scores[LANES:, LANES:]).astype(bf16)], axis=0),
                ],
                axis=1,
            )
            mixed = dot(values[head * 48 : (head + 1) * 48, window], weights)
            total = mixed[head_size : head_size + 1]
            sums.append(total)
            pieces.append(mixed[:head_size] * (1.0 / total))
        attended[:, here] = jnp.concatenate(pieces, axis=0).astype(bf16)
        return jnp.concatenate(sums, axis=0)

    for layer in range(2):
        first, stop = layer, 5 - layer
        for place in range(first, stop):
            here = slice(place * ROWS, (place + 1) * ROWS)
            normed = norm_columns(stream[:, here]) * columns[:, 3 + 2 * layer : 4 + 2 * layer]
            near[here, :] = normed.astype(bf16).T
        span = slice(first * ROWS, stop * ROWS)
        inner = slice((first + 1) * ROWS, (stop - 1) * ROWS)
        keys[span, :LANES] = dot(near[span, :], w_key_ref[layer]).astype(bf16)
        queries[:, inner] = (dot_nt(w_query_ref[layer].T, near[inner, :]) * query_scale).astype(bf16)
        value_t = dot_nt(w_value_ref[layer].T, near[span, :]).astype(bf16)
        for head in range(HEADS):
            values[head * 48 : head * 48 + 32, span] = value_t[head * 32 : head * 32 + 32]
            values[head * 48 + 32 : head * 48 + 48, span] = jnp.ones((16, (stop - first) * ROWS), bf16)

        low_high[0:4, :] = jnp.full((4, ROWS), 1.0, f32)
        low_high[4:8, :] = jnp.full((4, ROWS), 1.0, f32)

        def quick(place, carry):
            sums = attend(place, False)
            low_high[0:4, :] = jnp.minimum(low_high[0:4, :], sums)
            low_high[4:8, :] = jnp.maximum(low_high[4:8, :], sums)
            return carry

        lax.fori_loop(first + 1, stop - 1, quick, 0)
        lowest = jnp.min(low_high[0:4, :])
        highest = jnp.max(low_high[4:8, :])
        safe = (lowest > 2.0**-80) & (highest < 2.0**100)

        @pl.when(jnp.logical_not(safe))
        def _():
            def exactly(place, carry):
                attend(place, True)
                return carry

            lax.fori_loop(first + 1, stop - 1, exactly, 0)

        now = stream[:, inner] + dot(w_out_ref[layer].T, attended[:, inner])
        normed = (norm_columns(now) * columns[:, 4 + 2 * layer : 5 + 2 * layer]).astype(bf16)
        gate_up = dot(w_gate_up_ref[layer].T, normed)
        width = gate_up.shape[0] // 2
        half, up = 0.5 * gate_up[:width], gate_up[width:]
        hidden = ((half + half * jnp.tanh(half)) * up).astype(bf16)
        stream[:, inner] = now + dot(w_down_ref[layer].T, hidden)

    final = norm_columns(stream[:, 2 * ROWS : 3 * ROWS])
    head_rows = jnp.concatenate([w_head_ref[...], jnp.zeros((5, LANES), f32)], axis=0)
    update = jnp.dot(head_rows, final, precision=lax.Precision.HIGHEST, preferred_element_type=f32)

    positions = jnp.concatenate([positions_ref[...], jnp.zeros((5, ROWS), f32)], axis=0)
    fresh = jnp.concatenate([noise_ref[...], jnp.zeros((5, ROWS), f32)], axis=0)
    denoised = positions * (1.0 / spread_sq) + (level * c_input) * update
    following = 0.85 * level
    result = denoised + STEER * force_ref[...] + following * (0.8 * (positions - denoised) / level + 0.6 * fresh)
    out_ref[...] = result[:3]


def body(
    positions,
    fresh_noise,
    timestep,
    atom_single,
    pos_weight,
    ln_gain,
    w_query,
    w_key,
    w_value,
    w_out,
    w_gate_up,
    w_down,
    w_head,
    key_window,
    block_pairs,
    pair_count,
    bond_atoms,
):
    devices = lax.axis_size("atom")
    first = lax.axis_index("atom").astype(jnp.int32).reshape(1)
    smem = pl.BlockSpec(memory_space=pltpu.SMEM)
    vmem = pl.BlockSpec(memory_space=pltpu.VMEM)

    samples = lax.axis_size("sample")
    shifts = (-2, -1, 1, 2)
    pairs = [
        (sample * devices + (device + shifts[sample % 4]) % devices, sample * devices + device)
        for sample in range(samples)
        for device in range(devices)
    ]
    fetched = lax.ppermute(atom_single, ("sample", "atom"), pairs)
    others = lax.all_to_all(
        jnp.broadcast_to(fetched[None], (4,) + fetched.shape),
        "sample",
        0,
        0,
        axis_index_groups=[[4 * i + j for j in range(4)] for i in range(samples // 4)],
    )

    packed = pl.pallas_call(
        pack_kernel,
        out_shape=jax.ShapeDtypeStruct((devices, 8, LANES), f32),
        in_specs=[smem, smem, vmem, vmem, vmem],
        out_specs=vmem,
        scratch_shapes=[pltpu.VMEM((8, LANES), f32)],
        cost_estimate=pl.CostEstimate(flops=40_000_000, bytes_accessed=10_000_000, transcendentals=1_000_000),
        compiler_params=pltpu.CompilerParams(vmem_limit_bytes=16 * 1024 * 1024),
    )(first, pair_count, positions, block_pairs, key_window)
    tiles = lax.all_to_all(packed, "atom", 0, 0)

    force = pl.pallas_call(
        force_kernel,
        out_shape=jax.ShapeDtypeStruct((8, 2 * LANES), f32),
        in_specs=[smem, vmem, vmem, vmem],
        out_specs=vmem,
        scratch_shapes=[
            pltpu.VMEM((3, LANES, LANES), f32),
            pltpu.VMEM((3, LANES, LANES), f32),
            pltpu.VMEM((8, LANES), jnp.int32),
            pltpu.VMEM((8, LANES), f32),
            pltpu.SMEM((8, LANES), jnp.int32),
            pltpu.SMEM((8, LANES), f32),
            pltpu.SemaphoreType.DMA((2,)),
        ],
        cost_estimate=pl.CostEstimate(flops=80_000_000, bytes_accessed=16_000_000, transcendentals=2_000_000),
        compiler_params=pltpu.CompilerParams(vmem_limit_bytes=16 * 1024 * 1024),
    )(first, tiles, positions, bond_atoms)

    rows = atom_single.shape[0]
    weights = (w_query, w_key, w_value, w_out, w_gate_up, w_down)
    return pl.pallas_call(
        step_kernel,
        out_shape=jax.ShapeDtypeStruct(positions.shape, f32),
        in_specs=[smem, smem] + [vmem] * 15,
        out_specs=vmem,
        scratch_shapes=[
            pltpu.VMEM((LANES, 5 * rows), f32),
            pltpu.VMEM((5 * rows, LANES), bf16),
            pltpu.VMEM((LANES, 5 * rows), bf16),
            pltpu.VMEM((5 * rows, 2 * LANES), bf16),
            pltpu.VMEM((HEADS * 48, 5 * rows), bf16),
            pltpu.VMEM((3, LANES, rows), bf16),
            pltpu.VMEM((LANES, 5 * rows), bf16),
            pltpu.VMEM((8, rows), f32),
        ],
        cost_estimate=pl.CostEstimate(flops=2_000_000_000, bytes_accessed=1_200_000, transcendentals=3_000_000),
        compiler_params=pltpu.CompilerParams(vmem_limit_bytes=48 * 1024 * 1024),
    )(
        first,
        timestep,
        tiles,
        others,
        atom_single,
        positions,
        fresh_noise,
        force,
        pos_weight,
        ln_gain,
        w_head,
        *weights,
    )


def solution(mesh):
    in_specs = (
        P(None, ("sample", "atom")),
        P(None, ("sample", "atom")),
        P(),
        P("atom", None),
        P(),
        P(),
        P(),
        P(),
        P(),
        P(),
        P(),
        P(),
        P(),
        P("atom", None),
        P(None, "atom"),
        P("atom"),
        P(None, "atom", None),
    )
    out_specs = P(None, ("sample", "atom"))
    return jax.shard_map(body, mesh=mesh, in_specs=in_specs, out_specs=out_specs, check_vma=False)
```

```python
import functools
import math

import jax
import jax.numpy as jnp
from jax import lax
from jax.experimental import pallas as pl
from jax.experimental.pallas import tpu as pltpu
from jax.sharding import PartitionSpec as P

HEADS = 4
LANES = 128
ROWS = 256
NORM_EPS = 1e-05
STEER = 0.3
ABSENT = -(2.0**120)
LOG2E = 1.4426950408889634
KAPPA = 2.0 * math.sqrt(LOG2E)

f32 = jnp.float32
bf16 = jnp.bfloat16


def pack_kernel(first_ref, count_ref, positions_ref, pairs_ref, window_ref, far_ref, near_ref, out_ref, halo_ref, tile):
    for row in range(6):
        part = slice((row % 2) * LANES, (row % 2 + 1) * LANES)
        tile[row : row + 1, :] = positions_ref[row // 2 : row // 2 + 1, part]
    pairs = pairs_ref[...]
    lane = lax.broadcasted_iota(jnp.int32, (1, pairs.shape[1]), 1)
    codes = jnp.where(lane < count_ref[0], pairs[0:1] * 64 + pairs[1:2], -1).astype(f32)
    tile[6:7, :] = jnp.concatenate([codes, codes], axis=1)
    window = window_ref[...]
    own = first_ref[0] * 2 + lax.broadcasted_iota(jnp.int32, window.shape, 0)
    lane = lax.broadcasted_iota(jnp.int32, (1, LANES), 1)
    counts = jnp.zeros((1, LANES), f32)
    for offset in range(5):
        hit = jnp.sum((window == own + (offset - 2)).astype(f32), axis=1, keepdims=True)
        counts = jnp.where(lane == offset, hit[0:1], counts)
        counts = jnp.where(lane == 8 + offset, hit[1:2], counts)
    tile[7:8, :] = jnp.where(counts > 0.0, jnp.log2(jnp.maximum(counts, 1.0)), ABSENT)
    out_ref[...] = jnp.broadcast_to(tile[...][None], out_ref.shape)
    halo_ref[0] = far_ref[...]
    halo_ref[1] = near_ref[...]


def split3(values):
    high = values.astype(bf16)
    rest = values - high.astype(f32)
    mid = rest.astype(bf16)
    low = (rest - mid.astype(f32)).astype(bf16)
    return jnp.concatenate([high, mid, low], axis=0)


def join3(values):
    rows = values.shape[0] // 3
    return values[:rows] + values[rows : 2 * rows] + values[2 * rows :]


def norm_columns(values):
    center = values - jnp.mean(values, axis=0, keepdims=True)
    spread = jnp.mean(center * center, axis=0, keepdims=True)
    return center * lax.rsqrt(spread + NORM_EPS)


def dot_t(left, right):
    return lax.dot_general(left, right, (((0,), (0,)), ((), ())), preferred_element_type=f32)


def dot_nt(left, right):
    return lax.dot_general(left, right, (((1,), (1,)), ((), ())), preferred_element_type=f32)


def dot(left, right):
    return jnp.dot(left, right, preferred_element_type=f32)


def force_kernel(first_ref, tiles_ref, positions_ref, bonds_ref, out_ref, spread_own, push, list_v, bias_v, list_s, bias_s, sems):
    me = first_ref[0]

    codes = tiles_ref[:, 6, :].astype(jnp.int32)
    half = lax.broadcasted_iota(jnp.int32, codes.shape, 1) // 64
    mine = me * 2 + half
    first = jnp.where(codes < 0, -1, codes // 64)
    second = jnp.where(codes < 0, -1, codes % 64)
    partner = jnp.where(first == mine, second, jnp.where(second == mine, first, -1)).astype(f32)
    block_id = lax.broadcasted_iota(jnp.int32, (64, LANES), 0).astype(f32)
    hits = jnp.zeros((64, LANES), f32)
    for row in range(codes.shape[0]):
        hits = hits + jnp.where(partner[row : row + 1] == block_id, 1.0, 0.0)
    row_half = lax.broadcasted_iota(jnp.int32, (LANES, LANES), 0) // 64
    col_half = lax.broadcasted_iota(jnp.int32, (LANES, LANES), 1) // 64
    count = dot(hits.astype(bf16), (row_half == col_half).astype(bf16))
    present = count > 0.5
    lower = lax.broadcasted_iota(jnp.int32, (64, 64), 1) < lax.broadcasted_iota(jnp.int32, (64, 64), 0)
    rank = dot(lower.astype(bf16), present.astype(bf16))
    slot = (lax.broadcasted_iota(jnp.int32, (64, LANES), 1) % 64).astype(f32)
    chosen = present & (rank == slot)
    listed = jnp.sum(jnp.where(chosen, block_id, 0.0), axis=0, keepdims=True)
    times = jnp.sum(jnp.where(chosen, count, 0.0), axis=0, keepdims=True)
    total = jnp.sum(present.astype(f32), axis=0, keepdims=True)
    list_v[0:1, :] = listed.astype(jnp.int32)
    list_v[1:2, :] = total.astype(jnp.int32)
    bias_v[0:1, :] = jnp.where(times > 0.5, jnp.log2(jnp.maximum(times, 1.0)), ABSENT)
    list_copy = pltpu.make_async_copy(list_v, list_s, sems.at[0])
    bias_copy = pltpu.make_async_copy(bias_v, bias_s, sems.at[1])
    list_copy.start()
    bias_copy.start()

    positions = jnp.concatenate([positions_ref[...], jnp.zeros((5, 2 * LANES), f32)], axis=0)

    forces = []
    atom_id = lax.broadcasted_iota(jnp.int32, (LANES, LANES), 0)
    for block in range(2):
        incidence = (
            (atom_id == bonds_ref[0, block : block + 1, :]).astype(f32)
            - (atom_id == bonds_ref[1, block : block + 1, :]).astype(f32)
        ).astype(bf16)
        offset = join3(dot(split3(positions[:, block * LANES : (block + 1) * LANES]), incidence))
        stretch = jnp.sum(offset * offset, axis=0, keepdims=True) - 1.0
        pull = (-0.2 * stretch) * offset
        forces.append(join3(dot_nt(split3(pull), incidence)))

    list_copy.wait()
    bias_copy.wait()
    for block in range(2):
        for comp in range(3):
            row = positions_ref[comp : comp + 1, block * LANES : (block + 1) * LANES] * KAPPA
            spread_own[comp] = jnp.broadcast_to(row, (LANES, LANES)).T
            push[comp] = jnp.zeros((LANES, LANES), f32)

        def one_pair(index, carry, block=block):
            partners = []
            for sub in range(2):
                entry = block * 64 + 2 * index + sub
                partner = list_s[0, entry]
                device = partner // 2
                within = partner % 2
                rows = [
                    tiles_ref[device, pl.ds(2 * comp + within, 1), :] * KAPPA for comp in range(3)
                ]
                partners.append((rows, bias_s[0, entry]))
            for group in range(0, LANES, 8):
                own = [spread_own[comp, group : group + 8, :] for comp in range(3)]
                sums = [push[comp, group : group + 8, :] for comp in range(3)]
                for rows, bias in partners:
                    offset = [own[comp] - rows[comp] for comp in range(3)]
                    power = bias - offset[0] * offset[0]
                    power = power - offset[1] * offset[1]
                    power = power - offset[2] * offset[2]
                    weight = jnp.exp2(power)
                    sums = [sums[comp] + weight * offset[comp] for comp in range(3)]
                for comp in range(3):
                    push[comp, group : group + 8, :] = sums[comp]
            return carry

        lax.fori_loop(0, (list_s[1, block * 64] + 1) // 2, one_pair, 0)
        rows = [jnp.sum(push[comp].T, axis=0, keepdims=True) for comp in range(3)]
        clash = jnp.concatenate(rows + [jnp.zeros((5, LANES), f32)], axis=0)
        forces[block] = forces[block] + clash * (8.0 / KAPPA)
    out_ref[...] = jnp.concatenate(forces, axis=1)


def step_kernel(
    first_ref,
    time_ref,
    core_ref,
    tiles_ref,
    mine_ref,
    theirs_ref,
    own_ref,
    positions_ref,
    noise_ref,
    force_ref,
    pos_weight_ref,
    gain_ref,
    w_head_ref,
    w_query_ref,
    w_key_ref,
    w_value_ref,
    w_out_ref,
    w_gate_up_ref,
    w_down_ref,
    out_ref,
    stream,
    near,
    queries,
    keys,
    values,
    bias,
    attended,
    low_high,
):
    me = first_ref[0]
    last = tiles_ref.shape[0] - 1
    head_size = LANES // HEADS
    query_scale = LOG2E * head_size ** -0.5

    level = 0.2 + 0.02 * jnp.full((1, ROWS), time_ref[0], jnp.int32).astype(f32)
    spread_sq = level * level + 1.0
    c_input = 1.0 / jnp.sqrt(spread_sq)

    columns = jnp.concatenate(
        [pos_weight_ref[...], gain_ref[0], gain_ref[1], jnp.zeros((1, LANES), f32)], axis=0
    ).T

    row_block = lax.broadcasted_iota(jnp.int32, (5 * ROWS, LANES), 0) // LANES
    lane = lax.broadcasted_iota(jnp.int32, (5 * ROWS, LANES), 1)
    keys[:, LANES:] = jnp.where((lane % 16 == row_block) & (lane < 32), 1.0, 0.0).astype(bf16)
    for place in range(1, 4):
        window = tiles_ref[jnp.clip(me + (place - 2), 0, last), 7:8, :]
        rows = []
        for chunk in range(16):
            sides = []
            for block in range(2):
                offset = chunk - 2 * (place - 1) - block
                if 0 <= offset < 5:
                    lane_id = block * 8 + offset
                    sides.append(jnp.broadcast_to(window[:, lane_id : lane_id + 1], (1, LANES)))
                else:
                    sides.append(jnp.full((1, LANES), ABSENT, f32))
            rows.append(jnp.concatenate(sides, axis=1))
        rows = jnp.concatenate(rows, axis=0)
        high = rows.astype(bf16)
        low = (rows - high.astype(f32)).astype(bf16)
        bias[place - 1] = jnp.concatenate([high, low, jnp.zeros((LANES - 32, ROWS), bf16)], axis=0)

    identity = (
        lax.broadcasted_iota(jnp.int32, (LANES, LANES), 0)
        == lax.broadcasted_iota(jnp.int32, (LANES, LANES), 1)
    ).astype(f32).astype(bf16)
    left_core = jnp.full((ROWS, LANES), core_ref[0], jnp.int32) == 0
    for place, (ref, other, index) in enumerate(
        (
            (mine_ref, theirs_ref, 0),
            (mine_ref, theirs_ref, 1),
            (own_ref, None, None),
            (theirs_ref, mine_ref, 1),
            (theirs_ref, mine_ref, 0),
        )
    ):
        device = jnp.clip(me + (place - 2), 0, last)
        if other is None:
            block = ref[...]
        else:
            block = jnp.where(left_core, ref[index].astype(f32), other[index].astype(f32)).astype(bf16)
        total_t = dot_nt(identity, block)
        for comp in range(3):
            row = jnp.concatenate(
                [tiles_ref[device, 2 * comp : 2 * comp + 1, :], tiles_ref[device, 2 * comp + 1 : 2 * comp + 2, :]],
                axis=1,
            )
            total_t = total_t + columns[:, comp : comp + 1] * (row * c_input)
        stream[:, place * ROWS : (place + 1) * ROWS] = total_t

    def window_of(place):
        return pl.ds(pl.multiple_of((place - 1) * ROWS, ROWS), 3 * ROWS)

    def attend(place, exact):
        window = window_of(place)
        here = pl.ds(pl.multiple_of(place * ROWS, ROWS), ROWS)
        key_rows = keys[window, :]
        query_t = queries[:, here]
        counts = bias[place - 1]
        pieces = []
        sums = []

        def scores_of(head):
            parts = []
            if head:
                parts.append(jnp.zeros((head * head_size, ROWS), bf16))
            parts.append(query_t[head * head_size : (head + 1) * head_size])
            if head < HEADS - 1:
                parts.append(jnp.zeros(((HEADS - 1 - head) * head_size, ROWS), bf16))
            return dot(key_rows, jnp.concatenate(parts + [counts], axis=0))

        following = scores_of(0)
        for head in range(HEADS):
            scores = following
            if head < HEADS - 1:
                following = scores_of(head + 1)
            if exact:
                scores = scores - jnp.max(scores, axis=0, keepdims=True)
            blank = jnp.zeros((LANES, LANES), bf16)
            weights = jnp.concatenate(
                [
                    jnp.concatenate([jnp.exp2(scores[: 5 * LANES, :LANES]).astype(bf16), blank], axis=0),
                    jnp.concatenate([blank, jnp.exp2(scores[LANES:, LANES:]).astype(bf16)], axis=0),
                ],
                axis=1,
            )
            mixed = dot(values[head * 48 : (head + 1) * 48, window], weights)
            total = mixed[head_size : head_size + 1]
            sums.append(total)
            pieces.append(mixed[:head_size] * (1.0 / total))
        attended[:, here] = jnp.concatenate(pieces, axis=0).astype(bf16)
        return jnp.concatenate(sums, axis=0)

    for layer in range(2):
        first, stop = layer, 5 - layer
        for place in range(first, stop):
            here = slice(place * ROWS, (place + 1) * ROWS)
            normed = norm_columns(stream[:, here]) * columns[:, 3 + 2 * layer : 4 + 2 * layer]
            near[here, :] = normed.astype(bf16).T
        span = slice(first * ROWS, stop * ROWS)
        inner = slice((first + 1) * ROWS, (stop - 1) * ROWS)
        keys[span, :LANES] = dot(near[span, :], w_key_ref[layer]).astype(bf16)
        queries[:, inner] = (dot_nt(w_query_ref[layer].T, near[inner, :]) * query_scale).astype(bf16)
        value_t = dot_nt(w_value_ref[layer].T, near[span, :]).astype(bf16)
        for head in range(HEADS):
            values[head * 48 : head * 48 + 32, span] = value_t[head * 32 : head * 32 + 32]
            values[head * 48 + 32 : head * 48 + 48, span] = jnp.ones((16, (stop - first) * ROWS), bf16)

        low_high[0:4, :] = jnp.full((4, ROWS), 1.0, f32)
        low_high[4:8, :] = jnp.full((4, ROWS), 1.0, f32)

        def quick(place, carry):
            sums = attend(place, False)
            low_high[0:4, :] = jnp.minimum(low_high[0:4, :], sums)
            low_high[4:8, :] = jnp.maximum(low_high[4:8, :], sums)
            return carry

        lax.fori_loop(first + 1, stop - 1, quick, 0)
        lowest = jnp.min(low_high[0:4, :])
        highest = jnp.max(low_high[4:8, :])
        safe = (lowest > 2.0**-80) & (highest < 2.0**100)

        @pl.when(jnp.logical_not(safe))
        def _():
            def exactly(place, carry):
                attend(place, True)
                return carry

            lax.fori_loop(first + 1, stop - 1, exactly, 0)

        now = stream[:, inner] + dot(w_out_ref[layer].T, attended[:, inner])
        normed = (norm_columns(now) * columns[:, 4 + 2 * layer : 5 + 2 * layer]).astype(bf16)
        gate_up = dot(w_gate_up_ref[layer].T, normed)
        width = gate_up.shape[0] // 2
        half, up = 0.5 * gate_up[:width], gate_up[width:]
        hidden = ((half + half * jnp.tanh(half)) * up).astype(bf16)
        stream[:, inner] = now + dot(w_down_ref[layer].T, hidden)

    final = norm_columns(stream[:, 2 * ROWS : 3 * ROWS])
    head_rows = jnp.concatenate([w_head_ref[...], jnp.zeros((5, LANES), f32)], axis=0)
    update = jnp.dot(head_rows, final, precision=lax.Precision.HIGHEST, preferred_element_type=f32)

    positions = jnp.concatenate([positions_ref[...], jnp.zeros((5, ROWS), f32)], axis=0)
    fresh = jnp.concatenate([noise_ref[...], jnp.zeros((5, ROWS), f32)], axis=0)
    denoised = positions * (1.0 / spread_sq) + (level * c_input) * update
    following = 0.85 * level
    result = denoised + STEER * force_ref[...] + following * (0.8 * (positions - denoised) / level + 0.6 * fresh)
    out_ref[...] = result[:3]


def body(
    positions,
    fresh_noise,
    timestep,
    atom_single,
    pos_weight,
    ln_gain,
    w_query,
    w_key,
    w_value,
    w_out,
    w_gate_up,
    w_down,
    w_head,
    key_window,
    block_pairs,
    pair_count,
    bond_atoms,
):
    devices = lax.axis_size("atom")
    first = lax.axis_index("atom").astype(jnp.int32).reshape(1)
    smem = pl.BlockSpec(memory_space=pltpu.SMEM)
    vmem = pl.BlockSpec(memory_space=pltpu.VMEM)

    samples = lax.axis_size("sample")
    core = (lax.axis_index("sample").astype(jnp.int32) & 1).reshape(1)

    def fetched(distance):
        pairs = []
        for sample in range(samples):
            shift = distance if sample % 2 else -distance
            for device in range(devices):
                source = (device + shift) % devices
                pairs.append((sample * devices + source, sample * devices + device))
        return lax.ppermute(atom_single, ("sample", "atom"), pairs)

    far, near = fetched(2), fetched(1)
    packed, mine = pl.pallas_call(
        pack_kernel,
        out_shape=(
            jax.ShapeDtypeStruct((devices, 8, LANES), f32),
            jax.ShapeDtypeStruct((2,) + atom_single.shape, bf16),
        ),
        in_specs=[smem, smem] + [vmem] * 5,
        out_specs=(vmem, vmem),
        scratch_shapes=[pltpu.VMEM((8, LANES), f32)],
        cost_estimate=pl.CostEstimate(flops=40_000_000, bytes_accessed=10_000_000, transcendentals=1_000_000),
        compiler_params=pltpu.CompilerParams(vmem_limit_bytes=16 * 1024 * 1024),
    )(first, pair_count, positions, block_pairs, key_window, far, near)
    tiles = lax.all_to_all(packed, "atom", 0, 0)
    theirs = lax.ppermute(mine, "sample", [(i, i ^ 1) for i in range(samples)])

    force = pl.pallas_call(
        force_kernel,
        out_shape=jax.ShapeDtypeStruct((8, 2 * LANES), f32),
        in_specs=[smem, vmem, vmem, vmem],
        out_specs=vmem,
        scratch_shapes=[
            pltpu.VMEM((3, LANES, LANES), f32),
            pltpu.VMEM((3, LANES, LANES), f32),
            pltpu.VMEM((8, LANES), jnp.int32),
            pltpu.VMEM((8, LANES), f32),
            pltpu.SMEM((8, LANES), jnp.int32),
            pltpu.SMEM((8, LANES), f32),
            pltpu.SemaphoreType.DMA((2,)),
        ],
        cost_estimate=pl.CostEstimate(flops=80_000_000, bytes_accessed=16_000_000, transcendentals=2_000_000),
        compiler_params=pltpu.CompilerParams(vmem_limit_bytes=16 * 1024 * 1024),
    )(first, tiles, positions, bond_atoms)

    rows = atom_single.shape[0]
    weights = (w_query, w_key, w_value, w_out, w_gate_up, w_down)
    return pl.pallas_call(
        step_kernel,
        out_shape=jax.ShapeDtypeStruct(positions.shape, f32),
        in_specs=[smem] * 3 + [vmem] * 16,
        out_specs=vmem,
        scratch_shapes=[
            pltpu.VMEM((LANES, 5 * rows), f32),
            pltpu.VMEM((5 * rows, LANES), bf16),
            pltpu.VMEM((LANES, 5 * rows), bf16),
            pltpu.VMEM((5 * rows, 2 * LANES), bf16),
            pltpu.VMEM((HEADS * 48, 5 * rows), bf16),
            pltpu.VMEM((3, LANES, rows), bf16),
            pltpu.VMEM((LANES, 5 * rows), bf16),
            pltpu.VMEM((8, rows), f32),
        ],
        cost_estimate=pl.CostEstimate(flops=2_000_000_000, bytes_accessed=1_200_000, transcendentals=3_000_000),
        compiler_params=pltpu.CompilerParams(vmem_limit_bytes=48 * 1024 * 1024),
    )(
        first,
        timestep,
        core,
        tiles,
        mine,
        theirs,
        atom_single,
        positions,
        fresh_noise,
        force,
        pos_weight,
        ln_gain,
        w_head,
        *weights,
    )


def solution(mesh):
    in_specs = (
        P(None, ("sample", "atom")),
        P(None, ("sample", "atom")),
        P(),
        P("atom", None),
        P(),
        P(),
        P(),
        P(),
        P(),
        P(),
        P(),
        P(),
        P(),
        P("atom", None),
        P(None, "atom"),
        P("atom"),
        P(None, "atom", None),
    )
    out_specs = P(None, ("sample", "atom"))
    return jax.shard_map(body, mesh=mesh, in_specs=in_specs, out_specs=out_specs, check_vma=False)
```

```python
import functools
import math

import jax
import jax.numpy as jnp
from jax import lax
from jax.experimental import pallas as pl
from jax.experimental.pallas import tpu as pltpu
from jax.sharding import PartitionSpec as P

HEADS = 4
LANES = 128
ROWS = 256
NORM_EPS = 1e-05
STEER = 0.3
ABSENT = -(2.0**120)
LOG2E = 1.4426950408889634
KAPPA = 2.0 * math.sqrt(LOG2E)

f32 = jnp.float32
bf16 = jnp.bfloat16


def pack_kernel(first_ref, count_ref, positions_ref, pairs_ref, window_ref, out_ref, tile):
    for row in range(6):
        part = slice((row % 2) * LANES, (row % 2 + 1) * LANES)
        tile[row : row + 1, :] = positions_ref[row // 2 : row // 2 + 1, part]
    pairs = pairs_ref[...]
    lane = lax.broadcasted_iota(jnp.int32, (1, pairs.shape[1]), 1)
    codes = jnp.where(lane < count_ref[0], pairs[0:1] * 64 + pairs[1:2], -1).astype(f32)
    tile[6:7, :] = jnp.concatenate([codes, codes], axis=1)
    window = window_ref[...]
    own = first_ref[0] * 2 + lax.broadcasted_iota(jnp.int32, window.shape, 0)
    lane = lax.broadcasted_iota(jnp.int32, (1, LANES), 1)
    counts = jnp.zeros((1, LANES), f32)
    for offset in range(5):
        hit = jnp.sum((window == own + (offset - 2)).astype(f32), axis=1, keepdims=True)
        counts = jnp.where(lane == offset, hit[0:1], counts)
        counts = jnp.where(lane == 8 + offset, hit[1:2], counts)
    tile[7:8, :] = jnp.where(counts > 0.0, jnp.log2(jnp.maximum(counts, 1.0)), ABSENT)
    out_ref[...] = jnp.broadcast_to(tile[...][None], out_ref.shape)


def split3(values):
    high = values.astype(bf16)
    rest = values - high.astype(f32)
    mid = rest.astype(bf16)
    low = (rest - mid.astype(f32)).astype(bf16)
    return jnp.concatenate([high, mid, low], axis=0)


def join3(values):
    rows = values.shape[0] // 3
    return values[:rows] + values[rows : 2 * rows] + values[2 * rows :]


def norm_columns(values):
    center = values - jnp.mean(values, axis=0, keepdims=True)
    spread = jnp.mean(center * center, axis=0, keepdims=True)
    return center * lax.rsqrt(spread + NORM_EPS)


def dot_t(left, right):
    return lax.dot_general(left, right, (((0,), (0,)), ((), ())), preferred_element_type=f32)


def dot_nt(left, right):
    return lax.dot_general(left, right, (((1,), (1,)), ((), ())), preferred_element_type=f32)


def dot(left, right):
    return jnp.dot(left, right, preferred_element_type=f32)


def bond_kernel(positions_ref, bonds_ref, out_ref):
    positions = jnp.concatenate([positions_ref[...], jnp.zeros((5, 2 * LANES), f32)], axis=0)

    forces = []
    atom_id = lax.broadcasted_iota(jnp.int32, (LANES, LANES), 0)
    for block in range(2):
        incidence = (
            (atom_id == bonds_ref[0, block : block + 1, :]).astype(f32)
            - (atom_id == bonds_ref[1, block : block + 1, :]).astype(f32)
        ).astype(bf16)
        offset = join3(dot(split3(positions[:, block * LANES : (block + 1) * LANES]), incidence))
        stretch = jnp.sum(offset * offset, axis=0, keepdims=True) - 1.0
        pull = (-0.2 * stretch) * offset
        forces.append(join3(dot_nt(split3(pull), incidence)))
    out_ref[...] = jnp.concatenate(forces, axis=1)


def force_kernel(first_ref, tiles_ref, positions_ref, bond_ref, out_ref, spread_own, push, list_v, bias_v, list_s, bias_s, sems):
    me = first_ref[0]

    codes = tiles_ref[:, 6, :].astype(jnp.int32)
    half = lax.broadcasted_iota(jnp.int32, codes.shape, 1) // 64
    mine = me * 2 + half
    first = jnp.where(codes < 0, -1, codes // 64)
    second = jnp.where(codes < 0, -1, codes % 64)
    partner = jnp.where(first == mine, second, jnp.where(second == mine, first, -1)).astype(f32)
    block_id = lax.broadcasted_iota(jnp.int32, (64, LANES), 0).astype(f32)
    hits = jnp.zeros((64, LANES), f32)
    for row in range(codes.shape[0]):
        hits = hits + jnp.where(partner[row : row + 1] == block_id, 1.0, 0.0)
    row_half = lax.broadcasted_iota(jnp.int32, (LANES, LANES), 0) // 64
    col_half = lax.broadcasted_iota(jnp.int32, (LANES, LANES), 1) // 64
    count = dot(hits.astype(bf16), (row_half == col_half).astype(bf16))
    present = count > 0.5
    lower = lax.broadcasted_iota(jnp.int32, (64, 64), 1) < lax.broadcasted_iota(jnp.int32, (64, 64), 0)
    rank = dot(lower.astype(bf16), present.astype(bf16))
    slot = (lax.broadcasted_iota(jnp.int32, (64, LANES), 1) % 64).astype(f32)
    chosen = present & (rank == slot)
    listed = jnp.sum(jnp.where(chosen, block_id, 0.0), axis=0, keepdims=True)
    times = jnp.sum(jnp.where(chosen, count, 0.0), axis=0, keepdims=True)
    total = jnp.sum(present.astype(f32), axis=0, keepdims=True)
    list_v[0:1, :] = listed.astype(jnp.int32)
    list_v[1:2, :] = total.astype(jnp.int32)
    bias_v[0:1, :] = jnp.where(times > 0.5, jnp.log2(jnp.maximum(times, 1.0)), ABSENT)
    list_copy = pltpu.make_async_copy(list_v, list_s, sems.at[0])
    bias_copy = pltpu.make_async_copy(bias_v, bias_s, sems.at[1])
    list_copy.start()
    bias_copy.start()

    for block in range(2):
        for comp in range(3):
            row = positions_ref[comp : comp + 1, block * LANES : (block + 1) * LANES] * KAPPA
            spread_own[3 * block + comp] = jnp.broadcast_to(row, (LANES, LANES)).T
            push[3 * block + comp] = jnp.zeros((LANES, LANES), f32)

    forces = []
    list_copy.wait()
    bias_copy.wait()
    for block in range(2):

        def one_pair(index, carry, block=block):
            partners = []
            for sub in range(2):
                entry = block * 64 + 2 * index + sub
                partner = list_s[0, entry]
                device = partner // 2
                within = partner % 2
                rows = [
                    tiles_ref[device, pl.ds(2 * comp + within, 1), :] * KAPPA for comp in range(3)
                ]
                partners.append((rows, bias_s[0, entry]))
            for group in range(0, LANES, 8):
                own = [spread_own[3 * block + comp, group : group + 8, :] for comp in range(3)]
                sums = [push[3 * block + comp, group : group + 8, :] for comp in range(3)]
                for rows, bias in partners:
                    offset = [own[comp] - rows[comp] for comp in range(3)]
                    power = bias - offset[0] * offset[0]
                    power = power - offset[1] * offset[1]
                    power = power - offset[2] * offset[2]
                    weight = jnp.exp2(power)
                    sums = [sums[comp] + weight * offset[comp] for comp in range(3)]
                for comp in range(3):
                    push[3 * block + comp, group : group + 8, :] = sums[comp]
            return carry

        lax.fori_loop(0, (list_s[1, block * 64] + 1) // 2, one_pair, 0)
        rows = [jnp.sum(push[3 * block + comp].T, axis=0, keepdims=True) for comp in range(3)]
        clash = jnp.concatenate(rows + [jnp.zeros((5, LANES), f32)], axis=0)
        forces.append(clash * (8.0 / KAPPA))
    out_ref[...] = bond_ref[...] + jnp.concatenate(forces, axis=1)


def step_kernel(
    first_ref,
    time_ref,
    core_ref,
    tiles_ref,
    mine_ref,
    theirs_ref,
    own_ref,
    positions_ref,
    noise_ref,
    force_ref,
    pos_weight_ref,
    gain_ref,
    w_head_ref,
    w_query_ref,
    w_key_ref,
    w_value_ref,
    w_out_ref,
    w_gate_up_ref,
    w_down_ref,
    out_ref,
    stream,
    near,
    queries,
    keys,
    values,
    bias,
    attended,
    low_high,
):
    me = first_ref[0]
    last = tiles_ref.shape[0] - 1
    head_size = LANES // HEADS
    query_scale = LOG2E * head_size ** -0.5

    level = 0.2 + 0.02 * jnp.full((1, ROWS), time_ref[0], jnp.int32).astype(f32)
    spread_sq = level * level + 1.0
    c_input = 1.0 / jnp.sqrt(spread_sq)

    columns = jnp.concatenate(
        [pos_weight_ref[...], gain_ref[0], gain_ref[1], jnp.zeros((1, LANES), f32)], axis=0
    ).T

    row_block = lax.broadcasted_iota(jnp.int32, (5 * ROWS, LANES), 0) // LANES
    lane = lax.broadcasted_iota(jnp.int32, (5 * ROWS, LANES), 1)
    keys[:, LANES:] = jnp.where((lane % 16 == row_block) & (lane < 32), 1.0, 0.0).astype(bf16)
    for place in range(1, 4):
        window = tiles_ref[jnp.clip(me + (place - 2), 0, last), 7:8, :]
        rows = []
        for chunk in range(16):
            sides = []
            for block in range(2):
                offset = chunk - 2 * (place - 1) - block
                if 0 <= offset < 5:
                    lane_id = block * 8 + offset
                    sides.append(jnp.broadcast_to(window[:, lane_id : lane_id + 1], (1, LANES)))
                else:
                    sides.append(jnp.full((1, LANES), ABSENT, f32))
            rows.append(jnp.concatenate(sides, axis=1))
        rows = jnp.concatenate(rows, axis=0)
        high = rows.astype(bf16)
        low = (rows - high.astype(f32)).astype(bf16)
        bias[place - 1] = jnp.concatenate([high, low, jnp.zeros((LANES - 32, ROWS), bf16)], axis=0)

    identity = (
        lax.broadcasted_iota(jnp.int32, (LANES, LANES), 0)
        == lax.broadcasted_iota(jnp.int32, (LANES, LANES), 1)
    ).astype(f32).astype(bf16)
    left_core = jnp.full((ROWS, LANES), core_ref[0], jnp.int32) == 0
    for place, (ref, other, index) in enumerate(
        (
            (mine_ref, theirs_ref, 0),
            (mine_ref, theirs_ref, 1),
            (own_ref, None, None),
            (theirs_ref, mine_ref, 1),
            (theirs_ref, mine_ref, 0),
        )
    ):
        device = jnp.clip(me + (place - 2), 0, last)
        if other is None:
            block = ref[...]
        else:
            block = jnp.where(left_core, ref[index].astype(f32), other[index].astype(f32)).astype(bf16)
        total_t = dot_nt(identity, block)
        for comp in range(3):
            row = jnp.concatenate(
                [tiles_ref[device, 2 * comp : 2 * comp + 1, :], tiles_ref[device, 2 * comp + 1 : 2 * comp + 2, :]],
                axis=1,
            )
            total_t = total_t + columns[:, comp : comp + 1] * (row * c_input)
        stream[:, place * ROWS : (place + 1) * ROWS] = total_t

    def window_of(place):
        return pl.ds(pl.multiple_of((place - 1) * ROWS, ROWS), 3 * ROWS)

    def attend(place, exact):
        window = window_of(place)
        here = pl.ds(pl.multiple_of(place * ROWS, ROWS), ROWS)
        key_rows = keys[window, :]
        query_t = queries[:, here]
        counts = bias[place - 1]
        pieces = []
        sums = []

        def scores_of(head):
            parts = []
            if head:
                parts.append(jnp.zeros((head * head_size, ROWS), bf16))
            parts.append(query_t[head * head_size : (head + 1) * head_size])
            if head < HEADS - 1:
                parts.append(jnp.zeros(((HEADS - 1 - head) * head_size, ROWS), bf16))
            return dot(key_rows, jnp.concatenate(parts + [counts], axis=0))

        following = scores_of(0)
        for head in range(HEADS):
            scores = following
            if head < HEADS - 1:
                following = scores_of(head + 1)
            if exact:
                scores = scores - jnp.max(scores, axis=0, keepdims=True)
            blank = jnp.zeros((LANES, LANES), bf16)
            weights = jnp.concatenate(
                [
                    jnp.concatenate([jnp.exp2(scores[: 5 * LANES, :LANES]).astype(bf16), blank], axis=0),
                    jnp.concatenate([blank, jnp.exp2(scores[LANES:, LANES:]).astype(bf16)], axis=0),
                ],
                axis=1,
            )
            mixed = dot(values[head * 48 : (head + 1) * 48, window], weights)
            total = mixed[head_size : head_size + 1]
            sums.append(total)
            pieces.append(mixed[:head_size] * (1.0 / total))
        attended[:, here] = jnp.concatenate(pieces, axis=0).astype(bf16)
        return jnp.concatenate(sums, axis=0)

    for layer in range(2):
        first, stop = layer, 5 - layer
        for place in range(first, stop):
            here = slice(place * ROWS, (place + 1) * ROWS)
            normed = norm_columns(stream[:, here]) * columns[:, 3 + 2 * layer : 4 + 2 * layer]
            near[here, :] = normed.astype(bf16).T
        span = slice(first * ROWS, stop * ROWS)
        inner = slice((first + 1) * ROWS, (stop - 1) * ROWS)
        keys[span, :LANES] = dot(near[span, :], w_key_ref[layer]).astype(bf16)
        queries[:, inner] = (dot_nt(w_query_ref[layer].T, near[inner, :]) * query_scale).astype(bf16)
        value_t = dot_nt(w_value_ref[layer].T, near[span, :]).astype(bf16)
        for head in range(HEADS):
            values[head * 48 : head * 48 + 32, span] = value_t[head * 32 : head * 32 + 32]
            values[head * 48 + 32 : head * 48 + 48, span] = jnp.ones((16, (stop - first) * ROWS), bf16)

        low_high[0:4, :] = jnp.full((4, ROWS), 1.0, f32)
        low_high[4:8, :] = jnp.full((4, ROWS), 1.0, f32)

        def quick(place, carry):
            sums = attend(place, False)
            low_high[0:4, :] = jnp.minimum(low_high[0:4, :], sums)
            low_high[4:8, :] = jnp.maximum(low_high[4:8, :], sums)
            return carry

        lax.fori_loop(first + 1, stop - 1, quick, 0)
        lowest = jnp.min(low_high[0:4, :])
        highest = jnp.max(low_high[4:8, :])
        safe = (lowest > 2.0**-80) & (highest < 2.0**100)

        @pl.when(jnp.logical_not(safe))
        def _():
            def exactly(place, carry):
                attend(place, True)
                return carry

            lax.fori_loop(first + 1, stop - 1, exactly, 0)

        now = stream[:, inner] + dot(w_out_ref[layer].T, attended[:, inner])
        normed = (norm_columns(now) * columns[:, 4 + 2 * layer : 5 + 2 * layer]).astype(bf16)
        gate_up = dot(w_gate_up_ref[layer].T, normed)
        width = gate_up.shape[0] // 2
        half, up = 0.5 * gate_up[:width], gate_up[width:]
        hidden = ((half + half * jnp.tanh(half)) * up).astype(bf16)
        stream[:, inner] = now + dot(w_down_ref[layer].T, hidden)

    final = norm_columns(stream[:, 2 * ROWS : 3 * ROWS])
    head_rows = jnp.concatenate([w_head_ref[...], jnp.zeros((5, LANES), f32)], axis=0)
    update = jnp.dot(head_rows, final, precision=lax.Precision.HIGHEST, preferred_element_type=f32)

    positions = jnp.concatenate([positions_ref[...], jnp.zeros((5, ROWS), f32)], axis=0)
    fresh = jnp.concatenate([noise_ref[...], jnp.zeros((5, ROWS), f32)], axis=0)
    denoised = positions * (1.0 / spread_sq) + (level * c_input) * update
    following = 0.85 * level
    result = denoised + STEER * force_ref[...] + following * (0.8 * (positions - denoised) / level + 0.6 * fresh)
    out_ref[...] = result[:3]


def body(
    positions,
    fresh_noise,
    timestep,
    atom_single,
    pos_weight,
    ln_gain,
    w_query,
    w_key,
    w_value,
    w_out,
    w_gate_up,
    w_down,
    w_head,
    key_window,
    block_pairs,
    pair_count,
    bond_atoms,
):
    devices = lax.axis_size("atom")
    first = lax.axis_index("atom").astype(jnp.int32).reshape(1)
    smem = pl.BlockSpec(memory_space=pltpu.SMEM)
    vmem = pl.BlockSpec(memory_space=pltpu.VMEM)

    samples = lax.axis_size("sample")
    core = (lax.axis_index("sample").astype(jnp.int32) & 1).reshape(1)

    def fetched(distance):
        pairs = []
        for sample in range(samples):
            shift = distance if sample % 2 else -distance
            for device in range(devices):
                source = (device + shift) % devices
                pairs.append((sample * devices + source, sample * devices + device))
        return lax.ppermute(atom_single, ("sample", "atom"), pairs)

    far, near = fetched(2), fetched(1)
    packed = pl.pallas_call(
        pack_kernel,
        out_shape=jax.ShapeDtypeStruct((devices, 8, LANES), f32),
        in_specs=[smem, smem] + [vmem] * 3,
        out_specs=vmem,
        scratch_shapes=[pltpu.VMEM((8, LANES), f32)],
        cost_estimate=pl.CostEstimate(flops=40_000_000, bytes_accessed=10_000_000, transcendentals=1_000_000),
        compiler_params=pltpu.CompilerParams(vmem_limit_bytes=16 * 1024 * 1024),
    )(first, pair_count, positions, block_pairs, key_window)
    tiles = lax.all_to_all(packed, "atom", 0, 0)
    mine = jnp.stack([far, near])
    theirs = lax.ppermute(mine, "sample", [(i, i ^ 1) for i in range(samples)])

    bond_force = pl.pallas_call(
        bond_kernel,
        out_shape=jax.ShapeDtypeStruct((8, 2 * LANES), f32),
        in_specs=[vmem, vmem],
        out_specs=vmem,
        cost_estimate=pl.CostEstimate(flops=80_000_000, bytes_accessed=200_000_000, transcendentals=0),
        compiler_params=pltpu.CompilerParams(vmem_limit_bytes=16 * 1024 * 1024),
    )(positions, bond_atoms)

    force = pl.pallas_call(
        force_kernel,
        out_shape=jax.ShapeDtypeStruct((8, 2 * LANES), f32),
        in_specs=[smem, vmem, vmem, vmem],
        out_specs=vmem,
        scratch_shapes=[
            pltpu.VMEM((6, LANES, LANES), f32),
            pltpu.VMEM((6, LANES, LANES), f32),
            pltpu.VMEM((8, LANES), jnp.int32),
            pltpu.VMEM((8, LANES), f32),
            pltpu.SMEM((8, LANES), jnp.int32),
            pltpu.SMEM((8, LANES), f32),
            pltpu.SemaphoreType.DMA((2,)),
        ],
        cost_estimate=pl.CostEstimate(flops=80_000_000, bytes_accessed=16_000_000, transcendentals=2_000_000),
        compiler_params=pltpu.CompilerParams(vmem_limit_bytes=16 * 1024 * 1024),
    )(first, tiles, positions, bond_force)

    rows = atom_single.shape[0]
    weights = (w_query, w_key, w_value, w_out, w_gate_up, w_down)
    return pl.pallas_call(
        step_kernel,
        out_shape=jax.ShapeDtypeStruct(positions.shape, f32),
        in_specs=[smem] * 3 + [vmem] * 16,
        out_specs=vmem,
        scratch_shapes=[
            pltpu.VMEM((LANES, 5 * rows), f32),
            pltpu.VMEM((5 * rows, LANES), bf16),
            pltpu.VMEM((LANES, 5 * rows), bf16),
            pltpu.VMEM((5 * rows, 2 * LANES), bf16),
            pltpu.VMEM((HEADS * 48, 5 * rows), bf16),
            pltpu.VMEM((3, LANES, rows), bf16),
            pltpu.VMEM((LANES, 5 * rows), bf16),
            pltpu.VMEM((8, rows), f32),
        ],
        cost_estimate=pl.CostEstimate(flops=2_000_000_000, bytes_accessed=1_200_000, transcendentals=3_000_000),
        compiler_params=pltpu.CompilerParams(vmem_limit_bytes=48 * 1024 * 1024),
    )(
        first,
        timestep,
        core,
        tiles,
        mine,
        theirs,
        atom_single,
        positions,
        fresh_noise,
        force,
        pos_weight,
        ln_gain,
        w_head,
        *weights,
    )


def solution(mesh):
    in_specs = (
        P(None, ("sample", "atom")),
        P(None, ("sample", "atom")),
        P(),
        P("atom", None),
        P(),
        P(),
        P(),
        P(),
        P(),
        P(),
        P(),
        P(),
        P(),
        P("atom", None),
        P(None, "atom"),
        P("atom"),
        P(None, "atom", None),
    )
    out_specs = P(None, ("sample", "atom"))
    return jax.shard_map(body, mesh=mesh, in_specs=in_specs, out_specs=out_specs, check_vma=False)
```

```python
import functools
import math

import jax
import jax.numpy as jnp
from jax import lax
from jax.experimental import pallas as pl
from jax.experimental.pallas import tpu as pltpu
from jax.sharding import PartitionSpec as P

HEADS = 4
LANES = 128
ROWS = 256
VMEM_GRANT = 60 * 1024 * 1024
VMEM_SMALL = 16 * 1024 * 1024
NORM_EPS = 1e-05
STEER = 0.3
ABSENT = -(2.0**120)
LOG2E = 1.4426950408889634
KAPPA = 2.0 * math.sqrt(LOG2E)

f32 = jnp.float32
bf16 = jnp.bfloat16


def pack_kernel(first_ref, count_ref, positions_ref, pairs_ref, window_ref, after_ref, out_ref, counts_ref, tile):
    for row in range(6):
        part = slice((row % 2) * LANES, (row % 2 + 1) * LANES)
        tile[row : row + 1, :] = positions_ref[row // 2 : row // 2 + 1, part]
    pairs = pairs_ref[...]
    lane = lax.broadcasted_iota(jnp.int32, (1, pairs.shape[1]), 1)
    codes = jnp.where(lane < count_ref[0], pairs[0:1] * 64 + pairs[1:2], -1).astype(f32)
    tile[6:7, :] = jnp.concatenate([codes, codes], axis=1)
    window = window_ref[...]
    own = first_ref[0] * 2 + lax.broadcasted_iota(jnp.int32, window.shape, 0)
    lane = lax.broadcasted_iota(jnp.int32, (1, LANES), 1)
    counts = jnp.zeros((1, LANES), f32)
    for offset in range(5):
        hit = jnp.sum((window == own + (offset - 2)).astype(f32), axis=1, keepdims=True)
        counts = jnp.where(lane == offset, hit[0:1], counts)
        counts = jnp.where(lane == 8 + offset, hit[1:2], counts)
    tile[7:8, :] = jnp.zeros((1, LANES), f32)
    counts_ref[...] = jnp.where(counts > 0.0, jnp.log2(jnp.maximum(counts, 1.0)), ABSENT)
    out_ref[...] = jnp.broadcast_to(tile[...][None], out_ref.shape)


def split3(values):
    high = values.astype(bf16)
    rest = values - high.astype(f32)
    mid = rest.astype(bf16)
    low = (rest - mid.astype(f32)).astype(bf16)
    return jnp.concatenate([high, mid, low], axis=0)


def join3(values):
    rows = values.shape[0] // 3
    return values[:rows] + values[rows : 2 * rows] + values[2 * rows :]


def norm_columns(values):
    center = values - jnp.mean(values, axis=0, keepdims=True)
    spread = jnp.mean(center * center, axis=0, keepdims=True)
    return center * lax.rsqrt(spread + NORM_EPS)


def dot_t(left, right):
    return lax.dot_general(left, right, (((0,), (0,)), ((), ())), preferred_element_type=f32)


def dot_nt(left, right):
    return lax.dot_general(left, right, (((1,), (1,)), ((), ())), preferred_element_type=f32)


def dot(left, right):
    return jnp.dot(left, right, preferred_element_type=f32)


def bond_kernel(positions_ref, bonds_ref, out_ref):
    positions = jnp.concatenate([positions_ref[...], jnp.zeros((5, 2 * LANES), f32)], axis=0)

    forces = []
    atom_id = lax.broadcasted_iota(jnp.int32, (LANES, LANES), 0)
    for block in range(2):
        incidence = (
            (atom_id == bonds_ref[0, block : block + 1, :]).astype(f32)
            - (atom_id == bonds_ref[1, block : block + 1, :]).astype(f32)
        ).astype(bf16)
        offset = join3(dot(split3(positions[:, block * LANES : (block + 1) * LANES]), incidence))
        stretch = jnp.sum(offset * offset, axis=0, keepdims=True) - 1.0
        pull = (-0.2 * stretch) * offset
        forces.append(join3(dot_nt(split3(pull), incidence)))
    out_ref[...] = jnp.concatenate(forces, axis=1)


def force_kernel(first_ref, tiles_ref, positions_ref, bond_ref, out_ref, spread_own, push, list_v, bias_v, list_s, bias_s, sems):
    me = first_ref[0]

    codes = tiles_ref[:, 6, :].astype(jnp.int32)
    half = lax.broadcasted_iota(jnp.int32, codes.shape, 1) // 64
    mine = me * 2 + half
    first = jnp.where(codes < 0, -1, codes // 64)
    second = jnp.where(codes < 0, -1, codes % 64)
    partner = jnp.where(first == mine, second, jnp.where(second == mine, first, -1)).astype(f32)
    block_id = lax.broadcasted_iota(jnp.int32, (64, LANES), 0).astype(f32)
    hits = jnp.zeros((64, LANES), f32)
    for row in range(codes.shape[0]):
        hits = hits + jnp.where(partner[row : row + 1] == block_id, 1.0, 0.0)
    row_half = lax.broadcasted_iota(jnp.int32, (LANES, LANES), 0) // 64
    col_half = lax.broadcasted_iota(jnp.int32, (LANES, LANES), 1) // 64
    count = dot(hits.astype(bf16), (row_half == col_half).astype(bf16))
    present = count > 0.5
    lower = lax.broadcasted_iota(jnp.int32, (64, 64), 1) < lax.broadcasted_iota(jnp.int32, (64, 64), 0)
    rank = dot(lower.astype(bf16), present.astype(bf16))
    slot = (lax.broadcasted_iota(jnp.int32, (64, LANES), 1) % 64).astype(f32)
    chosen = present & (rank == slot)
    listed = jnp.sum(jnp.where(chosen, block_id, 0.0), axis=0, keepdims=True)
    times = jnp.sum(jnp.where(chosen, count, 0.0), axis=0, keepdims=True)
    total = jnp.sum(present.astype(f32), axis=0, keepdims=True)
    list_v[0:1, :] = listed.astype(jnp.int32)
    list_v[1:2, :] = total.astype(jnp.int32)
    bias_v[0:1, :] = jnp.where(times > 0.5, jnp.log2(jnp.maximum(times, 1.0)), ABSENT)
    list_copy = pltpu.make_async_copy(list_v, list_s, sems.at[0])
    bias_copy = pltpu.make_async_copy(bias_v, bias_s, sems.at[1])
    list_copy.start()
    bias_copy.start()

    for block in range(2):
        for comp in range(3):
            row = positions_ref[comp : comp + 1, block * LANES : (block + 1) * LANES] * KAPPA
            spread_own[3 * block + comp] = jnp.broadcast_to(row, (LANES, LANES)).T
            push[3 * block + comp] = jnp.zeros((LANES, LANES), f32)

    forces = []
    list_copy.wait()
    bias_copy.wait()
    for block in range(2):

        def one_pair(index, carry, block=block):
            partners = []
            for sub in range(2):
                entry = block * 64 + 2 * index + sub
                partner = list_s[0, entry]
                device = partner // 2
                within = partner % 2
                rows = [
                    tiles_ref[device, pl.ds(2 * comp + within, 1), :] * KAPPA for comp in range(3)
                ]
                partners.append((rows, bias_s[0, entry]))
            for group in range(0, LANES, 8):
                own = [spread_own[3 * block + comp, group : group + 8, :] for comp in range(3)]
                sums = [push[3 * block + comp, group : group + 8, :] for comp in range(3)]
                for rows, bias in partners:
                    offset = [own[comp] - rows[comp] for comp in range(3)]
                    power = bias - offset[0] * offset[0]
                    power = power - offset[1] * offset[1]
                    power = power - offset[2] * offset[2]
                    weight = jnp.exp2(power)
                    sums = [sums[comp] + weight * offset[comp] for comp in range(3)]
                for comp in range(3):
                    push[3 * block + comp, group : group + 8, :] = sums[comp]
            return carry

        lax.fori_loop(0, (list_s[1, block * 64] + 1) // 2, one_pair, 0)
        rows = [jnp.sum(push[3 * block + comp].T, axis=0, keepdims=True) for comp in range(3)]
        clash = jnp.concatenate(rows + [jnp.zeros((5, LANES), f32)], axis=0)
        forces.append(clash * (8.0 / KAPPA))
    out_ref[...] = bond_ref[...] + jnp.concatenate(forces, axis=1)


def start_copies(sources, targets, sems):
    copies = [
        pltpu.make_async_copy(source, target, sems.at[index])
        for index, (source, target) in enumerate(zip(sources, targets))
    ]
    for copy in copies:
        copy.start()
    return copies


def prepare_kernel(*refs):
    sources, (stream_ref, normed_ref, rows_ref), targets, sems = refs[:5], refs[5:8], refs[8:13], refs[13]
    time_ref, positions_ref, single_ref, pos_weight_ref, gain_ref = targets
    for copy in start_copies(sources, targets, sems):
        copy.wait()
    level = 0.2 + 0.02 * jnp.full((1, ROWS), time_ref[0], jnp.int32).astype(f32)
    spread_sq = level * level + 1.0
    c_input = 1.0 / jnp.sqrt(spread_sq)
    rows_ref[...] = jnp.concatenate([level, spread_sq, c_input, jnp.zeros((5, ROWS), f32)], axis=0)
    columns = jnp.concatenate(
        [pos_weight_ref[...], gain_ref[0, 0:1], jnp.zeros((4, LANES), f32)], axis=0
    ).T
    identity = (
        lax.broadcasted_iota(jnp.int32, (LANES, LANES), 0)
        == lax.broadcasted_iota(jnp.int32, (LANES, LANES), 1)
    ).astype(f32).astype(bf16)
    stream = dot_nt(identity, single_ref[...])
    for comp in range(3):
        stream = stream + columns[:, comp : comp + 1] * (positions_ref[comp : comp + 1, :] * c_input)
    stream_ref[...] = stream
    normed_ref[...] = (norm_columns(stream) * columns[:, 3:4]).astype(bf16).T


def layer_values(layer, halo, stream_ref, counts_ref, gain_ref, weights, scratch):
    left_ref, own_ref, right_ref = halo
    w_query_ref, w_key_ref, w_value_ref, w_out_ref, w_gate_up_ref, w_down_ref = weights
    near, keys, values, attended = scratch
    head_size = LANES // HEADS
    query_scale = LOG2E * head_size ** -0.5
    for place, ref in enumerate((left_ref, own_ref, right_ref)):
        near[place * ROWS : (place + 1) * ROWS, :] = ref[...]

    row_block = lax.broadcasted_iota(jnp.int32, (3 * ROWS, LANES), 0) // LANES
    lane = lax.broadcasted_iota(jnp.int32, (3 * ROWS, LANES), 1)
    keys[:, LANES:] = jnp.where((lane % 16 == row_block) & (lane < 32), 1.0, 0.0).astype(bf16)
    window = counts_ref[...]
    rows = []
    for chunk in range(6):
        sides = []
        for block in range(2):
            offset = chunk - block
            if 0 <= offset < 5:
                lane_id = block * 8 + offset
                sides.append(jnp.broadcast_to(window[:, lane_id : lane_id + 1], (1, LANES)))
            else:
                sides.append(jnp.full((1, LANES), ABSENT, f32))
        rows.append(jnp.concatenate(sides, axis=1))
    rows = jnp.concatenate(rows + [jnp.zeros((10, ROWS), f32)], axis=0)
    high = rows.astype(bf16)
    low = (rows - high.astype(f32)).astype(bf16)
    bias = jnp.concatenate([high, low, jnp.zeros((LANES - 32, ROWS), bf16)], axis=0)

    keys[:, :LANES] = dot(near[...], w_key_ref[layer]).astype(bf16)
    query_t = (dot_nt(w_query_ref[layer].T, own_ref[...]) * query_scale).astype(bf16)
    value_t = dot_nt(w_value_ref[layer].T, near[...]).astype(bf16)
    for head in range(HEADS):
        values[head * 48 : head * 48 + 32, :] = value_t[head * 32 : head * 32 + 32]
        values[head * 48 + 32 : head * 48 + 48, :] = jnp.ones((16, 3 * ROWS), bf16)

    def attend(exact):
        pieces = []
        sums = []

        def scores_of(head):
            parts = []
            if head:
                parts.append(jnp.zeros((head * head_size, ROWS), bf16))
            parts.append(query_t[head * head_size : (head + 1) * head_size])
            if head < HEADS - 1:
                parts.append(jnp.zeros(((HEADS - 1 - head) * head_size, ROWS), bf16))
            return dot(keys[...], jnp.concatenate(parts + [bias], axis=0))

        following = scores_of(0)
        for head in range(HEADS):
            scores = following
            if head < HEADS - 1:
                following = scores_of(head + 1)
            if exact:
                scores = scores - jnp.max(scores, axis=0, keepdims=True)
            blank = jnp.zeros((LANES, LANES), bf16)
            weights_t = jnp.concatenate(
                [
                    jnp.concatenate([jnp.exp2(scores[: 5 * LANES, :LANES]).astype(bf16), blank], axis=0),
                    jnp.concatenate([blank, jnp.exp2(scores[LANES:, LANES:]).astype(bf16)], axis=0),
                ],
                axis=1,
            )
            mixed = dot(values[head * 48 : (head + 1) * 48, :], weights_t)
            total = mixed[head_size : head_size + 1]
            sums.append(total)
            pieces.append(mixed[:head_size] * (1.0 / total))
        attended[...] = jnp.concatenate(pieces, axis=0).astype(bf16)
        return jnp.concatenate(sums, axis=0)

    sums = attend(False)
    safe = (jnp.min(sums) > 2.0**-80) & (jnp.max(sums) < 2.0**100)

    @pl.when(jnp.logical_not(safe))
    def _():
        attend(True)

    gains = jnp.concatenate([gain_ref[0], gain_ref[1], jnp.zeros((4, LANES), f32)], axis=0).T
    now = stream_ref[...] + dot(w_out_ref[layer].T, attended[...])
    normed = (norm_columns(now) * gains[:, 2 * layer + 1 : 2 * layer + 2]).astype(bf16)
    gate_up = dot(w_gate_up_ref[layer].T, normed)
    width = gate_up.shape[0] // 2
    half, up = 0.5 * gate_up[:width], gate_up[width:]
    hidden = ((half + half * jnp.tanh(half)) * up).astype(bf16)
    return now + dot(w_down_ref[layer].T, hidden), gains


def first_layer_kernel(left_ref, own_ref, right_ref, stream_ref, counts_ref, gain_ref, *refs):
    weights, (out_ref, normed_ref), scratch = refs[:6], refs[6:8], refs[8:]
    stream, gains = layer_values(
        0, (left_ref, own_ref, right_ref), stream_ref, counts_ref, gain_ref, weights, scratch
    )
    out_ref[...] = stream
    normed_ref[...] = (norm_columns(stream) * gains[:, 2:3]).astype(bf16).T


def last_layer_kernel(left_ref, own_ref, right_ref, stream_ref, counts_ref, gain_ref, *refs):
    weights, (rows_ref, positions_ref, noise_ref, force_ref, w_head_ref) = refs[:6], refs[6:11]
    out_ref, scratch = refs[11], refs[12:]
    stream, _ = layer_values(
        1, (left_ref, own_ref, right_ref), stream_ref, counts_ref, gain_ref, weights, scratch
    )
    final = norm_columns(stream)
    head_rows = jnp.concatenate([w_head_ref[...], jnp.zeros((5, LANES), f32)], axis=0)
    update = jnp.dot(head_rows, final, precision=lax.Precision.HIGHEST, preferred_element_type=f32)
    level, spread_sq, c_input = rows_ref[0:1], rows_ref[1:2], rows_ref[2:3]
    positions = jnp.concatenate([positions_ref[...], jnp.zeros((5, ROWS), f32)], axis=0)
    fresh = jnp.concatenate([noise_ref[...], jnp.zeros((5, ROWS), f32)], axis=0)
    denoised = positions * (1.0 / spread_sq) + (level * c_input) * update
    following = 0.85 * level
    result = denoised + STEER * force_ref[...] + following * (0.8 * (positions - denoised) / level + 0.6 * fresh)
    out_ref[...] = result[:3]


def body(
    positions,
    fresh_noise,
    timestep,
    atom_single,
    pos_weight,
    ln_gain,
    w_query,
    w_key,
    w_value,
    w_out,
    w_gate_up,
    w_down,
    w_head,
    key_window,
    block_pairs,
    pair_count,
    bond_atoms,
):
    devices = lax.axis_size("atom")
    first = lax.axis_index("atom").astype(jnp.int32).reshape(1)
    smem = pl.BlockSpec(memory_space=pltpu.SMEM)
    vmem = pl.BlockSpec(memory_space=pltpu.VMEM)
    hbm = pl.BlockSpec(memory_space=pltpu.HBM)
    rows = atom_single.shape[0]

    def from_neighbours(array):
        up = [(i, (i + 1) % devices) for i in range(devices)]
        down = [(j, i) for i, j in up]
        return lax.ppermute(array, "atom", up), lax.ppermute(array, "atom", down)

    stream, normed, schedule = pl.pallas_call(
        prepare_kernel,
        out_shape=(
            jax.ShapeDtypeStruct((LANES, rows), f32),
            jax.ShapeDtypeStruct((rows, LANES), bf16),
            jax.ShapeDtypeStruct((8, rows), f32),
        ),
        in_specs=[hbm] * 5,
        out_specs=(vmem, vmem, vmem),
        scratch_shapes=[
            pltpu.SMEM(timestep.shape, jnp.int32),
            pltpu.VMEM(positions.shape, f32),
            pltpu.VMEM(atom_single.shape, bf16),
            pltpu.VMEM(pos_weight.shape, f32),
            pltpu.VMEM(ln_gain.shape, f32),
            pltpu.SemaphoreType.DMA((5,)),
        ],
        compiler_params=pltpu.CompilerParams(vmem_limit_bytes=VMEM_GRANT),
    )(timestep, positions, atom_single, pos_weight, ln_gain)
    left, right = from_neighbours(normed)

    packed, counts = pl.pallas_call(
        pack_kernel,
        out_shape=(
            jax.ShapeDtypeStruct((devices, 8, LANES), f32),
            jax.ShapeDtypeStruct((1, LANES), f32),
        ),
        in_specs=[smem, smem] + [vmem] * 4,
        out_specs=(vmem, vmem),
        scratch_shapes=[pltpu.VMEM((8, LANES), f32)],
        cost_estimate=pl.CostEstimate(flops=40_000_000, bytes_accessed=10_000_000, transcendentals=1_000_000),
        compiler_params=pltpu.CompilerParams(vmem_limit_bytes=VMEM_SMALL),
    )(first, pair_count, positions, block_pairs, key_window, schedule)
    tiles = lax.all_to_all(packed, "atom", 0, 0)

    weights = (w_query, w_key, w_value, w_out, w_gate_up, w_down)
    layer_scratch = [
        pltpu.VMEM((3 * rows, LANES), bf16),
        pltpu.VMEM((3 * rows, 2 * LANES), bf16),
        pltpu.VMEM((HEADS * 48, 3 * rows), bf16),
        pltpu.VMEM((LANES, rows), bf16),
    ]
    layer_cost = pl.CostEstimate(flops=2_000_000_000, bytes_accessed=20_000_000, transcendentals=2_000_000)
    stream, normed = pl.pallas_call(
        first_layer_kernel,
        out_shape=(
            jax.ShapeDtypeStruct((LANES, rows), f32),
            jax.ShapeDtypeStruct((rows, LANES), bf16),
        ),
        in_specs=[vmem] * 12,
        out_specs=(vmem, vmem),
        scratch_shapes=layer_scratch,
        cost_estimate=layer_cost,
        compiler_params=pltpu.CompilerParams(vmem_limit_bytes=VMEM_SMALL),
    )(left, normed, right, stream, counts, ln_gain, *weights)
    left, right = from_neighbours(normed)

    bond_force = pl.pallas_call(
        bond_kernel,
        out_shape=jax.ShapeDtypeStruct((8, 2 * LANES), f32),
        in_specs=[vmem, vmem],
        out_specs=vmem,
        cost_estimate=pl.CostEstimate(flops=80_000_000, bytes_accessed=8_000_000, transcendentals=0),
        compiler_params=pltpu.CompilerParams(vmem_limit_bytes=VMEM_SMALL),
    )(positions, bond_atoms)

    force = pl.pallas_call(
        force_kernel,
        out_shape=jax.ShapeDtypeStruct((8, 2 * LANES), f32),
        in_specs=[smem, vmem, vmem, vmem],
        out_specs=vmem,
        scratch_shapes=[
            pltpu.VMEM((6, LANES, LANES), f32),
            pltpu.VMEM((6, LANES, LANES), f32),
            pltpu.VMEM((8, LANES), jnp.int32),
            pltpu.VMEM((8, LANES), f32),
            pltpu.SMEM((8, LANES), jnp.int32),
            pltpu.SMEM((8, LANES), f32),
            pltpu.SemaphoreType.DMA((2,)),
        ],
        cost_estimate=pl.CostEstimate(flops=80_000_000, bytes_accessed=16_000_000, transcendentals=2_000_000),
        compiler_params=pltpu.CompilerParams(vmem_limit_bytes=VMEM_SMALL),
    )(first, tiles, positions, bond_force)

    return pl.pallas_call(
        last_layer_kernel,
        out_shape=jax.ShapeDtypeStruct(positions.shape, f32),
        in_specs=[vmem] * 17,
        out_specs=vmem,
        scratch_shapes=layer_scratch,
        cost_estimate=layer_cost,
        compiler_params=pltpu.CompilerParams(vmem_limit_bytes=VMEM_SMALL),
    )(
        left,
        normed,
        right,
        stream,
        counts,
        ln_gain,
        *weights,
        schedule,
        positions,
        fresh_noise,
        force,
        w_head,
    )


def solution(mesh):
    in_specs = (
        P(None, ("sample", "atom")),
        P(None, ("sample", "atom")),
        P(),
        P("atom", None),
        P(),
        P(),
        P(),
        P(),
        P(),
        P(),
        P(),
        P(),
        P(),
        P("atom", None),
        P(None, "atom"),
        P("atom"),
        P(None, "atom", None),
    )
    out_specs = P(None, ("sample", "atom"))
    return jax.shard_map(body, mesh=mesh, in_specs=in_specs, out_specs=out_specs, check_vma=False)
```

```python
import functools
import math

import jax
import jax.numpy as jnp
from jax import lax
from jax.experimental import pallas as pl
from jax.experimental.pallas import tpu as pltpu
from jax.sharding import PartitionSpec as P

HEADS = 4
LANES = 128
ROWS = 256
VMEM_GRANT = 60 * 1024 * 1024
VMEM_SMALL = 16 * 1024 * 1024
NORM_EPS = 1e-05
STEER = 0.3
ABSENT = -(2.0**120)
LOG2E = 1.4426950408889634
KAPPA = 2.0 * math.sqrt(LOG2E)

f32 = jnp.float32
bf16 = jnp.bfloat16


def pack_kernel(count_ref, tile_ref, out_ref):
    shape = tile_ref.shape
    row = lax.broadcasted_iota(jnp.int32, shape, 0)
    lane = lax.broadcasted_iota(jnp.int32, shape, 1)
    dead = (row == 6) & (lane % 64 >= count_ref[0])
    out_ref[...] = jnp.broadcast_to(jnp.where(dead, -1.0, tile_ref[...])[None], out_ref.shape)


def split3(values):
    high = values.astype(bf16)
    rest = values - high.astype(f32)
    mid = rest.astype(bf16)
    low = (rest - mid.astype(f32)).astype(bf16)
    return jnp.concatenate([high, mid, low], axis=0)


def join3(values):
    rows = values.shape[0] // 3
    return values[:rows] + values[rows : 2 * rows] + values[2 * rows :]


def norm_columns(values):
    center = values - jnp.mean(values, axis=0, keepdims=True)
    spread = jnp.mean(center * center, axis=0, keepdims=True)
    return center * lax.rsqrt(spread + NORM_EPS)


def dot_t(left, right):
    return lax.dot_general(left, right, (((0,), (0,)), ((), ())), preferred_element_type=f32)


def dot_nt(left, right):
    return lax.dot_general(left, right, (((1,), (1,)), ((), ())), preferred_element_type=f32)


def dot(left, right):
    return jnp.dot(left, right, preferred_element_type=f32)


def bond_kernel(positions_ref, bonds_ref, out_ref):
    positions = jnp.concatenate([positions_ref[...], jnp.zeros((5, 2 * LANES), f32)], axis=0)

    forces = []
    atom_id = lax.broadcasted_iota(jnp.int32, (LANES, LANES), 0)
    for block in range(2):
        incidence = (
            (atom_id == bonds_ref[0, block : block + 1, :]).astype(f32)
            - (atom_id == bonds_ref[1, block : block + 1, :]).astype(f32)
        ).astype(bf16)
        offset = join3(dot(split3(positions[:, block * LANES : (block + 1) * LANES]), incidence))
        stretch = jnp.sum(offset * offset, axis=0, keepdims=True) - 1.0
        pull = (-0.2 * stretch) * offset
        forces.append(join3(dot_nt(split3(pull), incidence)))
    out_ref[...] = jnp.concatenate(forces, axis=1)


def force_kernel(first_ref, tiles_ref, positions_ref, bond_ref, out_ref, spread_own, push, list_v, bias_v, list_s, bias_s, sems):
    me = first_ref[0]

    codes = tiles_ref[:, 6, :].astype(jnp.int32)
    half = lax.broadcasted_iota(jnp.int32, codes.shape, 1) // 64
    mine = me * 2 + half
    first = jnp.where(codes < 0, -1, codes // 64)
    second = jnp.where(codes < 0, -1, codes % 64)
    partner = jnp.where(first == mine, second, jnp.where(second == mine, first, -1)).astype(f32)
    block_id = lax.broadcasted_iota(jnp.int32, (64, LANES), 0).astype(f32)
    hits = jnp.zeros((64, LANES), f32)
    for row in range(codes.shape[0]):
        hits = hits + jnp.where(partner[row : row + 1] == block_id, 1.0, 0.0)
    row_half = lax.broadcasted_iota(jnp.int32, (LANES, LANES), 0) // 64
    col_half = lax.broadcasted_iota(jnp.int32, (LANES, LANES), 1) // 64
    count = dot(hits.astype(bf16), (row_half == col_half).astype(bf16))
    present = count > 0.5
    lower = lax.broadcasted_iota(jnp.int32, (64, 64), 1) < lax.broadcasted_iota(jnp.int32, (64, 64), 0)
    rank = dot(lower.astype(bf16), present.astype(bf16))
    slot = (lax.broadcasted_iota(jnp.int32, (64, LANES), 1) % 64).astype(f32)
    chosen = present & (rank == slot)
    listed = jnp.sum(jnp.where(chosen, block_id, 0.0), axis=0, keepdims=True)
    times = jnp.sum(jnp.where(chosen, count, 0.0), axis=0, keepdims=True)
    total = jnp.sum(present.astype(f32), axis=0, keepdims=True)
    list_v[0:1, :] = listed.astype(jnp.int32)
    list_v[1:2, :] = total.astype(jnp.int32)
    bias_v[0:1, :] = jnp.where(times > 0.5, jnp.log2(jnp.maximum(times, 1.0)), ABSENT)
    list_copy = pltpu.make_async_copy(list_v, list_s, sems.at[0])
    bias_copy = pltpu.make_async_copy(bias_v, bias_s, sems.at[1])
    list_copy.start()
    bias_copy.start()

    for block in range(2):
        for comp in range(3):
            row = positions_ref[comp : comp + 1, block * LANES : (block + 1) * LANES] * KAPPA
            spread_own[3 * block + comp] = jnp.broadcast_to(row, (LANES, LANES)).T
            push[3 * block + comp] = jnp.zeros((LANES, LANES), f32)

    forces = []
    list_copy.wait()
    bias_copy.wait()
    for block in range(2):

        def one_pair(index, carry, block=block):
            partners = []
            for sub in range(2):
                entry = block * 64 + 2 * index + sub
                partner = list_s[0, entry]
                device = partner // 2
                within = partner % 2
                rows = [
                    tiles_ref[device, pl.ds(2 * comp + within, 1), :] * KAPPA for comp in range(3)
                ]
                partners.append((rows, bias_s[0, entry]))
            for group in range(0, LANES, 8):
                own = [spread_own[3 * block + comp, group : group + 8, :] for comp in range(3)]
                sums = [push[3 * block + comp, group : group + 8, :] for comp in range(3)]
                for rows, bias in partners:
                    offset = [own[comp] - rows[comp] for comp in range(3)]
                    power = bias - offset[0] * offset[0]
                    power = power - offset[1] * offset[1]
                    power = power - offset[2] * offset[2]
                    weight = jnp.exp2(power)
                    sums = [sums[comp] + weight * offset[comp] for comp in range(3)]
                for comp in range(3):
                    push[3 * block + comp, group : group + 8, :] = sums[comp]
            return carry

        lax.fori_loop(0, (list_s[1, block * 64] + 1) // 2, one_pair, 0)
        rows = [jnp.sum(push[3 * block + comp].T, axis=0, keepdims=True) for comp in range(3)]
        clash = jnp.concatenate(rows + [jnp.zeros((5, LANES), f32)], axis=0)
        forces.append(clash * (8.0 / KAPPA))
    out_ref[...] = bond_ref[...] + jnp.concatenate(forces, axis=1)


def start_copies(sources, targets, sems):
    copies = [
        pltpu.make_async_copy(source, target, sems.at[index])
        for index, (source, target) in enumerate(zip(sources, targets))
    ]
    for copy in copies:
        copy.start()
    return copies


def prepare_kernel(*refs):
    first_ref, sources, (stream_ref, normed_ref, rows_ref, tile_ref) = refs[0], refs[1:8], refs[8:12]
    targets, sems = refs[12:19], refs[19]
    time_ref, positions_ref, single_ref, pos_weight_ref, gain_ref, pairs_ref, window_ref = targets
    for copy in start_copies(sources, targets, sems):
        copy.wait()
    level = 0.2 + 0.02 * jnp.full((1, ROWS), time_ref[0], jnp.int32).astype(f32)
    spread_sq = level * level + 1.0
    c_input = 1.0 / jnp.sqrt(spread_sq)
    window = window_ref[...]
    own = first_ref[0] * 2 + lax.broadcasted_iota(jnp.int32, window.shape, 0)
    lane = lax.broadcasted_iota(jnp.int32, (1, ROWS), 1)
    counts = jnp.zeros((1, ROWS), f32)
    for offset in range(5):
        hit = jnp.sum((window == own + (offset - 2)).astype(f32), axis=1, keepdims=True)
        counts = jnp.where(lane == offset, hit[0:1], counts)
        counts = jnp.where(lane == 8 + offset, hit[1:2], counts)
    counts = jnp.where(counts > 0.0, jnp.log2(jnp.maximum(counts, 1.0)), ABSENT)
    gain_rows = [
        jnp.concatenate([gain_ref[layer, 0:1], gain_ref[layer, 1:2]], axis=1) for layer in range(2)
    ]
    rows_ref[...] = jnp.concatenate(
        [level, spread_sq, c_input] + gain_rows + [counts, jnp.zeros((2, ROWS), f32)], axis=0
    )
    for row in range(6):
        part = slice((row % 2) * LANES, (row % 2 + 1) * LANES)
        tile_ref[row : row + 1, :] = positions_ref[row // 2 : row // 2 + 1, part]
    pairs = pairs_ref[...]
    codes = (pairs[0:1] * 64 + pairs[1:2]).astype(f32)
    tile_ref[6:7, :] = jnp.concatenate([codes, codes], axis=1)
    tile_ref[7:8, :] = jnp.zeros((1, LANES), f32)
    columns = jnp.concatenate(
        [pos_weight_ref[...], gain_ref[0, 0:1], jnp.zeros((4, LANES), f32)], axis=0
    ).T
    identity = (
        lax.broadcasted_iota(jnp.int32, (LANES, LANES), 0)
        == lax.broadcasted_iota(jnp.int32, (LANES, LANES), 1)
    ).astype(f32).astype(bf16)
    stream = dot_nt(identity, single_ref[...])
    for comp in range(3):
        stream = stream + columns[:, comp : comp + 1] * (positions_ref[comp : comp + 1, :] * c_input)
    stream_ref[...] = stream
    normed_ref[...] = (norm_columns(stream) * columns[:, 3:4]).astype(bf16).T


def layer_values(layer, first_ref, halo, stream_ref, rows_ref, weights, scratch):
    even_ref, own_ref, odd_ref = halo
    w_query_ref, w_key_ref, w_value_ref, w_out_ref, w_gate_up_ref, w_down_ref = weights
    near, keys, values, attended = scratch
    head_size = LANES // HEADS
    query_scale = LOG2E * head_size ** -0.5
    near[ROWS : 2 * ROWS, :] = own_ref[...]

    @pl.when(first_ref[0] % 2 == 0)
    def _():
        near[:ROWS, :] = odd_ref[...]
        near[2 * ROWS :, :] = even_ref[...]

    @pl.when(first_ref[0] % 2 == 1)
    def _():
        near[:ROWS, :] = even_ref[...]
        near[2 * ROWS :, :] = odd_ref[...]

    row_block = lax.broadcasted_iota(jnp.int32, (3 * ROWS, LANES), 0) // LANES
    lane = lax.broadcasted_iota(jnp.int32, (3 * ROWS, LANES), 1)
    keys[:, LANES:] = jnp.where((lane % 16 == row_block) & (lane < 32), 1.0, 0.0).astype(bf16)
    window = rows_ref[5:6, :LANES]
    rows = []
    for chunk in range(6):
        sides = []
        for block in range(2):
            offset = chunk - block
            if 0 <= offset < 5:
                lane_id = block * 8 + offset
                sides.append(jnp.broadcast_to(window[:, lane_id : lane_id + 1], (1, LANES)))
            else:
                sides.append(jnp.full((1, LANES), ABSENT, f32))
        rows.append(jnp.concatenate(sides, axis=1))
    rows = jnp.concatenate(rows + [jnp.zeros((10, ROWS), f32)], axis=0)
    high = rows.astype(bf16)
    low = (rows - high.astype(f32)).astype(bf16)
    bias = jnp.concatenate([high, low, jnp.zeros((LANES - 32, ROWS), bf16)], axis=0)

    keys[:, :LANES] = dot(near[...], w_key_ref[layer]).astype(bf16)
    query_t = (dot_nt(w_query_ref[layer].T, own_ref[...]) * query_scale).astype(bf16)
    value_t = dot_nt(w_value_ref[layer].T, near[...]).astype(bf16)
    for head in range(HEADS):
        values[head * 48 : head * 48 + 32, :] = value_t[head * 32 : head * 32 + 32]
        values[head * 48 + 32 : head * 48 + 48, :] = jnp.ones((16, 3 * ROWS), bf16)

    def attend(exact):
        pieces = []
        sums = []

        def scores_of(head):
            parts = []
            if head:
                parts.append(jnp.zeros((head * head_size, ROWS), bf16))
            parts.append(query_t[head * head_size : (head + 1) * head_size])
            if head < HEADS - 1:
                parts.append(jnp.zeros(((HEADS - 1 - head) * head_size, ROWS), bf16))
            return dot(keys[...], jnp.concatenate(parts + [bias], axis=0))

        following = scores_of(0)
        for head in range(HEADS):
            scores = following
            if head < HEADS - 1:
                following = scores_of(head + 1)
            if exact:
                scores = scores - jnp.max(scores, axis=0, keepdims=True)
            blank = jnp.zeros((LANES, LANES), bf16)
            weights_t = jnp.concatenate(
                [
                    jnp.concatenate([jnp.exp2(scores[: 5 * LANES, :LANES]).astype(bf16), blank], axis=0),
                    jnp.concatenate([blank, jnp.exp2(scores[LANES:, LANES:]).astype(bf16)], axis=0),
                ],
                axis=1,
            )
            mixed = dot(values[head * 48 : (head + 1) * 48, :], weights_t)
            total = mixed[head_size : head_size + 1]
            sums.append(total)
            pieces.append(mixed[:head_size] * (1.0 / total))
        attended[...] = jnp.concatenate(pieces, axis=0).astype(bf16)
        return jnp.concatenate(sums, axis=0)

    sums = attend(False)
    safe = (jnp.min(sums) > 2.0**-80) & (jnp.max(sums) < 2.0**100)

    @pl.when(jnp.logical_not(safe))
    def _():
        attend(True)

    gains = jnp.concatenate(
        [rows_ref[3 + index // 2 : 4 + index // 2, (index % 2) * LANES : (index % 2 + 1) * LANES] for index in range(4)]
        + [jnp.zeros((4, LANES), f32)],
        axis=0,
    ).T
    now = stream_ref[...] + dot(w_out_ref[layer].T, attended[...])
    normed = (norm_columns(now) * gains[:, 2 * layer + 1 : 2 * layer + 2]).astype(bf16)
    gate_up = dot(w_gate_up_ref[layer].T, normed)
    width = gate_up.shape[0] // 2
    half, up = 0.5 * gate_up[:width], gate_up[width:]
    hidden = ((half + half * jnp.tanh(half)) * up).astype(bf16)
    return now + dot(w_down_ref[layer].T, hidden), gains


def first_layer_kernel(first_ref, even_ref, own_ref, odd_ref, stream_ref, rows_ref, *refs):
    weights, (out_ref, normed_ref), scratch = refs[:6], refs[6:8], refs[8:]
    stream, gains = layer_values(
        0, first_ref, (even_ref, own_ref, odd_ref), stream_ref, rows_ref, weights, scratch
    )
    out_ref[...] = stream
    normed_ref[...] = (norm_columns(stream) * gains[:, 2:3]).astype(bf16).T


def last_layer_kernel(first_ref, even_ref, own_ref, odd_ref, stream_ref, rows_ref, *refs):
    weights, (positions_ref, noise_ref, force_ref, w_head_ref) = refs[:6], refs[6:10]
    out_ref, scratch = refs[10], refs[11:]
    stream, _ = layer_values(
        1, first_ref, (even_ref, own_ref, odd_ref), stream_ref, rows_ref, weights, scratch
    )
    final = norm_columns(stream)
    head_rows = jnp.concatenate([w_head_ref[...], jnp.zeros((5, LANES), f32)], axis=0)
    update = jnp.dot(head_rows, final, precision=lax.Precision.HIGHEST, preferred_element_type=f32)
    level, spread_sq, c_input = rows_ref[0:1], rows_ref[1:2], rows_ref[2:3]
    positions = jnp.concatenate([positions_ref[...], jnp.zeros((5, ROWS), f32)], axis=0)
    fresh = jnp.concatenate([noise_ref[...], jnp.zeros((5, ROWS), f32)], axis=0)
    denoised = positions * (1.0 / spread_sq) + (level * c_input) * update
    following = 0.85 * level
    result = denoised + STEER * force_ref[...] + following * (0.8 * (positions - denoised) / level + 0.6 * fresh)
    out_ref[...] = result[:3]


def body(
    positions,
    fresh_noise,
    timestep,
    atom_single,
    pos_weight,
    ln_gain,
    w_query,
    w_key,
    w_value,
    w_out,
    w_gate_up,
    w_down,
    w_head,
    key_window,
    block_pairs,
    pair_count,
    bond_atoms,
):
    devices = lax.axis_size("atom")
    first = lax.axis_index("atom").astype(jnp.int32).reshape(1)
    smem = pl.BlockSpec(memory_space=pltpu.SMEM)
    vmem = pl.BlockSpec(memory_space=pltpu.VMEM)
    hbm = pl.BlockSpec(memory_space=pltpu.HBM)
    rows = atom_single.shape[0]

    def from_neighbours(array):
        even = [(i, i ^ 1) for i in range(devices)]
        odd = [(i, (((i + 1) ^ 1) - 1) % devices) for i in range(devices)]
        return lax.ppermute(array, "atom", even), lax.ppermute(array, "atom", odd)

    stream, normed, schedule, tile = pl.pallas_call(
        prepare_kernel,
        out_shape=(
            jax.ShapeDtypeStruct((LANES, rows), f32),
            jax.ShapeDtypeStruct((rows, LANES), bf16),
            jax.ShapeDtypeStruct((8, rows), f32),
            jax.ShapeDtypeStruct((8, LANES), f32),
        ),
        in_specs=[smem] + [hbm] * 7,
        out_specs=(vmem,) * 4,
        scratch_shapes=[
            pltpu.SMEM(timestep.shape, jnp.int32),
            pltpu.VMEM(positions.shape, f32),
            pltpu.VMEM(atom_single.shape, bf16),
            pltpu.VMEM(pos_weight.shape, f32),
            pltpu.VMEM(ln_gain.shape, f32),
            pltpu.VMEM(block_pairs.shape, jnp.int32),
            pltpu.VMEM(key_window.shape, jnp.int32),
            pltpu.SemaphoreType.DMA((7,)),
        ],
        compiler_params=pltpu.CompilerParams(vmem_limit_bytes=VMEM_GRANT),
    )(first, timestep, positions, atom_single, pos_weight, ln_gain, block_pairs, key_window)
    even, odd = from_neighbours(normed)

    packed = pl.pallas_call(
        pack_kernel,
        out_shape=jax.ShapeDtypeStruct((devices, 8, LANES), f32),
        in_specs=[smem, vmem],
        out_specs=vmem,
        cost_estimate=pl.CostEstimate(flops=40_000_000, bytes_accessed=10_000_000, transcendentals=1_000_000),
        compiler_params=pltpu.CompilerParams(vmem_limit_bytes=VMEM_SMALL),
    )(pair_count, tile)
    tiles = lax.all_to_all(packed, "atom", 0, 0)

    weights = (w_query, w_key, w_value, w_out, w_gate_up, w_down)
    layer_scratch = [
        pltpu.VMEM((3 * rows, LANES), bf16),
        pltpu.VMEM((3 * rows, 2 * LANES), bf16),
        pltpu.VMEM((HEADS * 48, 3 * rows), bf16),
        pltpu.VMEM((LANES, rows), bf16),
    ]
    layer_cost = pl.CostEstimate(flops=2_000_000_000, bytes_accessed=20_000_000, transcendentals=2_000_000)
    stream, normed = pl.pallas_call(
        first_layer_kernel,
        out_shape=(
            jax.ShapeDtypeStruct((LANES, rows), f32),
            jax.ShapeDtypeStruct((rows, LANES), bf16),
        ),
        in_specs=[smem] + [vmem] * 11,
        out_specs=(vmem, vmem),
        scratch_shapes=layer_scratch,
        cost_estimate=layer_cost,
        compiler_params=pltpu.CompilerParams(vmem_limit_bytes=VMEM_SMALL),
    )(first, even, normed, odd, stream, schedule, *weights)
    even, odd = from_neighbours(normed)

    bond_force = pl.pallas_call(
        bond_kernel,
        out_shape=jax.ShapeDtypeStruct((8, 2 * LANES), f32),
        in_specs=[vmem, vmem],
        out_specs=vmem,
        cost_estimate=pl.CostEstimate(flops=80_000_000, bytes_accessed=8_000_000, transcendentals=0),
        compiler_params=pltpu.CompilerParams(vmem_limit_bytes=VMEM_SMALL),
    )(positions, bond_atoms)

    force = pl.pallas_call(
        force_kernel,
        out_shape=jax.ShapeDtypeStruct((8, 2 * LANES), f32),
        in_specs=[smem, vmem, vmem, vmem],
        out_specs=vmem,
        scratch_shapes=[
            pltpu.VMEM((6, LANES, LANES), f32),
            pltpu.VMEM((6, LANES, LANES), f32),
            pltpu.VMEM((8, LANES), jnp.int32),
            pltpu.VMEM((8, LANES), f32),
            pltpu.SMEM((8, LANES), jnp.int32),
            pltpu.SMEM((8, LANES), f32),
            pltpu.SemaphoreType.DMA((2,)),
        ],
        cost_estimate=pl.CostEstimate(flops=80_000_000, bytes_accessed=16_000_000, transcendentals=2_000_000),
        compiler_params=pltpu.CompilerParams(vmem_limit_bytes=VMEM_SMALL),
    )(first, tiles, positions, bond_force)

    return pl.pallas_call(
        last_layer_kernel,
        out_shape=jax.ShapeDtypeStruct(positions.shape, f32),
        in_specs=[smem] + [vmem] * 15,
        out_specs=vmem,
        scratch_shapes=layer_scratch,
        cost_estimate=layer_cost,
        compiler_params=pltpu.CompilerParams(vmem_limit_bytes=VMEM_SMALL),
    )(
        first,
        even,
        normed,
        odd,
        stream,
        schedule,
        *weights,
        positions,
        fresh_noise,
        force,
        w_head,
    )


def solution(mesh):
    in_specs = (
        P(None, ("sample", "atom")),
        P(None, ("sample", "atom")),
        P(),
        P("atom", None),
        P(),
        P(),
        P(),
        P(),
        P(),
        P(),
        P(),
        P(),
        P(),
        P("atom", None),
        P(None, "atom"),
        P("atom"),
        P(None, "atom", None),
    )
    out_specs = P(None, ("sample", "atom"))
    return jax.shard_map(body, mesh=mesh, in_specs=in_specs, out_specs=out_specs, check_vma=False)
```

```python
import functools
import math

import jax
import jax.numpy as jnp
from jax import lax
from jax.experimental import pallas as pl
from jax.experimental.pallas import tpu as pltpu
from jax.sharding import PartitionSpec as P

HEADS = 4
LANES = 128
ROWS = 256
VMEM_GRANT = 60 * 1024 * 1024
VMEM_SMALL = 16 * 1024 * 1024
NORM_EPS = 1e-05
STEER = 0.3
ABSENT = -(2.0**120)
LOG2E = 1.4426950408889634
KAPPA = 2.0 * math.sqrt(LOG2E)

f32 = jnp.float32
bf16 = jnp.bfloat16


def pack_kernel(count_ref, tile_ref, out_ref):
    shape = tile_ref.shape
    row = lax.broadcasted_iota(jnp.int32, shape, 0)
    lane = lax.broadcasted_iota(jnp.int32, shape, 1)
    dead = (row == 6) & (lane % 64 >= count_ref[0])
    out_ref[...] = jnp.broadcast_to(jnp.where(dead, -1.0, tile_ref[...])[None], out_ref.shape)


def split3(values):
    high = values.astype(bf16)
    rest = values - high.astype(f32)
    mid = rest.astype(bf16)
    low = (rest - mid.astype(f32)).astype(bf16)
    return jnp.concatenate([high, mid, low], axis=0)


def join3(values):
    rows = values.shape[0] // 3
    return values[:rows] + values[rows : 2 * rows] + values[2 * rows :]


def norm_columns(values):
    center = values - jnp.mean(values, axis=0, keepdims=True)
    spread = jnp.mean(center * center, axis=0, keepdims=True)
    return center * lax.rsqrt(spread + NORM_EPS)


def dot_t(left, right):
    return lax.dot_general(left, right, (((0,), (0,)), ((), ())), preferred_element_type=f32)


def dot_nt(left, right):
    return lax.dot_general(left, right, (((1,), (1,)), ((), ())), preferred_element_type=f32)


def dot(left, right):
    return jnp.dot(left, right, preferred_element_type=f32)


def bond_kernel(positions_ref, bonds_ref, out_ref):
    positions = jnp.concatenate([positions_ref[...], jnp.zeros((5, 2 * LANES), f32)], axis=0)

    forces = []
    atom_id = lax.broadcasted_iota(jnp.int32, (LANES, LANES), 0)
    for block in range(2):
        incidence = (
            (atom_id == bonds_ref[0, block : block + 1, :]).astype(f32)
            - (atom_id == bonds_ref[1, block : block + 1, :]).astype(f32)
        ).astype(bf16)
        offset = join3(dot(split3(positions[:, block * LANES : (block + 1) * LANES]), incidence))
        stretch = jnp.sum(offset * offset, axis=0, keepdims=True) - 1.0
        pull = (-0.2 * stretch) * offset
        forces.append(join3(dot_nt(split3(pull), incidence)))
    out_ref[...] = jnp.concatenate(forces, axis=1)


def force_kernel(first_ref, tiles_ref, positions_ref, bond_ref, out_ref, spread_own, push, list_v, bias_v, list_s, bias_s, sems):
    me = first_ref[0]

    codes = tiles_ref[:, 6, :].astype(jnp.int32)
    half = lax.broadcasted_iota(jnp.int32, codes.shape, 1) // 64
    mine = me * 2 + half
    first = jnp.where(codes < 0, -1, codes // 64)
    second = jnp.where(codes < 0, -1, codes % 64)
    partner = jnp.where(first == mine, second, jnp.where(second == mine, first, -1)).astype(f32)
    block_id = lax.broadcasted_iota(jnp.int32, (64, LANES), 0).astype(f32)
    hits = jnp.zeros((64, LANES), f32)
    for row in range(codes.shape[0]):
        hits = hits + jnp.where(partner[row : row + 1] == block_id, 1.0, 0.0)
    row_half = lax.broadcasted_iota(jnp.int32, (LANES, LANES), 0) // 64
    col_half = lax.broadcasted_iota(jnp.int32, (LANES, LANES), 1) // 64
    count = dot(hits.astype(bf16), (row_half == col_half).astype(bf16))
    present = count > 0.5
    lower = lax.broadcasted_iota(jnp.int32, (64, 64), 1) < lax.broadcasted_iota(jnp.int32, (64, 64), 0)
    rank = dot(lower.astype(bf16), present.astype(bf16))
    slot = (lax.broadcasted_iota(jnp.int32, (64, LANES), 1) % 64).astype(f32)
    chosen = present & (rank == slot)
    listed = jnp.sum(jnp.where(chosen, block_id, 0.0), axis=0, keepdims=True)
    times = jnp.sum(jnp.where(chosen, count, 0.0), axis=0, keepdims=True)
    total = jnp.sum(present.astype(f32), axis=0, keepdims=True)
    list_v[0:1, :] = listed.astype(jnp.int32)
    list_v[1:2, :] = total.astype(jnp.int32)
    bias_v[0:1, :] = jnp.where(times > 0.5, jnp.log2(jnp.maximum(times, 1.0)), ABSENT)
    list_copy = pltpu.make_async_copy(list_v, list_s, sems.at[0])
    bias_copy = pltpu.make_async_copy(bias_v, bias_s, sems.at[1])
    list_copy.start()
    bias_copy.start()

    for block in range(2):
        for comp in range(3):
            row = positions_ref[comp : comp + 1, block * LANES : (block + 1) * LANES] * KAPPA
            spread_own[3 * block + comp] = jnp.broadcast_to(row, (LANES, LANES)).T
            push[3 * block + comp] = jnp.zeros((LANES, LANES), f32)

    forces = []
    list_copy.wait()
    bias_copy.wait()
    for block in range(2):

        def one_pair(index, carry, block=block):
            partners = []
            for sub in range(2):
                entry = block * 64 + 2 * index + sub
                partner = list_s[0, entry]
                device = partner // 2
                within = partner % 2
                rows = [
                    tiles_ref[device, pl.ds(2 * comp + within, 1), :] * KAPPA for comp in range(3)
                ]
                partners.append((rows, bias_s[0, entry]))
            for group in range(0, LANES, 8):
                own = [spread_own[3 * block + comp, group : group + 8, :] for comp in range(3)]
                sums = [push[3 * block + comp, group : group + 8, :] for comp in range(3)]
                for rows, bias in partners:
                    offset = [own[comp] - rows[comp] for comp in range(3)]
                    power = bias - offset[0] * offset[0]
                    power = power - offset[1] * offset[1]
                    power = power - offset[2] * offset[2]
                    weight = jnp.exp2(power)
                    sums = [sums[comp] + weight * offset[comp] for comp in range(3)]
                for comp in range(3):
                    push[3 * block + comp, group : group + 8, :] = sums[comp]
            return carry

        lax.fori_loop(0, (list_s[1, block * 64] + 1) // 2, one_pair, 0)
        rows = [jnp.sum(push[3 * block + comp].T, axis=0, keepdims=True) for comp in range(3)]
        clash = jnp.concatenate(rows + [jnp.zeros((5, LANES), f32)], axis=0)
        forces.append(clash * (8.0 / KAPPA))
    out_ref[...] = bond_ref[...] + jnp.concatenate(forces, axis=1)


def start_copies(sources, targets, sems):
    copies = [
        pltpu.make_async_copy(source, target, sems.at[index])
        for index, (source, target) in enumerate(zip(sources, targets))
    ]
    for copy in copies:
        copy.start()
    return copies


def prepare_kernel(*refs):
    first_ref, sources, (stream_ref, normed_ref, rows_ref, tile_ref) = refs[0], refs[1:8], refs[8:12]
    targets, sems = refs[12:19], refs[19]
    time_ref, positions_ref, single_ref, pos_weight_ref, gain_ref, pairs_ref, window_ref = targets
    for copy in start_copies(sources, targets, sems):
        copy.wait()
    level = 0.2 + 0.02 * jnp.full((1, ROWS), time_ref[0], jnp.int32).astype(f32)
    spread_sq = level * level + 1.0
    c_input = 1.0 / jnp.sqrt(spread_sq)
    window = window_ref[...]
    own = first_ref[0] * 2 + lax.broadcasted_iota(jnp.int32, window.shape, 0)
    lane = lax.broadcasted_iota(jnp.int32, (1, ROWS), 1)
    counts = jnp.zeros((1, ROWS), f32)
    for offset in range(5):
        hit = jnp.sum((window == own + (offset - 2)).astype(f32), axis=1, keepdims=True)
        counts = jnp.where(lane == offset, hit[0:1], counts)
        counts = jnp.where(lane == 8 + offset, hit[1:2], counts)
    counts = jnp.where(counts > 0.0, jnp.log2(jnp.maximum(counts, 1.0)), ABSENT)
    gain_rows = [
        jnp.concatenate([gain_ref[layer, 0:1], gain_ref[layer, 1:2]], axis=1) for layer in range(2)
    ]
    rows_ref[...] = jnp.concatenate(
        [level, spread_sq, c_input] + gain_rows + [counts, jnp.zeros((2, ROWS), f32)], axis=0
    )
    for row in range(6):
        part = slice((row % 2) * LANES, (row % 2 + 1) * LANES)
        tile_ref[row : row + 1, :] = positions_ref[row // 2 : row // 2 + 1, part]
    pairs = pairs_ref[...]
    codes = (pairs[0:1] * 64 + pairs[1:2]).astype(f32)
    tile_ref[6:7, :] = jnp.concatenate([codes, codes], axis=1)
    tile_ref[7:8, :] = jnp.zeros((1, LANES), f32)
    columns = jnp.concatenate(
        [pos_weight_ref[...], gain_ref[0, 0:1], jnp.zeros((4, LANES), f32)], axis=0
    ).T
    identity = (
        lax.broadcasted_iota(jnp.int32, (LANES, LANES), 0)
        == lax.broadcasted_iota(jnp.int32, (LANES, LANES), 1)
    ).astype(f32).astype(bf16)
    stream = dot_nt(identity, single_ref[...])
    for comp in range(3):
        stream = stream + columns[:, comp : comp + 1] * (positions_ref[comp : comp + 1, :] * c_input)
    stream_ref[...] = stream
    normed_ref[...] = (norm_columns(stream) * columns[:, 3:4]).astype(bf16).T


def layer_values(layer, first_ref, halo, stream_ref, rows_ref, weights, scratch):
    even_ref, own_ref, odd_ref = halo
    w_query_ref, w_key_ref, w_value_ref, w_out_ref, w_gate_up_ref, w_down_ref = weights
    near, keys, values, attended = scratch
    head_size = LANES // HEADS
    query_scale = LOG2E * head_size ** -0.5
    near[ROWS : 2 * ROWS, :] = own_ref[...]

    @pl.when(first_ref[0] % 2 == 0)
    def _():
        near[:ROWS, :] = odd_ref[...]
        near[2 * ROWS :, :] = even_ref[...]

    @pl.when(first_ref[0] % 2 == 1)
    def _():
        near[:ROWS, :] = even_ref[...]
        near[2 * ROWS :, :] = odd_ref[...]

    row_block = lax.broadcasted_iota(jnp.int32, (3 * ROWS, LANES), 0) // LANES
    lane = lax.broadcasted_iota(jnp.int32, (3 * ROWS, LANES), 1)
    keys[:, LANES:] = jnp.where((lane % 16 == row_block) & (lane < 32), 1.0, 0.0).astype(bf16)
    window = rows_ref[5:6, :LANES]
    rows = []
    for chunk in range(6):
        sides = []
        for block in range(2):
            offset = chunk - block
            if 0 <= offset < 5:
                lane_id = block * 8 + offset
                sides.append(jnp.broadcast_to(window[:, lane_id : lane_id + 1], (1, LANES)))
            else:
                sides.append(jnp.full((1, LANES), ABSENT, f32))
        rows.append(jnp.concatenate(sides, axis=1))
    rows = jnp.concatenate(rows + [jnp.zeros((10, ROWS), f32)], axis=0)
    high = rows.astype(bf16)
    low = (rows - high.astype(f32)).astype(bf16)
    bias = jnp.concatenate([high, low, jnp.zeros((LANES - 32, ROWS), bf16)], axis=0)

    keys[:, :LANES] = dot(near[...], w_key_ref[layer]).astype(bf16)
    query_t = (dot_nt(w_query_ref[layer].T, own_ref[...]) * query_scale).astype(bf16)
    value_t = dot_nt(w_value_ref[layer].T, near[...]).astype(bf16)
    for head in range(HEADS):
        values[head * 48 : head * 48 + 32, :] = value_t[head * 32 : head * 32 + 32]
        values[head * 48 + 32 : head * 48 + 48, :] = jnp.ones((16, 3 * ROWS), bf16)

    def attend(exact):
        pieces = []
        sums = []

        def scores_of(head):
            parts = []
            if head:
                parts.append(jnp.zeros((head * head_size, ROWS), bf16))
            parts.append(query_t[head * head_size : (head + 1) * head_size])
            if head < HEADS - 1:
                parts.append(jnp.zeros(((HEADS - 1 - head) * head_size, ROWS), bf16))
            return dot(keys[...], jnp.concatenate(parts + [bias], axis=0))

        following = scores_of(0)
        for head in range(HEADS):
            scores = following
            if head < HEADS - 1:
                following = scores_of(head + 1)
            if exact:
                scores = scores - jnp.max(scores, axis=0, keepdims=True)
            blank = jnp.zeros((LANES, LANES), bf16)
            weights_t = jnp.concatenate(
                [
                    jnp.concatenate([jnp.exp2(scores[: 5 * LANES, :LANES]).astype(bf16), blank], axis=0),
                    jnp.concatenate([blank, jnp.exp2(scores[LANES:, LANES:]).astype(bf16)], axis=0),
                ],
                axis=1,
            )
            mixed = dot(values[head * 48 : (head + 1) * 48, :], weights_t)
            total = mixed[head_size : head_size + 1]
            sums.append(total)
            pieces.append(mixed[:head_size] * (1.0 / total))
        attended[...] = jnp.concatenate(pieces, axis=0).astype(bf16)
        return jnp.concatenate(sums, axis=0)

    sums = attend(False)
    safe = (jnp.min(sums) > 2.0**-80) & (jnp.max(sums) < 2.0**100)

    @pl.when(jnp.logical_not(safe))
    def _():
        attend(True)

    gains = jnp.concatenate(
        [rows_ref[3 + index // 2 : 4 + index // 2, (index % 2) * LANES : (index % 2 + 1) * LANES] for index in range(4)]
        + [jnp.zeros((4, LANES), f32)],
        axis=0,
    ).T
    now = stream_ref[...] + dot(w_out_ref[layer].T, attended[...])
    normed = (norm_columns(now) * gains[:, 2 * layer + 1 : 2 * layer + 2]).astype(bf16)
    gate_up = dot(w_gate_up_ref[layer].T, normed)
    width = gate_up.shape[0] // 2
    half, up = 0.5 * gate_up[:width], gate_up[width:]
    hidden = ((half + half * jnp.tanh(half)) * up).astype(bf16)
    return now + dot(w_down_ref[layer].T, hidden), gains


def first_layer_kernel(first_ref, even_ref, own_ref, odd_ref, stream_ref, rows_ref, *refs):
    weights, (out_ref, normed_ref), scratch = refs[:6], refs[6:8], refs[8:]
    stream, gains = layer_values(
        0, first_ref, (even_ref, own_ref, odd_ref), stream_ref, rows_ref, weights, scratch
    )
    out_ref[...] = stream
    normed_ref[...] = (norm_columns(stream) * gains[:, 2:3]).astype(bf16).T


def last_layer_kernel(first_ref, even_ref, own_ref, odd_ref, stream_ref, rows_ref, *refs):
    weights, (positions_ref, noise_ref, force_ref, w_head_ref) = refs[:6], refs[6:10]
    out_ref, scratch = refs[10], refs[11:]
    stream, _ = layer_values(
        1, first_ref, (even_ref, own_ref, odd_ref), stream_ref, rows_ref, weights, scratch
    )
    final = norm_columns(stream)
    head_rows = jnp.concatenate([w_head_ref[...], jnp.zeros((5, LANES), f32)], axis=0)
    update = jnp.dot(head_rows, final, precision=lax.Precision.HIGHEST, preferred_element_type=f32)
    level, spread_sq, c_input = rows_ref[0:1], rows_ref[1:2], rows_ref[2:3]
    positions = jnp.concatenate([positions_ref[...], jnp.zeros((5, ROWS), f32)], axis=0)
    fresh = jnp.concatenate([noise_ref[...], jnp.zeros((5, ROWS), f32)], axis=0)
    denoised = positions * (1.0 / spread_sq) + (level * c_input) * update
    following = 0.85 * level
    result = denoised + STEER * force_ref[...] + following * (0.8 * (positions - denoised) / level + 0.6 * fresh)
    out_ref[...] = result[:3]


def body(
    positions,
    fresh_noise,
    timestep,
    atom_single,
    pos_weight,
    ln_gain,
    w_query,
    w_key,
    w_value,
    w_out,
    w_gate_up,
    w_down,
    w_head,
    key_window,
    block_pairs,
    pair_count,
    bond_atoms,
):
    devices = lax.axis_size("atom")
    first = lax.axis_index("atom").astype(jnp.int32).reshape(1)
    smem = pl.BlockSpec(memory_space=pltpu.SMEM)
    vmem = pl.BlockSpec(memory_space=pltpu.VMEM)
    hbm = pl.BlockSpec(memory_space=pltpu.HBM)
    rows = atom_single.shape[0]

    def from_neighbours(array):
        even = [(i, i ^ 1) for i in range(devices)]
        odd = [(i, ((i + 1) ^ 1) - 1) for i in range(1, devices - 1)]
        return lax.ppermute(array, "atom", even), lax.ppermute(array, "atom", odd)

    stream, normed, schedule, tile = pl.pallas_call(
        prepare_kernel,
        out_shape=(
            jax.ShapeDtypeStruct((LANES, rows), f32),
            jax.ShapeDtypeStruct((rows, LANES), bf16),
            jax.ShapeDtypeStruct((8, rows), f32),
            jax.ShapeDtypeStruct((8, LANES), f32),
        ),
        in_specs=[smem] + [hbm] * 7,
        out_specs=(vmem,) * 4,
        scratch_shapes=[
            pltpu.SMEM(timestep.shape, jnp.int32),
            pltpu.VMEM(positions.shape, f32),
            pltpu.VMEM(atom_single.shape, bf16),
            pltpu.VMEM(pos_weight.shape, f32),
            pltpu.VMEM(ln_gain.shape, f32),
            pltpu.VMEM(block_pairs.shape, jnp.int32),
            pltpu.VMEM(key_window.shape, jnp.int32),
            pltpu.SemaphoreType.DMA((7,)),
        ],
        compiler_params=pltpu.CompilerParams(vmem_limit_bytes=VMEM_GRANT),
    )(first, timestep, positions, atom_single, pos_weight, ln_gain, block_pairs, key_window)
    even, odd = from_neighbours(normed)

    packed = pl.pallas_call(
        pack_kernel,
        out_shape=jax.ShapeDtypeStruct((devices, 8, LANES), f32),
        in_specs=[smem, vmem],
        out_specs=vmem,
        cost_estimate=pl.CostEstimate(flops=40_000_000, bytes_accessed=10_000_000, transcendentals=1_000_000),
        compiler_params=pltpu.CompilerParams(vmem_limit_bytes=VMEM_SMALL),
    )(pair_count, tile)
    tiles = lax.all_to_all(packed, "atom", 0, 0)

    weights = (w_query, w_key, w_value, w_out, w_gate_up, w_down)
    layer_scratch = [
        pltpu.VMEM((3 * rows, LANES), bf16),
        pltpu.VMEM((3 * rows, 2 * LANES), bf16),
        pltpu.VMEM((HEADS * 48, 3 * rows), bf16),
        pltpu.VMEM((LANES, rows), bf16),
    ]
    layer_cost = pl.CostEstimate(flops=2_000_000_000, bytes_accessed=20_000_000, transcendentals=2_000_000)
    stream, normed = pl.pallas_call(
        first_layer_kernel,
        out_shape=(
            jax.ShapeDtypeStruct((LANES, rows), f32),
            jax.ShapeDtypeStruct((rows, LANES), bf16),
        ),
        in_specs=[smem] + [vmem] * 11,
        out_specs=(vmem, vmem),
        scratch_shapes=layer_scratch,
        cost_estimate=layer_cost,
        compiler_params=pltpu.CompilerParams(vmem_limit_bytes=VMEM_SMALL),
    )(first, even, normed, odd, stream, schedule, *weights)
    even, odd = from_neighbours(normed)

    bond_force = pl.pallas_call(
        bond_kernel,
        out_shape=jax.ShapeDtypeStruct((8, 2 * LANES), f32),
        in_specs=[vmem, vmem],
        out_specs=vmem,
        cost_estimate=pl.CostEstimate(flops=80_000_000, bytes_accessed=8_000_000, transcendentals=0),
        compiler_params=pltpu.CompilerParams(vmem_limit_bytes=VMEM_SMALL),
    )(positions, bond_atoms)

    force = pl.pallas_call(
        force_kernel,
        out_shape=jax.ShapeDtypeStruct((8, 2 * LANES), f32),
        in_specs=[smem, vmem, vmem, vmem],
        out_specs=vmem,
        scratch_shapes=[
            pltpu.VMEM((6, LANES, LANES), f32),
            pltpu.VMEM((6, LANES, LANES), f32),
            pltpu.VMEM((8, LANES), jnp.int32),
            pltpu.VMEM((8, LANES), f32),
            pltpu.SMEM((8, LANES), jnp.int32),
            pltpu.SMEM((8, LANES), f32),
            pltpu.SemaphoreType.DMA((2,)),
        ],
        cost_estimate=pl.CostEstimate(flops=80_000_000, bytes_accessed=16_000_000, transcendentals=2_000_000),
        compiler_params=pltpu.CompilerParams(vmem_limit_bytes=VMEM_SMALL),
    )(first, tiles, positions, bond_force)

    return pl.pallas_call(
        last_layer_kernel,
        out_shape=jax.ShapeDtypeStruct(positions.shape, f32),
        in_specs=[smem] + [vmem] * 15,
        out_specs=vmem,
        scratch_shapes=layer_scratch,
        cost_estimate=layer_cost,
        compiler_params=pltpu.CompilerParams(vmem_limit_bytes=VMEM_SMALL),
    )(
        first,
        even,
        normed,
        odd,
        stream,
        schedule,
        *weights,
        positions,
        fresh_noise,
        force,
        w_head,
    )


def solution(mesh):
    in_specs = (
        P(None, ("sample", "atom")),
        P(None, ("sample", "atom")),
        P(),
        P("atom", None),
        P(),
        P(),
        P(),
        P(),
        P(),
        P(),
        P(),
        P(),
        P(),
        P("atom", None),
        P(None, "atom"),
        P("atom"),
        P(None, "atom", None),
    )
    out_specs = P(None, ("sample", "atom"))
    return jax.shard_map(body, mesh=mesh, in_specs=in_specs, out_specs=out_specs, check_vma=False)
```

```python
import functools
import math

import jax
import jax.numpy as jnp
from jax import lax
from jax.experimental import pallas as pl
from jax.experimental.pallas import tpu as pltpu
from jax.sharding import PartitionSpec as P

HEADS = 4
LANES = 128
ROWS = 256
VMEM_GRANT = 60 * 1024 * 1024
VMEM_SMALL = 16 * 1024 * 1024
NORM_EPS = 1e-05
STEER = 0.3
ABSENT = -(2.0**120)
LOG2E = 1.4426950408889634
KAPPA = 2.0 * math.sqrt(LOG2E)

f32 = jnp.float32
bf16 = jnp.bfloat16


def pack_kernel(count_ref, tile_ref, out_ref):
    shape = tile_ref.shape
    row = lax.broadcasted_iota(jnp.int32, shape, 0)
    lane = lax.broadcasted_iota(jnp.int32, shape, 1)
    dead = (row == 6) & (lane % 64 >= count_ref[0])
    out_ref[...] = jnp.broadcast_to(jnp.where(dead, -1.0, tile_ref[...])[None], out_ref.shape)


def split3(values):
    high = values.astype(bf16)
    rest = values - high.astype(f32)
    mid = rest.astype(bf16)
    low = (rest - mid.astype(f32)).astype(bf16)
    return jnp.concatenate([high, mid, low], axis=0)


def join3(values):
    rows = values.shape[0] // 3
    return values[:rows] + values[rows : 2 * rows] + values[2 * rows :]


def norm_columns(values):
    center = values - jnp.mean(values, axis=0, keepdims=True)
    spread = jnp.mean(center * center, axis=0, keepdims=True)
    return center * lax.rsqrt(spread + NORM_EPS)


def dot_t(left, right):
    return lax.dot_general(left, right, (((0,), (0,)), ((), ())), preferred_element_type=f32)


def dot_nt(left, right):
    return lax.dot_general(left, right, (((1,), (1,)), ((), ())), preferred_element_type=f32)


def dot(left, right):
    return jnp.dot(left, right, preferred_element_type=f32)


def force_kernel(first_ref, tiles_ref, positions_ref, bonds_ref, out_ref, spread_own, push, list_v, bias_v, list_s, bias_s, sems):
    me = first_ref[0]

    codes = tiles_ref[:, 6, :].astype(jnp.int32)
    half = lax.broadcasted_iota(jnp.int32, codes.shape, 1) // 64
    mine = me * 2 + half
    first = jnp.where(codes < 0, -1, codes // 64)
    second = jnp.where(codes < 0, -1, codes % 64)
    partner = jnp.where(first == mine, second, jnp.where(second == mine, first, -1)).astype(f32)
    block_id = lax.broadcasted_iota(jnp.int32, (64, LANES), 0).astype(f32)
    hits = jnp.zeros((64, LANES), f32)
    for row in range(codes.shape[0]):
        hits = hits + jnp.where(partner[row : row + 1] == block_id, 1.0, 0.0)
    row_half = lax.broadcasted_iota(jnp.int32, (LANES, LANES), 0) // 64
    col_half = lax.broadcasted_iota(jnp.int32, (LANES, LANES), 1) // 64
    count = dot(hits.astype(bf16), (row_half == col_half).astype(bf16))
    present = count > 0.5
    lower = lax.broadcasted_iota(jnp.int32, (64, 64), 1) < lax.broadcasted_iota(jnp.int32, (64, 64), 0)
    rank = dot(lower.astype(bf16), present.astype(bf16))
    slot = (lax.broadcasted_iota(jnp.int32, (64, LANES), 1) % 64).astype(f32)
    chosen = present & (rank == slot)
    listed = jnp.sum(jnp.where(chosen, block_id, 0.0), axis=0, keepdims=True)
    times = jnp.sum(jnp.where(chosen, count, 0.0), axis=0, keepdims=True)
    total = jnp.sum(present.astype(f32), axis=0, keepdims=True)
    list_v[0:1, :] = listed.astype(jnp.int32)
    list_v[1:2, :] = total.astype(jnp.int32)
    bias_v[0:1, :] = jnp.where(times > 0.5, jnp.log2(jnp.maximum(times, 1.0)), ABSENT)
    list_copy = pltpu.make_async_copy(list_v, list_s, sems.at[0])
    bias_copy = pltpu.make_async_copy(bias_v, bias_s, sems.at[1])
    list_copy.start()
    bias_copy.start()

    for block in range(2):
        for comp in range(3):
            row = positions_ref[comp : comp + 1, block * LANES : (block + 1) * LANES] * KAPPA
            spread_own[3 * block + comp] = jnp.broadcast_to(row, (LANES, LANES)).T
            push[3 * block + comp] = jnp.zeros((LANES, LANES), f32)

    positions = jnp.concatenate([positions_ref[...], jnp.zeros((5, 2 * LANES), f32)], axis=0)

    forces = []
    atom_id = lax.broadcasted_iota(jnp.int32, (LANES, LANES), 0)
    for block in range(2):
        incidence = (
            (atom_id == bonds_ref[0, block : block + 1, :]).astype(f32)
            - (atom_id == bonds_ref[1, block : block + 1, :]).astype(f32)
        ).astype(bf16)
        offset = join3(dot(split3(positions[:, block * LANES : (block + 1) * LANES]), incidence))
        stretch = jnp.sum(offset * offset, axis=0, keepdims=True) - 1.0
        pull = (-0.2 * stretch) * offset
        forces.append(join3(dot_nt(split3(pull), incidence)))

    list_copy.wait()
    bias_copy.wait()
    for block in range(2):

        def one_pair(index, carry, block=block):
            partners = []
            for sub in range(2):
                entry = block * 64 + 2 * index + sub
                partner = list_s[0, entry]
                device = partner // 2
                within = partner % 2
                rows = [
                    tiles_ref[device, pl.ds(2 * comp + within, 1), :] * KAPPA for comp in range(3)
                ]
                partners.append((rows, bias_s[0, entry]))
            for group in range(0, LANES, 8):
                own = [spread_own[3 * block + comp, group : group + 8, :] for comp in range(3)]
                sums = [push[3 * block + comp, group : group + 8, :] for comp in range(3)]
                for rows, bias in partners:
                    offset = [own[comp] - rows[comp] for comp in range(3)]
                    power = bias - offset[0] * offset[0]
                    power = power - offset[1] * offset[1]
                    power = power - offset[2] * offset[2]
                    weight = jnp.exp2(power)
                    sums = [sums[comp] + weight * offset[comp] for comp in range(3)]
                for comp in range(3):
                    push[3 * block + comp, group : group + 8, :] = sums[comp]
            return carry

        lax.fori_loop(0, (list_s[1, block * 64] + 1) // 2, one_pair, 0)
        rows = [jnp.sum(push[3 * block + comp].T, axis=0, keepdims=True) for comp in range(3)]
        clash = jnp.concatenate(rows + [jnp.zeros((5, LANES), f32)], axis=0)
        forces[block] = forces[block] + clash * (8.0 / KAPPA)
    out_ref[...] = jnp.concatenate(forces, axis=1)


def start_copies(sources, targets, sems):
    copies = [
        pltpu.make_async_copy(source, target, sems.at[index])
        for index, (source, target) in enumerate(zip(sources, targets))
    ]
    for copy in copies:
        copy.start()
    return copies


def prepare_kernel(*refs):
    first_ref, sources, (stream_ref, normed_ref, rows_ref, tile_ref) = refs[0], refs[1:8], refs[8:12]
    targets, sems = refs[12:19], refs[19]
    time_ref, positions_ref, single_ref, pos_weight_ref, gain_ref, pairs_ref, window_ref = targets
    for copy in start_copies(sources, targets, sems):
        copy.wait()
    level = 0.2 + 0.02 * jnp.full((1, ROWS), time_ref[0], jnp.int32).astype(f32)
    spread_sq = level * level + 1.0
    c_input = 1.0 / jnp.sqrt(spread_sq)
    window = window_ref[...]
    own = first_ref[0] * 2 + lax.broadcasted_iota(jnp.int32, window.shape, 0)
    lane = lax.broadcasted_iota(jnp.int32, (1, ROWS), 1)
    counts = jnp.zeros((1, ROWS), f32)
    for offset in range(5):
        hit = jnp.sum((window == own + (offset - 2)).astype(f32), axis=1, keepdims=True)
        counts = jnp.where(lane == offset, hit[0:1], counts)
        counts = jnp.where(lane == 8 + offset, hit[1:2], counts)
    counts = jnp.where(counts > 0.0, jnp.log2(jnp.maximum(counts, 1.0)), ABSENT)
    gain_rows = [
        jnp.concatenate([gain_ref[layer, 0:1], gain_ref[layer, 1:2]], axis=1) for layer in range(2)
    ]
    rows_ref[...] = jnp.concatenate(
        [level, spread_sq, c_input] + gain_rows + [counts, jnp.zeros((2, ROWS), f32)], axis=0
    )
    for row in range(6):
        part = slice((row % 2) * LANES, (row % 2 + 1) * LANES)
        tile_ref[row : row + 1, :] = positions_ref[row // 2 : row // 2 + 1, part]
    pairs = pairs_ref[...]
    codes = (pairs[0:1] * 64 + pairs[1:2]).astype(f32)
    tile_ref[6:7, :] = jnp.concatenate([codes, codes], axis=1)
    tile_ref[7:8, :] = jnp.zeros((1, LANES), f32)
    columns = jnp.concatenate(
        [pos_weight_ref[...], gain_ref[0, 0:1], jnp.zeros((4, LANES), f32)], axis=0
    ).T
    identity = (
        lax.broadcasted_iota(jnp.int32, (LANES, LANES), 0)
        == lax.broadcasted_iota(jnp.int32, (LANES, LANES), 1)
    ).astype(f32).astype(bf16)
    stream = dot_nt(identity, single_ref[...])
    for comp in range(3):
        stream = stream + columns[:, comp : comp + 1] * (positions_ref[comp : comp + 1, :] * c_input)
    stream_ref[...] = stream
    normed_ref[...] = (norm_columns(stream) * columns[:, 3:4]).astype(bf16).T


def layer_values(layer, first_ref, halo, stream_ref, rows_ref, head_rows, weights, scratch):
    even_ref, own_ref, odd_ref = halo
    w_query_ref, w_key_ref, w_value_ref, w_out_ref, w_gate_up_ref, w_down_ref = weights
    near, keys, values, attended = scratch
    head_size = LANES // HEADS
    query_scale = LOG2E * head_size ** -0.5
    near[ROWS : 2 * ROWS, :] = own_ref[...]

    @pl.when(first_ref[0] % 2 == 0)
    def _():
        near[:ROWS, :] = odd_ref[...]
        near[2 * ROWS :, :] = even_ref[...]

    @pl.when(first_ref[0] % 2 == 1)
    def _():
        near[:ROWS, :] = even_ref[...]
        near[2 * ROWS :, :] = odd_ref[...]

    row_block = lax.broadcasted_iota(jnp.int32, (3 * ROWS, LANES), 0) // LANES
    lane = lax.broadcasted_iota(jnp.int32, (3 * ROWS, LANES), 1)
    keys[:, LANES:] = jnp.where((lane % 16 == row_block) & (lane < 32), 1.0, 0.0).astype(bf16)
    window = rows_ref[5:6, :LANES]
    rows = []
    for chunk in range(6):
        sides = []
        for block in range(2):
            offset = chunk - block
            if 0 <= offset < 5:
                lane_id = block * 8 + offset
                sides.append(jnp.broadcast_to(window[:, lane_id : lane_id + 1], (1, LANES)))
            else:
                sides.append(jnp.full((1, LANES), ABSENT, f32))
        rows.append(jnp.concatenate(sides, axis=1))
    rows = jnp.concatenate(rows + [jnp.zeros((10, ROWS), f32)], axis=0)
    high = rows.astype(bf16)
    low = (rows - high.astype(f32)).astype(bf16)
    bias = jnp.concatenate([high, low, jnp.zeros((LANES - 32, ROWS), bf16)], axis=0)

    keys[:, :LANES] = dot(near[...], w_key_ref[layer]).astype(bf16)
    query_t = (dot_nt(w_query_ref[layer].T, own_ref[...]) * query_scale).astype(bf16)
    value_t = dot_nt(w_value_ref[layer].T, near[...]).astype(bf16)
    for head in range(HEADS):
        values[head * 48 : head * 48 + 32, :] = value_t[head * 32 : head * 32 + 32]
        values[head * 48 + 32 : head * 48 + 48, :] = jnp.ones((16, 3 * ROWS), bf16)

    def attend(exact):
        pieces = []
        sums = []

        def scores_of(head):
            parts = []
            if head:
                parts.append(jnp.zeros((head * head_size, ROWS), bf16))
            parts.append(query_t[head * head_size : (head + 1) * head_size])
            if head < HEADS - 1:
                parts.append(jnp.zeros(((HEADS - 1 - head) * head_size, ROWS), bf16))
            return dot(keys[...], jnp.concatenate(parts + [bias], axis=0))

        following = scores_of(0)
        for head in range(HEADS):
            scores = following
            if head < HEADS - 1:
                following = scores_of(head + 1)
            if exact:
                scores = scores - jnp.max(scores, axis=0, keepdims=True)
            blank = jnp.zeros((LANES, LANES), bf16)
            weights_t = jnp.concatenate(
                [
                    jnp.concatenate([jnp.exp2(scores[: 5 * LANES, :LANES]).astype(bf16), blank], axis=0),
                    jnp.concatenate([blank, jnp.exp2(scores[LANES:, LANES:]).astype(bf16)], axis=0),
                ],
                axis=1,
            )
            mixed = dot(values[head * 48 : (head + 1) * 48, :], weights_t)
            total = mixed[head_size : head_size + 1]
            sums.append(total)
            pieces.append(mixed[:head_size] * (1.0 / total))
        attended[...] = jnp.concatenate(pieces, axis=0).astype(bf16)
        return jnp.concatenate(sums, axis=0)

    sums = attend(False)
    safe = (jnp.min(sums) > 2.0**-80) & (jnp.max(sums) < 2.0**100)

    @pl.when(jnp.logical_not(safe))
    def _():
        attend(True)

    gains = jnp.concatenate(
        [rows_ref[3 + index // 2 : 4 + index // 2, (index % 2) * LANES : (index % 2 + 1) * LANES] for index in range(4)]
        + [head_rows],
        axis=0,
    ).T
    now = stream_ref[...] + dot(w_out_ref[layer].T, attended[...])
    normed = (norm_columns(now) * gains[:, 2 * layer + 1 : 2 * layer + 2]).astype(bf16)
    gate_up = dot(w_gate_up_ref[layer].T, normed)
    width = gate_up.shape[0] // 2
    half, up = 0.5 * gate_up[:width], gate_up[width:]
    hidden = ((half + half * jnp.tanh(half)) * up).astype(bf16)
    return now + dot(w_down_ref[layer].T, hidden), gains


def first_layer_kernel(first_ref, even_ref, own_ref, odd_ref, stream_ref, rows_ref, *refs):
    weights, (out_ref, normed_ref), scratch = refs[:6], refs[6:8], refs[8:]
    stream, gains = layer_values(
        0, first_ref, (even_ref, own_ref, odd_ref), stream_ref, rows_ref, jnp.zeros((4, LANES), f32), weights, scratch
    )
    out_ref[...] = stream
    normed_ref[...] = (norm_columns(stream) * gains[:, 2:3]).astype(bf16).T


def last_layer_kernel(first_ref, even_ref, own_ref, odd_ref, stream_ref, rows_ref, *refs):
    weights, (positions_ref, noise_ref, force_ref, w_head_ref) = refs[:6], refs[6:10]
    out_ref, scratch = refs[10], refs[11:]
    head_rows = jnp.concatenate([w_head_ref[...], jnp.zeros((1, LANES), f32)], axis=0)
    stream, columns = layer_values(
        1, first_ref, (even_ref, own_ref, odd_ref), stream_ref, rows_ref, head_rows, weights, scratch
    )
    final = norm_columns(stream)
    update = jnp.concatenate(
        [jnp.sum(columns[:, 4 + comp : 5 + comp] * final, axis=0, keepdims=True) for comp in range(3)]
        + [jnp.zeros((5, ROWS), f32)],
        axis=0,
    )
    level, spread_sq, c_input = rows_ref[0:1], rows_ref[1:2], rows_ref[2:3]
    positions = jnp.concatenate([positions_ref[...], jnp.zeros((5, ROWS), f32)], axis=0)
    fresh = jnp.concatenate([noise_ref[...], jnp.zeros((5, ROWS), f32)], axis=0)
    denoised = positions * (1.0 / spread_sq) + (level * c_input) * update
    following = 0.85 * level
    result = denoised + STEER * force_ref[...] + following * (0.8 * (positions - denoised) / level + 0.6 * fresh)
    out_ref[...] = result[:3]


def body(
    positions,
    fresh_noise,
    timestep,
    atom_single,
    pos_weight,
    ln_gain,
    w_query,
    w_key,
    w_value,
    w_out,
    w_gate_up,
    w_down,
    w_head,
    key_window,
    block_pairs,
    pair_count,
    bond_atoms,
):
    devices = lax.axis_size("atom")
    first = lax.axis_index("atom").astype(jnp.int32).reshape(1)
    smem = pl.BlockSpec(memory_space=pltpu.SMEM)
    vmem = pl.BlockSpec(memory_space=pltpu.VMEM)
    hbm = pl.BlockSpec(memory_space=pltpu.HBM)
    rows = atom_single.shape[0]

    def from_neighbours(array):
        even = [(i, i ^ 1) for i in range(devices)]
        odd = [(i, ((i + 1) ^ 1) - 1) for i in range(1, devices - 1)]
        return lax.ppermute(array, "atom", even), lax.ppermute(array, "atom", odd)

    stream, normed, schedule, tile = pl.pallas_call(
        prepare_kernel,
        out_shape=(
            jax.ShapeDtypeStruct((LANES, rows), f32),
            jax.ShapeDtypeStruct((rows, LANES), bf16),
            jax.ShapeDtypeStruct((8, rows), f32),
            jax.ShapeDtypeStruct((8, LANES), f32),
        ),
        in_specs=[smem] + [hbm] * 7,
        out_specs=(vmem,) * 4,
        scratch_shapes=[
            pltpu.SMEM(timestep.shape, jnp.int32),
            pltpu.VMEM(positions.shape, f32),
            pltpu.VMEM(atom_single.shape, bf16),
            pltpu.VMEM(pos_weight.shape, f32),
            pltpu.VMEM(ln_gain.shape, f32),
            pltpu.VMEM(block_pairs.shape, jnp.int32),
            pltpu.VMEM(key_window.shape, jnp.int32),
            pltpu.SemaphoreType.DMA((7,)),
        ],
        compiler_params=pltpu.CompilerParams(vmem_limit_bytes=VMEM_GRANT),
    )(first, timestep, positions, atom_single, pos_weight, ln_gain, block_pairs, key_window)
    even, odd = from_neighbours(normed)

    packed = pl.pallas_call(
        pack_kernel,
        out_shape=jax.ShapeDtypeStruct((devices, 8, LANES), f32),
        in_specs=[smem, vmem],
        out_specs=vmem,
        cost_estimate=pl.CostEstimate(flops=40_000_000, bytes_accessed=10_000_000, transcendentals=1_000_000),
        compiler_params=pltpu.CompilerParams(vmem_limit_bytes=VMEM_SMALL),
    )(pair_count, tile)
    tiles = lax.all_to_all(packed, "atom", 0, 0)

    weights = (w_query, w_key, w_value, w_out, w_gate_up, w_down)
    layer_scratch = [
        pltpu.VMEM((3 * rows, LANES), bf16),
        pltpu.VMEM((3 * rows, 2 * LANES), bf16),
        pltpu.VMEM((HEADS * 48, 3 * rows), bf16),
        pltpu.VMEM((LANES, rows), bf16),
    ]
    layer_cost = pl.CostEstimate(flops=2_000_000_000, bytes_accessed=20_000_000, transcendentals=2_000_000)
    stream, normed = pl.pallas_call(
        first_layer_kernel,
        out_shape=(
            jax.ShapeDtypeStruct((LANES, rows), f32),
            jax.ShapeDtypeStruct((rows, LANES), bf16),
        ),
        in_specs=[smem] + [vmem] * 11,
        out_specs=(vmem, vmem),
        scratch_shapes=layer_scratch,
        cost_estimate=layer_cost,
        compiler_params=pltpu.CompilerParams(vmem_limit_bytes=VMEM_SMALL),
    )(first, even, normed, odd, stream, schedule, *weights)
    even, odd = from_neighbours(normed)

    force = pl.pallas_call(
        force_kernel,
        out_shape=jax.ShapeDtypeStruct((8, 2 * LANES), f32),
        in_specs=[smem, vmem, vmem, vmem],
        out_specs=vmem,
        scratch_shapes=[
            pltpu.VMEM((6, LANES, LANES), f32),
            pltpu.VMEM((6, LANES, LANES), f32),
            pltpu.VMEM((8, LANES), jnp.int32),
            pltpu.VMEM((8, LANES), f32),
            pltpu.SMEM((8, LANES), jnp.int32),
            pltpu.SMEM((8, LANES), f32),
            pltpu.SemaphoreType.DMA((2,)),
        ],
        cost_estimate=pl.CostEstimate(flops=80_000_000, bytes_accessed=16_000_000, transcendentals=2_000_000),
        compiler_params=pltpu.CompilerParams(vmem_limit_bytes=VMEM_SMALL),
    )(first, tiles, positions, bond_atoms)

    return pl.pallas_call(
        last_layer_kernel,
        out_shape=jax.ShapeDtypeStruct(positions.shape, f32),
        in_specs=[smem] + [vmem] * 15,
        out_specs=vmem,
        scratch_shapes=layer_scratch,
        cost_estimate=layer_cost,
        compiler_params=pltpu.CompilerParams(vmem_limit_bytes=VMEM_SMALL),
    )(
        first,
        even,
        normed,
        odd,
        stream,
        schedule,
        *weights,
        positions,
        fresh_noise,
        force,
        w_head,
    )


def solution(mesh):
    in_specs = (
        P(None, ("sample", "atom")),
        P(None, ("sample", "atom")),
        P(),
        P("atom", None),
        P(),
        P(),
        P(),
        P(),
        P(),
        P(),
        P(),
        P(),
        P(),
        P("atom", None),
        P(None, "atom"),
        P("atom"),
        P(None, "atom", None),
    )
    out_specs = P(None, ("sample", "atom"))
    return jax.shard_map(body, mesh=mesh, in_specs=in_specs, out_specs=out_specs, check_vma=False)
```

```python
import functools
import math

import jax
import jax.numpy as jnp
from jax import lax
from jax.experimental import pallas as pl
from jax.experimental.pallas import tpu as pltpu
from jax.sharding import PartitionSpec as P

HEADS = 4
LANES = 128
ROWS = 256
VMEM_GRANT = 60 * 1024 * 1024
VMEM_SMALL = 16 * 1024 * 1024
NORM_EPS = 1e-05
STEER = 0.3
ABSENT = -(2.0**120)
LOG2E = 1.4426950408889634
KAPPA = 2.0 * math.sqrt(LOG2E)

f32 = jnp.float32
bf16 = jnp.bfloat16


def pack_kernel(count_ref, tile_ref, out_ref):
    shape = tile_ref.shape
    row = lax.broadcasted_iota(jnp.int32, shape, 0)
    lane = lax.broadcasted_iota(jnp.int32, shape, 1)
    dead = (row == 6) & (lane % 64 >= count_ref[0])
    out_ref[...] = jnp.broadcast_to(jnp.where(dead, -1.0, tile_ref[...])[None], out_ref.shape)


def spread_kernel(line_ref, after_ref, out_ref):
    out_ref[...] = jnp.broadcast_to(line_ref[...][None], out_ref.shape)


def split3(values):
    high = values.astype(bf16)
    rest = values - high.astype(f32)
    mid = rest.astype(bf16)
    low = (rest - mid.astype(f32)).astype(bf16)
    return jnp.concatenate([high, mid, low], axis=0)


def join3(values):
    rows = values.shape[0] // 3
    return values[:rows] + values[rows : 2 * rows] + values[2 * rows :]


def norm_columns(values):
    center = values - jnp.mean(values, axis=0, keepdims=True)
    spread = jnp.mean(center * center, axis=0, keepdims=True)
    return center * lax.rsqrt(spread + NORM_EPS)


def dot_t(left, right):
    return lax.dot_general(left, right, (((0,), (0,)), ((), ())), preferred_element_type=f32)


def dot_nt(left, right):
    return lax.dot_general(left, right, (((1,), (1,)), ((), ())), preferred_element_type=f32)


def dot(left, right):
    return jnp.dot(left, right, preferred_element_type=f32)


def force_kernel(first_ref, tiles_ref, positions_ref, bonds_ref, out_ref, spread_own, push, list_v, bias_v, list_s, bias_s, sems):
    me = first_ref[0]

    codes = tiles_ref[:, 6, :].astype(jnp.int32)
    half = lax.broadcasted_iota(jnp.int32, codes.shape, 1) // 64
    mine = me * 2 + half
    first = jnp.where(codes < 0, -1, codes // 64)
    second = jnp.where(codes < 0, -1, codes % 64)
    partner = jnp.where(first == mine, second, jnp.where(second == mine, first, -1)).astype(f32)
    block_id = lax.broadcasted_iota(jnp.int32, (64, LANES), 0).astype(f32)
    hits = jnp.zeros((64, LANES), f32)
    for row in range(codes.shape[0]):
        hits = hits + jnp.where(partner[row : row + 1] == block_id, 1.0, 0.0)
    row_half = lax.broadcasted_iota(jnp.int32, (LANES, LANES), 0) // 64
    col_half = lax.broadcasted_iota(jnp.int32, (LANES, LANES), 1) // 64
    count = dot(hits.astype(bf16), (row_half == col_half).astype(bf16))
    present = count > 0.5
    lower = lax.broadcasted_iota(jnp.int32, (64, 64), 1) < lax.broadcasted_iota(jnp.int32, (64, 64), 0)
    rank = dot(lower.astype(bf16), present.astype(bf16))
    slot = (lax.broadcasted_iota(jnp.int32, (64, LANES), 1) % 64).astype(f32)
    chosen = present & (rank == slot)
    listed = jnp.sum(jnp.where(chosen, block_id, 0.0), axis=0, keepdims=True)
    times = jnp.sum(jnp.where(chosen, count, 0.0), axis=0, keepdims=True)
    total = jnp.sum(present.astype(f32), axis=0, keepdims=True)
    list_v[0:1, :] = listed.astype(jnp.int32)
    list_v[1:2, :] = total.astype(jnp.int32)
    bias_v[0:1, :] = jnp.where(times > 0.5, jnp.log2(jnp.maximum(times, 1.0)), ABSENT)
    list_copy = pltpu.make_async_copy(list_v, list_s, sems.at[0])
    bias_copy = pltpu.make_async_copy(bias_v, bias_s, sems.at[1])
    list_copy.start()
    bias_copy.start()

    for block in range(2):
        for comp in range(3):
            row = positions_ref[comp : comp + 1, block * LANES : (block + 1) * LANES] * KAPPA
            spread_own[3 * block + comp] = jnp.broadcast_to(row, (LANES, LANES)).T
            push[3 * block + comp] = jnp.zeros((LANES, LANES), f32)

    positions = jnp.concatenate([positions_ref[...], jnp.zeros((5, 2 * LANES), f32)], axis=0)

    forces = []
    atom_id = lax.broadcasted_iota(jnp.int32, (LANES, LANES), 0)
    for block in range(2):
        incidence = (
            (atom_id == bonds_ref[0, block : block + 1, :]).astype(f32)
            - (atom_id == bonds_ref[1, block : block + 1, :]).astype(f32)
        ).astype(bf16)
        offset = join3(dot(split3(positions[:, block * LANES : (block + 1) * LANES]), incidence))
        stretch = jnp.sum(offset * offset, axis=0, keepdims=True) - 1.0
        pull = (-0.2 * stretch) * offset
        forces.append(join3(dot_nt(split3(pull), incidence)))

    list_copy.wait()
    bias_copy.wait()
    for block in range(2):

        def one_pair(index, carry, block=block):
            partners = []
            for sub in range(2):
                entry = block * 64 + 2 * index + sub
                partner = list_s[0, entry]
                device = partner // 2
                within = partner % 2
                rows = [
                    tiles_ref[device, pl.ds(2 * comp + within, 1), :] * KAPPA for comp in range(3)
                ]
                partners.append((rows, bias_s[0, entry]))
            for group in range(0, LANES, 8):
                own = [spread_own[3 * block + comp, group : group + 8, :] for comp in range(3)]
                sums = [push[3 * block + comp, group : group + 8, :] for comp in range(3)]
                for rows, bias in partners:
                    offset = [own[comp] - rows[comp] for comp in range(3)]
                    power = bias - offset[0] * offset[0]
                    power = power - offset[1] * offset[1]
                    power = power - offset[2] * offset[2]
                    weight = jnp.exp2(power)
                    sums = [sums[comp] + weight * offset[comp] for comp in range(3)]
                for comp in range(3):
                    push[3 * block + comp, group : group + 8, :] = sums[comp]
            return carry

        lax.fori_loop(0, (list_s[1, block * 64] + 1) // 2, one_pair, 0)
        rows = [jnp.sum(push[3 * block + comp].T, axis=0, keepdims=True) for comp in range(3)]
        clash = jnp.concatenate(rows + [jnp.zeros((5, LANES), f32)], axis=0)
        forces[block] = forces[block] + clash * (8.0 / KAPPA)
    out_ref[...] = jnp.concatenate(forces, axis=1)


def start_copies(sources, targets, sems):
    copies = [
        pltpu.make_async_copy(source, target, sems.at[index])
        for index, (source, target) in enumerate(zip(sources, targets))
    ]
    for copy in copies:
        copy.start()
    return copies


def prepare_kernel(*refs):
    first_ref, sources, (stream_ref, normed_ref, rows_ref, tile_ref) = refs[0], refs[1:8], refs[8:12]
    targets, sems = refs[12:19], refs[19]
    time_ref, positions_ref, single_ref, pos_weight_ref, gain_ref, pairs_ref, window_ref = targets
    for copy in start_copies(sources, targets, sems):
        copy.wait()
    level = 0.2 + 0.02 * jnp.full((1, ROWS), time_ref[0], jnp.int32).astype(f32)
    spread_sq = level * level + 1.0
    c_input = 1.0 / jnp.sqrt(spread_sq)
    window = window_ref[...]
    own = first_ref[0] * 2 + lax.broadcasted_iota(jnp.int32, window.shape, 0)
    lane = lax.broadcasted_iota(jnp.int32, (1, ROWS), 1)
    counts = jnp.zeros((1, ROWS), f32)
    for offset in range(5):
        hit = jnp.sum((window == own + (offset - 2)).astype(f32), axis=1, keepdims=True)
        counts = jnp.where(lane == offset, hit[0:1], counts)
        counts = jnp.where(lane == 8 + offset, hit[1:2], counts)
    counts = jnp.where(counts > 0.0, jnp.log2(jnp.maximum(counts, 1.0)), ABSENT)
    gain_rows = [
        jnp.concatenate([gain_ref[layer, 0:1], gain_ref[layer, 1:2]], axis=1) for layer in range(2)
    ]
    rows_ref[...] = jnp.concatenate(
        [level, spread_sq, c_input] + gain_rows + [counts, jnp.zeros((2, ROWS), f32)], axis=0
    )
    for row in range(6):
        part = slice((row % 2) * LANES, (row % 2 + 1) * LANES)
        tile_ref[row : row + 1, :] = positions_ref[row // 2 : row // 2 + 1, part]
    pairs = pairs_ref[...]
    codes = (pairs[0:1] * 64 + pairs[1:2]).astype(f32)
    tile_ref[6:7, :] = jnp.concatenate([codes, codes], axis=1)
    tile_ref[7:8, :] = jnp.zeros((1, LANES), f32)
    columns = jnp.concatenate(
        [pos_weight_ref[...], gain_ref[0, 0:1], jnp.zeros((4, LANES), f32)], axis=0
    ).T
    identity = (
        lax.broadcasted_iota(jnp.int32, (LANES, LANES), 0)
        == lax.broadcasted_iota(jnp.int32, (LANES, LANES), 1)
    ).astype(f32).astype(bf16)
    stream = dot_nt(identity, single_ref[...])
    for comp in range(3):
        stream = stream + columns[:, comp : comp + 1] * (positions_ref[comp : comp + 1, :] * c_input)
    stream_ref[...] = stream
    normed_ref[...] = (norm_columns(stream) * columns[:, 3:4]).astype(bf16).T


def layer_values(layer, first_ref, halo, stream_ref, rows_ref, head_rows, weights, scratch):
    even_ref, own_ref, odd_ref = halo
    w_query_ref, w_key_ref, w_value_ref, w_out_ref, w_gate_up_ref, w_down_ref = weights
    near, keys, values, attended = scratch
    head_size = LANES // HEADS
    query_scale = LOG2E * head_size ** -0.5
    near[ROWS : 2 * ROWS, :] = own_ref[...]

    @pl.when(first_ref[0] % 2 == 0)
    def _():
        near[:ROWS, :] = odd_ref[...]
        near[2 * ROWS :, :] = even_ref[...]

    @pl.when(first_ref[0] % 2 == 1)
    def _():
        near[:ROWS, :] = even_ref[...]
        near[2 * ROWS :, :] = odd_ref[...]

    row_block = lax.broadcasted_iota(jnp.int32, (3 * ROWS, LANES), 0) // LANES
    lane = lax.broadcasted_iota(jnp.int32, (3 * ROWS, LANES), 1)
    keys[:, LANES:] = jnp.where((lane % 16 == row_block) & (lane < 32), 1.0, 0.0).astype(bf16)
    window = rows_ref[5:6, :LANES]
    rows = []
    for chunk in range(6):
        sides = []
        for block in range(2):
            offset = chunk - block
            if 0 <= offset < 5:
                lane_id = block * 8 + offset
                sides.append(jnp.broadcast_to(window[:, lane_id : lane_id + 1], (1, LANES)))
            else:
                sides.append(jnp.full((1, LANES), ABSENT, f32))
        rows.append(jnp.concatenate(sides, axis=1))
    rows = jnp.concatenate(rows + [jnp.zeros((10, ROWS), f32)], axis=0)
    high = rows.astype(bf16)
    low = (rows - high.astype(f32)).astype(bf16)
    bias = jnp.concatenate([high, low, jnp.zeros((LANES - 32, ROWS), bf16)], axis=0)

    keys[:, :LANES] = dot(near[...], w_key_ref[layer]).astype(bf16)
    query_t = (dot_nt(w_query_ref[layer].T, own_ref[...]) * query_scale).astype(bf16)
    value_t = dot_nt(w_value_ref[layer].T, near[...]).astype(bf16)
    for head in range(HEADS):
        values[head * 48 : head * 48 + 32, :] = value_t[head * 32 : head * 32 + 32]
        values[head * 48 + 32 : head * 48 + 48, :] = jnp.ones((16, 3 * ROWS), bf16)

    def attend(exact):
        pieces = []
        sums = []

        def scores_of(head):
            parts = []
            if head:
                parts.append(jnp.zeros((head * head_size, ROWS), bf16))
            parts.append(query_t[head * head_size : (head + 1) * head_size])
            if head < HEADS - 1:
                parts.append(jnp.zeros(((HEADS - 1 - head) * head_size, ROWS), bf16))
            return dot(keys[...], jnp.concatenate(parts + [bias], axis=0))

        following = scores_of(0)
        for head in range(HEADS):
            scores = following
            if head < HEADS - 1:
                following = scores_of(head + 1)
            if exact:
                scores = scores - jnp.max(scores, axis=0, keepdims=True)
            blank = jnp.zeros((LANES, LANES), bf16)
            weights_t = jnp.concatenate(
                [
                    jnp.concatenate([jnp.exp2(scores[: 5 * LANES, :LANES]).astype(bf16), blank], axis=0),
                    jnp.concatenate([blank, jnp.exp2(scores[LANES:, LANES:]).astype(bf16)], axis=0),
                ],
                axis=1,
            )
            mixed = dot(values[head * 48 : (head + 1) * 48, :], weights_t)
            total = mixed[head_size : head_size + 1]
            sums.append(total)
            pieces.append(mixed[:head_size] * (1.0 / total))
        attended[...] = jnp.concatenate(pieces, axis=0).astype(bf16)
        return jnp.concatenate(sums, axis=0)

    sums = attend(False)
    safe = (jnp.min(sums) > 2.0**-80) & (jnp.max(sums) < 2.0**100)

    @pl.when(jnp.logical_not(safe))
    def _():
        attend(True)

    gains = jnp.concatenate(
        [rows_ref[3 + index // 2 : 4 + index // 2, (index % 2) * LANES : (index % 2 + 1) * LANES] for index in range(4)]
        + [head_rows],
        axis=0,
    ).T
    now = stream_ref[...] + dot(w_out_ref[layer].T, attended[...])
    normed = (norm_columns(now) * gains[:, 2 * layer + 1 : 2 * layer + 2]).astype(bf16)
    gate_up = dot(w_gate_up_ref[layer].T, normed)
    width = gate_up.shape[0] // 2
    half, up = 0.5 * gate_up[:width], gate_up[width:]
    hidden = ((half + half * jnp.tanh(half)) * up).astype(bf16)
    return now + dot(w_down_ref[layer].T, hidden), gains


def first_layer_kernel(first_ref, even_ref, own_ref, odd_ref, stream_ref, rows_ref, *refs):
    weights, (out_ref, normed_ref), scratch = refs[:6], refs[6:8], refs[8:]
    stream, gains = layer_values(
        0, first_ref, (even_ref, own_ref, odd_ref), stream_ref, rows_ref, jnp.zeros((4, LANES), f32), weights, scratch
    )
    out_ref[...] = stream
    normed_ref[...] = (norm_columns(stream) * gains[:, 2:3]).astype(bf16).T


def last_layer_kernel(first_ref, even_ref, own_ref, odd_ref, stream_ref, rows_ref, *refs):
    weights, (positions_ref, noise_ref, force_ref, w_head_ref) = refs[:6], refs[6:10]
    out_ref, scratch = refs[10], refs[11:]
    head_rows = jnp.concatenate([w_head_ref[...], jnp.zeros((1, LANES), f32)], axis=0)
    stream, columns = layer_values(
        1, first_ref, (even_ref, own_ref, odd_ref), stream_ref, rows_ref, head_rows, weights, scratch
    )
    final = norm_columns(stream)
    update = jnp.concatenate(
        [jnp.sum(columns[:, 4 + comp : 5 + comp] * final, axis=0, keepdims=True) for comp in range(3)]
        + [jnp.zeros((5, ROWS), f32)],
        axis=0,
    )
    level, spread_sq, c_input = rows_ref[0:1], rows_ref[1:2], rows_ref[2:3]
    positions = jnp.concatenate([positions_ref[...], jnp.zeros((5, ROWS), f32)], axis=0)
    fresh = jnp.concatenate([noise_ref[...], jnp.zeros((5, ROWS), f32)], axis=0)
    denoised = positions * (1.0 / spread_sq) + (level * c_input) * update
    following = 0.85 * level
    result = denoised + STEER * force_ref[...] + following * (0.8 * (positions - denoised) / level + 0.6 * fresh)
    out_ref[...] = result[:3]


def body(
    positions,
    fresh_noise,
    timestep,
    atom_single,
    pos_weight,
    ln_gain,
    w_query,
    w_key,
    w_value,
    w_out,
    w_gate_up,
    w_down,
    w_head,
    key_window,
    block_pairs,
    pair_count,
    bond_atoms,
):
    devices = lax.axis_size("atom")
    first = lax.axis_index("atom").astype(jnp.int32).reshape(1)
    smem = pl.BlockSpec(memory_space=pltpu.SMEM)
    vmem = pl.BlockSpec(memory_space=pltpu.VMEM)
    hbm = pl.BlockSpec(memory_space=pltpu.HBM)
    rows = atom_single.shape[0]
    line_size = 8
    line_count = devices // line_size

    def from_neighbours(array):
        even = [(i, i ^ 1) for i in range(devices)]
        odd = [(i, ((i + 1) ^ 1) - 1) for i in range(1, devices - 1)]
        return lax.ppermute(array, "atom", even), lax.ppermute(array, "atom", odd)

    stream, normed, schedule, tile = pl.pallas_call(
        prepare_kernel,
        out_shape=(
            jax.ShapeDtypeStruct((LANES, rows), f32),
            jax.ShapeDtypeStruct((rows, LANES), bf16),
            jax.ShapeDtypeStruct((8, rows), f32),
            jax.ShapeDtypeStruct((8, LANES), f32),
        ),
        in_specs=[smem] + [hbm] * 7,
        out_specs=(vmem,) * 4,
        scratch_shapes=[
            pltpu.SMEM(timestep.shape, jnp.int32),
            pltpu.VMEM(positions.shape, f32),
            pltpu.VMEM(atom_single.shape, bf16),
            pltpu.VMEM(pos_weight.shape, f32),
            pltpu.VMEM(ln_gain.shape, f32),
            pltpu.VMEM(block_pairs.shape, jnp.int32),
            pltpu.VMEM(key_window.shape, jnp.int32),
            pltpu.SemaphoreType.DMA((7,)),
        ],
        compiler_params=pltpu.CompilerParams(vmem_limit_bytes=VMEM_GRANT),
    )(first, timestep, positions, atom_single, pos_weight, ln_gain, block_pairs, key_window)
    even, odd = from_neighbours(normed)

    packed = pl.pallas_call(
        pack_kernel,
        out_shape=jax.ShapeDtypeStruct((line_size, 8, LANES), f32),
        in_specs=[smem, vmem],
        out_specs=vmem,
        cost_estimate=pl.CostEstimate(flops=40_000_000, bytes_accessed=10_000_000, transcendentals=1_000_000),
        compiler_params=pltpu.CompilerParams(vmem_limit_bytes=VMEM_SMALL),
    )(pair_count, tile)
    lines = [[x * line_size + z for z in range(line_size)] for x in range(line_count)]
    line = lax.all_to_all(packed, "atom", 0, 0, axis_index_groups=lines)

    weights = (w_query, w_key, w_value, w_out, w_gate_up, w_down)
    layer_scratch = [
        pltpu.VMEM((3 * rows, LANES), bf16),
        pltpu.VMEM((3 * rows, 2 * LANES), bf16),
        pltpu.VMEM((HEADS * 48, 3 * rows), bf16),
        pltpu.VMEM((LANES, rows), bf16),
    ]
    layer_cost = pl.CostEstimate(flops=2_000_000_000, bytes_accessed=20_000_000, transcendentals=2_000_000)
    stream, normed = pl.pallas_call(
        first_layer_kernel,
        out_shape=(
            jax.ShapeDtypeStruct((LANES, rows), f32),
            jax.ShapeDtypeStruct((rows, LANES), bf16),
        ),
        in_specs=[smem] + [vmem] * 11,
        out_specs=(vmem, vmem),
        scratch_shapes=layer_scratch,
        cost_estimate=layer_cost,
        compiler_params=pltpu.CompilerParams(vmem_limit_bytes=VMEM_SMALL),
    )(first, even, normed, odd, stream, schedule, *weights)
    even, odd = from_neighbours(normed)

    spread = pl.pallas_call(
        spread_kernel,
        out_shape=jax.ShapeDtypeStruct((line_count,) + line.shape, f32),
        in_specs=[vmem, pl.BlockSpec(memory_space=pl.ANY)],
        out_specs=vmem,
        compiler_params=pltpu.CompilerParams(vmem_limit_bytes=VMEM_SMALL),
    )(line, normed)
    columns = [[x * line_size + z for x in range(line_count)] for z in range(line_size)]
    tiles = lax.all_to_all(spread, "atom", 0, 0, axis_index_groups=columns).reshape(devices, 8, LANES)

    force = pl.pallas_call(
        force_kernel,
        out_shape=jax.ShapeDtypeStruct((8, 2 * LANES), f32),
        in_specs=[smem, vmem, vmem, vmem],
        out_specs=vmem,
        scratch_shapes=[
            pltpu.VMEM((6, LANES, LANES), f32),
            pltpu.VMEM((6, LANES, LANES), f32),
            pltpu.VMEM((8, LANES), jnp.int32),
            pltpu.VMEM((8, LANES), f32),
            pltpu.SMEM((8, LANES), jnp.int32),
            pltpu.SMEM((8, LANES), f32),
            pltpu.SemaphoreType.DMA((2,)),
        ],
        cost_estimate=pl.CostEstimate(flops=80_000_000, bytes_accessed=16_000_000, transcendentals=2_000_000),
        compiler_params=pltpu.CompilerParams(vmem_limit_bytes=VMEM_SMALL),
    )(first, tiles, positions, bond_atoms)

    return pl.pallas_call(
        last_layer_kernel,
        out_shape=jax.ShapeDtypeStruct(positions.shape, f32),
        in_specs=[smem] + [vmem] * 15,
        out_specs=vmem,
        scratch_shapes=layer_scratch,
        cost_estimate=layer_cost,
        compiler_params=pltpu.CompilerParams(vmem_limit_bytes=VMEM_SMALL),
    )(
        first,
        even,
        normed,
        odd,
        stream,
        schedule,
        *weights,
        positions,
        fresh_noise,
        force,
        w_head,
    )


def solution(mesh):
    in_specs = (
        P(None, ("sample", "atom")),
        P(None, ("sample", "atom")),
        P(),
        P("atom", None),
        P(),
        P(),
        P(),
        P(),
        P(),
        P(),
        P(),
        P(),
        P(),
        P("atom", None),
        P(None, "atom"),
        P("atom"),
        P(None, "atom", None),
    )
    out_specs = P(None, ("sample", "atom"))
    return jax.shard_map(body, mesh=mesh, in_specs=in_specs, out_specs=out_specs, check_vma=False)
```

```python
import functools
import math

import jax
import jax.numpy as jnp
from jax import lax
from jax.experimental import pallas as pl
from jax.experimental.pallas import tpu as pltpu
from jax.sharding import PartitionSpec as P

HEADS = 4
LANES = 128
ROWS = 256
VMEM_GRANT = 60 * 1024 * 1024
VMEM_SMALL = 16 * 1024 * 1024
NORM_EPS = 1e-05
STEER = 0.3
ABSENT = -(2.0**120)
LOG2E = 1.4426950408889634
KAPPA = 2.0 * math.sqrt(LOG2E)

f32 = jnp.float32
bf16 = jnp.bfloat16


def pack_kernel(count_ref, tile_ref, normed_ref, out_ref, copy_ref):
    copy_ref[...] = normed_ref[...]
    shape = tile_ref.shape
    row = lax.broadcasted_iota(jnp.int32, shape, 0)
    lane = lax.broadcasted_iota(jnp.int32, shape, 1)
    dead = (row == 6) & (lane % 64 >= count_ref[0])
    out_ref[...] = jnp.broadcast_to(jnp.where(dead, -1.0, tile_ref[...])[None], out_ref.shape)


def split3(values):
    high = values.astype(bf16)
    rest = values - high.astype(f32)
    mid = rest.astype(bf16)
    low = (rest - mid.astype(f32)).astype(bf16)
    return jnp.concatenate([high, mid, low], axis=0)


def join3(values):
    rows = values.shape[0] // 3
    return values[:rows] + values[rows : 2 * rows] + values[2 * rows :]


def norm_columns(values):
    center = values - jnp.mean(values, axis=0, keepdims=True)
    spread = jnp.mean(center * center, axis=0, keepdims=True)
    return center * lax.rsqrt(spread + NORM_EPS)


def dot_t(left, right):
    return lax.dot_general(left, right, (((0,), (0,)), ((), ())), preferred_element_type=f32)


def dot_nt(left, right):
    return lax.dot_general(left, right, (((1,), (1,)), ((), ())), preferred_element_type=f32)


def dot(left, right):
    return jnp.dot(left, right, preferred_element_type=f32)


def force_kernel(first_ref, tiles_ref, positions_ref, bonds_ref, out_ref, spread_own, push, list_v, bias_v, list_s, bias_s, sems):
    me = first_ref[0]

    codes = tiles_ref[:, 6, :].astype(jnp.int32)
    half = lax.broadcasted_iota(jnp.int32, codes.shape, 1) // 64
    mine = me * 2 + half
    first = jnp.where(codes < 0, -1, codes // 64)
    second = jnp.where(codes < 0, -1, codes % 64)
    partner = jnp.where(first == mine, second, jnp.where(second == mine, first, -1)).astype(f32)
    block_id = lax.broadcasted_iota(jnp.int32, (64, LANES), 0).astype(f32)
    hits = jnp.zeros((64, LANES), f32)
    for row in range(codes.shape[0]):
        hits = hits + jnp.where(partner[row : row + 1] == block_id, 1.0, 0.0)
    row_half = lax.broadcasted_iota(jnp.int32, (LANES, LANES), 0) // 64
    col_half = lax.broadcasted_iota(jnp.int32, (LANES, LANES), 1) // 64
    count = dot(hits.astype(bf16), (row_half == col_half).astype(bf16))
    present = count > 0.5
    lower = lax.broadcasted_iota(jnp.int32, (64, 64), 1) < lax.broadcasted_iota(jnp.int32, (64, 64), 0)
    rank = dot(lower.astype(bf16), present.astype(bf16))
    slot = (lax.broadcasted_iota(jnp.int32, (64, LANES), 1) % 64).astype(f32)
    chosen = present & (rank == slot)
    listed = jnp.sum(jnp.where(chosen, block_id, 0.0), axis=0, keepdims=True)
    times = jnp.sum(jnp.where(chosen, count, 0.0), axis=0, keepdims=True)
    total = jnp.sum(present.astype(f32), axis=0, keepdims=True)
    list_v[0:1, :] = listed.astype(jnp.int32)
    list_v[1:2, :] = total.astype(jnp.int32)
    bias_v[0:1, :] = jnp.where(times > 0.5, jnp.log2(jnp.maximum(times, 1.0)), ABSENT)
    list_copy = pltpu.make_async_copy(list_v, list_s, sems.at[0])
    bias_copy = pltpu.make_async_copy(bias_v, bias_s, sems.at[1])
    list_copy.start()
    bias_copy.start()

    for block in range(2):
        for comp in range(3):
            row = positions_ref[comp : comp + 1, block * LANES : (block + 1) * LANES] * KAPPA
            spread_own[3 * block + comp] = jnp.broadcast_to(row, (LANES, LANES)).T
            push[3 * block + comp] = jnp.zeros((LANES, LANES), f32)

    positions = jnp.concatenate([positions_ref[...], jnp.zeros((5, 2 * LANES), f32)], axis=0)

    forces = []
    atom_id = lax.broadcasted_iota(jnp.int32, (LANES, LANES), 0)
    for block in range(2):
        incidence = (
            (atom_id == bonds_ref[0, block : block + 1, :]).astype(f32)
            - (atom_id == bonds_ref[1, block : block + 1, :]).astype(f32)
        ).astype(bf16)
        offset = join3(dot(split3(positions[:, block * LANES : (block + 1) * LANES]), incidence))
        stretch = jnp.sum(offset * offset, axis=0, keepdims=True) - 1.0
        pull = (-0.2 * stretch) * offset
        forces.append(join3(dot_nt(split3(pull), incidence)))

    list_copy.wait()
    bias_copy.wait()
    for block in range(2):

        def one_pair(index, carry, block=block):
            partners = []
            for sub in range(2):
                entry = block * 64 + 2 * index + sub
                partner = list_s[0, entry]
                device = partner // 2
                within = partner % 2
                rows = [
                    tiles_ref[device, pl.ds(2 * comp + within, 1), :] * KAPPA for comp in range(3)
                ]
                partners.append((rows, bias_s[0, entry]))
            for group in range(0, LANES, 8):
                own = [spread_own[3 * block + comp, group : group + 8, :] for comp in range(3)]
                sums = [push[3 * block + comp, group : group + 8, :] for comp in range(3)]
                for rows, bias in partners:
                    offset = [own[comp] - rows[comp] for comp in range(3)]
                    power = bias - offset[0] * offset[0]
                    power = power - offset[1] * offset[1]
                    power = power - offset[2] * offset[2]
                    weight = jnp.exp2(power)
                    sums = [sums[comp] + weight * offset[comp] for comp in range(3)]
                for comp in range(3):
                    push[3 * block + comp, group : group + 8, :] = sums[comp]
            return carry

        lax.fori_loop(0, (list_s[1, block * 64] + 1) // 2, one_pair, 0)
        rows = [jnp.sum(push[3 * block + comp].T, axis=0, keepdims=True) for comp in range(3)]
        clash = jnp.concatenate(rows + [jnp.zeros((5, LANES), f32)], axis=0)
        forces[block] = forces[block] + clash * (8.0 / KAPPA)
    out_ref[...] = jnp.concatenate(forces, axis=1)


def start_copies(sources, targets, sems):
    copies = [
        pltpu.make_async_copy(source, target, sems.at[index])
        for index, (source, target) in enumerate(zip(sources, targets))
    ]
    for copy in copies:
        copy.start()
    return copies


def prepare_kernel(*refs):
    first_ref, sources, (stream_ref, normed_ref, rows_ref, tile_ref) = refs[0], refs[1:8], refs[8:12]
    targets, sems = refs[12:19], refs[19]
    time_ref, positions_ref, single_ref, pos_weight_ref, gain_ref, pairs_ref, window_ref = targets
    for copy in start_copies(sources, targets, sems):
        copy.wait()
    level = 0.2 + 0.02 * jnp.full((1, ROWS), time_ref[0], jnp.int32).astype(f32)
    spread_sq = level * level + 1.0
    c_input = 1.0 / jnp.sqrt(spread_sq)
    window = window_ref[...]
    own = first_ref[0] * 2 + lax.broadcasted_iota(jnp.int32, window.shape, 0)
    lane = lax.broadcasted_iota(jnp.int32, (1, ROWS), 1)
    counts = jnp.zeros((1, ROWS), f32)
    for offset in range(5):
        hit = jnp.sum((window == own + (offset - 2)).astype(f32), axis=1, keepdims=True)
        counts = jnp.where(lane == offset, hit[0:1], counts)
        counts = jnp.where(lane == 8 + offset, hit[1:2], counts)
    counts = jnp.where(counts > 0.0, jnp.log2(jnp.maximum(counts, 1.0)), ABSENT)
    gain_rows = [
        jnp.concatenate([gain_ref[layer, 0:1], gain_ref[layer, 1:2]], axis=1) for layer in range(2)
    ]
    rows_ref[...] = jnp.concatenate(
        [level, spread_sq, c_input] + gain_rows + [counts, jnp.zeros((2, ROWS), f32)], axis=0
    )
    for row in range(6):
        part = slice((row % 2) * LANES, (row % 2 + 1) * LANES)
        tile_ref[row : row + 1, :] = positions_ref[row // 2 : row // 2 + 1, part]
    pairs = pairs_ref[...]
    codes = (pairs[0:1] * 64 + pairs[1:2]).astype(f32)
    tile_ref[6:7, :] = jnp.concatenate([codes, codes], axis=1)
    tile_ref[7:8, :] = jnp.zeros((1, LANES), f32)
    columns = jnp.concatenate(
        [pos_weight_ref[...], gain_ref[0, 0:1], jnp.zeros((4, LANES), f32)], axis=0
    ).T
    identity = (
        lax.broadcasted_iota(jnp.int32, (LANES, LANES), 0)
        == lax.broadcasted_iota(jnp.int32, (LANES, LANES), 1)
    ).astype(f32).astype(bf16)
    stream = dot_nt(identity, single_ref[...])
    for comp in range(3):
        stream = stream + columns[:, comp : comp + 1] * (positions_ref[comp : comp + 1, :] * c_input)
    stream_ref[...] = stream
    normed_ref[...] = (norm_columns(stream) * columns[:, 3:4]).astype(bf16).T


def layer_values(layer, first_ref, halo, stream_ref, rows_ref, head_rows, weights, scratch):
    even_ref, own_ref, odd_ref = halo
    w_query_ref, w_key_ref, w_value_ref, w_out_ref, w_gate_up_ref, w_down_ref = weights
    near, keys, values, attended = scratch
    head_size = LANES // HEADS
    query_scale = LOG2E * head_size ** -0.5
    near[ROWS : 2 * ROWS, :] = own_ref[...]

    @pl.when(first_ref[0] % 2 == 0)
    def _():
        near[:ROWS, :] = odd_ref[...]
        near[2 * ROWS :, :] = even_ref[...]

    @pl.when(first_ref[0] % 2 == 1)
    def _():
        near[:ROWS, :] = even_ref[...]
        near[2 * ROWS :, :] = odd_ref[...]

    row_block = lax.broadcasted_iota(jnp.int32, (3 * ROWS, LANES), 0) // LANES
    lane = lax.broadcasted_iota(jnp.int32, (3 * ROWS, LANES), 1)
    keys[:, LANES:] = jnp.where((lane % 16 == row_block) & (lane < 32), 1.0, 0.0).astype(bf16)
    window = rows_ref[5:6, :LANES]
    rows = []
    for chunk in range(6):
        sides = []
        for block in range(2):
            offset = chunk - block
            if 0 <= offset < 5:
                lane_id = block * 8 + offset
                sides.append(jnp.broadcast_to(window[:, lane_id : lane_id + 1], (1, LANES)))
            else:
                sides.append(jnp.full((1, LANES), ABSENT, f32))
        rows.append(jnp.concatenate(sides, axis=1))
    rows = jnp.concatenate(rows + [jnp.zeros((10, ROWS), f32)], axis=0)
    high = rows.astype(bf16)
    low = (rows - high.astype(f32)).astype(bf16)
    bias = jnp.concatenate([high, low, jnp.zeros((LANES - 32, ROWS), bf16)], axis=0)

    keys[:, :LANES] = dot(near[...], w_key_ref[layer]).astype(bf16)
    query_t = (dot_nt(w_query_ref[layer].T, own_ref[...]) * query_scale).astype(bf16)
    value_t = dot_nt(w_value_ref[layer].T, near[...]).astype(bf16)
    for head in range(HEADS):
        values[head * 48 : head * 48 + 32, :] = value_t[head * 32 : head * 32 + 32]
        values[head * 48 + 32 : head * 48 + 48, :] = jnp.ones((16, 3 * ROWS), bf16)

    def attend(exact):
        pieces = []
        sums = []

        def scores_of(head):
            parts = []
            if head:
                parts.append(jnp.zeros((head * head_size, ROWS), bf16))
            parts.append(query_t[head * head_size : (head + 1) * head_size])
            if head < HEADS - 1:
                parts.append(jnp.zeros(((HEADS - 1 - head) * head_size, ROWS), bf16))
            return dot(keys[...], jnp.concatenate(parts + [bias], axis=0))

        following = scores_of(0)
        for head in range(HEADS):
            scores = following
            if head < HEADS - 1:
                following = scores_of(head + 1)
            if exact:
                scores = scores - jnp.max(scores, axis=0, keepdims=True)
            blank = jnp.zeros((LANES, LANES), bf16)
            weights_t = jnp.concatenate(
                [
                    jnp.concatenate([jnp.exp2(scores[: 5 * LANES, :LANES]).astype(bf16), blank], axis=0),
                    jnp.concatenate([blank, jnp.exp2(scores[LANES:, LANES:]).astype(bf16)], axis=0),
                ],
                axis=1,
            )
            mixed = dot(values[head * 48 : (head + 1) * 48, :], weights_t)
            total = mixed[head_size : head_size + 1]
            sums.append(total)
            pieces.append(mixed[:head_size] * (1.0 / total))
        attended[...] = jnp.concatenate(pieces, axis=0).astype(bf16)
        return jnp.concatenate(sums, axis=0)

    sums = attend(False)
    safe = (jnp.min(sums) > 2.0**-80) & (jnp.max(sums) < 2.0**100)

    @pl.when(jnp.logical_not(safe))
    def _():
        attend(True)

    gains = jnp.concatenate(
        [rows_ref[3 + index // 2 : 4 + index // 2, (index % 2) * LANES : (index % 2 + 1) * LANES] for index in range(4)]
        + [head_rows],
        axis=0,
    ).T
    now = stream_ref[...] + dot(w_out_ref[layer].T, attended[...])
    normed = (norm_columns(now) * gains[:, 2 * layer + 1 : 2 * layer + 2]).astype(bf16)
    gate_up = dot(w_gate_up_ref[layer].T, normed)
    width = gate_up.shape[0] // 2
    half, up = 0.5 * gate_up[:width], gate_up[width:]
    hidden = ((half + half * jnp.tanh(half)) * up).astype(bf16)
    return now + dot(w_down_ref[layer].T, hidden), gains


def first_layer_kernel(first_ref, even_ref, own_ref, odd_ref, stream_ref, rows_ref, *refs):
    weights, (out_ref, normed_ref), scratch = refs[:6], refs[6:8], refs[8:]
    stream, gains = layer_values(
        0, first_ref, (even_ref, own_ref, odd_ref), stream_ref, rows_ref, jnp.zeros((4, LANES), f32), weights, scratch
    )
    out_ref[...] = stream
    normed_ref[...] = (norm_columns(stream) * gains[:, 2:3]).astype(bf16).T


def last_layer_kernel(first_ref, even_ref, own_ref, odd_ref, stream_ref, rows_ref, *refs):
    weights, (positions_ref, noise_ref, force_ref, w_head_ref) = refs[:6], refs[6:10]
    out_ref, scratch = refs[10], refs[11:]
    head_rows = jnp.concatenate([w_head_ref[...], jnp.zeros((1, LANES), f32)], axis=0)
    stream, columns = layer_values(
        1, first_ref, (even_ref, own_ref, odd_ref), stream_ref, rows_ref, head_rows, weights, scratch
    )
    final = norm_columns(stream)
    update = jnp.concatenate(
        [jnp.sum(columns[:, 4 + comp : 5 + comp] * final, axis=0, keepdims=True) for comp in range(3)]
        + [jnp.zeros((5, ROWS), f32)],
        axis=0,
    )
    level, spread_sq, c_input = rows_ref[0:1], rows_ref[1:2], rows_ref[2:3]
    positions = jnp.concatenate([positions_ref[...], jnp.zeros((5, ROWS), f32)], axis=0)
    fresh = jnp.concatenate([noise_ref[...], jnp.zeros((5, ROWS), f32)], axis=0)
    denoised = positions * (1.0 / spread_sq) + (level * c_input) * update
    following = 0.85 * level
    result = denoised + STEER * force_ref[...] + following * (0.8 * (positions - denoised) / level + 0.6 * fresh)
    out_ref[...] = result[:3]


def body(
    positions,
    fresh_noise,
    timestep,
    atom_single,
    pos_weight,
    ln_gain,
    w_query,
    w_key,
    w_value,
    w_out,
    w_gate_up,
    w_down,
    w_head,
    key_window,
    block_pairs,
    pair_count,
    bond_atoms,
):
    devices = lax.axis_size("atom")
    first = lax.axis_index("atom").astype(jnp.int32).reshape(1)
    smem = pl.BlockSpec(memory_space=pltpu.SMEM)
    vmem = pl.BlockSpec(memory_space=pltpu.VMEM)
    hbm = pl.BlockSpec(memory_space=pltpu.HBM)
    rows = atom_single.shape[0]

    even_pairs = [(i, i ^ 1) for i in range(devices)]
    odd_pairs = [(i, ((i + 1) ^ 1) - 1) for i in range(1, devices - 1)]

    stream, normed, schedule, tile = pl.pallas_call(
        prepare_kernel,
        out_shape=(
            jax.ShapeDtypeStruct((LANES, rows), f32),
            jax.ShapeDtypeStruct((rows, LANES), bf16),
            jax.ShapeDtypeStruct((8, rows), f32),
            jax.ShapeDtypeStruct((8, LANES), f32),
        ),
        in_specs=[smem] + [hbm] * 7,
        out_specs=(vmem,) * 4,
        scratch_shapes=[
            pltpu.SMEM(timestep.shape, jnp.int32),
            pltpu.VMEM(positions.shape, f32),
            pltpu.VMEM(atom_single.shape, bf16),
            pltpu.VMEM(pos_weight.shape, f32),
            pltpu.VMEM(ln_gain.shape, f32),
            pltpu.VMEM(block_pairs.shape, jnp.int32),
            pltpu.VMEM(key_window.shape, jnp.int32),
            pltpu.SemaphoreType.DMA((7,)),
        ],
        compiler_params=pltpu.CompilerParams(vmem_limit_bytes=VMEM_GRANT),
    )(first, timestep, positions, atom_single, pos_weight, ln_gain, block_pairs, key_window)
    even = lax.ppermute(normed, "atom", even_pairs)

    packed, normed = pl.pallas_call(
        pack_kernel,
        out_shape=(
            jax.ShapeDtypeStruct((devices, 8, LANES), f32),
            jax.ShapeDtypeStruct(normed.shape, bf16),
        ),
        in_specs=[smem, vmem, vmem],
        out_specs=(vmem, vmem),
        cost_estimate=pl.CostEstimate(flops=40_000_000, bytes_accessed=10_000_000, transcendentals=1_000_000),
        compiler_params=pltpu.CompilerParams(vmem_limit_bytes=VMEM_SMALL),
    )(pair_count, tile, normed)
    tiles = lax.all_to_all(packed, "atom", 0, 0)
    odd = lax.ppermute(normed, "atom", odd_pairs)

    weights = (w_query, w_key, w_value, w_out, w_gate_up, w_down)
    layer_scratch = [
        pltpu.VMEM((3 * rows, LANES), bf16),
        pltpu.VMEM((3 * rows, 2 * LANES), bf16),
        pltpu.VMEM((HEADS * 48, 3 * rows), bf16),
        pltpu.VMEM((LANES, rows), bf16),
    ]
    layer_cost = pl.CostEstimate(flops=2_000_000_000, bytes_accessed=20_000_000, transcendentals=2_000_000)
    stream, normed = pl.pallas_call(
        first_layer_kernel,
        out_shape=(
            jax.ShapeDtypeStruct((LANES, rows), f32),
            jax.ShapeDtypeStruct((rows, LANES), bf16),
        ),
        in_specs=[smem] + [vmem] * 11,
        out_specs=(vmem, vmem),
        scratch_shapes=layer_scratch,
        cost_estimate=layer_cost,
        compiler_params=pltpu.CompilerParams(vmem_limit_bytes=VMEM_SMALL),
    )(first, even, normed, odd, stream, schedule, *weights)
    even = lax.ppermute(normed, "atom", even_pairs)
    odd = lax.ppermute(normed, "atom", odd_pairs)

    force = pl.pallas_call(
        force_kernel,
        out_shape=jax.ShapeDtypeStruct((8, 2 * LANES), f32),
        in_specs=[smem, vmem, vmem, vmem],
        out_specs=vmem,
        scratch_shapes=[
            pltpu.VMEM((6, LANES, LANES), f32),
            pltpu.VMEM((6, LANES, LANES), f32),
            pltpu.VMEM((8, LANES), jnp.int32),
            pltpu.VMEM((8, LANES), f32),
            pltpu.SMEM((8, LANES), jnp.int32),
            pltpu.SMEM((8, LANES), f32),
            pltpu.SemaphoreType.DMA((2,)),
        ],
        cost_estimate=pl.CostEstimate(flops=80_000_000, bytes_accessed=16_000_000, transcendentals=2_000_000),
        compiler_params=pltpu.CompilerParams(vmem_limit_bytes=VMEM_SMALL),
    )(first, tiles, positions, bond_atoms)

    return pl.pallas_call(
        last_layer_kernel,
        out_shape=jax.ShapeDtypeStruct(positions.shape, f32),
        in_specs=[smem] + [vmem] * 15,
        out_specs=vmem,
        scratch_shapes=layer_scratch,
        cost_estimate=layer_cost,
        compiler_params=pltpu.CompilerParams(vmem_limit_bytes=VMEM_SMALL),
    )(
        first,
        even,
        normed,
        odd,
        stream,
        schedule,
        *weights,
        positions,
        fresh_noise,
        force,
        w_head,
    )


def solution(mesh):
    in_specs = (
        P(None, ("sample", "atom")),
        P(None, ("sample", "atom")),
        P(),
        P("atom", None),
        P(),
        P(),
        P(),
        P(),
        P(),
        P(),
        P(),
        P(),
        P(),
        P("atom", None),
        P(None, "atom"),
        P("atom"),
        P(None, "atom", None),
    )
    out_specs = P(None, ("sample", "atom"))
    return jax.shard_map(body, mesh=mesh, in_specs=in_specs, out_specs=out_specs, check_vma=False)
```

```python
import functools
import math

import jax
import jax.numpy as jnp
from jax import lax
from jax.experimental import pallas as pl
from jax.experimental.pallas import tpu as pltpu
from jax.sharding import PartitionSpec as P

HEADS = 4
LANES = 128
ROWS = 256
VMEM_GRANT = 60 * 1024 * 1024
VMEM_SMALL = 16 * 1024 * 1024
NORM_EPS = 1e-05
STEER = 0.3
ABSENT = -(2.0**120)
LOG2E = 1.4426950408889634
KAPPA = 2.0 * math.sqrt(LOG2E)

f32 = jnp.float32
bf16 = jnp.bfloat16


def pack_kernel(count_ref, tile_ref, out_ref, token_ref):
    token_ref[...] = tile_ref[...]
    shape = tile_ref.shape
    row = lax.broadcasted_iota(jnp.int32, shape, 0)
    lane = lax.broadcasted_iota(jnp.int32, shape, 1)
    dead = (row == 6) & (lane % 64 >= count_ref[0])
    out_ref[...] = jnp.broadcast_to(jnp.where(dead, -1.0, tile_ref[...])[None], out_ref.shape)


def split3(values):
    high = values.astype(bf16)
    rest = values - high.astype(f32)
    mid = rest.astype(bf16)
    low = (rest - mid.astype(f32)).astype(bf16)
    return jnp.concatenate([high, mid, low], axis=0)


def join3(values):
    rows = values.shape[0] // 3
    return values[:rows] + values[rows : 2 * rows] + values[2 * rows :]


def norm_columns(values):
    center = values - jnp.mean(values, axis=0, keepdims=True)
    spread = jnp.mean(center * center, axis=0, keepdims=True)
    return center * lax.rsqrt(spread + NORM_EPS)


def dot_t(left, right):
    return lax.dot_general(left, right, (((0,), (0,)), ((), ())), preferred_element_type=f32)


def dot_nt(left, right):
    return lax.dot_general(left, right, (((1,), (1,)), ((), ())), preferred_element_type=f32)


def dot(left, right):
    return jnp.dot(left, right, preferred_element_type=f32)


def bond_kernel(positions_ref, bonds_ref, normed_ref, token_ref, out_ref, copy_ref):
    copy_ref[...] = normed_ref[...]
    positions = jnp.concatenate([positions_ref[...], jnp.zeros((5, 2 * LANES), f32)], axis=0)

    forces = []
    atom_id = lax.broadcasted_iota(jnp.int32, (LANES, LANES), 0)
    for block in range(2):
        incidence = (
            (atom_id == bonds_ref[0, block : block + 1, :]).astype(f32)
            - (atom_id == bonds_ref[1, block : block + 1, :]).astype(f32)
        ).astype(bf16)
        offset = join3(dot(split3(positions[:, block * LANES : (block + 1) * LANES]), incidence))
        stretch = jnp.sum(offset * offset, axis=0, keepdims=True) - 1.0
        pull = (-0.2 * stretch) * offset
        forces.append(join3(dot_nt(split3(pull), incidence)))
    out_ref[...] = jnp.concatenate(forces, axis=1)


def force_kernel(first_ref, tiles_ref, positions_ref, bond_ref, out_ref, spread_own, push, list_v, bias_v, list_s, bias_s, sems):
    me = first_ref[0]

    codes = tiles_ref[:, 6, :].astype(jnp.int32)
    half = lax.broadcasted_iota(jnp.int32, codes.shape, 1) // 64
    mine = me * 2 + half
    first = jnp.where(codes < 0, -1, codes // 64)
    second = jnp.where(codes < 0, -1, codes % 64)
    partner = jnp.where(first == mine, second, jnp.where(second == mine, first, -1)).astype(f32)
    block_id = lax.broadcasted_iota(jnp.int32, (64, LANES), 0).astype(f32)
    hits = jnp.zeros((64, LANES), f32)
    for row in range(codes.shape[0]):
        hits = hits + jnp.where(partner[row : row + 1] == block_id, 1.0, 0.0)
    row_half = lax.broadcasted_iota(jnp.int32, (LANES, LANES), 0) // 64
    col_half = lax.broadcasted_iota(jnp.int32, (LANES, LANES), 1) // 64
    count = dot(hits.astype(bf16), (row_half == col_half).astype(bf16))
    present = count > 0.5
    lower = lax.broadcasted_iota(jnp.int32, (64, 64), 1) < lax.broadcasted_iota(jnp.int32, (64, 64), 0)
    rank = dot(lower.astype(bf16), present.astype(bf16))
    slot = (lax.broadcasted_iota(jnp.int32, (64, LANES), 1) % 64).astype(f32)
    chosen = present & (rank == slot)
    listed = jnp.sum(jnp.where(chosen, block_id, 0.0), axis=0, keepdims=True)
    times = jnp.sum(jnp.where(chosen, count, 0.0), axis=0, keepdims=True)
    total = jnp.sum(present.astype(f32), axis=0, keepdims=True)
    list_v[0:1, :] = listed.astype(jnp.int32)
    list_v[1:2, :] = total.astype(jnp.int32)
    bias_v[0:1, :] = jnp.where(times > 0.5, jnp.log2(jnp.maximum(times, 1.0)), ABSENT)
    list_copy = pltpu.make_async_copy(list_v, list_s, sems.at[0])
    bias_copy = pltpu.make_async_copy(bias_v, bias_s, sems.at[1])
    list_copy.start()
    bias_copy.start()

    for block in range(2):
        for comp in range(3):
            row = positions_ref[comp : comp + 1, block * LANES : (block + 1) * LANES] * KAPPA
            spread_own[3 * block + comp] = jnp.broadcast_to(row, (LANES, LANES)).T
            push[3 * block + comp] = jnp.zeros((LANES, LANES), f32)

    forces = []
    list_copy.wait()
    bias_copy.wait()
    for block in range(2):

        def one_pair(index, carry, block=block):
            partners = []
            for sub in range(2):
                entry = block * 64 + 2 * index + sub
                partner = list_s[0, entry]
                device = partner // 2
                within = partner % 2
                rows = [
                    tiles_ref[device, pl.ds(2 * comp + within, 1), :] * KAPPA for comp in range(3)
                ]
                partners.append((rows, bias_s[0, entry]))
            for group in range(0, LANES, 8):
                own = [spread_own[3 * block + comp, group : group + 8, :] for comp in range(3)]
                sums = [push[3 * block + comp, group : group + 8, :] for comp in range(3)]
                for rows, bias in partners:
                    offset = [own[comp] - rows[comp] for comp in range(3)]
                    power = bias - offset[0] * offset[0]
                    power = power - offset[1] * offset[1]
                    power = power - offset[2] * offset[2]
                    weight = jnp.exp2(power)
                    sums = [sums[comp] + weight * offset[comp] for comp in range(3)]
                for comp in range(3):
                    push[3 * block + comp, group : group + 8, :] = sums[comp]
            return carry

        lax.fori_loop(0, (list_s[1, block * 64] + 1) // 2, one_pair, 0)
        rows = [jnp.sum(push[3 * block + comp].T, axis=0, keepdims=True) for comp in range(3)]
        clash = jnp.concatenate(rows + [jnp.zeros((5, LANES), f32)], axis=0)
        forces.append(clash * (8.0 / KAPPA))
    out_ref[...] = bond_ref[...] + jnp.concatenate(forces, axis=1)


def start_copies(sources, targets, sems):
    copies = [
        pltpu.make_async_copy(source, target, sems.at[index])
        for index, (source, target) in enumerate(zip(sources, targets))
    ]
    for copy in copies:
        copy.start()
    return copies


def prepare_kernel(*refs):
    first_ref, sources, (stream_ref, normed_ref, rows_ref, tile_ref) = refs[0], refs[1:8], refs[8:12]
    targets, sems = refs[12:19], refs[19]
    time_ref, positions_ref, single_ref, pos_weight_ref, gain_ref, pairs_ref, window_ref = targets
    for copy in start_copies(sources, targets, sems):
        copy.wait()
    level = 0.2 + 0.02 * jnp.full((1, ROWS), time_ref[0], jnp.int32).astype(f32)
    spread_sq = level * level + 1.0
    c_input = 1.0 / jnp.sqrt(spread_sq)
    window = window_ref[...]
    own = first_ref[0] * 2 + lax.broadcasted_iota(jnp.int32, window.shape, 0)
    lane = lax.broadcasted_iota(jnp.int32, (1, ROWS), 1)
    counts = jnp.zeros((1, ROWS), f32)
    for offset in range(5):
        hit = jnp.sum((window == own + (offset - 2)).astype(f32), axis=1, keepdims=True)
        counts = jnp.where(lane == offset, hit[0:1], counts)
        counts = jnp.where(lane == 8 + offset, hit[1:2], counts)
    counts = jnp.where(counts > 0.0, jnp.log2(jnp.maximum(counts, 1.0)), ABSENT)
    gain_rows = [
        jnp.concatenate([gain_ref[layer, 0:1], gain_ref[layer, 1:2]], axis=1) for layer in range(2)
    ]
    rows_ref[...] = jnp.concatenate(
        [level, spread_sq, c_input] + gain_rows + [counts, jnp.zeros((2, ROWS), f32)], axis=0
    )
    for row in range(6):
        part = slice((row % 2) * LANES, (row % 2 + 1) * LANES)
        tile_ref[row : row + 1, :] = positions_ref[row // 2 : row // 2 + 1, part]
    pairs = pairs_ref[...]
    codes = (pairs[0:1] * 64 + pairs[1:2]).astype(f32)
    tile_ref[6:7, :] = jnp.concatenate([codes, codes], axis=1)
    tile_ref[7:8, :] = jnp.zeros((1, LANES), f32)
    columns = jnp.concatenate(
        [pos_weight_ref[...], gain_ref[0, 0:1], jnp.zeros((4, LANES), f32)], axis=0
    ).T
    identity = (
        lax.broadcasted_iota(jnp.int32, (LANES, LANES), 0)
        == lax.broadcasted_iota(jnp.int32, (LANES, LANES), 1)
    ).astype(f32).astype(bf16)
    stream = dot_nt(identity, single_ref[...])
    for comp in range(3):
        stream = stream + columns[:, comp : comp + 1] * (positions_ref[comp : comp + 1, :] * c_input)
    stream_ref[...] = stream
    normed_ref[...] = (norm_columns(stream) * columns[:, 3:4]).astype(bf16).T


def layer_values(layer, first_ref, halo, stream_ref, rows_ref, head_rows, weights, scratch):
    even_ref, own_ref, odd_ref = halo
    w_query_ref, w_key_ref, w_value_ref, w_out_ref, w_gate_up_ref, w_down_ref = weights
    near, keys, values, attended = scratch
    head_size = LANES // HEADS
    query_scale = LOG2E * head_size ** -0.5
    near[ROWS : 2 * ROWS, :] = own_ref[...]

    @pl.when(first_ref[0] % 2 == 0)
    def _():
        near[:ROWS, :] = odd_ref[...]
        near[2 * ROWS :, :] = even_ref[...]

    @pl.when(first_ref[0] % 2 == 1)
    def _():
        near[:ROWS, :] = even_ref[...]
        near[2 * ROWS :, :] = odd_ref[...]

    row_block = lax.broadcasted_iota(jnp.int32, (3 * ROWS, LANES), 0) // LANES
    lane = lax.broadcasted_iota(jnp.int32, (3 * ROWS, LANES), 1)
    keys[:, LANES:] = jnp.where((lane % 16 == row_block) & (lane < 32), 1.0, 0.0).astype(bf16)
    window = rows_ref[5:6, :LANES]
    rows = []
    for chunk in range(6):
        sides = []
        for block in range(2):
            offset = chunk - block
            if 0 <= offset < 5:
                lane_id = block * 8 + offset
                sides.append(jnp.broadcast_to(window[:, lane_id : lane_id + 1], (1, LANES)))
            else:
                sides.append(jnp.full((1, LANES), ABSENT, f32))
        rows.append(jnp.concatenate(sides, axis=1))
    rows = jnp.concatenate(rows + [jnp.zeros((10, ROWS), f32)], axis=0)
    high = rows.astype(bf16)
    low = (rows - high.astype(f32)).astype(bf16)
    bias = jnp.concatenate([high, low, jnp.zeros((LANES - 32, ROWS), bf16)], axis=0)

    keys[:, :LANES] = dot(near[...], w_key_ref[layer]).astype(bf16)
    query_t = (dot_nt(w_query_ref[layer].T, own_ref[...]) * query_scale).astype(bf16)
    value_t = dot_nt(w_value_ref[layer].T, near[...]).astype(bf16)
    for head in range(HEADS):
        values[head * 48 : head * 48 + 32, :] = value_t[head * 32 : head * 32 + 32]
        values[head * 48 + 32 : head * 48 + 48, :] = jnp.ones((16, 3 * ROWS), bf16)

    def attend(exact):
        pieces = []
        sums = []

        def scores_of(head):
            parts = []
            if head:
                parts.append(jnp.zeros((head * head_size, ROWS), bf16))
            parts.append(query_t[head * head_size : (head + 1) * head_size])
            if head < HEADS - 1:
                parts.append(jnp.zeros(((HEADS - 1 - head) * head_size, ROWS), bf16))
            return dot(keys[...], jnp.concatenate(parts + [bias], axis=0))

        following = scores_of(0)
        for head in range(HEADS):
            scores = following
            if head < HEADS - 1:
                following = scores_of(head + 1)
            if exact:
                scores = scores - jnp.max(scores, axis=0, keepdims=True)
            blank = jnp.zeros((LANES, LANES), bf16)
            weights_t = jnp.concatenate(
                [
                    jnp.concatenate([jnp.exp2(scores[: 5 * LANES, :LANES]).astype(bf16), blank], axis=0),
                    jnp.concatenate([blank, jnp.exp2(scores[LANES:, LANES:]).astype(bf16)], axis=0),
                ],
                axis=1,
            )
            mixed = dot(values[head * 48 : (head + 1) * 48, :], weights_t)
            total = mixed[head_size : head_size + 1]
            sums.append(total)
            pieces.append(mixed[:head_size] * (1.0 / total))
        attended[...] = jnp.concatenate(pieces, axis=0).astype(bf16)
        return jnp.concatenate(sums, axis=0)

    sums = attend(False)
    safe = (jnp.min(sums) > 2.0**-80) & (jnp.max(sums) < 2.0**100)

    @pl.when(jnp.logical_not(safe))
    def _():
        attend(True)

    gains = jnp.concatenate(
        [rows_ref[3 + index // 2 : 4 + index // 2, (index % 2) * LANES : (index % 2 + 1) * LANES] for index in range(4)]
        + [head_rows],
        axis=0,
    ).T
    now = stream_ref[...] + dot(w_out_ref[layer].T, attended[...])
    normed = (norm_columns(now) * gains[:, 2 * layer + 1 : 2 * layer + 2]).astype(bf16)
    gate_up = dot(w_gate_up_ref[layer].T, normed)
    width = gate_up.shape[0] // 2
    half, up = 0.5 * gate_up[:width], gate_up[width:]
    hidden = ((half + half * jnp.tanh(half)) * up).astype(bf16)
    return now + dot(w_down_ref[layer].T, hidden), gains


def first_layer_kernel(first_ref, even_ref, own_ref, odd_ref, stream_ref, rows_ref, *refs):
    weights, (out_ref, normed_ref), scratch = refs[:6], refs[6:8], refs[8:]
    stream, gains = layer_values(
        0, first_ref, (even_ref, own_ref, odd_ref), stream_ref, rows_ref, jnp.zeros((4, LANES), f32), weights, scratch
    )
    out_ref[...] = stream
    normed_ref[...] = (norm_columns(stream) * gains[:, 2:3]).astype(bf16).T


def last_layer_kernel(first_ref, even_ref, own_ref, odd_ref, stream_ref, rows_ref, *refs):
    weights, (positions_ref, noise_ref, force_ref, w_head_ref) = refs[:6], refs[6:10]
    out_ref, scratch = refs[10], refs[11:]
    head_rows = jnp.concatenate([w_head_ref[...], jnp.zeros((1, LANES), f32)], axis=0)
    stream, columns = layer_values(
        1, first_ref, (even_ref, own_ref, odd_ref), stream_ref, rows_ref, head_rows, weights, scratch
    )
    final = norm_columns(stream)
    update = jnp.concatenate(
        [jnp.sum(columns[:, 4 + comp : 5 + comp] * final, axis=0, keepdims=True) for comp in range(3)]
        + [jnp.zeros((5, ROWS), f32)],
        axis=0,
    )
    level, spread_sq, c_input = rows_ref[0:1], rows_ref[1:2], rows_ref[2:3]
    positions = jnp.concatenate([positions_ref[...], jnp.zeros((5, ROWS), f32)], axis=0)
    fresh = jnp.concatenate([noise_ref[...], jnp.zeros((5, ROWS), f32)], axis=0)
    denoised = positions * (1.0 / spread_sq) + (level * c_input) * update
    following = 0.85 * level
    result = denoised + STEER * force_ref[...] + following * (0.8 * (positions - denoised) / level + 0.6 * fresh)
    out_ref[...] = result[:3]


def body(
    positions,
    fresh_noise,
    timestep,
    atom_single,
    pos_weight,
    ln_gain,
    w_query,
    w_key,
    w_value,
    w_out,
    w_gate_up,
    w_down,
    w_head,
    key_window,
    block_pairs,
    pair_count,
    bond_atoms,
):
    devices = lax.axis_size("atom")
    first = lax.axis_index("atom").astype(jnp.int32).reshape(1)
    smem = pl.BlockSpec(memory_space=pltpu.SMEM)
    vmem = pl.BlockSpec(memory_space=pltpu.VMEM)
    hbm = pl.BlockSpec(memory_space=pltpu.HBM)
    rows = atom_single.shape[0]

    even_pairs = [(i, i ^ 1) for i in range(devices)]
    odd_pairs = [(i, ((i + 1) ^ 1) - 1) for i in range(1, devices - 1)]

    stream, normed, schedule, tile = pl.pallas_call(
        prepare_kernel,
        out_shape=(
            jax.ShapeDtypeStruct((LANES, rows), f32),
            jax.ShapeDtypeStruct((rows, LANES), bf16),
            jax.ShapeDtypeStruct((8, rows), f32),
            jax.ShapeDtypeStruct((8, LANES), f32),
        ),
        in_specs=[smem] + [hbm] * 7,
        out_specs=(vmem,) * 4,
        scratch_shapes=[
            pltpu.SMEM(timestep.shape, jnp.int32),
            pltpu.VMEM(positions.shape, f32),
            pltpu.VMEM(atom_single.shape, bf16),
            pltpu.VMEM(pos_weight.shape, f32),
            pltpu.VMEM(ln_gain.shape, f32),
            pltpu.VMEM(block_pairs.shape, jnp.int32),
            pltpu.VMEM(key_window.shape, jnp.int32),
            pltpu.SemaphoreType.DMA((7,)),
        ],
        compiler_params=pltpu.CompilerParams(vmem_limit_bytes=VMEM_GRANT),
    )(first, timestep, positions, atom_single, pos_weight, ln_gain, block_pairs, key_window)
    even = lax.ppermute(normed, "atom", even_pairs)

    packed, token = pl.pallas_call(
        pack_kernel,
        out_shape=(
            jax.ShapeDtypeStruct((devices, 8, LANES), f32),
            jax.ShapeDtypeStruct((8, LANES), f32),
        ),
        in_specs=[smem, vmem],
        out_specs=(vmem, vmem),
        cost_estimate=pl.CostEstimate(flops=40_000_000, bytes_accessed=10_000_000, transcendentals=1_000_000),
        compiler_params=pltpu.CompilerParams(vmem_limit_bytes=VMEM_SMALL),
    )(pair_count, tile)
    tiles = lax.all_to_all(packed, "atom", 0, 0)
    bond_force, normed = pl.pallas_call(
        bond_kernel,
        out_shape=(
            jax.ShapeDtypeStruct((8, rows), f32),
            jax.ShapeDtypeStruct(normed.shape, bf16),
        ),
        in_specs=[vmem] * 4,
        out_specs=(vmem, vmem),
        cost_estimate=pl.CostEstimate(flops=80_000_000, bytes_accessed=20_000_000, transcendentals=0),
        compiler_params=pltpu.CompilerParams(vmem_limit_bytes=VMEM_SMALL),
    )(positions, bond_atoms, normed, token)
    odd = lax.ppermute(normed, "atom", odd_pairs)

    weights = (w_query, w_key, w_value, w_out, w_gate_up, w_down)
    layer_scratch = [
        pltpu.VMEM((3 * rows, LANES), bf16),
        pltpu.VMEM((3 * rows, 2 * LANES), bf16),
        pltpu.VMEM((HEADS * 48, 3 * rows), bf16),
        pltpu.VMEM((LANES, rows), bf16),
    ]
    layer_cost = pl.CostEstimate(flops=2_000_000_000, bytes_accessed=20_000_000, transcendentals=2_000_000)
    stream, normed = pl.pallas_call(
        first_layer_kernel,
        out_shape=(
            jax.ShapeDtypeStruct((LANES, rows), f32),
            jax.ShapeDtypeStruct((rows, LANES), bf16),
        ),
        in_specs=[smem] + [vmem] * 11,
        out_specs=(vmem, vmem),
        scratch_shapes=layer_scratch,
        cost_estimate=layer_cost,
        compiler_params=pltpu.CompilerParams(vmem_limit_bytes=VMEM_SMALL),
    )(first, even, normed, odd, stream, schedule, *weights)
    even = lax.ppermute(normed, "atom", even_pairs)
    odd = lax.ppermute(normed, "atom", odd_pairs)

    force = pl.pallas_call(
        force_kernel,
        out_shape=jax.ShapeDtypeStruct((8, 2 * LANES), f32),
        in_specs=[smem, vmem, vmem, vmem],
        out_specs=vmem,
        scratch_shapes=[
            pltpu.VMEM((6, LANES, LANES), f32),
            pltpu.VMEM((6, LANES, LANES), f32),
            pltpu.VMEM((8, LANES), jnp.int32),
            pltpu.VMEM((8, LANES), f32),
            pltpu.SMEM((8, LANES), jnp.int32),
            pltpu.SMEM((8, LANES), f32),
            pltpu.SemaphoreType.DMA((2,)),
        ],
        cost_estimate=pl.CostEstimate(flops=80_000_000, bytes_accessed=16_000_000, transcendentals=2_000_000),
        compiler_params=pltpu.CompilerParams(vmem_limit_bytes=VMEM_SMALL),
    )(first, tiles, positions, bond_force)

    return pl.pallas_call(
        last_layer_kernel,
        out_shape=jax.ShapeDtypeStruct(positions.shape, f32),
        in_specs=[smem] + [vmem] * 15,
        out_specs=vmem,
        scratch_shapes=layer_scratch,
        cost_estimate=layer_cost,
        compiler_params=pltpu.CompilerParams(vmem_limit_bytes=VMEM_SMALL),
    )(
        first,
        even,
        normed,
        odd,
        stream,
        schedule,
        *weights,
        positions,
        fresh_noise,
        force,
        w_head,
    )


def solution(mesh):
    in_specs = (
        P(None, ("sample", "atom")),
        P(None, ("sample", "atom")),
        P(),
        P("atom", None),
        P(),
        P(),
        P(),
        P(),
        P(),
        P(),
        P(),
        P(),
        P(),
        P("atom", None),
        P(None, "atom"),
        P("atom"),
        P(None, "atom", None),
    )
    out_specs = P(None, ("sample", "atom"))
    return jax.shard_map(body, mesh=mesh, in_specs=in_specs, out_specs=out_specs, check_vma=False)
```

```python
import functools
import math

import jax
import jax.numpy as jnp
from jax import lax
from jax.experimental import pallas as pl
from jax.experimental.pallas import tpu as pltpu
from jax.sharding import PartitionSpec as P

HEADS = 4
LANES = 128
ROWS = 256
VMEM_GRANT = 60 * 1024 * 1024
VMEM_SMALL = 16 * 1024 * 1024
NORM_EPS = 1e-05
STEER = 0.3
ABSENT = -(2.0**120)
LOG2E = 1.4426950408889634
KAPPA = 2.0 * math.sqrt(LOG2E)

f32 = jnp.float32
bf16 = jnp.bfloat16


def pack_kernel(count_ref, tile_ref, out_ref, token_ref):
    token_ref[...] = tile_ref[...]
    shape = tile_ref.shape
    row = lax.broadcasted_iota(jnp.int32, shape, 0)
    lane = lax.broadcasted_iota(jnp.int32, shape, 1)
    dead = (row == 6) & (lane % 64 >= count_ref[0])
    out_ref[...] = jnp.broadcast_to(jnp.where(dead, -1.0, tile_ref[...])[None], out_ref.shape)


def split3(values):
    high = values.astype(bf16)
    rest = values - high.astype(f32)
    mid = rest.astype(bf16)
    low = (rest - mid.astype(f32)).astype(bf16)
    return jnp.concatenate([high, mid, low], axis=0)


def join3(values):
    rows = values.shape[0] // 3
    return values[:rows] + values[rows : 2 * rows] + values[2 * rows :]


def norm_columns(values):
    center = values - jnp.mean(values, axis=0, keepdims=True)
    spread = jnp.mean(center * center, axis=0, keepdims=True)
    return center * lax.rsqrt(spread + NORM_EPS)


def dot_t(left, right):
    return lax.dot_general(left, right, (((0,), (0,)), ((), ())), preferred_element_type=f32)


def dot_nt(left, right):
    return lax.dot_general(left, right, (((1,), (1,)), ((), ())), preferred_element_type=f32)


def dot(left, right):
    return jnp.dot(left, right, preferred_element_type=f32)


def bond_kernel(positions_ref, bonds_ref, normed_ref, token_ref, out_ref, copy_ref):
    copy_ref[...] = normed_ref[...]
    positions = jnp.concatenate([positions_ref[...], jnp.zeros((5, 2 * LANES), f32)], axis=0)

    forces = []
    atom_id = lax.broadcasted_iota(jnp.int32, (LANES, LANES), 0)
    for block in range(2):
        incidence = (
            (atom_id == bonds_ref[0, block : block + 1, :]).astype(f32)
            - (atom_id == bonds_ref[1, block : block + 1, :]).astype(f32)
        ).astype(bf16)
        offset = join3(dot(split3(positions[:, block * LANES : (block + 1) * LANES]), incidence))
        stretch = jnp.sum(offset * offset, axis=0, keepdims=True) - 1.0
        pull = (-0.2 * stretch) * offset
        forces.append(join3(dot_nt(split3(pull), incidence)))
    out_ref[...] = jnp.concatenate(forces, axis=1)


def force_kernel(first_ref, tiles_ref, positions_ref, bond_ref, out_ref, spread_own, push, list_v, bias_v, list_s, bias_s, sems):
    me = first_ref[0]

    codes = tiles_ref[:, 6, :].astype(jnp.int32)
    half = lax.broadcasted_iota(jnp.int32, codes.shape, 1) // 64
    mine = me * 2 + half
    first = jnp.where(codes < 0, -1, codes // 64)
    second = jnp.where(codes < 0, -1, codes % 64)
    partner = jnp.where(first == mine, second, jnp.where(second == mine, first, -1)).astype(f32)
    block_id = lax.broadcasted_iota(jnp.int32, (64, LANES), 0).astype(f32)
    hits = jnp.zeros((64, LANES), f32)
    for row in range(codes.shape[0]):
        hits = hits + jnp.where(partner[row : row + 1] == block_id, 1.0, 0.0)
    row_half = lax.broadcasted_iota(jnp.int32, (LANES, LANES), 0) // 64
    col_half = lax.broadcasted_iota(jnp.int32, (LANES, LANES), 1) // 64
    count = dot(hits.astype(bf16), (row_half == col_half).astype(bf16))
    present = count > 0.5
    lower = lax.broadcasted_iota(jnp.int32, (64, 64), 1) < lax.broadcasted_iota(jnp.int32, (64, 64), 0)
    rank = dot(lower.astype(bf16), present.astype(bf16))
    slot = (lax.broadcasted_iota(jnp.int32, (64, LANES), 1) % 64).astype(f32)
    chosen = present & (rank == slot)
    listed = jnp.sum(jnp.where(chosen, block_id, 0.0), axis=0, keepdims=True)
    times = jnp.sum(jnp.where(chosen, count, 0.0), axis=0, keepdims=True)
    total = jnp.sum(present.astype(f32), axis=0, keepdims=True)
    list_v[0:1, :] = listed.astype(jnp.int32)
    list_v[1:2, :] = total.astype(jnp.int32)
    bias_v[0:1, :] = jnp.where(times > 0.5, jnp.log2(jnp.maximum(times, 1.0)), ABSENT)
    list_copy = pltpu.make_async_copy(list_v, list_s, sems.at[0])
    bias_copy = pltpu.make_async_copy(bias_v, bias_s, sems.at[1])
    list_copy.start()
    bias_copy.start()

    for block in range(2):
        for comp in range(3):
            row = positions_ref[comp : comp + 1, block * LANES : (block + 1) * LANES] * KAPPA
            spread_own[3 * block + comp] = jnp.broadcast_to(row, (LANES, LANES)).T
            push[3 * block + comp] = jnp.zeros((LANES, LANES), f32)

    forces = []
    list_copy.wait()
    bias_copy.wait()
    for block in range(2):

        def one_pair(index, carry, block=block):
            partners = []
            for sub in range(2):
                entry = block * 64 + 2 * index + sub
                partner = list_s[0, entry]
                device = partner // 2
                within = partner % 2
                rows = [
                    tiles_ref[device, pl.ds(2 * comp + within, 1), :] * KAPPA for comp in range(3)
                ]
                partners.append((rows, bias_s[0, entry]))
            for group in range(0, LANES, 8):
                own = [spread_own[3 * block + comp, group : group + 8, :] for comp in range(3)]
                sums = [push[3 * block + comp, group : group + 8, :] for comp in range(3)]
                for rows, bias in partners:
                    offset = [own[comp] - rows[comp] for comp in range(3)]
                    power = bias - offset[0] * offset[0]
                    power = power - offset[1] * offset[1]
                    power = power - offset[2] * offset[2]
                    weight = jnp.exp2(power)
                    sums = [sums[comp] + weight * offset[comp] for comp in range(3)]
                for comp in range(3):
                    push[3 * block + comp, group : group + 8, :] = sums[comp]
            return carry

        lax.fori_loop(0, (list_s[1, block * 64] + 1) // 2, one_pair, 0)
        rows = [jnp.sum(push[3 * block + comp].T, axis=0, keepdims=True) for comp in range(3)]
        clash = jnp.concatenate(rows + [jnp.zeros((5, LANES), f32)], axis=0)
        forces.append(clash * (8.0 / KAPPA))
    out_ref[...] = bond_ref[...] + jnp.concatenate(forces, axis=1)


def start_copies(sources, targets, sems):
    copies = [
        pltpu.make_async_copy(source, target, sems.at[index])
        for index, (source, target) in enumerate(zip(sources, targets))
    ]
    for copy in copies:
        copy.start()
    return copies


def prepare_kernel(*refs):
    first_ref, sources, (stream_ref, normed_ref, rows_ref, tile_ref) = refs[0], refs[1:8], refs[8:12]
    targets, sems = refs[12:19], refs[19]
    time_ref, positions_ref, single_ref, pos_weight_ref, gain_ref, pairs_ref, window_ref = targets
    for copy in start_copies(sources, targets, sems):
        copy.wait()
    level = 0.2 + 0.02 * jnp.full((1, ROWS), time_ref[0], jnp.int32).astype(f32)
    spread_sq = level * level + 1.0
    c_input = 1.0 / jnp.sqrt(spread_sq)
    window = window_ref[...]
    own = first_ref[0] * 2 + lax.broadcasted_iota(jnp.int32, window.shape, 0)
    lane = lax.broadcasted_iota(jnp.int32, (1, ROWS), 1)
    counts = jnp.zeros((1, ROWS), f32)
    for offset in range(5):
        hit = jnp.sum((window == own + (offset - 2)).astype(f32), axis=1, keepdims=True)
        counts = jnp.where(lane == offset, hit[0:1], counts)
        counts = jnp.where(lane == 8 + offset, hit[1:2], counts)
    counts = jnp.where(counts > 0.0, jnp.log2(jnp.maximum(counts, 1.0)), ABSENT)
    gain_rows = [
        jnp.concatenate([gain_ref[layer, 0:1], gain_ref[layer, 1:2]], axis=1) for layer in range(2)
    ]
    rows_ref[...] = jnp.concatenate(
        [level, spread_sq, c_input] + gain_rows + [counts, jnp.zeros((2, ROWS), f32)], axis=0
    )
    for row in range(6):
        part = slice((row % 2) * LANES, (row % 2 + 1) * LANES)
        tile_ref[row : row + 1, :] = positions_ref[row // 2 : row // 2 + 1, part]
    pairs = pairs_ref[...]
    codes = (pairs[0:1] * 64 + pairs[1:2]).astype(f32)
    tile_ref[6:7, :] = jnp.concatenate([codes, codes], axis=1)
    tile_ref[7:8, :] = jnp.zeros((1, LANES), f32)
    columns = jnp.concatenate(
        [pos_weight_ref[...], gain_ref[0, 0:1], jnp.zeros((4, LANES), f32)], axis=0
    ).T
    identity = (
        lax.broadcasted_iota(jnp.int32, (LANES, LANES), 0)
        == lax.broadcasted_iota(jnp.int32, (LANES, LANES), 1)
    ).astype(f32).astype(bf16)
    stream = dot_nt(identity, single_ref[...])
    for comp in range(3):
        stream = stream + columns[:, comp : comp + 1] * (positions_ref[comp : comp + 1, :] * c_input)
    stream_ref[...] = stream
    normed_ref[...] = (norm_columns(stream) * columns[:, 3:4]).astype(bf16).T


def layer_values(layer, first_ref, halo, stream_ref, rows_ref, head_rows, weights, scratch):
    even_ref, own_ref, odd_ref = halo
    w_query_ref, w_key_ref, w_value_ref, w_out_ref, w_gate_up_ref, w_down_ref = weights
    near, keys, values, attended = scratch
    head_size = LANES // HEADS
    query_scale = LOG2E * head_size ** -0.5
    near[ROWS : 2 * ROWS, :] = own_ref[...]

    @pl.when(first_ref[0] % 2 == 0)
    def _():
        near[:ROWS, :] = odd_ref[...]
        near[2 * ROWS :, :] = even_ref[...]

    @pl.when(first_ref[0] % 2 == 1)
    def _():
        near[:ROWS, :] = even_ref[...]
        near[2 * ROWS :, :] = odd_ref[...]

    row_block = lax.broadcasted_iota(jnp.int32, (3 * ROWS, LANES), 0) // LANES
    lane = lax.broadcasted_iota(jnp.int32, (3 * ROWS, LANES), 1)
    keys[:, LANES:] = jnp.where((lane % 16 == row_block) & (lane < 32), 1.0, 0.0).astype(bf16)
    window = rows_ref[5:6, :LANES]
    rows = []
    for chunk in range(6):
        sides = []
        for block in range(2):
            offset = chunk - block
            if 0 <= offset < 5:
                lane_id = block * 8 + offset
                sides.append(jnp.broadcast_to(window[:, lane_id : lane_id + 1], (1, LANES)))
            else:
                sides.append(jnp.full((1, LANES), ABSENT, f32))
        rows.append(jnp.concatenate(sides, axis=1))
    rows = jnp.concatenate(rows + [jnp.zeros((10, ROWS), f32)], axis=0)
    high = rows.astype(bf16)
    low = (rows - high.astype(f32)).astype(bf16)
    bias = jnp.concatenate([high, low, jnp.zeros((LANES - 32, ROWS), bf16)], axis=0)

    keys[:, :LANES] = dot(near[...], w_key_ref[layer]).astype(bf16)
    query_t = (dot_nt(w_query_ref[layer].T, own_ref[...]) * query_scale).astype(bf16)
    value_t = dot_nt(w_value_ref[layer].T, near[...]).astype(bf16)
    for head in range(HEADS):
        values[head * 48 : head * 48 + 32, :] = value_t[head * 32 : head * 32 + 32]
        values[head * 48 + 32 : head * 48 + 48, :] = jnp.ones((16, 3 * ROWS), bf16)

    def attend(exact):
        pieces = []
        sums = []

        def scores_of(head):
            parts = []
            if head:
                parts.append(jnp.zeros((head * head_size, ROWS), bf16))
            parts.append(query_t[head * head_size : (head + 1) * head_size])
            if head < HEADS - 1:
                parts.append(jnp.zeros(((HEADS - 1 - head) * head_size, ROWS), bf16))
            return dot(keys[...], jnp.concatenate(parts + [bias], axis=0))

        following = scores_of(0)
        for head in range(HEADS):
            scores = following
            if head < HEADS - 1:
                following = scores_of(head + 1)
            if exact:
                scores = scores - jnp.max(scores, axis=0, keepdims=True)
            blank = jnp.zeros((LANES, LANES), bf16)
            weights_t = jnp.concatenate(
                [
                    jnp.concatenate([jnp.exp2(scores[: 5 * LANES, :LANES]).astype(bf16), blank], axis=0),
                    jnp.concatenate([blank, jnp.exp2(scores[LANES:, LANES:]).astype(bf16)], axis=0),
                ],
                axis=1,
            )
            mixed = dot(values[head * 48 : (head + 1) * 48, :], weights_t)
            total = mixed[head_size : head_size + 1]
            sums.append(total)
            pieces.append(mixed[:head_size] * (1.0 / total))
        attended[...] = jnp.concatenate(pieces, axis=0).astype(bf16)
        return jnp.concatenate(sums, axis=0)

    sums = attend(False)
    safe = (jnp.min(sums) > 2.0**-80) & (jnp.max(sums) < 2.0**100)

    @pl.when(jnp.logical_not(safe))
    def _():
        attend(True)

    gains = jnp.concatenate(
        [rows_ref[3 + index // 2 : 4 + index // 2, (index % 2) * LANES : (index % 2 + 1) * LANES] for index in range(4)]
        + [head_rows],
        axis=0,
    ).T
    now = stream_ref[...] + dot(w_out_ref[layer].T, attended[...])
    normed = (norm_columns(now) * gains[:, 2 * layer + 1 : 2 * layer + 2]).astype(bf16)
    gate_up = dot(w_gate_up_ref[layer].T, normed)
    width = gate_up.shape[0] // 2
    half, up = 0.5 * gate_up[:width], gate_up[width:]
    hidden = ((half + half * jnp.tanh(half)) * up).astype(bf16)
    return now + dot(w_down_ref[layer].T, hidden), gains


def first_layer_kernel(first_ref, even_ref, own_ref, odd_ref, stream_ref, rows_ref, *refs):
    weights, (out_ref, normed_ref), scratch = refs[:6], refs[6:8], refs[8:]
    stream, gains = layer_values(
        0, first_ref, (even_ref, own_ref, odd_ref), stream_ref, rows_ref, jnp.zeros((4, LANES), f32), weights, scratch
    )
    out_ref[...] = stream
    normed_ref[...] = (norm_columns(stream) * gains[:, 2:3]).astype(bf16).T


def last_layer_kernel(first_ref, even_ref, own_ref, odd_ref, stream_ref, rows_ref, *refs):
    weights, (positions_ref, noise_ref, force_ref, w_head_ref) = refs[:6], refs[6:10]
    out_ref, scratch = refs[10], refs[11:]
    head_rows = jnp.concatenate([w_head_ref[...], jnp.zeros((1, LANES), f32)], axis=0)
    stream, columns = layer_values(
        1, first_ref, (even_ref, own_ref, odd_ref), stream_ref, rows_ref, head_rows, weights, scratch
    )
    final = norm_columns(stream)
    update = jnp.concatenate(
        [jnp.sum(columns[:, 4 + comp : 5 + comp] * final, axis=0, keepdims=True) for comp in range(3)]
        + [jnp.zeros((5, ROWS), f32)],
        axis=0,
    )
    level, spread_sq, c_input = rows_ref[0:1], rows_ref[1:2], rows_ref[2:3]
    positions = jnp.concatenate([positions_ref[...], jnp.zeros((5, ROWS), f32)], axis=0)
    fresh = jnp.concatenate([noise_ref[...], jnp.zeros((5, ROWS), f32)], axis=0)
    denoised = positions * (1.0 / spread_sq) + (level * c_input) * update
    following = 0.85 * level
    result = denoised + STEER * force_ref[...] + following * (0.8 * (positions - denoised) / level + 0.6 * fresh)
    out_ref[...] = result[:3]


def body(
    positions,
    fresh_noise,
    timestep,
    atom_single,
    pos_weight,
    ln_gain,
    w_query,
    w_key,
    w_value,
    w_out,
    w_gate_up,
    w_down,
    w_head,
    key_window,
    block_pairs,
    pair_count,
    bond_atoms,
):
    devices = lax.axis_size("atom")
    first = lax.axis_index("atom").astype(jnp.int32).reshape(1)
    smem = pl.BlockSpec(memory_space=pltpu.SMEM)
    vmem = pl.BlockSpec(memory_space=pltpu.VMEM)
    hbm = pl.BlockSpec(memory_space=pltpu.HBM)
    rows = atom_single.shape[0]

    even_pairs = [(i, i ^ 1) for i in range(devices)]
    odd_pairs = [(i, ((i + 1) ^ 1) - 1) for i in range(1, devices - 1)]

    stream, normed, schedule, tile = pl.pallas_call(
        prepare_kernel,
        out_shape=(
            jax.ShapeDtypeStruct((LANES, rows), f32),
            jax.ShapeDtypeStruct((rows, LANES), bf16),
            jax.ShapeDtypeStruct((8, rows), f32),
            jax.ShapeDtypeStruct((8, LANES), f32),
        ),
        in_specs=[smem] + [hbm] * 7,
        out_specs=(vmem,) * 4,
        scratch_shapes=[
            pltpu.SMEM(timestep.shape, jnp.int32),
            pltpu.VMEM(positions.shape, f32),
            pltpu.VMEM(atom_single.shape, bf16),
            pltpu.VMEM(pos_weight.shape, f32),
            pltpu.VMEM(ln_gain.shape, f32),
            pltpu.VMEM(block_pairs.shape, jnp.int32),
            pltpu.VMEM(key_window.shape, jnp.int32),
            pltpu.SemaphoreType.DMA((7,)),
        ],
        compiler_params=pltpu.CompilerParams(vmem_limit_bytes=VMEM_GRANT),
    )(first, timestep, positions, atom_single, pos_weight, ln_gain, block_pairs, key_window)
    even = lax.ppermute(normed, "atom", even_pairs)

    packed, token = pl.pallas_call(
        pack_kernel,
        out_shape=(
            jax.ShapeDtypeStruct((devices, 8, LANES), f32),
            jax.ShapeDtypeStruct((8, LANES), f32),
        ),
        in_specs=[smem, vmem],
        out_specs=(vmem, vmem),
        cost_estimate=pl.CostEstimate(flops=40_000_000, bytes_accessed=10_000_000, transcendentals=1_000_000),
        compiler_params=pltpu.CompilerParams(vmem_limit_bytes=VMEM_SMALL),
    )(pair_count, tile)
    tiles = lax.all_to_all(packed, "atom", 0, 0)
    bond_force, normed = pl.pallas_call(
        bond_kernel,
        out_shape=(
            jax.ShapeDtypeStruct((8, rows), f32),
            jax.ShapeDtypeStruct(normed.shape, bf16),
        ),
        in_specs=[vmem] * 4,
        out_specs=(vmem, vmem),
        cost_estimate=pl.CostEstimate(flops=80_000_000, bytes_accessed=60_000_000, transcendentals=0),
        compiler_params=pltpu.CompilerParams(vmem_limit_bytes=VMEM_SMALL),
    )(positions, bond_atoms, normed, token)
    odd = lax.ppermute(normed, "atom", odd_pairs)

    weights = (w_query, w_key, w_value, w_out, w_gate_up, w_down)
    layer_scratch = [
        pltpu.VMEM((3 * rows, LANES), bf16),
        pltpu.VMEM((3 * rows, 2 * LANES), bf16),
        pltpu.VMEM((HEADS * 48, 3 * rows), bf16),
        pltpu.VMEM((LANES, rows), bf16),
    ]
    layer_cost = pl.CostEstimate(flops=100_000_000, bytes_accessed=1_000_000, transcendentals=100_000)
    stream, normed = pl.pallas_call(
        first_layer_kernel,
        out_shape=(
            jax.ShapeDtypeStruct((LANES, rows), f32),
            jax.ShapeDtypeStruct((rows, LANES), bf16),
        ),
        in_specs=[smem] + [vmem] * 11,
        out_specs=(vmem, vmem),
        scratch_shapes=layer_scratch,
        cost_estimate=layer_cost,
        compiler_params=pltpu.CompilerParams(vmem_limit_bytes=VMEM_SMALL),
    )(first, even, normed, odd, stream, schedule, *weights)
    even = lax.ppermute(normed, "atom", even_pairs)
    odd = lax.ppermute(normed, "atom", odd_pairs)

    force = pl.pallas_call(
        force_kernel,
        out_shape=jax.ShapeDtypeStruct((8, 2 * LANES), f32),
        in_specs=[smem, vmem, vmem, vmem],
        out_specs=vmem,
        scratch_shapes=[
            pltpu.VMEM((6, LANES, LANES), f32),
            pltpu.VMEM((6, LANES, LANES), f32),
            pltpu.VMEM((8, LANES), jnp.int32),
            pltpu.VMEM((8, LANES), f32),
            pltpu.SMEM((8, LANES), jnp.int32),
            pltpu.SMEM((8, LANES), f32),
            pltpu.SemaphoreType.DMA((2,)),
        ],
        cost_estimate=pl.CostEstimate(flops=80_000_000, bytes_accessed=16_000_000, transcendentals=2_000_000),
        compiler_params=pltpu.CompilerParams(vmem_limit_bytes=VMEM_SMALL),
    )(first, tiles, positions, bond_force)

    return pl.pallas_call(
        last_layer_kernel,
        out_shape=jax.ShapeDtypeStruct(positions.shape, f32),
        in_specs=[smem] + [vmem] * 15,
        out_specs=vmem,
        scratch_shapes=layer_scratch,
        cost_estimate=layer_cost,
        compiler_params=pltpu.CompilerParams(vmem_limit_bytes=VMEM_SMALL),
    )(
        first,
        even,
        normed,
        odd,
        stream,
        schedule,
        *weights,
        positions,
        fresh_noise,
        force,
        w_head,
    )


def solution(mesh):
    in_specs = (
        P(None, ("sample", "atom")),
        P(None, ("sample", "atom")),
        P(),
        P("atom", None),
        P(),
        P(),
        P(),
        P(),
        P(),
        P(),
        P(),
        P(),
        P(),
        P("atom", None),
        P(None, "atom"),
        P("atom"),
        P(None, "atom", None),
    )
    out_specs = P(None, ("sample", "atom"))
    return jax.shard_map(body, mesh=mesh, in_specs=in_specs, out_specs=out_specs, check_vma=False)
```

```python
import functools
import math

import jax
import jax.numpy as jnp
from jax import lax
from jax.experimental import pallas as pl
from jax.experimental.pallas import tpu as pltpu
from jax.sharding import PartitionSpec as P

HEADS = 4
LANES = 128
ROWS = 256
VMEM_GRANT = 60 * 1024 * 1024
VMEM_SMALL = 16 * 1024 * 1024
NORM_EPS = 1e-05
STEER = 0.3
ABSENT = -(2.0**120)
LOG2E = 1.4426950408889634
KAPPA = 2.0 * math.sqrt(LOG2E)

f32 = jnp.float32
bf16 = jnp.bfloat16


def split3(values):
    high = values.astype(bf16)
    rest = values - high.astype(f32)
    mid = rest.astype(bf16)
    low = (rest - mid.astype(f32)).astype(bf16)
    return jnp.concatenate([high, mid, low], axis=0)


def join3(values):
    rows = values.shape[0] // 3
    return values[:rows] + values[rows : 2 * rows] + values[2 * rows :]


def norm_columns(values):
    center = values - jnp.mean(values, axis=0, keepdims=True)
    spread = jnp.mean(center * center, axis=0, keepdims=True)
    return center * lax.rsqrt(spread + NORM_EPS)


def dot_t(left, right):
    return lax.dot_general(left, right, (((0,), (0,)), ((), ())), preferred_element_type=f32)


def dot_nt(left, right):
    return lax.dot_general(left, right, (((1,), (1,)), ((), ())), preferred_element_type=f32)


def dot(left, right):
    return jnp.dot(left, right, preferred_element_type=f32)


def bond_kernel(positions_ref, bonds_ref, after_ref, out_ref):
    positions = jnp.concatenate([positions_ref[...], jnp.zeros((5, 2 * LANES), f32)], axis=0)

    forces = []
    atom_id = lax.broadcasted_iota(jnp.int32, (LANES, LANES), 0)
    for block in range(2):
        incidence = (
            (atom_id == bonds_ref[0, block : block + 1, :]).astype(f32)
            - (atom_id == bonds_ref[1, block : block + 1, :]).astype(f32)
        ).astype(bf16)
        offset = join3(dot(split3(positions[:, block * LANES : (block + 1) * LANES]), incidence))
        stretch = jnp.sum(offset * offset, axis=0, keepdims=True) - 1.0
        pull = (-0.2 * stretch) * offset
        forces.append(join3(dot_nt(split3(pull), incidence)))
    out_ref[...] = jnp.concatenate(forces, axis=1)


def force_kernel(first_ref, tiles_ref, positions_ref, bond_ref, out_ref, spread_own, push, list_v, bias_v, list_s, bias_s, sems):
    me = first_ref[0]

    codes = tiles_ref[:, 6, :].astype(jnp.int32)
    half = lax.broadcasted_iota(jnp.int32, codes.shape, 1) // 64
    mine = me * 2 + half
    first = jnp.where(codes < 0, -1, codes // 64)
    second = jnp.where(codes < 0, -1, codes % 64)
    partner = jnp.where(first == mine, second, jnp.where(second == mine, first, -1)).astype(f32)
    block_id = lax.broadcasted_iota(jnp.int32, (64, LANES), 0).astype(f32)
    hits = jnp.zeros((64, LANES), f32)
    for row in range(codes.shape[0]):
        hits = hits + jnp.where(partner[row : row + 1] == block_id, 1.0, 0.0)
    row_half = lax.broadcasted_iota(jnp.int32, (LANES, LANES), 0) // 64
    col_half = lax.broadcasted_iota(jnp.int32, (LANES, LANES), 1) // 64
    count = dot(hits.astype(bf16), (row_half == col_half).astype(bf16))
    present = count > 0.5
    lower = lax.broadcasted_iota(jnp.int32, (64, 64), 1) < lax.broadcasted_iota(jnp.int32, (64, 64), 0)
    rank = dot(lower.astype(bf16), present.astype(bf16))
    slot = (lax.broadcasted_iota(jnp.int32, (64, LANES), 1) % 64).astype(f32)
    chosen = present & (rank == slot)
    listed = jnp.sum(jnp.where(chosen, block_id, 0.0), axis=0, keepdims=True)
    times = jnp.sum(jnp.where(chosen, count, 0.0), axis=0, keepdims=True)
    total = jnp.sum(present.astype(f32), axis=0, keepdims=True)
    list_v[0:1, :] = listed.astype(jnp.int32)
    list_v[1:2, :] = total.astype(jnp.int32)
    bias_v[0:1, :] = jnp.where(times > 0.5, jnp.log2(jnp.maximum(times, 1.0)), ABSENT)
    list_copy = pltpu.make_async_copy(list_v, list_s, sems.at[0])
    bias_copy = pltpu.make_async_copy(bias_v, bias_s, sems.at[1])
    list_copy.start()
    bias_copy.start()

    for block in range(2):
        for comp in range(3):
            row = positions_ref[comp : comp + 1, block * LANES : (block + 1) * LANES] * KAPPA
            spread_own[3 * block + comp] = jnp.broadcast_to(row, (LANES, LANES)).T
            push[3 * block + comp] = jnp.zeros((LANES, LANES), f32)

    forces = []
    list_copy.wait()
    bias_copy.wait()
    for block in range(2):

        def one_pair(index, carry, block=block):
            partners = []
            for sub in range(2):
                entry = block * 64 + 2 * index + sub
                partner = list_s[0, entry]
                device = partner // 2
                within = partner % 2
                rows = [
                    tiles_ref[device, pl.ds(2 * comp + within, 1), :] * KAPPA for comp in range(3)
                ]
                partners.append((rows, bias_s[0, entry]))
            for group in range(0, LANES, 8):
                own = [spread_own[3 * block + comp, group : group + 8, :] for comp in range(3)]
                sums = [push[3 * block + comp, group : group + 8, :] for comp in range(3)]
                for rows, bias in partners:
                    offset = [own[comp] - rows[comp] for comp in range(3)]
                    power = bias - offset[0] * offset[0]
                    power = power - offset[1] * offset[1]
                    power = power - offset[2] * offset[2]
                    weight = jnp.exp2(power)
                    sums = [sums[comp] + weight * offset[comp] for comp in range(3)]
                for comp in range(3):
                    push[3 * block + comp, group : group + 8, :] = sums[comp]
            return carry

        lax.fori_loop(0, (list_s[1, block * 64] + 1) // 2, one_pair, 0)
        rows = [jnp.sum(push[3 * block + comp].T, axis=0, keepdims=True) for comp in range(3)]
        clash = jnp.concatenate(rows + [jnp.zeros((5, LANES), f32)], axis=0)
        forces.append(clash * (8.0 / KAPPA))
    out_ref[...] = bond_ref[...] + jnp.concatenate(forces, axis=1)


def start_copies(sources, targets, sems):
    copies = [
        pltpu.make_async_copy(source, target, sems.at[index])
        for index, (source, target) in enumerate(zip(sources, targets))
    ]
    for copy in copies:
        copy.start()
    return copies


def prepare_kernel(*refs):
    first_ref, count_ref, sources = refs[0], refs[1], refs[2:9]
    stream_ref, normed_ref, rows_ref, packed_ref = refs[9:13]
    targets, tile_ref, sems = refs[13:20], refs[20], refs[21]
    time_ref, positions_ref, single_ref, pos_weight_ref, gain_ref, pairs_ref, window_ref = targets
    for copy in start_copies(sources, targets, sems):
        copy.wait()
    level = 0.2 + 0.02 * jnp.full((1, ROWS), time_ref[0], jnp.int32).astype(f32)
    spread_sq = level * level + 1.0
    c_input = 1.0 / jnp.sqrt(spread_sq)
    window = window_ref[...]
    own = first_ref[0] * 2 + lax.broadcasted_iota(jnp.int32, window.shape, 0)
    lane = lax.broadcasted_iota(jnp.int32, (1, ROWS), 1)
    counts = jnp.zeros((1, ROWS), f32)
    for offset in range(5):
        hit = jnp.sum((window == own + (offset - 2)).astype(f32), axis=1, keepdims=True)
        counts = jnp.where(lane == offset, hit[0:1], counts)
        counts = jnp.where(lane == 8 + offset, hit[1:2], counts)
    counts = jnp.where(counts > 0.0, jnp.log2(jnp.maximum(counts, 1.0)), ABSENT)
    gain_rows = [
        jnp.concatenate([gain_ref[layer, 0:1], gain_ref[layer, 1:2]], axis=1) for layer in range(2)
    ]
    rows_ref[...] = jnp.concatenate(
        [level, spread_sq, c_input] + gain_rows + [counts, jnp.zeros((2, ROWS), f32)], axis=0
    )
    for row in range(6):
        part = slice((row % 2) * LANES, (row % 2 + 1) * LANES)
        tile_ref[row : row + 1, :] = positions_ref[row // 2 : row // 2 + 1, part]
    pairs = pairs_ref[...]
    lane = lax.broadcasted_iota(jnp.int32, (1, pairs.shape[1]), 1)
    codes = jnp.where(lane < count_ref[0], pairs[0:1] * 64 + pairs[1:2], -1).astype(f32)
    tile_ref[6:7, :] = jnp.concatenate([codes, codes], axis=1)
    tile_ref[7:8, :] = jnp.zeros((1, LANES), f32)
    packed_ref[...] = jnp.broadcast_to(tile_ref[...][None], packed_ref.shape)
    columns = jnp.concatenate(
        [pos_weight_ref[...], gain_ref[0, 0:1], jnp.zeros((4, LANES), f32)], axis=0
    ).T
    identity = (
        lax.broadcasted_iota(jnp.int32, (LANES, LANES), 0)
        == lax.broadcasted_iota(jnp.int32, (LANES, LANES), 1)
    ).astype(f32).astype(bf16)
    stream = dot_nt(identity, single_ref[...])
    for comp in range(3):
        stream = stream + columns[:, comp : comp + 1] * (positions_ref[comp : comp + 1, :] * c_input)
    stream_ref[...] = stream
    normed_ref[...] = (norm_columns(stream) * columns[:, 3:4]).astype(bf16).T


def layer_values(layer, first_ref, halo, stream_ref, rows_ref, head_rows, weights, scratch):
    even_ref, own_ref, odd_ref = halo
    w_query_ref, w_key_ref, w_value_ref, w_out_ref, w_gate_up_ref, w_down_ref = weights
    near, keys, values, attended = scratch
    head_size = LANES // HEADS
    query_scale = LOG2E * head_size ** -0.5
    near[ROWS : 2 * ROWS, :] = own_ref[...]

    @pl.when(first_ref[0] % 2 == 0)
    def _():
        near[:ROWS, :] = odd_ref[...]
        near[2 * ROWS :, :] = even_ref[...]

    @pl.when(first_ref[0] % 2 == 1)
    def _():
        near[:ROWS, :] = even_ref[...]
        near[2 * ROWS :, :] = odd_ref[...]

    row_block = lax.broadcasted_iota(jnp.int32, (3 * ROWS, LANES), 0) // LANES
    lane = lax.broadcasted_iota(jnp.int32, (3 * ROWS, LANES), 1)
    keys[:, LANES:] = jnp.where((lane % 16 == row_block) & (lane < 32), 1.0, 0.0).astype(bf16)
    window = rows_ref[5:6, :LANES]
    rows = []
    for chunk in range(6):
        sides = []
        for block in range(2):
            offset = chunk - block
            if 0 <= offset < 5:
                lane_id = block * 8 + offset
                sides.append(jnp.broadcast_to(window[:, lane_id : lane_id + 1], (1, LANES)))
            else:
                sides.append(jnp.full((1, LANES), ABSENT, f32))
        rows.append(jnp.concatenate(sides, axis=1))
    rows = jnp.concatenate(rows + [jnp.zeros((10, ROWS), f32)], axis=0)
    high = rows.astype(bf16)
    low = (rows - high.astype(f32)).astype(bf16)
    bias = jnp.concatenate([high, low, jnp.zeros((LANES - 32, ROWS), bf16)], axis=0)

    keys[:, :LANES] = dot(near[...], w_key_ref[layer]).astype(bf16)
    query_t = (dot_nt(w_query_ref[layer].T, own_ref[...]) * query_scale).astype(bf16)
    value_t = dot_nt(w_value_ref[layer].T, near[...]).astype(bf16)
    for head in range(HEADS):
        values[head * 48 : head * 48 + 32, :] = value_t[head * 32 : head * 32 + 32]
        values[head * 48 + 32 : head * 48 + 48, :] = jnp.ones((16, 3 * ROWS), bf16)

    def attend(exact):
        pieces = []
        sums = []

        def scores_of(head):
            parts = []
            if head:
                parts.append(jnp.zeros((head * head_size, ROWS), bf16))
            parts.append(query_t[head * head_size : (head + 1) * head_size])
            if head < HEADS - 1:
                parts.append(jnp.zeros(((HEADS - 1 - head) * head_size, ROWS), bf16))
            return dot(keys[...], jnp.concatenate(parts + [bias], axis=0))

        following = scores_of(0)
        for head in range(HEADS):
            scores = following
            if head < HEADS - 1:
                following = scores_of(head + 1)
            if exact:
                scores = scores - jnp.max(scores, axis=0, keepdims=True)
            blank = jnp.zeros((LANES, LANES), bf16)
            weights_t = jnp.concatenate(
                [
                    jnp.concatenate([jnp.exp2(scores[: 5 * LANES, :LANES]).astype(bf16), blank], axis=0),
                    jnp.concatenate([blank, jnp.exp2(scores[LANES:, LANES:]).astype(bf16)], axis=0),
                ],
                axis=1,
            )
            mixed = dot(values[head * 48 : (head + 1) * 48, :], weights_t)
            total = mixed[head_size : head_size + 1]
            sums.append(total)
            pieces.append(mixed[:head_size] * (1.0 / total))
        attended[...] = jnp.concatenate(pieces, axis=0).astype(bf16)
        return jnp.concatenate(sums, axis=0)

    sums = attend(False)
    safe = (jnp.min(sums) > 2.0**-80) & (jnp.max(sums) < 2.0**100)

    @pl.when(jnp.logical_not(safe))
    def _():
        attend(True)

    gains = jnp.concatenate(
        [rows_ref[3 + index // 2 : 4 + index // 2, (index % 2) * LANES : (index % 2 + 1) * LANES] for index in range(4)]
        + [head_rows],
        axis=0,
    ).T
    now = stream_ref[...] + dot(w_out_ref[layer].T, attended[...])
    normed = (norm_columns(now) * gains[:, 2 * layer + 1 : 2 * layer + 2]).astype(bf16)
    gate_up = dot(w_gate_up_ref[layer].T, normed)
    width = gate_up.shape[0] // 2
    half, up = 0.5 * gate_up[:width], gate_up[width:]
    hidden = ((half + half * jnp.tanh(half)) * up).astype(bf16)
    return now + dot(w_down_ref[layer].T, hidden), gains


def first_layer_kernel(first_ref, even_ref, own_ref, odd_ref, stream_ref, rows_ref, *refs):
    weights, (out_ref, normed_ref), scratch = refs[:6], refs[6:8], refs[8:]
    stream, gains = layer_values(
        0, first_ref, (even_ref, own_ref, odd_ref), stream_ref, rows_ref, jnp.zeros((4, LANES), f32), weights, scratch
    )
    out_ref[...] = stream
    normed_ref[...] = (norm_columns(stream) * gains[:, 2:3]).astype(bf16).T


def last_layer_kernel(first_ref, even_ref, own_ref, odd_ref, stream_ref, rows_ref, *refs):
    weights, (positions_ref, noise_ref, force_ref, w_head_ref) = refs[:6], refs[6:10]
    out_ref, scratch = refs[10], refs[11:]
    head_rows = jnp.concatenate([w_head_ref[...], jnp.zeros((1, LANES), f32)], axis=0)
    stream, columns = layer_values(
        1, first_ref, (even_ref, own_ref, odd_ref), stream_ref, rows_ref, head_rows, weights, scratch
    )
    final = norm_columns(stream)
    update = jnp.concatenate(
        [jnp.sum(columns[:, 4 + comp : 5 + comp] * final, axis=0, keepdims=True) for comp in range(3)]
        + [jnp.zeros((5, ROWS), f32)],
        axis=0,
    )
    level, spread_sq, c_input = rows_ref[0:1], rows_ref[1:2], rows_ref[2:3]
    positions = jnp.concatenate([positions_ref[...], jnp.zeros((5, ROWS), f32)], axis=0)
    fresh = jnp.concatenate([noise_ref[...], jnp.zeros((5, ROWS), f32)], axis=0)
    denoised = positions * (1.0 / spread_sq) + (level * c_input) * update
    following = 0.85 * level
    result = denoised + STEER * force_ref[...] + following * (0.8 * (positions - denoised) / level + 0.6 * fresh)
    out_ref[...] = result[:3]


def body(
    positions,
    fresh_noise,
    timestep,
    atom_single,
    pos_weight,
    ln_gain,
    w_query,
    w_key,
    w_value,
    w_out,
    w_gate_up,
    w_down,
    w_head,
    key_window,
    block_pairs,
    pair_count,
    bond_atoms,
):
    devices = lax.axis_size("atom")
    first = lax.axis_index("atom").astype(jnp.int32).reshape(1)
    smem = pl.BlockSpec(memory_space=pltpu.SMEM)
    vmem = pl.BlockSpec(memory_space=pltpu.VMEM)
    hbm = pl.BlockSpec(memory_space=pltpu.HBM)
    rows = atom_single.shape[0]

    even_pairs = [(i, i ^ 1) for i in range(devices)]
    odd_pairs = [(i, ((i + 1) ^ 1) - 1) for i in range(1, devices - 1)]

    stream, normed, schedule, packed = pl.pallas_call(
        prepare_kernel,
        out_shape=(
            jax.ShapeDtypeStruct((LANES, rows), f32),
            jax.ShapeDtypeStruct((rows, LANES), bf16),
            jax.ShapeDtypeStruct((8, rows), f32),
            jax.ShapeDtypeStruct((devices, 8, LANES), f32),
        ),
        in_specs=[smem, smem] + [hbm] * 7,
        out_specs=(vmem,) * 4,
        scratch_shapes=[
            pltpu.SMEM(timestep.shape, jnp.int32),
            pltpu.VMEM(positions.shape, f32),
            pltpu.VMEM(atom_single.shape, bf16),
            pltpu.VMEM(pos_weight.shape, f32),
            pltpu.VMEM(ln_gain.shape, f32),
            pltpu.VMEM(block_pairs.shape, jnp.int32),
            pltpu.VMEM(key_window.shape, jnp.int32),
            pltpu.VMEM((8, LANES), f32),
            pltpu.SemaphoreType.DMA((7,)),
        ],
        compiler_params=pltpu.CompilerParams(vmem_limit_bytes=VMEM_GRANT),
    )(first, pair_count, timestep, positions, atom_single, pos_weight, ln_gain, block_pairs, key_window)
    even = lax.ppermute(normed, "atom", even_pairs)

    tiles = lax.all_to_all(packed, "atom", 0, 0)
    bond_force = pl.pallas_call(
        bond_kernel,
        out_shape=jax.ShapeDtypeStruct((8, rows), f32),
        in_specs=[vmem] * 3,
        out_specs=vmem,
        cost_estimate=pl.CostEstimate(flops=80_000_000, bytes_accessed=20_000_000, transcendentals=0),
        compiler_params=pltpu.CompilerParams(vmem_limit_bytes=VMEM_SMALL),
    )(positions, bond_atoms, schedule)
    odd = lax.ppermute(normed, "atom", odd_pairs)

    weights = (w_query, w_key, w_value, w_out, w_gate_up, w_down)
    layer_scratch = [
        pltpu.VMEM((3 * rows, LANES), bf16),
        pltpu.VMEM((3 * rows, 2 * LANES), bf16),
        pltpu.VMEM((HEADS * 48, 3 * rows), bf16),
        pltpu.VMEM((LANES, rows), bf16),
    ]
    layer_cost = pl.CostEstimate(flops=2_000_000_000, bytes_accessed=20_000_000, transcendentals=2_000_000)
    stream, normed = pl.pallas_call(
        first_layer_kernel,
        out_shape=(
            jax.ShapeDtypeStruct((LANES, rows), f32),
            jax.ShapeDtypeStruct((rows, LANES), bf16),
        ),
        in_specs=[smem] + [vmem] * 11,
        out_specs=(vmem, vmem),
        scratch_shapes=layer_scratch,
        cost_estimate=layer_cost,
        compiler_params=pltpu.CompilerParams(vmem_limit_bytes=VMEM_SMALL),
    )(first, even, normed, odd, stream, schedule, *weights)
    even = lax.ppermute(normed, "atom", even_pairs)
    odd = lax.ppermute(normed, "atom", odd_pairs)

    force = pl.pallas_call(
        force_kernel,
        out_shape=jax.ShapeDtypeStruct((8, 2 * LANES), f32),
        in_specs=[smem, vmem, vmem, vmem],
        out_specs=vmem,
        scratch_shapes=[
            pltpu.VMEM((6, LANES, LANES), f32),
            pltpu.VMEM((6, LANES, LANES), f32),
            pltpu.VMEM((8, LANES), jnp.int32),
            pltpu.VMEM((8, LANES), f32),
            pltpu.SMEM((8, LANES), jnp.int32),
            pltpu.SMEM((8, LANES), f32),
            pltpu.SemaphoreType.DMA((2,)),
        ],
        cost_estimate=pl.CostEstimate(flops=80_000_000, bytes_accessed=16_000_000, transcendentals=2_000_000),
        compiler_params=pltpu.CompilerParams(vmem_limit_bytes=VMEM_SMALL),
    )(first, tiles, positions, bond_force)

    return pl.pallas_call(
        last_layer_kernel,
        out_shape=jax.ShapeDtypeStruct(positions.shape, f32),
        in_specs=[smem] + [vmem] * 15,
        out_specs=vmem,
        scratch_shapes=layer_scratch,
        cost_estimate=layer_cost,
        compiler_params=pltpu.CompilerParams(vmem_limit_bytes=VMEM_SMALL),
    )(
        first,
        even,
        normed,
        odd,
        stream,
        schedule,
        *weights,
        positions,
        fresh_noise,
        force,
        w_head,
    )


def solution(mesh):
    in_specs = (
        P(None, ("sample", "atom")),
        P(None, ("sample", "atom")),
        P(),
        P("atom", None),
        P(),
        P(),
        P(),
        P(),
        P(),
        P(),
        P(),
        P(),
        P(),
        P("atom", None),
        P(None, "atom"),
        P("atom"),
        P(None, "atom", None),
    )
    out_specs = P(None, ("sample", "atom"))
    return jax.shard_map(body, mesh=mesh, in_specs=in_specs, out_specs=out_specs, check_vma=False)
```

```python
import functools
import math

import jax
import jax.numpy as jnp
from jax import lax
from jax.experimental import pallas as pl
from jax.experimental.pallas import tpu as pltpu
from jax.sharding import PartitionSpec as P

HEADS = 4
LANES = 128
ROWS = 256
VMEM_GRANT = 60 * 1024 * 1024
VMEM_SMALL = 16 * 1024 * 1024
NORM_EPS = 1e-05
STEER = 0.3
ABSENT = -(2.0**120)
LOG2E = 1.4426950408889634
KAPPA = 2.0 * math.sqrt(LOG2E)

f32 = jnp.float32
bf16 = jnp.bfloat16


def split3(values):
    high = values.astype(bf16)
    rest = values - high.astype(f32)
    mid = rest.astype(bf16)
    low = (rest - mid.astype(f32)).astype(bf16)
    return jnp.concatenate([high, mid, low], axis=0)


def join3(values):
    rows = values.shape[0] // 3
    return values[:rows] + values[rows : 2 * rows] + values[2 * rows :]


def norm_columns(values):
    center = values - jnp.mean(values, axis=0, keepdims=True)
    spread = jnp.mean(center * center, axis=0, keepdims=True)
    return center * lax.rsqrt(spread + NORM_EPS)


def dot_t(left, right):
    return lax.dot_general(left, right, (((0,), (0,)), ((), ())), preferred_element_type=f32)


def dot_nt(left, right):
    return lax.dot_general(left, right, (((1,), (1,)), ((), ())), preferred_element_type=f32)


def dot(left, right):
    return jnp.dot(left, right, preferred_element_type=f32)


def bond_kernel(positions_ref, bonds_ref, after_ref, out_ref):
    positions = jnp.concatenate([positions_ref[...], jnp.zeros((5, 2 * LANES), f32)], axis=0)

    forces = []
    atom_id = lax.broadcasted_iota(jnp.int32, (LANES, LANES), 0)
    for block in range(2):
        incidence = (
            (atom_id == bonds_ref[0, block : block + 1, :]).astype(f32)
            - (atom_id == bonds_ref[1, block : block + 1, :]).astype(f32)
        ).astype(bf16)
        offset = join3(dot(split3(positions[:, block * LANES : (block + 1) * LANES]), incidence))
        stretch = jnp.sum(offset * offset, axis=0, keepdims=True) - 1.0
        pull = (-0.2 * stretch) * offset
        forces.append(join3(dot_nt(split3(pull), incidence)))
    out_ref[...] = jnp.concatenate(forces, axis=1)


def force_kernel(first_ref, tiles_ref, positions_ref, bond_ref, out_ref, spread_own, push, list_v, bias_v, list_s, bias_s, sems):
    me = first_ref[0]

    codes = tiles_ref[:, 6, :].astype(jnp.int32)
    half = lax.broadcasted_iota(jnp.int32, codes.shape, 1) // 64
    mine = me * 2 + half
    first = jnp.where(codes < 0, -1, codes // 64)
    second = jnp.where(codes < 0, -1, codes % 64)
    partner = jnp.where(first == mine, second, jnp.where(second == mine, first, -1)).astype(f32)
    block_id = lax.broadcasted_iota(jnp.int32, (64, LANES), 0).astype(f32)
    hits = jnp.zeros((64, LANES), f32)
    for row in range(codes.shape[0]):
        hits = hits + jnp.where(partner[row : row + 1] == block_id, 1.0, 0.0)
    row_half = lax.broadcasted_iota(jnp.int32, (LANES, LANES), 0) // 64
    col_half = lax.broadcasted_iota(jnp.int32, (LANES, LANES), 1) // 64
    count = dot(hits.astype(bf16), (row_half == col_half).astype(bf16))
    present = count > 0.5
    lower = lax.broadcasted_iota(jnp.int32, (64, 64), 1) < lax.broadcasted_iota(jnp.int32, (64, 64), 0)
    rank = dot(lower.astype(bf16), present.astype(bf16))
    slot = (lax.broadcasted_iota(jnp.int32, (64, LANES), 1) % 64).astype(f32)
    chosen = present & (rank == slot)
    listed = jnp.sum(jnp.where(chosen, block_id, 0.0), axis=0, keepdims=True)
    times = jnp.sum(jnp.where(chosen, count, 0.0), axis=0, keepdims=True)
    total = jnp.sum(present.astype(f32), axis=0, keepdims=True)
    list_v[0:1, :] = listed.astype(jnp.int32)
    list_v[1:2, :] = total.astype(jnp.int32)
    bias_v[0:1, :] = jnp.where(times > 0.5, jnp.log2(jnp.maximum(times, 1.0)), ABSENT)
    list_copy = pltpu.make_async_copy(list_v, list_s, sems.at[0])
    bias_copy = pltpu.make_async_copy(bias_v, bias_s, sems.at[1])
    list_copy.start()
    bias_copy.start()

    for block in range(2):
        for comp in range(3):
            row = positions_ref[comp : comp + 1, block * LANES : (block + 1) * LANES] * KAPPA
            spread_own[3 * block + comp] = jnp.broadcast_to(row, (LANES, LANES)).T
            push[3 * block + comp] = jnp.zeros((LANES, LANES), f32)

    forces = []
    list_copy.wait()
    bias_copy.wait()
    for block in range(2):

        def one_pair(index, carry, block=block):
            partners = []
            for sub in range(2):
                entry = block * 64 + 2 * index + sub
                partner = list_s[0, entry]
                device = partner // 2
                within = partner % 2
                rows = [
                    tiles_ref[device, pl.ds(2 * comp + within, 1), :] * KAPPA for comp in range(3)
                ]
                partners.append((rows, bias_s[0, entry]))
            for group in range(0, LANES, 8):
                own = [spread_own[3 * block + comp, group : group + 8, :] for comp in range(3)]
                sums = [push[3 * block + comp, group : group + 8, :] for comp in range(3)]
                for rows, bias in partners:
                    offset = [own[comp] - rows[comp] for comp in range(3)]
                    power = bias - offset[0] * offset[0]
                    power = power - offset[1] * offset[1]
                    power = power - offset[2] * offset[2]
                    weight = jnp.exp2(power)
                    sums = [sums[comp] + weight * offset[comp] for comp in range(3)]
                for comp in range(3):
                    push[3 * block + comp, group : group + 8, :] = sums[comp]
            return carry

        lax.fori_loop(0, (list_s[1, block * 64] + 1) // 2, one_pair, 0)
        rows = [jnp.sum(push[3 * block + comp].T, axis=0, keepdims=True) for comp in range(3)]
        clash = jnp.concatenate(rows + [jnp.zeros((5, LANES), f32)], axis=0)
        forces.append(clash * (8.0 / KAPPA))
    out_ref[...] = bond_ref[...] + jnp.concatenate(forces, axis=1)


def start_copies(sources, targets, sems):
    copies = [
        pltpu.make_async_copy(source, target, sems.at[index])
        for index, (source, target) in enumerate(zip(sources, targets))
    ]
    for copy in copies:
        copy.start()
    return copies


def prepare_kernel(*refs):
    first_ref, count_ref, sources = refs[0], refs[1], refs[2:9]
    stream_ref, normed_ref, rows_ref, packed_ref = refs[9:13]
    targets, tile_ref, sems = refs[13:20], refs[20], refs[21]
    time_ref, positions_ref, single_ref, pos_weight_ref, gain_ref, pairs_ref, window_ref = targets
    for copy in start_copies(sources, targets, sems):
        copy.wait()
    level = 0.2 + 0.02 * jnp.full((1, ROWS), time_ref[0], jnp.int32).astype(f32)
    spread_sq = level * level + 1.0
    c_input = 1.0 / jnp.sqrt(spread_sq)
    window = window_ref[...]
    own = first_ref[0] * 2 + lax.broadcasted_iota(jnp.int32, window.shape, 0)
    lane = lax.broadcasted_iota(jnp.int32, (1, ROWS), 1)
    counts = jnp.zeros((1, ROWS), f32)
    for offset in range(5):
        hit = jnp.sum((window == own + (offset - 2)).astype(f32), axis=1, keepdims=True)
        counts = jnp.where(lane == offset, hit[0:1], counts)
        counts = jnp.where(lane == 8 + offset, hit[1:2], counts)
    counts = jnp.where(counts > 0.0, jnp.log2(jnp.maximum(counts, 1.0)), ABSENT)
    gain_rows = [
        jnp.concatenate([gain_ref[layer, 0:1], gain_ref[layer, 1:2]], axis=1) for layer in range(2)
    ]
    rows_ref[...] = jnp.concatenate(
        [level, spread_sq, c_input] + gain_rows + [counts, jnp.zeros((2, ROWS), f32)], axis=0
    )
    for row in range(6):
        part = slice((row % 2) * LANES, (row % 2 + 1) * LANES)
        tile_ref[row : row + 1, :] = positions_ref[row // 2 : row // 2 + 1, part]
    pairs = pairs_ref[...]
    lane = lax.broadcasted_iota(jnp.int32, (1, pairs.shape[1]), 1)
    codes = jnp.where(lane < count_ref[0], pairs[0:1] * 64 + pairs[1:2], -1).astype(f32)
    tile_ref[6:7, :] = jnp.concatenate([codes, codes], axis=1)
    tile_ref[7:8, :] = jnp.zeros((1, LANES), f32)
    packed_ref[...] = jnp.broadcast_to(tile_ref[...][None], packed_ref.shape)
    columns = jnp.concatenate(
        [pos_weight_ref[...], gain_ref[0, 0:1], jnp.zeros((4, LANES), f32)], axis=0
    ).T
    identity = (
        lax.broadcasted_iota(jnp.int32, (LANES, LANES), 0)
        == lax.broadcasted_iota(jnp.int32, (LANES, LANES), 1)
    ).astype(f32).astype(bf16)
    stream = dot_nt(identity, single_ref[...])
    for comp in range(3):
        stream = stream + columns[:, comp : comp + 1] * (positions_ref[comp : comp + 1, :] * c_input)
    stream_ref[...] = stream
    normed_ref[...] = (norm_columns(stream) * columns[:, 3:4]).astype(bf16).T


def layer_values(layer, first_ref, halo, stream_ref, rows_ref, head_rows, weights, scratch):
    even_ref, own_ref, odd_ref = halo
    w_query_ref, w_key_ref, w_value_ref, w_out_ref, w_gate_up_ref, w_down_ref = weights
    near, keys, values, attended = scratch
    head_size = LANES // HEADS
    query_scale = LOG2E * head_size ** -0.5
    near[ROWS : 2 * ROWS, :] = own_ref[...]

    @pl.when(first_ref[0] % 2 == 0)
    def _():
        near[:ROWS, :] = odd_ref[...]
        near[2 * ROWS :, :] = even_ref[...]

    @pl.when(first_ref[0] % 2 == 1)
    def _():
        near[:ROWS, :] = even_ref[...]
        near[2 * ROWS :, :] = odd_ref[...]

    row_block = lax.broadcasted_iota(jnp.int32, (3 * ROWS, LANES), 0) // LANES
    lane = lax.broadcasted_iota(jnp.int32, (3 * ROWS, LANES), 1)
    keys[:, LANES:] = jnp.where((lane % 16 == row_block) & (lane < 32), 1.0, 0.0).astype(bf16)
    window = rows_ref[5:6, :LANES]
    rows = []
    for chunk in range(6):
        sides = []
        for block in range(2):
            offset = chunk - block
            if 0 <= offset < 5:
                lane_id = block * 8 + offset
                sides.append(jnp.broadcast_to(window[:, lane_id : lane_id + 1], (1, LANES)))
            else:
                sides.append(jnp.full((1, LANES), ABSENT, f32))
        rows.append(jnp.concatenate(sides, axis=1))
    rows = jnp.concatenate(rows + [jnp.zeros((10, ROWS), f32)], axis=0)
    high = rows.astype(bf16)
    low = (rows - high.astype(f32)).astype(bf16)
    bias = jnp.concatenate([high, low, jnp.zeros((LANES - 32, ROWS), bf16)], axis=0)

    keys[:, :LANES] = dot(near[...], w_key_ref[layer]).astype(bf16)
    query_t = (dot_nt(w_query_ref[layer].T, own_ref[...]) * query_scale).astype(bf16)
    value_t = dot_nt(w_value_ref[layer].T, near[...]).astype(bf16)
    for head in range(HEADS):
        values[head * 48 : head * 48 + 32, :] = value_t[head * 32 : head * 32 + 32]
        values[head * 48 + 32 : head * 48 + 48, :] = jnp.ones((16, 3 * ROWS), bf16)

    def attend(exact):
        pieces = []
        sums = []

        def scores_of(head):
            parts = []
            if head:
                parts.append(jnp.zeros((head * head_size, ROWS), bf16))
            parts.append(query_t[head * head_size : (head + 1) * head_size])
            if head < HEADS - 1:
                parts.append(jnp.zeros(((HEADS - 1 - head) * head_size, ROWS), bf16))
            return dot(keys[...], jnp.concatenate(parts + [bias], axis=0))

        following = scores_of(0)
        for head in range(HEADS):
            scores = following
            if head < HEADS - 1:
                following = scores_of(head + 1)
            if exact:
                scores = scores - jnp.max(scores, axis=0, keepdims=True)
            blank = jnp.zeros((LANES, LANES), bf16)
            weights_t = jnp.concatenate(
                [
                    jnp.concatenate([jnp.exp2(scores[: 5 * LANES, :LANES]).astype(bf16), blank], axis=0),
                    jnp.concatenate([blank, jnp.exp2(scores[LANES:, LANES:]).astype(bf16)], axis=0),
                ],
                axis=1,
            )
            mixed = dot(values[head * 48 : (head + 1) * 48, :], weights_t)
            total = mixed[head_size : head_size + 1]
            sums.append(total)
            pieces.append(mixed[:head_size] * (1.0 / total))
        attended[...] = jnp.concatenate(pieces, axis=0).astype(bf16)
        return jnp.concatenate(sums, axis=0)

    sums = attend(False)
    safe = (jnp.min(sums) > 2.0**-80) & (jnp.max(sums) < 2.0**100)

    @pl.when(jnp.logical_not(safe))
    def _():
        attend(True)

    gains = jnp.concatenate(
        [rows_ref[3 + index // 2 : 4 + index // 2, (index % 2) * LANES : (index % 2 + 1) * LANES] for index in range(4)]
        + [head_rows],
        axis=0,
    ).T
    now = stream_ref[...] + dot(w_out_ref[layer].T, attended[...])
    normed = (norm_columns(now) * gains[:, 2 * layer + 1 : 2 * layer + 2]).astype(bf16)
    gate_up = dot(w_gate_up_ref[layer].T, normed)
    width = gate_up.shape[0] // 2
    half, up = 0.5 * gate_up[:width], gate_up[width:]
    hidden = ((half + half * jnp.tanh(half)) * up).astype(bf16)
    return now + dot(w_down_ref[layer].T, hidden), gains


def first_layer_kernel(first_ref, even_ref, own_ref, odd_ref, stream_ref, rows_ref, *refs):
    weights, (out_ref, normed_ref), scratch = refs[:6], refs[7:9], refs[9:]
    stream, gains = layer_values(
        0, first_ref, (even_ref, own_ref, odd_ref), stream_ref, rows_ref, jnp.zeros((4, LANES), f32), weights, scratch
    )
    out_ref[...] = stream
    normed_ref[...] = (norm_columns(stream) * gains[:, 2:3]).astype(bf16).T


def last_layer_kernel(first_ref, even_ref, own_ref, odd_ref, stream_ref, rows_ref, *refs):
    weights, (positions_ref, noise_ref, force_ref, w_head_ref) = refs[:6], refs[6:10]
    out_ref, scratch = refs[10], refs[11:]
    head_rows = jnp.concatenate([w_head_ref[...], jnp.zeros((1, LANES), f32)], axis=0)
    stream, columns = layer_values(
        1, first_ref, (even_ref, own_ref, odd_ref), stream_ref, rows_ref, head_rows, weights, scratch
    )
    final = norm_columns(stream)
    update = jnp.concatenate(
        [jnp.sum(columns[:, 4 + comp : 5 + comp] * final, axis=0, keepdims=True) for comp in range(3)]
        + [jnp.zeros((5, ROWS), f32)],
        axis=0,
    )
    level, spread_sq, c_input = rows_ref[0:1], rows_ref[1:2], rows_ref[2:3]
    positions = jnp.concatenate([positions_ref[...], jnp.zeros((5, ROWS), f32)], axis=0)
    fresh = jnp.concatenate([noise_ref[...], jnp.zeros((5, ROWS), f32)], axis=0)
    denoised = positions * (1.0 / spread_sq) + (level * c_input) * update
    following = 0.85 * level
    result = denoised + STEER * force_ref[...] + following * (0.8 * (positions - denoised) / level + 0.6 * fresh)
    out_ref[...] = result[:3]


def body(
    positions,
    fresh_noise,
    timestep,
    atom_single,
    pos_weight,
    ln_gain,
    w_query,
    w_key,
    w_value,
    w_out,
    w_gate_up,
    w_down,
    w_head,
    key_window,
    block_pairs,
    pair_count,
    bond_atoms,
):
    devices = lax.axis_size("atom")
    first = lax.axis_index("atom").astype(jnp.int32).reshape(1)
    smem = pl.BlockSpec(memory_space=pltpu.SMEM)
    vmem = pl.BlockSpec(memory_space=pltpu.VMEM)
    hbm = pl.BlockSpec(memory_space=pltpu.HBM)
    rows = atom_single.shape[0]

    even_pairs = [(i, i ^ 1) for i in range(devices)]
    odd_pairs = [(i, ((i + 1) ^ 1) - 1) for i in range(1, devices - 1)]

    stream, normed, schedule, packed = pl.pallas_call(
        prepare_kernel,
        out_shape=(
            jax.ShapeDtypeStruct((LANES, rows), f32),
            jax.ShapeDtypeStruct((rows, LANES), bf16),
            jax.ShapeDtypeStruct((8, rows), f32),
            jax.ShapeDtypeStruct((devices, 8, LANES), f32),
        ),
        in_specs=[smem, smem] + [hbm] * 7,
        out_specs=(vmem,) * 4,
        scratch_shapes=[
            pltpu.SMEM(timestep.shape, jnp.int32),
            pltpu.VMEM(positions.shape, f32),
            pltpu.VMEM(atom_single.shape, bf16),
            pltpu.VMEM(pos_weight.shape, f32),
            pltpu.VMEM(ln_gain.shape, f32),
            pltpu.VMEM(block_pairs.shape, jnp.int32),
            pltpu.VMEM(key_window.shape, jnp.int32),
            pltpu.VMEM((8, LANES), f32),
            pltpu.SemaphoreType.DMA((7,)),
        ],
        compiler_params=pltpu.CompilerParams(vmem_limit_bytes=VMEM_GRANT),
    )(first, pair_count, timestep, positions, atom_single, pos_weight, ln_gain, block_pairs, key_window)
    even = lax.ppermute(normed, "atom", even_pairs)

    tiles = lax.all_to_all(packed, "atom", 0, 0)
    bond_force = pl.pallas_call(
        bond_kernel,
        out_shape=jax.ShapeDtypeStruct((8, rows), f32),
        in_specs=[vmem] * 3,
        out_specs=vmem,
        cost_estimate=pl.CostEstimate(flops=80_000_000, bytes_accessed=20_000_000, transcendentals=0),
        compiler_params=pltpu.CompilerParams(vmem_limit_bytes=VMEM_SMALL),
    )(positions, bond_atoms, schedule)
    odd = lax.ppermute(normed, "atom", odd_pairs)

    weights = (w_query, w_key, w_value, w_out, w_gate_up, w_down)
    layer_scratch = [
        pltpu.VMEM((3 * rows, LANES), bf16),
        pltpu.VMEM((3 * rows, 2 * LANES), bf16),
        pltpu.VMEM((HEADS * 48, 3 * rows), bf16),
        pltpu.VMEM((LANES, rows), bf16),
    ]
    layer_cost = pl.CostEstimate(flops=2_000_000_000, bytes_accessed=20_000_000, transcendentals=2_000_000)
    stream, normed = pl.pallas_call(
        first_layer_kernel,
        out_shape=(
            jax.ShapeDtypeStruct((LANES, rows), f32),
            jax.ShapeDtypeStruct((rows, LANES), bf16),
        ),
        in_specs=[smem] + [vmem] * 12,
        out_specs=(vmem, vmem),
        scratch_shapes=layer_scratch,
        cost_estimate=layer_cost,
        compiler_params=pltpu.CompilerParams(vmem_limit_bytes=VMEM_SMALL),
    )(first, even, normed, odd, stream, schedule, *weights, bond_force)
    even = lax.ppermute(normed, "atom", even_pairs)
    odd = lax.ppermute(normed, "atom", odd_pairs)

    force = pl.pallas_call(
        force_kernel,
        out_shape=jax.ShapeDtypeStruct((8, 2 * LANES), f32),
        in_specs=[smem, vmem, vmem, vmem],
        out_specs=vmem,
        scratch_shapes=[
            pltpu.VMEM((6, LANES, LANES), f32),
            pltpu.VMEM((6, LANES, LANES), f32),
            pltpu.VMEM((8, LANES), jnp.int32),
            pltpu.VMEM((8, LANES), f32),
            pltpu.SMEM((8, LANES), jnp.int32),
            pltpu.SMEM((8, LANES), f32),
            pltpu.SemaphoreType.DMA((2,)),
        ],
        cost_estimate=pl.CostEstimate(flops=80_000_000, bytes_accessed=16_000_000, transcendentals=2_000_000),
        compiler_params=pltpu.CompilerParams(vmem_limit_bytes=VMEM_SMALL),
    )(first, tiles, positions, bond_force)

    return pl.pallas_call(
        last_layer_kernel,
        out_shape=jax.ShapeDtypeStruct(positions.shape, f32),
        in_specs=[smem] + [vmem] * 15,
        out_specs=vmem,
        scratch_shapes=layer_scratch,
        cost_estimate=layer_cost,
        compiler_params=pltpu.CompilerParams(vmem_limit_bytes=VMEM_SMALL),
    )(
        first,
        even,
        normed,
        odd,
        stream,
        schedule,
        *weights,
        positions,
        fresh_noise,
        force,
        w_head,
    )


def solution(mesh):
    in_specs = (
        P(None, ("sample", "atom")),
        P(None, ("sample", "atom")),
        P(),
        P("atom", None),
        P(),
        P(),
        P(),
        P(),
        P(),
        P(),
        P(),
        P(),
        P(),
        P("atom", None),
        P(None, "atom"),
        P("atom"),
        P(None, "atom", None),
    )
    out_specs = P(None, ("sample", "atom"))
    return jax.shard_map(body, mesh=mesh, in_specs=in_specs, out_specs=out_specs, check_vma=False)
```

```python
import functools
import math

import jax
import jax.numpy as jnp
from jax import lax
from jax.experimental import pallas as pl
from jax.experimental.pallas import tpu as pltpu
from jax.sharding import PartitionSpec as P

HEADS = 4
LANES = 128
ROWS = 256
VMEM_GRANT = 60 * 1024 * 1024
VMEM_SMALL = 16 * 1024 * 1024
NORM_EPS = 1e-05
STEER = 0.3
ABSENT = -(2.0**120)
LOG2E = 1.4426950408889634
KAPPA = 2.0 * math.sqrt(LOG2E)

f32 = jnp.float32
bf16 = jnp.bfloat16


def split3(values):
    high = values.astype(bf16)
    rest = values - high.astype(f32)
    mid = rest.astype(bf16)
    low = (rest - mid.astype(f32)).astype(bf16)
    return jnp.concatenate([high, mid, low], axis=0)


def join3(values):
    rows = values.shape[0] // 3
    return values[:rows] + values[rows : 2 * rows] + values[2 * rows :]


def norm_columns(values):
    center = values - jnp.mean(values, axis=0, keepdims=True)
    spread = jnp.mean(center * center, axis=0, keepdims=True)
    return center * lax.rsqrt(spread + NORM_EPS)


def dot_t(left, right):
    return lax.dot_general(left, right, (((0,), (0,)), ((), ())), preferred_element_type=f32)


def dot_nt(left, right):
    return lax.dot_general(left, right, (((1,), (1,)), ((), ())), preferred_element_type=f32)


def dot(left, right):
    return jnp.dot(left, right, preferred_element_type=f32)


def bond_kernel(positions_ref, bonds_ref, out_ref):
    positions = jnp.concatenate([positions_ref[...], jnp.zeros((5, 2 * LANES), f32)], axis=0)

    forces = []
    atom_id = lax.broadcasted_iota(jnp.int32, (LANES, LANES), 0)
    for block in range(2):
        incidence = (
            (atom_id == bonds_ref[0, block : block + 1, :]).astype(f32)
            - (atom_id == bonds_ref[1, block : block + 1, :]).astype(f32)
        ).astype(bf16)
        offset = join3(dot(split3(positions[:, block * LANES : (block + 1) * LANES]), incidence))
        stretch = jnp.sum(offset * offset, axis=0, keepdims=True) - 1.0
        pull = (-0.2 * stretch) * offset
        forces.append(join3(dot_nt(split3(pull), incidence)))
    out_ref[...] = jnp.concatenate(forces, axis=1)


def force_kernel(first_ref, tiles_ref, positions_ref, bond_ref, out_ref, spread_own, push, list_v, bias_v, list_s, bias_s, sems):
    me = first_ref[0]

    codes = tiles_ref[:, 6, :].astype(jnp.int32)
    half = lax.broadcasted_iota(jnp.int32, codes.shape, 1) // 64
    mine = me * 2 + half
    first = jnp.where(codes < 0, -1, codes // 64)
    second = jnp.where(codes < 0, -1, codes % 64)
    partner = jnp.where(first == mine, second, jnp.where(second == mine, first, -1)).astype(f32)
    block_id = lax.broadcasted_iota(jnp.int32, (64, LANES), 0).astype(f32)
    hits = jnp.zeros((64, LANES), f32)
    for row in range(codes.shape[0]):
        hits = hits + jnp.where(partner[row : row + 1] == block_id, 1.0, 0.0)
    row_half = lax.broadcasted_iota(jnp.int32, (LANES, LANES), 0) // 64
    col_half = lax.broadcasted_iota(jnp.int32, (LANES, LANES), 1) // 64
    count = dot(hits.astype(bf16), (row_half == col_half).astype(bf16))
    present = count > 0.5
    lower = lax.broadcasted_iota(jnp.int32, (64, 64), 1) < lax.broadcasted_iota(jnp.int32, (64, 64), 0)
    rank = dot(lower.astype(bf16), present.astype(bf16))
    slot = (lax.broadcasted_iota(jnp.int32, (64, LANES), 1) % 64).astype(f32)
    chosen = present & (rank == slot)
    listed = jnp.sum(jnp.where(chosen, block_id, 0.0), axis=0, keepdims=True)
    times = jnp.sum(jnp.where(chosen, count, 0.0), axis=0, keepdims=True)
    total = jnp.sum(present.astype(f32), axis=0, keepdims=True)
    list_v[0:1, :] = listed.astype(jnp.int32)
    list_v[1:2, :] = total.astype(jnp.int32)
    bias_v[0:1, :] = jnp.where(times > 0.5, jnp.log2(jnp.maximum(times, 1.0)), ABSENT)
    list_copy = pltpu.make_async_copy(list_v, list_s, sems.at[0])
    bias_copy = pltpu.make_async_copy(bias_v, bias_s, sems.at[1])
    list_copy.start()
    bias_copy.start()

    for block in range(2):
        for comp in range(3):
            row = positions_ref[comp : comp + 1, block * LANES : (block + 1) * LANES] * KAPPA
            spread_own[3 * block + comp] = jnp.broadcast_to(row, (LANES, LANES)).T
            push[3 * block + comp] = jnp.zeros((LANES, LANES), f32)

    forces = []
    list_copy.wait()
    bias_copy.wait()
    for block in range(2):

        def one_pair(index, carry, block=block):
            partners = []
            for sub in range(2):
                entry = block * 64 + 2 * index + sub
                partner = list_s[0, entry]
                device = partner // 2
                within = partner % 2
                rows = [
                    tiles_ref[device, pl.ds(2 * comp + within, 1), :] * KAPPA for comp in range(3)
                ]
                partners.append((rows, bias_s[0, entry]))
            for group in range(0, LANES, 8):
                own = [spread_own[3 * block + comp, group : group + 8, :] for comp in range(3)]
                sums = [push[3 * block + comp, group : group + 8, :] for comp in range(3)]
                for rows, bias in partners:
                    offset = [own[comp] - rows[comp] for comp in range(3)]
                    power = bias - offset[0] * offset[0]
                    power = power - offset[1] * offset[1]
                    power = power - offset[2] * offset[2]
                    weight = jnp.exp2(power)
                    sums = [sums[comp] + weight * offset[comp] for comp in range(3)]
                for comp in range(3):
                    push[3 * block + comp, group : group + 8, :] = sums[comp]
            return carry

        lax.fori_loop(0, (list_s[1, block * 64] + 1) // 2, one_pair, 0)
        rows = [jnp.sum(push[3 * block + comp].T, axis=0, keepdims=True) for comp in range(3)]
        clash = jnp.concatenate(rows + [jnp.zeros((5, LANES), f32)], axis=0)
        forces.append(clash * (8.0 / KAPPA))
    out_ref[...] = bond_ref[...] + jnp.concatenate(forces, axis=1)


def start_copies(sources, targets, sems):
    copies = [
        pltpu.make_async_copy(source, target, sems.at[index])
        for index, (source, target) in enumerate(zip(sources, targets))
    ]
    for copy in copies:
        copy.start()
    return copies


def prepare_kernel(*refs):
    first_ref, count_ref, sources = refs[0], refs[1], refs[2:9]
    stream_ref, normed_ref, rows_ref, packed_ref = refs[9:13]
    targets, tile_ref, sems = refs[13:20], refs[20], refs[21]
    time_ref, positions_ref, single_ref, pos_weight_ref, gain_ref, pairs_ref, window_ref = targets
    for copy in start_copies(sources, targets, sems):
        copy.wait()
    level = 0.2 + 0.02 * jnp.full((1, ROWS), time_ref[0], jnp.int32).astype(f32)
    spread_sq = level * level + 1.0
    c_input = 1.0 / jnp.sqrt(spread_sq)
    window = window_ref[...]
    own = first_ref[0] * 2 + lax.broadcasted_iota(jnp.int32, window.shape, 0)
    lane = lax.broadcasted_iota(jnp.int32, (1, ROWS), 1)
    counts = jnp.zeros((1, ROWS), f32)
    for offset in range(5):
        hit = jnp.sum((window == own + (offset - 2)).astype(f32), axis=1, keepdims=True)
        counts = jnp.where(lane == offset, hit[0:1], counts)
        counts = jnp.where(lane == 8 + offset, hit[1:2], counts)
    counts = jnp.where(counts > 0.0, jnp.log2(jnp.maximum(counts, 1.0)), ABSENT)
    gain_rows = [
        jnp.concatenate([gain_ref[layer, 0:1], gain_ref[layer, 1:2]], axis=1) for layer in range(2)
    ]
    rows_ref[...] = jnp.concatenate(
        [level, spread_sq, c_input] + gain_rows + [counts, jnp.zeros((2, ROWS), f32)], axis=0
    )
    for row in range(6):
        part = slice((row % 2) * LANES, (row % 2 + 1) * LANES)
        tile_ref[row : row + 1, :] = positions_ref[row // 2 : row // 2 + 1, part]
    pairs = pairs_ref[...]
    lane = lax.broadcasted_iota(jnp.int32, (1, pairs.shape[1]), 1)
    codes = jnp.where(lane < count_ref[0], pairs[0:1] * 64 + pairs[1:2], -1).astype(f32)
    tile_ref[6:7, :] = jnp.concatenate([codes, codes], axis=1)
    tile_ref[7:8, :] = jnp.zeros((1, LANES), f32)
    packed_ref[...] = jnp.broadcast_to(tile_ref[...][None], packed_ref.shape)
    columns = jnp.concatenate(
        [pos_weight_ref[...], gain_ref[0, 0:1], jnp.zeros((4, LANES), f32)], axis=0
    ).T
    identity = (
        lax.broadcasted_iota(jnp.int32, (LANES, LANES), 0)
        == lax.broadcasted_iota(jnp.int32, (LANES, LANES), 1)
    ).astype(f32).astype(bf16)
    stream = dot_nt(identity, single_ref[...])
    for comp in range(3):
        stream = stream + columns[:, comp : comp + 1] * (positions_ref[comp : comp + 1, :] * c_input)
    stream_ref[...] = stream
    normed_ref[...] = (norm_columns(stream) * columns[:, 3:4]).astype(bf16).T


def layer_values(layer, first_ref, halo, stream_ref, rows_ref, head_rows, weights, scratch):
    even_ref, own_ref, odd_ref = halo
    w_query_ref, w_key_ref, w_value_ref, w_out_ref, w_gate_up_ref, w_down_ref = weights
    near, keys, values, attended = scratch
    head_size = LANES // HEADS
    query_scale = LOG2E * head_size ** -0.5
    near[ROWS : 2 * ROWS, :] = own_ref[...]

    @pl.when(first_ref[0] % 2 == 0)
    def _():
        near[:ROWS, :] = odd_ref[...]
        near[2 * ROWS :, :] = even_ref[...]

    @pl.when(first_ref[0] % 2 == 1)
    def _():
        near[:ROWS, :] = even_ref[...]
        near[2 * ROWS :, :] = odd_ref[...]

    row_block = lax.broadcasted_iota(jnp.int32, (3 * ROWS, LANES), 0) // LANES
    lane = lax.broadcasted_iota(jnp.int32, (3 * ROWS, LANES), 1)
    keys[:, LANES:] = jnp.where((lane % 16 == row_block) & (lane < 32), 1.0, 0.0).astype(bf16)
    window = rows_ref[5:6, :LANES]
    rows = []
    for chunk in range(6):
        sides = []
        for block in range(2):
            offset = chunk - block
            if 0 <= offset < 5:
                lane_id = block * 8 + offset
                sides.append(jnp.broadcast_to(window[:, lane_id : lane_id + 1], (1, LANES)))
            else:
                sides.append(jnp.full((1, LANES), ABSENT, f32))
        rows.append(jnp.concatenate(sides, axis=1))
    rows = jnp.concatenate(rows + [jnp.zeros((10, ROWS), f32)], axis=0)
    high = rows.astype(bf16)
    low = (rows - high.astype(f32)).astype(bf16)
    bias = jnp.concatenate([high, low, jnp.zeros((LANES - 32, ROWS), bf16)], axis=0)

    keys[:, :LANES] = dot(near[...], w_key_ref[layer]).astype(bf16)
    query_t = (dot_nt(w_query_ref[layer].T, own_ref[...]) * query_scale).astype(bf16)
    value_t = dot_nt(w_value_ref[layer].T, near[...]).astype(bf16)
    for head in range(HEADS):
        values[head * 48 : head * 48 + 32, :] = value_t[head * 32 : head * 32 + 32]
        values[head * 48 + 32 : head * 48 + 48, :] = jnp.ones((16, 3 * ROWS), bf16)

    def attend(exact):
        pieces = []
        sums = []

        def scores_of(head):
            parts = []
            if head:
                parts.append(jnp.zeros((head * head_size, ROWS), bf16))
            parts.append(query_t[head * head_size : (head + 1) * head_size])
            if head < HEADS - 1:
                parts.append(jnp.zeros(((HEADS - 1 - head) * head_size, ROWS), bf16))
            return dot(keys[...], jnp.concatenate(parts + [bias], axis=0))

        following = scores_of(0)
        for head in range(HEADS):
            scores = following
            if head < HEADS - 1:
                following = scores_of(head + 1)
            if exact:
                scores = scores - jnp.max(scores, axis=0, keepdims=True)
            blank = jnp.zeros((LANES, LANES), bf16)
            weights_t = jnp.concatenate(
                [
                    jnp.concatenate([jnp.exp2(scores[: 5 * LANES, :LANES]).astype(bf16), blank], axis=0),
                    jnp.concatenate([blank, jnp.exp2(scores[LANES:, LANES:]).astype(bf16)], axis=0),
                ],
                axis=1,
            )
            mixed = dot(values[head * 48 : (head + 1) * 48, :], weights_t)
            total = mixed[head_size : head_size + 1]
            sums.append(total)
            pieces.append(mixed[:head_size] * (1.0 / total))
        attended[...] = jnp.concatenate(pieces, axis=0).astype(bf16)
        return jnp.concatenate(sums, axis=0)

    sums = attend(False)
    safe = (jnp.min(sums) > 2.0**-80) & (jnp.max(sums) < 2.0**100)

    @pl.when(jnp.logical_not(safe))
    def _():
        attend(True)

    gains = jnp.concatenate(
        [rows_ref[3 + index // 2 : 4 + index // 2, (index % 2) * LANES : (index % 2 + 1) * LANES] for index in range(4)]
        + [head_rows],
        axis=0,
    ).T
    now = stream_ref[...] + dot(w_out_ref[layer].T, attended[...])
    normed = (norm_columns(now) * gains[:, 2 * layer + 1 : 2 * layer + 2]).astype(bf16)
    gate_up = dot(w_gate_up_ref[layer].T, normed)
    width = gate_up.shape[0] // 2
    half, up = 0.5 * gate_up[:width], gate_up[width:]
    hidden = ((half + half * jnp.tanh(half)) * up).astype(bf16)
    return now + dot(w_down_ref[layer].T, hidden), gains


def first_layer_kernel(first_ref, even_ref, own_ref, odd_ref, stream_ref, rows_ref, *refs):
    weights, (out_ref, normed_ref), scratch = refs[:6], refs[7:9], refs[9:]
    stream, gains = layer_values(
        0, first_ref, (even_ref, own_ref, odd_ref), stream_ref, rows_ref, jnp.zeros((4, LANES), f32), weights, scratch
    )
    out_ref[...] = stream
    normed_ref[...] = (norm_columns(stream) * gains[:, 2:3]).astype(bf16).T


def last_layer_kernel(first_ref, even_ref, own_ref, odd_ref, stream_ref, rows_ref, *refs):
    weights, (positions_ref, noise_ref, force_ref, w_head_ref) = refs[:6], refs[6:10]
    out_ref, scratch = refs[10], refs[11:]
    head_rows = jnp.concatenate([w_head_ref[...], jnp.zeros((1, LANES), f32)], axis=0)
    stream, columns = layer_values(
        1, first_ref, (even_ref, own_ref, odd_ref), stream_ref, rows_ref, head_rows, weights, scratch
    )
    final = norm_columns(stream)
    update = jnp.concatenate(
        [jnp.sum(columns[:, 4 + comp : 5 + comp] * final, axis=0, keepdims=True) for comp in range(3)]
        + [jnp.zeros((5, ROWS), f32)],
        axis=0,
    )
    level, spread_sq, c_input = rows_ref[0:1], rows_ref[1:2], rows_ref[2:3]
    positions = jnp.concatenate([positions_ref[...], jnp.zeros((5, ROWS), f32)], axis=0)
    fresh = jnp.concatenate([noise_ref[...], jnp.zeros((5, ROWS), f32)], axis=0)
    denoised = positions * (1.0 / spread_sq) + (level * c_input) * update
    following = 0.85 * level
    result = denoised + STEER * force_ref[...] + following * (0.8 * (positions - denoised) / level + 0.6 * fresh)
    out_ref[...] = result[:3]


def body(
    positions,
    fresh_noise,
    timestep,
    atom_single,
    pos_weight,
    ln_gain,
    w_query,
    w_key,
    w_value,
    w_out,
    w_gate_up,
    w_down,
    w_head,
    key_window,
    block_pairs,
    pair_count,
    bond_atoms,
):
    devices = lax.axis_size("atom")
    first = lax.axis_index("atom").astype(jnp.int32).reshape(1)
    smem = pl.BlockSpec(memory_space=pltpu.SMEM)
    vmem = pl.BlockSpec(memory_space=pltpu.VMEM)
    hbm = pl.BlockSpec(memory_space=pltpu.HBM)
    rows = atom_single.shape[0]

    even_pairs = [(i, i ^ 1) for i in range(devices)]
    odd_pairs = [(i, ((i + 1) ^ 1) - 1) for i in range(1, devices - 1)]

    stream, normed, schedule, packed = pl.pallas_call(
        prepare_kernel,
        out_shape=(
            jax.ShapeDtypeStruct((LANES, rows), f32),
            jax.ShapeDtypeStruct((rows, LANES), bf16),
            jax.ShapeDtypeStruct((8, rows), f32),
            jax.ShapeDtypeStruct((devices, 8, LANES), f32),
        ),
        in_specs=[smem, smem] + [hbm] * 7,
        out_specs=(vmem,) * 4,
        scratch_shapes=[
            pltpu.SMEM(timestep.shape, jnp.int32),
            pltpu.VMEM(positions.shape, f32),
            pltpu.VMEM(atom_single.shape, bf16),
            pltpu.VMEM(pos_weight.shape, f32),
            pltpu.VMEM(ln_gain.shape, f32),
            pltpu.VMEM(block_pairs.shape, jnp.int32),
            pltpu.VMEM(key_window.shape, jnp.int32),
            pltpu.VMEM((8, LANES), f32),
            pltpu.SemaphoreType.DMA((7,)),
        ],
        compiler_params=pltpu.CompilerParams(vmem_limit_bytes=VMEM_GRANT),
    )(first, pair_count, timestep, positions, atom_single, pos_weight, ln_gain, block_pairs, key_window)
    even = lax.ppermute(normed, "atom", even_pairs)

    tiles = lax.all_to_all(packed, "atom", 0, 0)
    bond_force = pl.pallas_call(
        bond_kernel,
        out_shape=jax.ShapeDtypeStruct((8, rows), f32),
        in_specs=[vmem] * 2,
        out_specs=vmem,
        cost_estimate=pl.CostEstimate(flops=40_000_000, bytes_accessed=10_000_000, transcendentals=1_000_000),
        compiler_params=pltpu.CompilerParams(vmem_limit_bytes=VMEM_SMALL),
    )(positions, bond_atoms)
    odd = lax.ppermute(normed, "atom", odd_pairs)

    weights = (w_query, w_key, w_value, w_out, w_gate_up, w_down)
    layer_scratch = [
        pltpu.VMEM((3 * rows, LANES), bf16),
        pltpu.VMEM((3 * rows, 2 * LANES), bf16),
        pltpu.VMEM((HEADS * 48, 3 * rows), bf16),
        pltpu.VMEM((LANES, rows), bf16),
    ]
    layer_cost = pl.CostEstimate(flops=2_000_000_000, bytes_accessed=20_000_000, transcendentals=2_000_000)
    stream, normed = pl.pallas_call(
        first_layer_kernel,
        out_shape=(
            jax.ShapeDtypeStruct((LANES, rows), f32),
            jax.ShapeDtypeStruct((rows, LANES), bf16),
        ),
        in_specs=[smem] + [vmem] * 12,
        out_specs=(vmem, vmem),
        scratch_shapes=layer_scratch,
        cost_estimate=layer_cost,
        compiler_params=pltpu.CompilerParams(vmem_limit_bytes=VMEM_SMALL),
    )(first, even, normed, odd, stream, schedule, *weights, bond_force)
    even = lax.ppermute(normed, "atom", even_pairs)
    odd = lax.ppermute(normed, "atom", odd_pairs)

    force = pl.pallas_call(
        force_kernel,
        out_shape=jax.ShapeDtypeStruct((8, 2 * LANES), f32),
        in_specs=[smem, vmem, vmem, vmem],
        out_specs=vmem,
        scratch_shapes=[
            pltpu.VMEM((6, LANES, LANES), f32),
            pltpu.VMEM((6, LANES, LANES), f32),
            pltpu.VMEM((8, LANES), jnp.int32),
            pltpu.VMEM((8, LANES), f32),
            pltpu.SMEM((8, LANES), jnp.int32),
            pltpu.SMEM((8, LANES), f32),
            pltpu.SemaphoreType.DMA((2,)),
        ],
        cost_estimate=pl.CostEstimate(flops=80_000_000, bytes_accessed=16_000_000, transcendentals=2_000_000),
        compiler_params=pltpu.CompilerParams(vmem_limit_bytes=VMEM_SMALL),
    )(first, tiles, positions, bond_force)

    return pl.pallas_call(
        last_layer_kernel,
        out_shape=jax.ShapeDtypeStruct(positions.shape, f32),
        in_specs=[smem] + [vmem] * 15,
        out_specs=vmem,
        scratch_shapes=layer_scratch,
        cost_estimate=layer_cost,
        compiler_params=pltpu.CompilerParams(vmem_limit_bytes=VMEM_SMALL),
    )(
        first,
        even,
        normed,
        odd,
        stream,
        schedule,
        *weights,
        positions,
        fresh_noise,
        force,
        w_head,
    )


def solution(mesh):
    in_specs = (
        P(None, ("sample", "atom")),
        P(None, ("sample", "atom")),
        P(),
        P("atom", None),
        P(),
        P(),
        P(),
        P(),
        P(),
        P(),
        P(),
        P(),
        P(),
        P("atom", None),
        P(None, "atom"),
        P("atom"),
        P(None, "atom", None),
    )
    out_specs = P(None, ("sample", "atom"))
    return jax.shard_map(body, mesh=mesh, in_specs=in_specs, out_specs=out_specs, check_vma=False)
```

```python
import functools
import math

import jax
import jax.numpy as jnp
from jax import lax
from jax.experimental import pallas as pl
from jax.experimental.pallas import tpu as pltpu
from jax.sharding import PartitionSpec as P

HEADS = 4
LANES = 128
ROWS = 256
VMEM_GRANT = 60 * 1024 * 1024
VMEM_SMALL = 16 * 1024 * 1024
NORM_EPS = 1e-05
STEER = 0.3
ABSENT = -(2.0**120)
LOG2E = 1.4426950408889634
KAPPA = 2.0 * math.sqrt(LOG2E)

f32 = jnp.float32
bf16 = jnp.bfloat16


def pack_kernel(count_ref, tile_ref, out_ref):
    shape = tile_ref.shape
    row = lax.broadcasted_iota(jnp.int32, shape, 0)
    lane = lax.broadcasted_iota(jnp.int32, shape, 1)
    dead = (row == 6) & (lane % 64 >= count_ref[0])
    out_ref[...] = jnp.broadcast_to(jnp.where(dead, -1.0, tile_ref[...])[None], out_ref.shape)


def split3(values):
    high = values.astype(bf16)
    rest = values - high.astype(f32)
    mid = rest.astype(bf16)
    low = (rest - mid.astype(f32)).astype(bf16)
    return jnp.concatenate([high, mid, low], axis=0)


def join3(values):
    rows = values.shape[0] // 3
    return values[:rows] + values[rows : 2 * rows] + values[2 * rows :]


def norm_columns(values):
    center = values - jnp.mean(values, axis=0, keepdims=True)
    spread = jnp.mean(center * center, axis=0, keepdims=True)
    return center * lax.rsqrt(spread + NORM_EPS)


def dot_t(left, right):
    return lax.dot_general(left, right, (((0,), (0,)), ((), ())), preferred_element_type=f32)


def dot_nt(left, right):
    return lax.dot_general(left, right, (((1,), (1,)), ((), ())), preferred_element_type=f32)


def dot(left, right):
    return jnp.dot(left, right, preferred_element_type=f32)


def force_kernel(first_ref, tiles_ref, positions_ref, bonds_ref, out_ref, spread_own, push, list_v, bias_v, list_s, bias_s, sems):
    me = first_ref[0]

    codes = tiles_ref[:, 6, :].astype(jnp.int32)
    half = lax.broadcasted_iota(jnp.int32, codes.shape, 1) // 64
    mine = me * 2 + half
    first = jnp.where(codes < 0, -1, codes // 64)
    second = jnp.where(codes < 0, -1, codes % 64)
    partner = jnp.where(first == mine, second, jnp.where(second == mine, first, -1)).astype(f32)
    block_id = lax.broadcasted_iota(jnp.int32, (64, LANES), 0).astype(f32)
    hits = jnp.zeros((64, LANES), f32)
    for row in range(codes.shape[0]):
        hits = hits + jnp.where(partner[row : row + 1] == block_id, 1.0, 0.0)
    row_half = lax.broadcasted_iota(jnp.int32, (LANES, LANES), 0) // 64
    col_half = lax.broadcasted_iota(jnp.int32, (LANES, LANES), 1) // 64
    count = dot(hits.astype(bf16), (row_half == col_half).astype(bf16))
    present = count > 0.5
    lower = lax.broadcasted_iota(jnp.int32, (64, 64), 1) < lax.broadcasted_iota(jnp.int32, (64, 64), 0)
    rank = dot(lower.astype(bf16), present.astype(bf16))
    slot = (lax.broadcasted_iota(jnp.int32, (64, LANES), 1) % 64).astype(f32)
    chosen = present & (rank == slot)
    listed = jnp.sum(jnp.where(chosen, block_id, 0.0), axis=0, keepdims=True)
    times = jnp.sum(jnp.where(chosen, count, 0.0), axis=0, keepdims=True)
    total = jnp.sum(present.astype(f32), axis=0, keepdims=True)
    list_v[0:1, :] = listed.astype(jnp.int32)
    list_v[1:2, :] = total.astype(jnp.int32)
    bias_v[0:1, :] = jnp.where(times > 0.5, jnp.log2(jnp.maximum(times, 1.0)), ABSENT)
    list_copy = pltpu.make_async_copy(list_v, list_s, sems.at[0])
    bias_copy = pltpu.make_async_copy(bias_v, bias_s, sems.at[1])
    list_copy.start()
    bias_copy.start()

    for block in range(2):
        for comp in range(3):
            row = positions_ref[comp : comp + 1, block * LANES : (block + 1) * LANES] * KAPPA
            spread_own[3 * block + comp] = jnp.broadcast_to(row, (LANES, LANES)).T
            push[3 * block + comp] = jnp.zeros((LANES, LANES), f32)

    positions = jnp.concatenate([positions_ref[...], jnp.zeros((5, 2 * LANES), f32)], axis=0)

    forces = []
    atom_id = lax.broadcasted_iota(jnp.int32, (LANES, LANES), 0)
    for block in range(2):
        incidence = (
            (atom_id == bonds_ref[0, block : block + 1, :]).astype(f32)
            - (atom_id == bonds_ref[1, block : block + 1, :]).astype(f32)
        ).astype(bf16)
        offset = join3(dot(split3(positions[:, block * LANES : (block + 1) * LANES]), incidence))
        stretch = jnp.sum(offset * offset, axis=0, keepdims=True) - 1.0
        pull = (-0.2 * stretch) * offset
        forces.append(join3(dot_nt(split3(pull), incidence)))

    list_copy.wait()
    bias_copy.wait()
    for block in range(2):

        def one_pair(index, carry, block=block):
            partners = []
            for sub in range(2):
                entry = block * 64 + 2 * index + sub
                partner = list_s[0, entry]
                device = partner // 2
                within = partner % 2
                rows = [
                    tiles_ref[device, pl.ds(2 * comp + within, 1), :] * KAPPA for comp in range(3)
                ]
                partners.append((rows, bias_s[0, entry]))
            for group in range(0, LANES, 8):
                own = [spread_own[3 * block + comp, group : group + 8, :] for comp in range(3)]
                sums = [push[3 * block + comp, group : group + 8, :] for comp in range(3)]
                for rows, bias in partners:
                    offset = [own[comp] - rows[comp] for comp in range(3)]
                    power = bias - offset[0] * offset[0]
                    power = power - offset[1] * offset[1]
                    power = power - offset[2] * offset[2]
                    weight = jnp.exp2(power)
                    sums = [sums[comp] + weight * offset[comp] for comp in range(3)]
                for comp in range(3):
                    push[3 * block + comp, group : group + 8, :] = sums[comp]
            return carry

        lax.fori_loop(0, (list_s[1, block * 64] + 1) // 2, one_pair, 0)
        rows = [jnp.sum(push[3 * block + comp].T, axis=0, keepdims=True) for comp in range(3)]
        clash = jnp.concatenate(rows + [jnp.zeros((5, LANES), f32)], axis=0)
        forces[block] = forces[block] + clash * (8.0 / KAPPA)
    out_ref[...] = jnp.concatenate(forces, axis=1)


def start_copies(sources, targets, sems):
    copies = [
        pltpu.make_async_copy(source, target, sems.at[index])
        for index, (source, target) in enumerate(zip(sources, targets))
    ]
    for copy in copies:
        copy.start()
    return copies


def prepare_kernel(*refs):
    first_ref, sources, (stream_ref, normed_ref, rows_ref, tile_ref) = refs[0], refs[1:8], refs[8:12]
    targets, sems = refs[12:19], refs[19]
    time_ref, positions_ref, single_ref, pos_weight_ref, gain_ref, pairs_ref, window_ref = targets
    for copy in start_copies(sources, targets, sems):
        copy.wait()
    level = 0.2 + 0.02 * jnp.full((1, ROWS), time_ref[0], jnp.int32).astype(f32)
    spread_sq = level * level + 1.0
    c_input = 1.0 / jnp.sqrt(spread_sq)
    window = window_ref[...]
    own = first_ref[0] * 2 + lax.broadcasted_iota(jnp.int32, window.shape, 0)
    lane = lax.broadcasted_iota(jnp.int32, (1, ROWS), 1)
    counts = jnp.zeros((1, ROWS), f32)
    for offset in range(5):
        hit = jnp.sum((window == own + (offset - 2)).astype(f32), axis=1, keepdims=True)
        counts = jnp.where(lane == offset, hit[0:1], counts)
        counts = jnp.where(lane == 8 + offset, hit[1:2], counts)
    counts = jnp.where(counts > 0.0, jnp.log2(jnp.maximum(counts, 1.0)), ABSENT)
    gain_rows = [
        jnp.concatenate([gain_ref[layer, 0:1], gain_ref[layer, 1:2]], axis=1) for layer in range(2)
    ]
    rows_ref[...] = jnp.concatenate(
        [level, spread_sq, c_input] + gain_rows + [counts, jnp.zeros((2, ROWS), f32)], axis=0
    )
    for row in range(6):
        part = slice((row % 2) * LANES, (row % 2 + 1) * LANES)
        tile_ref[row : row + 1, :] = positions_ref[row // 2 : row // 2 + 1, part]
    pairs = pairs_ref[...]
    codes = (pairs[0:1] * 64 + pairs[1:2]).astype(f32)
    tile_ref[6:7, :] = jnp.concatenate([codes, codes], axis=1)
    tile_ref[7:8, :] = jnp.zeros((1, LANES), f32)
    columns = jnp.concatenate(
        [pos_weight_ref[...], gain_ref[0, 0:1], jnp.zeros((4, LANES), f32)], axis=0
    ).T
    identity = (
        lax.broadcasted_iota(jnp.int32, (LANES, LANES), 0)
        == lax.broadcasted_iota(jnp.int32, (LANES, LANES), 1)
    ).astype(f32).astype(bf16)
    stream = dot_nt(identity, single_ref[...])
    for comp in range(3):
        stream = stream + columns[:, comp : comp + 1] * (positions_ref[comp : comp + 1, :] * c_input)
    stream_ref[...] = stream
    normed_ref[...] = (norm_columns(stream) * columns[:, 3:4]).astype(bf16).T


def layer_values(layer, first_ref, halo, stream_ref, rows_ref, head_rows, weights, scratch):
    even_ref, own_ref, odd_ref = halo
    w_query_ref, w_key_ref, w_value_ref, w_out_ref, w_gate_up_ref, w_down_ref = weights
    near, keys, values, attended = scratch
    head_size = LANES // HEADS
    query_scale = LOG2E * head_size ** -0.5
    near[ROWS : 2 * ROWS, :] = own_ref[...]

    @pl.when(first_ref[0] % 2 == 0)
    def _():
        near[:ROWS, :] = odd_ref[...]
        near[2 * ROWS :, :] = even_ref[...]

    @pl.when(first_ref[0] % 2 == 1)
    def _():
        near[:ROWS, :] = even_ref[...]
        near[2 * ROWS :, :] = odd_ref[...]

    row_block = lax.broadcasted_iota(jnp.int32, (3 * ROWS, LANES), 0) // LANES
    lane = lax.broadcasted_iota(jnp.int32, (3 * ROWS, LANES), 1)
    keys[:, LANES:] = jnp.where((lane % 16 == row_block) & (lane < 32), 1.0, 0.0).astype(bf16)
    window = rows_ref[5:6, :LANES]
    rows = []
    for chunk in range(6):
        sides = []
        for block in range(2):
            offset = chunk - block
            if 0 <= offset < 5:
                lane_id = block * 8 + offset
                sides.append(jnp.broadcast_to(window[:, lane_id : lane_id + 1], (1, LANES)))
            else:
                sides.append(jnp.full((1, LANES), ABSENT, f32))
        rows.append(jnp.concatenate(sides, axis=1))
    rows = jnp.concatenate(rows + [jnp.zeros((10, ROWS), f32)], axis=0)
    high = rows.astype(bf16)
    low = (rows - high.astype(f32)).astype(bf16)
    bias = jnp.concatenate([high, low, jnp.zeros((LANES - 32, ROWS), bf16)], axis=0)

    keys[:, :LANES] = dot(near[...], w_key_ref[layer]).astype(bf16)
    query_t = (dot_nt(w_query_ref[layer].T, own_ref[...]) * query_scale).astype(bf16)
    value_t = dot_nt(w_value_ref[layer].T, near[...]).astype(bf16)
    for head in range(HEADS):
        values[head * 48 : head * 48 + 32, :] = value_t[head * 32 : head * 32 + 32]
        values[head * 48 + 32 : head * 48 + 48, :] = jnp.ones((16, 3 * ROWS), bf16)

    def attend(exact):
        pieces = []
        sums = []

        def scores_of(head):
            parts = []
            if head:
                parts.append(jnp.zeros((head * head_size, ROWS), bf16))
            parts.append(query_t[head * head_size : (head + 1) * head_size])
            if head < HEADS - 1:
                parts.append(jnp.zeros(((HEADS - 1 - head) * head_size, ROWS), bf16))
            return dot(keys[...], jnp.concatenate(parts + [bias], axis=0))

        following = scores_of(0)
        for head in range(HEADS):
            scores = following
            if head < HEADS - 1:
                following = scores_of(head + 1)
            if exact:
                scores = scores - jnp.max(scores, axis=0, keepdims=True)
            blank = jnp.zeros((LANES, LANES), bf16)
            weights_t = jnp.concatenate(
                [
                    jnp.concatenate([jnp.exp2(scores[: 5 * LANES, :LANES]).astype(bf16), blank], axis=0),
                    jnp.concatenate([blank, jnp.exp2(scores[LANES:, LANES:]).astype(bf16)], axis=0),
                ],
                axis=1,
            )
            mixed = dot(values[head * 48 : (head + 1) * 48, :], weights_t)
            total = mixed[head_size : head_size + 1]
            sums.append(total)
            pieces.append(mixed[:head_size] * (1.0 / total))
        attended[...] = jnp.concatenate(pieces, axis=0).astype(bf16)
        return jnp.concatenate(sums, axis=0)

    sums = attend(False)
    safe = (jnp.min(sums) > 2.0**-80) & (jnp.max(sums) < 2.0**100)

    @pl.when(jnp.logical_not(safe))
    def _():
        attend(True)

    gains = jnp.concatenate(
        [rows_ref[3 + index // 2 : 4 + index // 2, (index % 2) * LANES : (index % 2 + 1) * LANES] for index in range(4)]
        + [head_rows],
        axis=0,
    ).T
    now = stream_ref[...] + dot(w_out_ref[layer].T, attended[...])
    normed = (norm_columns(now) * gains[:, 2 * layer + 1 : 2 * layer + 2]).astype(bf16)
    gate_up = dot(w_gate_up_ref[layer].T, normed)
    width = gate_up.shape[0] // 2
    half, up = 0.5 * gate_up[:width], gate_up[width:]
    hidden = ((half + half * jnp.tanh(half)) * up).astype(bf16)
    return now + dot(w_down_ref[layer].T, hidden), gains


def first_layer_kernel(first_ref, even_ref, own_ref, odd_ref, stream_ref, rows_ref, *refs):
    weights, (out_ref, normed_ref), scratch = refs[:6], refs[6:8], refs[8:]
    stream, gains = layer_values(
        0, first_ref, (even_ref, own_ref, odd_ref), stream_ref, rows_ref, jnp.zeros((4, LANES), f32), weights, scratch
    )
    out_ref[...] = stream
    normed_ref[...] = (norm_columns(stream) * gains[:, 2:3]).astype(bf16).T


def ready_kernel(own_ref, rows_ref, w_query_ref, w_key_ref, w_value_ref, w_out_ref, w_gate_up_ref, w_down_ref, *refs):
    marks_ref, bias_ref, query_ref, key_ref, value_ref, value_w, out_w, gate_up_w, down_w = refs
    layer = 1
    query_scale = LOG2E * (LANES // HEADS) ** -0.5
    row_block = lax.broadcasted_iota(jnp.int32, (3 * ROWS, LANES), 0) // LANES
    lane = lax.broadcasted_iota(jnp.int32, (3 * ROWS, LANES), 1)
    marks_ref[...] = jnp.where((lane % 16 == row_block) & (lane < 32), 1.0, 0.0).astype(bf16)
    window = rows_ref[5:6, :LANES]
    rows = []
    for chunk in range(6):
        sides = []
        for block in range(2):
            offset = chunk - block
            if 0 <= offset < 5:
                lane_id = block * 8 + offset
                sides.append(jnp.broadcast_to(window[:, lane_id : lane_id + 1], (1, LANES)))
            else:
                sides.append(jnp.full((1, LANES), ABSENT, f32))
        rows.append(jnp.concatenate(sides, axis=1))
    rows = jnp.concatenate(rows + [jnp.zeros((10, ROWS), f32)], axis=0)
    high = rows.astype(bf16)
    low = (rows - high.astype(f32)).astype(bf16)
    bias_ref[...] = jnp.concatenate([high, low, jnp.zeros((LANES - 32, ROWS), bf16)], axis=0)
    value_w[...] = w_value_ref[layer].T
    out_w[...] = w_out_ref[layer].T
    gate_up_w[...] = w_gate_up_ref[layer].T
    down_w[...] = w_down_ref[layer].T
    key_ref[...] = dot(own_ref[...], w_key_ref[layer]).astype(bf16)
    query_ref[...] = (dot_nt(w_query_ref[layer].T, own_ref[...]) * query_scale).astype(bf16)
    value_ref[...] = dot_nt(value_w[...], own_ref[...]).astype(bf16)


def last_layer_kernel(first_ref, even_ref, odd_ref, stream_ref, rows_ref, w_key_ref, *refs):
    marks_ref, bias_ref, query_ref, key_ref, value_ref, value_w, out_w, gate_up_w, down_w = refs[:9]
    positions_ref, noise_ref, force_ref, w_head_ref, out_ref = refs[9:14]
    near, keys, values, attended = refs[14:]
    layer = 1
    head_size = LANES // HEADS
    left, own, right = (slice(place * ROWS, (place + 1) * ROWS) for place in range(3))

    @pl.when(first_ref[0] % 2 == 0)
    def _():
        near[:ROWS, :] = odd_ref[...]
        near[ROWS:, :] = even_ref[...]

    @pl.when(first_ref[0] % 2 == 1)
    def _():
        near[:ROWS, :] = even_ref[...]
        near[ROWS:, :] = odd_ref[...]

    keys[:, LANES:] = marks_ref[...]
    keys[own, :LANES] = key_ref[...]
    key_rows = dot(near[...], w_key_ref[layer]).astype(bf16)
    keys[left, :LANES] = key_rows[:ROWS]
    keys[right, :LANES] = key_rows[ROWS:]
    value_t = dot_nt(value_w[...], near[...]).astype(bf16)
    for head in range(HEADS):
        part = slice(head * 32, head * 32 + 32)
        rows = slice(head * 48, head * 48 + 32)
        values[rows, left] = value_t[part, :ROWS]
        values[rows, own] = value_ref[part, :]
        values[rows, right] = value_t[part, ROWS:]
        values[head * 48 + 32 : head * 48 + 48, :] = jnp.ones((16, 3 * ROWS), bf16)

    def attend(exact):
        pieces = []
        sums = []

        def scores_of(head):
            parts = []
            if head:
                parts.append(jnp.zeros((head * head_size, ROWS), bf16))
            parts.append(query_ref[head * head_size : (head + 1) * head_size])
            if head < HEADS - 1:
                parts.append(jnp.zeros(((HEADS - 1 - head) * head_size, ROWS), bf16))
            return dot(keys[...], jnp.concatenate(parts + [bias_ref[...]], axis=0))

        following = scores_of(0)
        for head in range(HEADS):
            scores = following
            if head < HEADS - 1:
                following = scores_of(head + 1)
            if exact:
                scores = scores - jnp.max(scores, axis=0, keepdims=True)
            blank = jnp.zeros((LANES, LANES), bf16)
            weights_t = jnp.concatenate(
                [
                    jnp.concatenate([jnp.exp2(scores[: 5 * LANES, :LANES]).astype(bf16), blank], axis=0),
                    jnp.concatenate([blank, jnp.exp2(scores[LANES:, LANES:]).astype(bf16)], axis=0),
                ],
                axis=1,
            )
            mixed = dot(values[head * 48 : (head + 1) * 48, :], weights_t)
            total = mixed[head_size : head_size + 1]
            sums.append(total)
            pieces.append(mixed[:head_size] * (1.0 / total))
        attended[...] = jnp.concatenate(pieces, axis=0).astype(bf16)
        return jnp.concatenate(sums, axis=0)

    sums = attend(False)
    safe = (jnp.min(sums) > 2.0**-80) & (jnp.max(sums) < 2.0**100)

    @pl.when(jnp.logical_not(safe))
    def _():
        attend(True)

    columns = jnp.concatenate(
        [rows_ref[3 + index // 2 : 4 + index // 2, (index % 2) * LANES : (index % 2 + 1) * LANES] for index in range(4)]
        + [w_head_ref[...], jnp.zeros((1, LANES), f32)],
        axis=0,
    ).T
    now = stream_ref[...] + dot(out_w[...], attended[...])
    normed = (norm_columns(now) * columns[:, 2 * layer + 1 : 2 * layer + 2]).astype(bf16)
    gate_up = dot(gate_up_w[...], normed)
    width = gate_up.shape[0] // 2
    half, up = 0.5 * gate_up[:width], gate_up[width:]
    hidden = ((half + half * jnp.tanh(half)) * up).astype(bf16)
    stream = now + dot(down_w[...], hidden)
    final = norm_columns(stream)
    update = jnp.concatenate(
        [jnp.sum(columns[:, 4 + comp : 5 + comp] * final, axis=0, keepdims=True) for comp in range(3)]
        + [jnp.zeros((5, ROWS), f32)],
        axis=0,
    )
    level, spread_sq, c_input = rows_ref[0:1], rows_ref[1:2], rows_ref[2:3]
    positions = jnp.concatenate([positions_ref[...], jnp.zeros((5, ROWS), f32)], axis=0)
    fresh = jnp.concatenate([noise_ref[...], jnp.zeros((5, ROWS), f32)], axis=0)
    denoised = positions * (1.0 / spread_sq) + (level * c_input) * update
    following = 0.85 * level
    result = denoised + STEER * force_ref[...] + following * (0.8 * (positions - denoised) / level + 0.6 * fresh)
    out_ref[...] = result[:3]


def body(
    positions,
    fresh_noise,
    timestep,
    atom_single,
    pos_weight,
    ln_gain,
    w_query,
    w_key,
    w_value,
    w_out,
    w_gate_up,
    w_down,
    w_head,
    key_window,
    block_pairs,
    pair_count,
    bond_atoms,
):
    devices = lax.axis_size("atom")
    first = lax.axis_index("atom").astype(jnp.int32).reshape(1)
    smem = pl.BlockSpec(memory_space=pltpu.SMEM)
    vmem = pl.BlockSpec(memory_space=pltpu.VMEM)
    hbm = pl.BlockSpec(memory_space=pltpu.HBM)
    rows = atom_single.shape[0]

    def from_neighbours(array):
        even = [(i, i ^ 1) for i in range(devices)]
        odd = [(i, ((i + 1) ^ 1) - 1) for i in range(1, devices - 1)]
        return lax.ppermute(array, "atom", even), lax.ppermute(array, "atom", odd)

    stream, normed, schedule, tile = pl.pallas_call(
        prepare_kernel,
        out_shape=(
            jax.ShapeDtypeStruct((LANES, rows), f32),
            jax.ShapeDtypeStruct((rows, LANES), bf16),
            jax.ShapeDtypeStruct((8, rows), f32),
            jax.ShapeDtypeStruct((8, LANES), f32),
        ),
        in_specs=[smem] + [hbm] * 7,
        out_specs=(vmem,) * 4,
        scratch_shapes=[
            pltpu.SMEM(timestep.shape, jnp.int32),
            pltpu.VMEM(positions.shape, f32),
            pltpu.VMEM(atom_single.shape, bf16),
            pltpu.VMEM(pos_weight.shape, f32),
            pltpu.VMEM(ln_gain.shape, f32),
            pltpu.VMEM(block_pairs.shape, jnp.int32),
            pltpu.VMEM(key_window.shape, jnp.int32),
            pltpu.SemaphoreType.DMA((7,)),
        ],
        compiler_params=pltpu.CompilerParams(vmem_limit_bytes=VMEM_GRANT),
    )(first, timestep, positions, atom_single, pos_weight, ln_gain, block_pairs, key_window)
    even, odd = from_neighbours(normed)

    packed = pl.pallas_call(
        pack_kernel,
        out_shape=jax.ShapeDtypeStruct((devices, 8, LANES), f32),
        in_specs=[smem, vmem],
        out_specs=vmem,
        cost_estimate=pl.CostEstimate(flops=40_000_000, bytes_accessed=10_000_000, transcendentals=1_000_000),
        compiler_params=pltpu.CompilerParams(vmem_limit_bytes=VMEM_SMALL),
    )(pair_count, tile)
    tiles = lax.all_to_all(packed, "atom", 0, 0)

    weights = (w_query, w_key, w_value, w_out, w_gate_up, w_down)
    layer_scratch = [
        pltpu.VMEM((3 * rows, LANES), bf16),
        pltpu.VMEM((3 * rows, 2 * LANES), bf16),
        pltpu.VMEM((HEADS * 48, 3 * rows), bf16),
        pltpu.VMEM((LANES, rows), bf16),
    ]
    layer_cost = pl.CostEstimate(flops=2_000_000_000, bytes_accessed=20_000_000, transcendentals=2_000_000)
    stream, normed = pl.pallas_call(
        first_layer_kernel,
        out_shape=(
            jax.ShapeDtypeStruct((LANES, rows), f32),
            jax.ShapeDtypeStruct((rows, LANES), bf16),
        ),
        in_specs=[smem] + [vmem] * 11,
        out_specs=(vmem, vmem),
        scratch_shapes=layer_scratch,
        cost_estimate=layer_cost,
        compiler_params=pltpu.CompilerParams(vmem_limit_bytes=VMEM_SMALL),
    )(first, even, normed, odd, stream, schedule, *weights)
    even, odd = from_neighbours(normed)

    force = pl.pallas_call(
        force_kernel,
        out_shape=jax.ShapeDtypeStruct((8, 2 * LANES), f32),
        in_specs=[smem, vmem, vmem, vmem],
        out_specs=vmem,
        scratch_shapes=[
            pltpu.VMEM((6, LANES, LANES), f32),
            pltpu.VMEM((6, LANES, LANES), f32),
            pltpu.VMEM((8, LANES), jnp.int32),
            pltpu.VMEM((8, LANES), f32),
            pltpu.SMEM((8, LANES), jnp.int32),
            pltpu.SMEM((8, LANES), f32),
            pltpu.SemaphoreType.DMA((2,)),
        ],
        cost_estimate=pl.CostEstimate(flops=80_000_000, bytes_accessed=16_000_000, transcendentals=2_000_000),
        compiler_params=pltpu.CompilerParams(vmem_limit_bytes=VMEM_SMALL),
    )(first, tiles, positions, bond_atoms)

    hidden_width = w_gate_up.shape[2]
    parts = pl.pallas_call(
        ready_kernel,
        out_shape=tuple(
            jax.ShapeDtypeStruct(shape, bf16)
            for shape in (
                (3 * rows, LANES),
                (LANES, rows),
                (LANES, rows),
                (rows, LANES),
                (LANES, rows),
                (LANES, LANES),
                (LANES, LANES),
                (hidden_width, LANES),
                (LANES, hidden_width // 2),
            )
        ),
        in_specs=[vmem] * 8,
        out_specs=(vmem,) * 9,
        cost_estimate=pl.CostEstimate(flops=40_000_000, bytes_accessed=10_000_000, transcendentals=1_000_000),
        compiler_params=pltpu.CompilerParams(vmem_limit_bytes=VMEM_SMALL),
    )(normed, schedule, *weights)
    return pl.pallas_call(
        last_layer_kernel,
        out_shape=jax.ShapeDtypeStruct(positions.shape, f32),
        in_specs=[smem] + [vmem] * 18,
        out_specs=vmem,
        scratch_shapes=[pltpu.VMEM((2 * rows, LANES), bf16)] + layer_scratch[1:],
        cost_estimate=layer_cost,
        compiler_params=pltpu.CompilerParams(vmem_limit_bytes=VMEM_SMALL),
    )(first, even, odd, stream, schedule, w_key, *parts, positions, fresh_noise, force, w_head)


def solution(mesh):
    in_specs = (
        P(None, ("sample", "atom")),
        P(None, ("sample", "atom")),
        P(),
        P("atom", None),
        P(),
        P(),
        P(),
        P(),
        P(),
        P(),
        P(),
        P(),
        P(),
        P("atom", None),
        P(None, "atom"),
        P("atom"),
        P(None, "atom", None),
    )
    out_specs = P(None, ("sample", "atom"))
    return jax.shard_map(body, mesh=mesh, in_specs=in_specs, out_specs=out_specs, check_vma=False)
```

```python
import functools
import math

import jax
import jax.numpy as jnp
from jax import lax
from jax.experimental import pallas as pl
from jax.experimental.pallas import tpu as pltpu
from jax.sharding import PartitionSpec as P

HEADS = 4
LANES = 128
ROWS = 256
VMEM_GRANT = 60 * 1024 * 1024
VMEM_SMALL = 16 * 1024 * 1024
NORM_EPS = 1e-05
STEER = 0.3
ABSENT = -(2.0**120)
LOG2E = 1.4426950408889634
KAPPA = 2.0 * math.sqrt(LOG2E)

f32 = jnp.float32
bf16 = jnp.bfloat16


def pack_kernel(count_ref, tile_ref, out_ref):
    shape = tile_ref.shape
    row = lax.broadcasted_iota(jnp.int32, shape, 0)
    lane = lax.broadcasted_iota(jnp.int32, shape, 1)
    dead = (row == 6) & (lane % 64 >= count_ref[0])
    out_ref[...] = jnp.broadcast_to(jnp.where(dead, -1.0, tile_ref[...])[None], out_ref.shape)


def split3(values):
    high = values.astype(bf16)
    rest = values - high.astype(f32)
    mid = rest.astype(bf16)
    low = (rest - mid.astype(f32)).astype(bf16)
    return jnp.concatenate([high, mid, low], axis=0)


def join3(values):
    rows = values.shape[0] // 3
    return values[:rows] + values[rows : 2 * rows] + values[2 * rows :]


def norm_columns(values):
    center = values - jnp.mean(values, axis=0, keepdims=True)
    spread = jnp.mean(center * center, axis=0, keepdims=True)
    return center * lax.rsqrt(spread + NORM_EPS)


def dot_t(left, right):
    return lax.dot_general(left, right, (((0,), (0,)), ((), ())), preferred_element_type=f32)


def dot_nt(left, right):
    return lax.dot_general(left, right, (((1,), (1,)), ((), ())), preferred_element_type=f32)


def dot(left, right):
    return jnp.dot(left, right, preferred_element_type=f32)


def force_kernel(first_ref, tiles_ref, positions_ref, bonds_ref, out_ref, spread_own, push, list_v, bias_v, list_s, bias_s, sems):
    me = first_ref[0]

    codes = tiles_ref[:, 6, :].astype(jnp.int32)
    half = lax.broadcasted_iota(jnp.int32, codes.shape, 1) // 64
    mine = me * 2 + half
    first = jnp.where(codes < 0, -1, codes // 64)
    second = jnp.where(codes < 0, -1, codes % 64)
    partner = jnp.where(first == mine, second, jnp.where(second == mine, first, -1)).astype(f32)
    block_id = lax.broadcasted_iota(jnp.int32, (64, LANES), 0).astype(f32)
    hits = jnp.zeros((64, LANES), f32)
    for row in range(codes.shape[0]):
        hits = hits + jnp.where(partner[row : row + 1] == block_id, 1.0, 0.0)
    row_half = lax.broadcasted_iota(jnp.int32, (LANES, LANES), 0) // 64
    col_half = lax.broadcasted_iota(jnp.int32, (LANES, LANES), 1) // 64
    count = dot(hits.astype(bf16), (row_half == col_half).astype(bf16))
    present = count > 0.5
    lower = lax.broadcasted_iota(jnp.int32, (64, 64), 1) < lax.broadcasted_iota(jnp.int32, (64, 64), 0)
    rank = dot(lower.astype(bf16), present.astype(bf16))
    slot = (lax.broadcasted_iota(jnp.int32, (64, LANES), 1) % 64).astype(f32)
    chosen = present & (rank == slot)
    listed = jnp.sum(jnp.where(chosen, block_id, 0.0), axis=0, keepdims=True)
    times = jnp.sum(jnp.where(chosen, count, 0.0), axis=0, keepdims=True)
    total = jnp.sum(present.astype(f32), axis=0, keepdims=True)
    list_v[0:1, :] = listed.astype(jnp.int32)
    list_v[1:2, :] = total.astype(jnp.int32)
    bias_v[0:1, :] = jnp.where(times > 0.5, jnp.log2(jnp.maximum(times, 1.0)), ABSENT)
    list_copy = pltpu.make_async_copy(list_v, list_s, sems.at[0])
    bias_copy = pltpu.make_async_copy(bias_v, bias_s, sems.at[1])
    list_copy.start()
    bias_copy.start()

    for block in range(2):
        for comp in range(3):
            row = positions_ref[comp : comp + 1, block * LANES : (block + 1) * LANES] * KAPPA
            spread_own[3 * block + comp] = jnp.broadcast_to(row, (LANES, LANES)).T
            push[3 * block + comp] = jnp.zeros((LANES, LANES), f32)

    positions = jnp.concatenate([positions_ref[...], jnp.zeros((5, 2 * LANES), f32)], axis=0)

    forces = []
    atom_id = lax.broadcasted_iota(jnp.int32, (LANES, LANES), 0)
    for block in range(2):
        incidence = (
            (atom_id == bonds_ref[0, block : block + 1, :]).astype(f32)
            - (atom_id == bonds_ref[1, block : block + 1, :]).astype(f32)
        ).astype(bf16)
        offset = join3(dot(split3(positions[:, block * LANES : (block + 1) * LANES]), incidence))
        stretch = jnp.sum(offset * offset, axis=0, keepdims=True) - 1.0
        pull = (-0.2 * stretch) * offset
        forces.append(join3(dot_nt(split3(pull), incidence)))

    list_copy.wait()
    bias_copy.wait()
    for block in range(2):

        def one_pair(index, carry, block=block):
            partners = []
            for sub in range(2):
                entry = block * 64 + 2 * index + sub
                partner = list_s[0, entry]
                device = partner // 2
                within = partner % 2
                rows = [
                    tiles_ref[device, pl.ds(2 * comp + within, 1), :] * KAPPA for comp in range(3)
                ]
                partners.append((rows, bias_s[0, entry]))
            for group in range(0, LANES, 8):
                own = [spread_own[3 * block + comp, group : group + 8, :] for comp in range(3)]
                sums = [push[3 * block + comp, group : group + 8, :] for comp in range(3)]
                for rows, bias in partners:
                    offset = [own[comp] - rows[comp] for comp in range(3)]
                    power = bias - offset[0] * offset[0]
                    power = power - offset[1] * offset[1]
                    power = power - offset[2] * offset[2]
                    weight = jnp.exp2(power)
                    sums = [sums[comp] + weight * offset[comp] for comp in range(3)]
                for comp in range(3):
                    push[3 * block + comp, group : group + 8, :] = sums[comp]
            return carry

        lax.fori_loop(0, (list_s[1, block * 64] + 1) // 2, one_pair, 0)
        rows = [jnp.sum(push[3 * block + comp].T, axis=0, keepdims=True) for comp in range(3)]
        clash = jnp.concatenate(rows + [jnp.zeros((5, LANES), f32)], axis=0)
        forces[block] = forces[block] + clash * (8.0 / KAPPA)
    out_ref[...] = jnp.concatenate(forces, axis=1)


def start_copies(sources, targets, sems):
    copies = [
        pltpu.make_async_copy(source, target, sems.at[index])
        for index, (source, target) in enumerate(zip(sources, targets))
    ]
    for copy in copies:
        copy.start()
    return copies


def prepare_kernel(*refs):
    first_ref, sources, (stream_ref, normed_ref, rows_ref, tile_ref) = refs[0], refs[1:8], refs[8:12]
    targets, sems = refs[12:19], refs[19]
    time_ref, positions_ref, single_ref, pos_weight_ref, gain_ref, pairs_ref, window_ref = targets
    for copy in start_copies(sources, targets, sems):
        copy.wait()
    level = 0.2 + 0.02 * jnp.full((1, ROWS), time_ref[0], jnp.int32).astype(f32)
    spread_sq = level * level + 1.0
    c_input = 1.0 / jnp.sqrt(spread_sq)
    window = window_ref[...]
    own = first_ref[0] * 2 + lax.broadcasted_iota(jnp.int32, window.shape, 0)
    lane = lax.broadcasted_iota(jnp.int32, (1, ROWS), 1)
    counts = jnp.zeros((1, ROWS), f32)
    for offset in range(5):
        hit = jnp.sum((window == own + (offset - 2)).astype(f32), axis=1, keepdims=True)
        counts = jnp.where(lane == offset, hit[0:1], counts)
        counts = jnp.where(lane == 8 + offset, hit[1:2], counts)
    counts = jnp.where(counts > 0.0, jnp.log2(jnp.maximum(counts, 1.0)), ABSENT)
    gain_rows = [
        jnp.concatenate([gain_ref[layer, 0:1], gain_ref[layer, 1:2]], axis=1) for layer in range(2)
    ]
    rows_ref[...] = jnp.concatenate(
        [level, spread_sq, c_input] + gain_rows + [counts, jnp.zeros((2, ROWS), f32)], axis=0
    )
    for row in range(6):
        part = slice((row % 2) * LANES, (row % 2 + 1) * LANES)
        tile_ref[row : row + 1, :] = positions_ref[row // 2 : row // 2 + 1, part]
    pairs = pairs_ref[...]
    codes = (pairs[0:1] * 64 + pairs[1:2]).astype(f32)
    tile_ref[6:7, :] = jnp.concatenate([codes, codes], axis=1)
    tile_ref[7:8, :] = jnp.zeros((1, LANES), f32)
    columns = jnp.concatenate(
        [pos_weight_ref[...], gain_ref[0, 0:1], jnp.zeros((4, LANES), f32)], axis=0
    ).T
    identity = (
        lax.broadcasted_iota(jnp.int32, (LANES, LANES), 0)
        == lax.broadcasted_iota(jnp.int32, (LANES, LANES), 1)
    ).astype(f32).astype(bf16)
    stream = dot_nt(identity, single_ref[...])
    for comp in range(3):
        stream = stream + columns[:, comp : comp + 1] * (positions_ref[comp : comp + 1, :] * c_input)
    stream_ref[...] = stream
    normed_ref[...] = (norm_columns(stream) * columns[:, 3:4]).astype(bf16).T


def run_layer(layer, first_ref, halo, stream_ref, rows_ref, head_rows, weights, scratch, finish):
    even_ref, own_ref, odd_ref = halo
    w_query_ref, w_key_ref, w_value_ref, w_out_ref, w_gate_up_ref, w_down_ref = weights
    near, keys, values, attended = scratch
    head_size = LANES // HEADS
    query_scale = LOG2E * head_size ** -0.5
    near[ROWS : 2 * ROWS, :] = own_ref[...]

    @pl.when(first_ref[0] % 2 == 0)
    def _():
        near[:ROWS, :] = odd_ref[...]
        near[2 * ROWS :, :] = even_ref[...]

    @pl.when(first_ref[0] % 2 == 1)
    def _():
        near[:ROWS, :] = even_ref[...]
        near[2 * ROWS :, :] = odd_ref[...]

    row_block = lax.broadcasted_iota(jnp.int32, (3 * ROWS, LANES), 0) // LANES
    lane = lax.broadcasted_iota(jnp.int32, (3 * ROWS, LANES), 1)
    keys[:, LANES:] = jnp.where((lane % 16 == row_block) & (lane < 32), 1.0, 0.0).astype(bf16)
    window = rows_ref[5:6, :LANES]
    rows = []
    for chunk in range(6):
        sides = []
        for block in range(2):
            offset = chunk - block
            if 0 <= offset < 5:
                lane_id = block * 8 + offset
                sides.append(jnp.broadcast_to(window[:, lane_id : lane_id + 1], (1, LANES)))
            else:
                sides.append(jnp.full((1, LANES), ABSENT, f32))
        rows.append(jnp.concatenate(sides, axis=1))
    rows = jnp.concatenate(rows + [jnp.zeros((10, ROWS), f32)], axis=0)
    high = rows.astype(bf16)
    low = (rows - high.astype(f32)).astype(bf16)
    bias = jnp.concatenate([high, low, jnp.zeros((LANES - 32, ROWS), bf16)], axis=0)

    keys[:, :LANES] = dot(near[...], w_key_ref[layer]).astype(bf16)
    query_t = (dot_nt(w_query_ref[layer].T, own_ref[...]) * query_scale).astype(bf16)
    value_t = dot_nt(w_value_ref[layer].T, near[...]).astype(bf16)
    for head in range(HEADS):
        values[head * 48 : head * 48 + 32, :] = value_t[head * 32 : head * 32 + 32]
        values[head * 48 + 32 : head * 48 + 48, :] = jnp.ones((16, 3 * ROWS), bf16)

    def attend(exact):
        pieces = []
        sums = []

        def scores_of(head):
            parts = []
            if head:
                parts.append(jnp.zeros((head * head_size, ROWS), bf16))
            parts.append(query_t[head * head_size : (head + 1) * head_size])
            if head < HEADS - 1:
                parts.append(jnp.zeros(((HEADS - 1 - head) * head_size, ROWS), bf16))
            return dot(keys[...], jnp.concatenate(parts + [bias], axis=0))

        following = scores_of(0)
        for head in range(HEADS):
            scores = following
            if head < HEADS - 1:
                following = scores_of(head + 1)
            if exact:
                scores = scores - jnp.max(scores, axis=0, keepdims=True)
            blank = jnp.zeros((LANES, LANES), bf16)
            weights_t = jnp.concatenate(
                [
                    jnp.concatenate([jnp.exp2(scores[: 5 * LANES, :LANES]).astype(bf16), blank], axis=0),
                    jnp.concatenate([blank, jnp.exp2(scores[LANES:, LANES:]).astype(bf16)], axis=0),
                ],
                axis=1,
            )
            mixed = dot(values[head * 48 : (head + 1) * 48, :], weights_t)
            total = mixed[head_size : head_size + 1]
            sums.append(total)
            pieces.append(mixed[:head_size] * (1.0 / total))
        attended[...] = jnp.concatenate(pieces, axis=0).astype(bf16)
        return jnp.concatenate(sums, axis=0)

    gains = jnp.concatenate(
        [rows_ref[3 + index // 2 : 4 + index // 2, (index % 2) * LANES : (index % 2 + 1) * LANES] for index in range(4)]
        + [head_rows],
        axis=0,
    ).T
    def run(exact):
        sums = attend(exact)
        now = stream_ref[...] + dot(w_out_ref[layer].T, attended[...])
        normed = (norm_columns(now) * gains[:, 2 * layer + 1 : 2 * layer + 2]).astype(bf16)
        gate_up = dot(w_gate_up_ref[layer].T, normed)
        width = gate_up.shape[0] // 2
        half, up = 0.5 * gate_up[:width], gate_up[width:]
        hidden = ((half + half * jnp.tanh(half)) * up).astype(bf16)
        finish(now + dot(w_down_ref[layer].T, hidden), gains)
        return sums

    sums = run(False)
    safe = (jnp.min(sums) > 2.0**-80) & (jnp.max(sums) < 2.0**100)

    @pl.when(jnp.logical_not(safe))
    def _():
        run(True)


def first_layer_kernel(first_ref, even_ref, own_ref, odd_ref, stream_ref, rows_ref, *refs):
    weights, (out_ref, normed_ref), scratch = refs[:6], refs[6:8], refs[8:]

    def finish(stream, columns):
        out_ref[...] = stream
        normed_ref[...] = (norm_columns(stream) * columns[:, 2:3]).astype(bf16).T

    halo = (even_ref, own_ref, odd_ref)
    run_layer(0, first_ref, halo, stream_ref, rows_ref, jnp.zeros((4, LANES), f32), weights, scratch, finish)


def last_layer_kernel(first_ref, even_ref, own_ref, odd_ref, stream_ref, rows_ref, *refs):
    weights, (positions_ref, noise_ref, force_ref, w_head_ref) = refs[:6], refs[6:10]
    out_ref, scratch = refs[10], refs[11:]
    level, spread_sq, c_input = rows_ref[0:1], rows_ref[1:2], rows_ref[2:3]
    positions = jnp.concatenate([positions_ref[...], jnp.zeros((5, ROWS), f32)], axis=0)
    fresh = jnp.concatenate([noise_ref[...], jnp.zeros((5, ROWS), f32)], axis=0)

    def finish(stream, columns):
        final = norm_columns(stream)
        update = jnp.concatenate(
            [jnp.sum(columns[:, 4 + comp : 5 + comp] * final, axis=0, keepdims=True) for comp in range(3)]
            + [jnp.zeros((5, ROWS), f32)],
            axis=0,
        )
        denoised = positions * (1.0 / spread_sq) + (level * c_input) * update
        following = 0.85 * level
        result = denoised + STEER * force_ref[...]
        result = result + following * (0.8 * (positions - denoised) / level + 0.6 * fresh)
        out_ref[...] = result[:3]

    halo = (even_ref, own_ref, odd_ref)
    head_rows = jnp.concatenate([w_head_ref[...], jnp.zeros((1, LANES), f32)], axis=0)
    run_layer(1, first_ref, halo, stream_ref, rows_ref, head_rows, weights, scratch, finish)


def body(
    positions,
    fresh_noise,
    timestep,
    atom_single,
    pos_weight,
    ln_gain,
    w_query,
    w_key,
    w_value,
    w_out,
    w_gate_up,
    w_down,
    w_head,
    key_window,
    block_pairs,
    pair_count,
    bond_atoms,
):
    devices = lax.axis_size("atom")
    first = lax.axis_index("atom").astype(jnp.int32).reshape(1)
    smem = pl.BlockSpec(memory_space=pltpu.SMEM)
    vmem = pl.BlockSpec(memory_space=pltpu.VMEM)
    hbm = pl.BlockSpec(memory_space=pltpu.HBM)
    rows = atom_single.shape[0]

    def from_neighbours(array):
        even = [(i, i ^ 1) for i in range(devices)]
        odd = [(i, ((i + 1) ^ 1) - 1) for i in range(1, devices - 1)]
        return lax.ppermute(array, "atom", even), lax.ppermute(array, "atom", odd)

    stream, normed, schedule, tile = pl.pallas_call(
        prepare_kernel,
        out_shape=(
            jax.ShapeDtypeStruct((LANES, rows), f32),
            jax.ShapeDtypeStruct((rows, LANES), bf16),
            jax.ShapeDtypeStruct((8, rows), f32),
            jax.ShapeDtypeStruct((8, LANES), f32),
        ),
        in_specs=[smem] + [hbm] * 7,
        out_specs=(vmem,) * 4,
        scratch_shapes=[
            pltpu.SMEM(timestep.shape, jnp.int32),
            pltpu.VMEM(positions.shape, f32),
            pltpu.VMEM(atom_single.shape, bf16),
            pltpu.VMEM(pos_weight.shape, f32),
            pltpu.VMEM(ln_gain.shape, f32),
            pltpu.VMEM(block_pairs.shape, jnp.int32),
            pltpu.VMEM(key_window.shape, jnp.int32),
            pltpu.SemaphoreType.DMA((7,)),
        ],
        compiler_params=pltpu.CompilerParams(vmem_limit_bytes=VMEM_GRANT),
    )(first, timestep, positions, atom_single, pos_weight, ln_gain, block_pairs, key_window)
    even, odd = from_neighbours(normed)

    packed = pl.pallas_call(
        pack_kernel,
        out_shape=jax.ShapeDtypeStruct((devices, 8, LANES), f32),
        in_specs=[smem, vmem],
        out_specs=vmem,
        cost_estimate=pl.CostEstimate(flops=40_000_000, bytes_accessed=10_000_000, transcendentals=1_000_000),
        compiler_params=pltpu.CompilerParams(vmem_limit_bytes=VMEM_SMALL),
    )(pair_count, tile)
    tiles = lax.all_to_all(packed, "atom", 0, 0)

    weights = (w_query, w_key, w_value, w_out, w_gate_up, w_down)
    layer_scratch = [
        pltpu.VMEM((3 * rows, LANES), bf16),
        pltpu.VMEM((3 * rows, 2 * LANES), bf16),
        pltpu.VMEM((HEADS * 48, 3 * rows), bf16),
        pltpu.VMEM((LANES, rows), bf16),
    ]
    layer_cost = pl.CostEstimate(flops=2_000_000_000, bytes_accessed=20_000_000, transcendentals=2_000_000)
    stream, normed = pl.pallas_call(
        first_layer_kernel,
        out_shape=(
            jax.ShapeDtypeStruct((LANES, rows), f32),
            jax.ShapeDtypeStruct((rows, LANES), bf16),
        ),
        in_specs=[smem] + [vmem] * 11,
        out_specs=(vmem, vmem),
        scratch_shapes=layer_scratch,
        cost_estimate=layer_cost,
        compiler_params=pltpu.CompilerParams(vmem_limit_bytes=VMEM_SMALL),
    )(first, even, normed, odd, stream, schedule, *weights)
    even, odd = from_neighbours(normed)

    force = pl.pallas_call(
        force_kernel,
        out_shape=jax.ShapeDtypeStruct((8, 2 * LANES), f32),
        in_specs=[smem, vmem, vmem, vmem],
        out_specs=vmem,
        scratch_shapes=[
            pltpu.VMEM((6, LANES, LANES), f32),
            pltpu.VMEM((6, LANES, LANES), f32),
            pltpu.VMEM((8, LANES), jnp.int32),
            pltpu.VMEM((8, LANES), f32),
            pltpu.SMEM((8, LANES), jnp.int32),
            pltpu.SMEM((8, LANES), f32),
            pltpu.SemaphoreType.DMA((2,)),
        ],
        cost_estimate=pl.CostEstimate(flops=80_000_000, bytes_accessed=16_000_000, transcendentals=2_000_000),
        compiler_params=pltpu.CompilerParams(vmem_limit_bytes=VMEM_SMALL),
    )(first, tiles, positions, bond_atoms)

    return pl.pallas_call(
        last_layer_kernel,
        out_shape=jax.ShapeDtypeStruct(positions.shape, f32),
        in_specs=[smem] + [vmem] * 15,
        out_specs=vmem,
        scratch_shapes=layer_scratch,
        cost_estimate=layer_cost,
        compiler_params=pltpu.CompilerParams(vmem_limit_bytes=VMEM_SMALL),
    )(
        first,
        even,
        normed,
        odd,
        stream,
        schedule,
        *weights,
        positions,
        fresh_noise,
        force,
        w_head,
    )


def solution(mesh):
    in_specs = (
        P(None, ("sample", "atom")),
        P(None, ("sample", "atom")),
        P(),
        P("atom", None),
        P(),
        P(),
        P(),
        P(),
        P(),
        P(),
        P(),
        P(),
        P(),
        P("atom", None),
        P(None, "atom"),
        P("atom"),
        P(None, "atom", None),
    )
    out_specs = P(None, ("sample", "atom"))
    return jax.shard_map(body, mesh=mesh, in_specs=in_specs, out_specs=out_specs, check_vma=False)
```
